32 devices in a mesh: dp: 8 (over y, x, core), ffn: 4 (over z).
Axes of the slice: x: 2, y: 2, z: 4, core: 2. Of those that a mesh axis runs over, the one named last changes fastest.
Arguments:
- text_hidden: bfloat16 [16384, 768], P(('dp', 'ffn')), may hold values from -6 to 6
- visual_maps: bfloat16 [1568, 2048], P(('dp', 'ffn')), may hold values from -1200 to 1200
- patch_order: int32 [32, 49], P(('dp', 'ffn')), may hold values from 0 to 48, each once within a row
- segment_ids: int32 [32, 561], P(('dp', 'ffn')), may hold values from 0 to 2, never falling along the last dimension, each value on 1 to 280 neighbouring positions
- rel_bucket: int32 [32, 561, 561], P(('dp', 'ffn')), may hold values from 0 to 31
- x_bucket: int32 [32, 561, 561], P(('dp', 'ffn')), may hold values from 0 to 63
- y_bucket: int32 [32, 561, 561], P(('dp', 'ffn')), may hold values from 0 to 63
- bn_scale: float32 [2048], replicated, may hold values from 0.1 to 1.9
- bn_shift: float32 [2048], replicated, may hold values from -3 to 3
- vis_proj: bfloat16 [2048, 768], P(('dp', 'ffn')), may hold values from -0.125 to 0.125
- w_query: bfloat16 [768, 768], P(('dp', 'ffn')), may hold values from -0.21875 to 0.21875
- w_key: bfloat16 [768, 768], P(('dp', 'ffn')), may hold values from -0.21875 to 0.21875
- w_value: bfloat16 [768, 768], P(('dp', 'ffn')), may hold values from -0.21875 to 0.21875
- w_output: bfloat16 [768, 768], P(('dp', 'ffn')), may hold values from -0.625 to 0.625
- rel_table: float32 [32, 12], replicated, may hold values from -4 to 4
- x_table: float32 [64, 12], replicated, may hold values from -4 to 4
- y_table: float32 [64, 12], replicated, may hold values from -4 to 4
- first_gain: float32 [768], replicated, may hold values from 0.1 to 1.9
- first_bias: float32 [768], replicated, may hold values from -2 to 2
- w_inner: bfloat16 [768, 3072], P('dp', 'ffn'), may hold values from -0.21875 to 0.21875
- b_inner: float32 [3072], replicated, may hold values from -2 to 2
- w_outer: bfloat16 [3072, 768], P('ffn', 'dp'), may hold values from -0.109375 to 0.109375
- b_outer: float32 [768], replicated, may hold values from -2 to 2
- second_gain: float32 [768], replicated, may hold values from 0.1 to 1.9
- second_bias: float32 [768], replicated, may hold values from -2 to 2
- cotangent: bfloat16 [17952, 768], P(('dp', 'ffn')), may hold values from -6 to 6
Outputs:
- output: bfloat16 [17952, 768], P(('dp', 'ffn'))
- text_grad: float32 [16384, 768], P(('dp', 'ffn'))
- visual_grad: float32 [1568, 2048], P(('dp', 'ffn'))
- bn_scale_grad: float32 [2048], replicated
- bn_shift_grad: float32 [2048], replicated
- vis_proj_grad: float32 [2048, 768], P(('dp', 'ffn'))
- w_query_grad: float32 [768, 768], P(('dp', 'ffn'))
- w_key_grad: float32 [768, 768], P(('dp', 'ffn'))
- w_value_grad: float32 [768, 768], P(('dp', 'ffn'))
- w_output_grad: float32 [768, 768], P(('dp', 'ffn'))
- rel_table_grad: float32 [32, 12], replicated
- x_table_grad: float32 [64, 12], replicated
- y_table_grad: float32 [64, 12], replicated
- first_gain_grad: float32 [768], replicated
- first_bias_grad: float32 [768], replicated
- w_inner_grad: float32 [768, 3072], P('dp', 'ffn')
- b_inner_grad: float32 [3072], replicated
- w_outer_grad: float32 [3072, 768], P('ffn', 'dp')
- b_outer_grad: float32 [768], replicated
- second_gain_grad: float32 [768], replicated
- second_bias_grad: float32 [768], replicated
The draws below stay inside these ranges and needn't reach their ends.
Inputs may be any that keep to these rules, and one draw needn't show every extreme that they name: Each row of patch_order names every one of the 49 cells of its packed row once. `segment_ids`: document numbers never fall along a packed row.
All inputs are finite; a program needn't handle non-finite values.
Results may differ from the reference program's by a relative error of at most 0.019.
Values may be sent and summed in bfloat16 or wider, within the bound.
No kernel may reach another device: no remote copies, remote signals or barrier semaphores. Data moves between devices by JAX's collectives and lax.ppermute only.
A program may use at most 320 MiB of HBM per device.

```python
import math
import jax
import jax.numpy as jnp
import numpy as np
from jax import lax

D = 768
H = 12
FF = 3072
CH = 2048
NB1 = 32
NB2 = 64
VIS = 49
TEXT = 512
SEQ = 561
SEQS = 32


def draw_visual_maps(key, part):
    rows = SEQS * VIS
    keys = jax.random.split(key, 4)
    row_place = jnp.arange(rows, dtype=jnp.float32) / max(rows - 1, 1)
    row_scale = jnp.exp(jnp.log(3.0) * row_place) * jnp.exp(jax.random.uniform(keys[0], (rows,), jnp.float32, 0.0, jnp.log(4.0)))
    col_scale = jnp.exp(jax.random.uniform(keys[1], (CH,), jnp.float32, 0.0, jnp.log(10.0)))
    offset = jnp.clip(jax.random.normal(keys[2], (CH,), jnp.float32), -3.0, 3.0)
    base = jnp.clip(jax.random.normal(keys[3], (rows, CH), jnp.float32), -5.0, 5.0)
    values = base * row_scale[:, None] + offset[None, :]
    return (values * col_scale[None, :]).astype(jnp.bfloat16)


def touch_ends(drawn, stream_key, smallest, largest):
    spot = [jax.random.randint(jax.random.fold_in(stream_key, axis), (), 0, length) for axis, length in enumerate(drawn.shape)]
    longest = drawn.shape.index(max(drawn.shape))
    beside = spot[:longest] + [(spot[longest] + 1) % drawn.shape[longest]] + spot[longest + 1:]
    return drawn.at[tuple(spot)].set(smallest).at[tuple(beside)].set(largest)


def level_of(key, shape, pieces, low, largest):
    level = 1.0
    for position, blocks in pieces:
        heights = jax.random.uniform(jax.random.fold_in(jax.random.fold_in(key, 6), position), (blocks,), jnp.float32, low / len(pieces), largest / len(pieces))
        level = level * jnp.repeat(jnp.exp(heights), shape[position] // blocks).reshape((-1,) + (1,) * (len(shape) - 1 - position))
    return level


def split_up(number_of, total, limit, skew):
    loads = [(1 << 20) // math.isqrt(rank ** skew) + 1 for rank in range(2, number_of + 1)]
    spare, holding = total - limit - (number_of - 1), [1] * (number_of - 1)
    while spare > 0:
        movable = [i for i in range(number_of - 1) if holding[i] < limit]
        pool, budget = sum([loads[i] for i in movable]), spare
        for i in movable:
            addition = min(limit - holding[i], max(1, budget * loads[i] // pool), spare)
            holding[i] = holding[i] + addition
            spare = spare - addition
    return np.array([limit] + holding)


def ragged_sizes(stream_key, amount, total, limit, lean):
    if amount == 2:
        one = jax.random.randint(stream_key, (), max(1, total - limit), min(limit, total - 1) + 1)
        return jnp.stack([one, total - one])
    sizes = jnp.asarray(split_up(amount, total, limit, lean), jnp.int32)
    pairs = (amount - 1) // 2
    donor, sink = sizes[1:1 + 2 * pairs:2], sizes[2:2 + 2 * pairs:2]
    room = jnp.minimum(donor - 1, limit - sink)
    shifted = jax.random.randint(jax.random.fold_in(stream_key, 1), (pairs,), 0, 1 << 20) % (room + 1)
    sizes = sizes.at[1:1 + 2 * pairs:2].set(donor - shifted).at[2:2 + 2 * pairs:2].set(sink + shifted)
    return sizes[jax.random.permutation(jax.random.fold_in(stream_key, 2), amount)]


def noise(stream_key, shape, scale, most, pieces=(), held_as=jnp.bfloat16):
    factor_of = level_of(stream_key, shape, pieces, -0.22, 0.18) if pieces else 1.0
    values = jax.random.normal(stream_key, shape, jnp.float32) * scale * factor_of
    return jnp.minimum(jnp.maximum(values, -most), most).astype(held_as)


def setup_inputs(seed: int = 0) -> dict:
    streams_of = jax.random.split(jax.random.key(seed), 27)
    text_hidden = noise(streams_of[0], (SEQS * TEXT, D), 1.0, 6.0, ((0, 32),))
    visual_maps = draw_visual_maps(jax.random.fold_in(streams_of[26], 71), 0)
    patch_order = jax.vmap(lambda own: jax.random.permutation(own, VIS))(jax.random.split(streams_of[2], SEQS)).reshape((SEQS, VIS)).astype(jnp.int32)
    segment_ids = jax.vmap(lambda own: jnp.searchsorted(jnp.cumsum(ragged_sizes(own, 3, SEQ, SEQ // 2, 2)), jnp.arange(SEQ), side="right"))(jax.random.split(streams_of[3], SEQS)).reshape((SEQS, SEQ)).astype(jnp.int32)
    rel_bucket = touch_ends(jax.random.randint(streams_of[4], (SEQS, SEQ, SEQ), 0, NB1), jax.random.fold_in(streams_of[4], 1), 0, NB1 - 1).astype(jnp.int32)
    x_bucket = touch_ends(jax.random.randint(streams_of[5], (SEQS, SEQ, SEQ), 0, NB2), jax.random.fold_in(streams_of[5], 1), 0, NB2 - 1).astype(jnp.int32)
    y_bucket = touch_ends(jax.random.randint(streams_of[6], (SEQS, SEQ, SEQ), 0, NB2), jax.random.fold_in(streams_of[6], 1), 0, NB2 - 1).astype(jnp.int32)
    bn_scale = jnp.clip(1.0 + 0.18 * jax.random.normal(streams_of[7], (CH,), jnp.float32), 0.1, 1.9)
    bn_shift = noise(streams_of[8], (CH,), 0.5, 3.0, (), jnp.float32)
    vis_proj = noise(streams_of[9], (CH, D), CH ** -0.5, 0.125, ((0, 32),))
    w_query = noise(streams_of[10], (D, D), D ** -0.5, 0.21875, ((0, 32),))
    w_key = noise(streams_of[11], (D, D), D ** -0.5, 0.21875, ((0, 32),))
    w_value = noise(streams_of[12], (D, D), D ** -0.5, 0.21875, ((0, 32),))
    w_output = noise(streams_of[13], (D, D), (D // 8) ** -0.5, 0.625, ((0, 32),))
    rel_table = noise(streams_of[14], (NB1, H), 1.0, 4.0, (), jnp.float32)
    x_table = noise(streams_of[15], (NB2, H), 1.0, 4.0, (), jnp.float32)
    y_table = noise(streams_of[16], (NB2, H), 1.0, 4.0, (), jnp.float32)
    first_gain = jnp.clip(1.0 + 0.18 * jax.random.normal(streams_of[17], (D,), jnp.float32), 0.1, 1.9)
    first_bias = noise(streams_of[18], (D,), 0.3, 2.0, (), jnp.float32)
    w_inner = noise(streams_of[19], (D, FF), D ** -0.5, 0.21875, ((0, 8), (1, 4)))
    b_inner = noise(streams_of[20], (FF,), 0.3, 2.0, (), jnp.float32)
    w_outer = noise(streams_of[21], (FF, D), FF ** -0.5, 0.109375, ((0, 4), (1, 8)))
    b_outer = noise(streams_of[22], (D,), 0.3, 2.0, (), jnp.float32)
    second_gain = jnp.clip(1.0 + 0.18 * jax.random.normal(streams_of[23], (D,), jnp.float32), 0.1, 1.9)
    second_bias = noise(streams_of[24], (D,), 0.3, 2.0, (), jnp.float32)
    cotangent = noise(streams_of[25], (SEQS * SEQ, D), 1.0, 6.0, ((0, 32),))
    return dict(text_hidden=text_hidden, visual_maps=visual_maps, patch_order=patch_order, segment_ids=segment_ids, rel_bucket=rel_bucket, x_bucket=x_bucket, y_bucket=y_bucket, bn_scale=bn_scale, bn_shift=bn_shift, vis_proj=vis_proj, w_query=w_query, w_key=w_key, w_value=w_value, w_output=w_output, rel_table=rel_table, x_table=x_table, y_table=y_table, first_gain=first_gain, first_bias=first_bias, w_inner=w_inner, b_inner=b_inner, w_outer=w_outer, b_outer=b_outer, second_gain=second_gain, second_bias=second_bias, cotangent=cotangent)


EPS = 1e-05
NEG = -1e+30
HIGH = lax.Precision.HIGHEST

@jax.custom_vjp
def low(v):
    return lax.optimization_barrier(v.astype(jnp.bfloat16)).astype(jnp.float32)

@jax.custom_vjp
def low_back(v):
    return v

def low_keep(v):
    return (low(v), None)

def low_pass(kept, grad):
    return (grad,)

def back_keep(v):
    return (v, None)

def back_low(kept, grad):
    return (low(grad),)
low.defvjp(low_keep, low_pass)
low_back.defvjp(back_keep, back_low)

def norm_layer(values, gain, bias):
    center = values - lax.optimization_barrier(jnp.mean(values, -1, keepdims=True))
    spread = lax.optimization_barrier(jnp.mean(center * center, -1, keepdims=True))
    return center * lax.rsqrt(spread + EPS) * gain + bias

def project(values, weight):
    return jnp.einsum('...d,de->...e', values, weight, precision=HIGH)

def table_bias(table, bucket):
    return jnp.moveaxis(table[bucket], -1, 1)

def encoder_block(hidden, segment, rel_ids, x_ids, y_ids, weights):
    w_query, w_key, w_value, w_output, rel_table, x_table, y_table, first_gain, first_bias, w_inner, b_inner, w_outer, b_outer, second_gain, second_bias = weights
    groups, length, width = hidden.shape
    heads = rel_table.shape[1]
    head_size = width // heads
    lowered = low(hidden)
    query = low(low_back(project(lowered, w_query))).reshape(groups, length, heads, head_size)
    key_rows = low(low_back(project(lowered, w_key))).reshape(groups, length, heads, head_size)
    value_rows = low(low_back(project(lowered, w_value))).reshape(groups, length, heads, head_size)
    raw = low_back(jnp.einsum('gihe,gjhe->ghij', query, key_rows, precision=HIGH))
    scores = raw * head_size ** (-0.5) + table_bias(rel_table, rel_ids)
    scores = scores + table_bias(x_table, x_ids) + table_bias(y_table, y_ids)
    allowed = (segment[:, :, None] == segment[:, None, :])[:, None]
    scores = jnp.where(allowed, scores, NEG)
    peak = lax.optimization_barrier(jnp.max(scores, -1, keepdims=True))
    expo = jnp.exp(scores - peak)
    probs = low(expo / lax.optimization_barrier(jnp.sum(expo, -1, keepdims=True)))
    mixed = jnp.einsum('ghij,gjhe->gihe', probs, value_rows, precision=HIGH).reshape(groups, length, width)
    attended = low_back(project(low(low_back(mixed)), w_output))
    first = norm_layer(hidden + attended, first_gain, first_bias)
    inner = low_back(project(low(first), w_inner)) + b_inner
    activated = low(jax.nn.gelu(inner, approximate=True))
    outer = low_back(project(activated, w_outer)) + b_outer
    return norm_layer(first + outer, second_gain, second_bias)

def forward(text_rows, visual, bn_scale, bn_shift, vis_proj, w_query, w_key, w_value, w_output, rel_table, x_table, y_table, first_gain, first_bias, w_inner, b_inner, w_outer, b_outer, second_gain, second_bias, patch_order, segment_ids, rel_bucket, x_bucket, y_bucket):
    center = visual - lax.optimization_barrier(jnp.mean(visual, 0))
    spread = lax.optimization_barrier(jnp.mean(center * center, 0))
    normed = low(center * lax.rsqrt(spread + EPS) * bn_scale + bn_shift)
    tokens = low_back(project(normed, vis_proj)).reshape(SEQS, VIS, D)
    picker = (patch_order[:, :, None] == jnp.arange(VIS, dtype=jnp.int32)[None, None, :]).astype(tokens.dtype)
    tokens = jnp.einsum('sjc,scd->sjd', picker, tokens, precision=HIGH)
    hidden = jnp.concatenate([text_rows.reshape(SEQS, TEXT, D), tokens], 1)
    group_size = 4 if SEQS % 4 == 0 else 1
    weights = (w_query, w_key, w_value, w_output, rel_table, x_table, y_table, first_gain, first_bias, w_inner, b_inner, w_outer, b_outer, second_gain, second_bias)

    def shaped(array):
        return array.reshape((SEQS // group_size, group_size) + array.shape[1:])

    def group_step(items):
        return encoder_block(items[0], items[1], items[2], items[3], items[4], weights)
    result = lax.map(jax.checkpoint(group_step), (shaped(hidden), shaped(segment_ids), shaped(rel_bucket), shaped(x_bucket), shaped(y_bucket)))
    return result.reshape(SEQS * SEQ, D)

def reference(text_hidden, visual_maps, patch_order, segment_ids, rel_bucket, x_bucket, y_bucket, bn_scale, bn_shift, vis_proj, w_query, w_key, w_value, w_output, rel_table, x_table, y_table, first_gain, first_bias, w_inner, b_inner, w_outer, b_outer, second_gain, second_bias, cotangent):
    floats = (text_hidden.astype(jnp.float32), visual_maps.astype(jnp.float32), bn_scale, bn_shift, vis_proj.astype(jnp.float32), w_query.astype(jnp.float32), w_key.astype(jnp.float32), w_value.astype(jnp.float32), w_output.astype(jnp.float32), rel_table, x_table, y_table, first_gain, first_bias, w_inner.astype(jnp.float32), b_inner, w_outer.astype(jnp.float32), b_outer, second_gain, second_bias)

    def wrapped(*values):
        return forward(*values, patch_order, segment_ids, rel_bucket, x_bucket, y_bucket)
    result, pullback = jax.vjp(wrapped, *floats)
    grads = pullback(cotangent.astype(jnp.float32))
    return (result.astype(jnp.bfloat16), grads[0], grads[1], grads[2], grads[3], grads[4], grads[5], grads[6], grads[7], grads[8], grads[9], grads[10], grads[11], grads[12], grads[13], grads[14], grads[15], grads[16], grads[17], grads[18], grads[19])
```

```python
import functools

import jax
import jax.numpy as jnp
from jax import lax
from jax.experimental import pallas as pl
from jax.experimental.pallas import tpu as pltpu
from jax.sharding import PartitionSpec as P

EPS = 1e-05
NEG = -1e30
F32 = jnp.float32
BF16 = jnp.bfloat16
ALL = ("dp", "ffn")
LEVELS = 21845.0
MIB = 2**20


def dot_nn(a, b):
    return lax.dot_general(a, b, (((1,), (0,)), ((), ())), preferred_element_type=F32)


def dot_nt(a, b):
    return lax.dot_general(a, b, (((1,), (1,)), ((), ())), preferred_element_type=F32)


def dot_tn(a, b):
    return lax.dot_general(a, b, (((0,), (0,)), ((), ())), preferred_element_type=F32)


def pad_rows(values, rows):
    return jnp.pad(values, ((0, rows - values.shape[0]), (0, 0)))


def send_dp(values, bits):
    size = lax.axis_size("dp")
    return lax.ppermute(values, "dp", [(i, i ^ bits) for i in range(size)])


def send_ffn(values, shift):
    size = lax.axis_size("ffn")
    return lax.ppermute(values, "ffn", [(i, (i + shift) % size) for i in range(size)])


def swap_ffn(values, bits):
    size = lax.axis_size("ffn")
    return lax.ppermute(values, "ffn", [(i, i ^ bits) for i in range(size)])


def exchanges():
    steps = []
    bit = 1
    while bit < lax.axis_size("dp"):
        steps.append(functools.partial(send_dp, bits=bit))
        bit *= 2
    bit = 1
    while bit < lax.axis_size("ffn"):
        steps.append(functools.partial(swap_ffn, bits=bit))
        bit *= 2
    return steps


def sum_all(values):
    for step in exchanges():
        values = values + step(values)
    return values


def moments_all(mean, spread, rows):
    pack = jnp.stack([mean, spread])
    for step in exchanges():
        other = step(pack)
        gap = pack[0] - other[0]
        pack = jnp.stack(
            [(pack[0] + other[0]) * 0.5, pack[1] + other[1] + gap * gap * (rows * 0.5)]
        )
        rows = rows * 2
    return pack[0], pack[1] / rows


def gather_ffn(shard):
    size = lax.axis_size("ffn")
    here = lax.axis_index("ffn")
    parts = [shard] + [send_ffn(shard, k) for k in range(1, size)]
    slots = []
    for slot in range(size):
        value = parts[0]
        for k in range(1, size):
            value = jnp.where((here - k + size) % size == slot, parts[k], value)
        slots.append(value)
    return jnp.stack(slots)


def gather_quads(block):
    quads = lax.axis_size("dp") // 2
    if quads != 4:
        return [block] + [send_dp(block, 2 * k) for k in range(1, quads)]
    half = block.shape[0] // 2
    from_x = send_dp(block, 2)
    from_y = send_dp(block, 4)
    low = send_dp(from_x[:half], 4)
    high = send_dp(from_y[half:], 2)
    return [block, from_x, from_y, (low, high)]


def scatter_all(blocks):
    quads = lax.axis_size("dp") // 2
    size = lax.axis_size("ffn")
    place = lax.axis_index("dp")
    core, quad = place % 2, place // 2
    here = lax.axis_index("ffn")
    blocks = blocks.reshape((quads, 2) + blocks.shape[1:])
    away = lax.dynamic_index_in_dim(blocks, 1 - core, 1, keepdims=False)
    mine = lax.dynamic_index_in_dim(blocks, core, 1, keepdims=False)
    mine = (mine.astype(F32) + send_dp(away, 1).astype(F32)).astype(BF16)

    def of_quad(k):
        return lax.dynamic_index_in_dim(mine, quad ^ k, 0, keepdims=False)

    if quads == 4:
        own, to_x, to_y, diag = [of_quad(k) for k in range(4)]
        half = diag.shape[1] // 2
        low = send_dp(diag[:, :half], 4)
        high = send_dp(diag[:, half:], 2)
        to_x = jnp.concatenate(
            [(to_x[:, :half].astype(F32) + low.astype(F32)).astype(BF16), to_x[:, half:]], 1
        )
        to_y = jnp.concatenate(
            [to_y[:, :half], (to_y[:, half:].astype(F32) + high.astype(F32)).astype(BF16)], 1
        )
        own = own.astype(F32) + send_dp(to_x, 2).astype(F32) + send_dp(to_y, 4).astype(F32)
    else:
        own = of_quad(0).astype(F32)
        for k in range(1, quads):
            own = own + send_dp(of_quad(k), 2 * k).astype(F32)
    total = lax.dynamic_index_in_dim(own, here, 0, keepdims=False)
    own = own.astype(BF16)
    for k in range(1, size):
        piece = lax.dynamic_index_in_dim(own, (here + k) % size, 0, keepdims=False)
        total = total + send_ffn(piece, k).astype(F32)
    return total


def place_kernel(layout, place_ref, *refs):
    count = len(layout)
    parts = refs[: -count - 1]
    outs = refs[-count - 1 : -1]
    sems = refs[-1]
    copies = []
    for n, pieces in enumerate(parts):
        device = place_ref[n]
        for m, (begin, rows) in enumerate(layout):
            copy = pltpu.make_async_copy(
                pieces.at[pl.ds(begin, rows), :],
                outs[m].at[pl.ds(pl.multiple_of(device * rows, 16), rows), :],
                sems.at[n, m],
            )
            copy.start()
            copies.append(copy)
    for copy in copies:
        copy.wait()


def place_blocks(parts, places, layout):
    width = parts[0].shape[1]
    count = len(parts)
    return pl.pallas_call(
        functools.partial(place_kernel, layout),
        in_specs=[pl.BlockSpec(memory_space=pltpu.SMEM)]
        + [pl.BlockSpec(memory_space=pl.ANY)] * count,
        out_specs=[pl.BlockSpec(memory_space=pl.ANY)] * len(layout),
        out_shape=[jax.ShapeDtypeStruct((rows * count, width), BF16) for _, rows in layout],
        scratch_shapes=[pltpu.SemaphoreType.DMA((count, len(layout)))],
        name="place_blocks",
    )(places, *parts)


def bias_kernel(rows_step, rel_ref, x_ref, y_ref, tab_ref, out_ref):
    pairs = out_ref.shape[0]
    both = [jnp.broadcast_to(tab_ref[p : p + 1, :], (8, 128)) for p in range(pairs)]
    rel = [jnp.broadcast_to(tab_ref[8 + p : 9 + p, :], (8, 128)) for p in range(pairs)]

    def pick(table, index):
        return jnp.take_along_axis(table, index, axis=1, mode="promise_in_bounds")

    for c in range(out_ref.shape[2] // 128):
        for r in range(rows_step // 8):
            rows, cols = pl.ds(r * 8, 8), pl.ds(c * 128, 128)
            rel_id = rel_ref[0, rows, cols] & 31
            x_id = x_ref[0, rows, cols] & 63
            y_id = (y_ref[0, rows, cols] & 63) + 64
            for p in range(pairs):
                out_ref[p, rows, cols] = (
                    pick(rel[p], rel_id) + pick(both[p], x_id) + pick(both[p], y_id)
                )


def bias_words(rel, x, y, table, rows, pairs):
    step = 64
    lanes = pl.cdiv(rows, 128) * 128
    ids = pl.BlockSpec((1, step, lanes), lambda i: (0, i, 0))
    return pl.pallas_call(
        functools.partial(bias_kernel, step),
        grid=(rows // step,),
        in_specs=[ids, ids, ids, pl.BlockSpec(table.shape, lambda i: (0, 0))],
        out_specs=pl.BlockSpec((pairs, step, lanes), lambda i: (0, i, 0)),
        out_shape=jax.ShapeDtypeStruct((pairs, rows, lanes), jnp.int32),
        compiler_params=pltpu.CompilerParams(vmem_limit_bytes=40 * MIB),
        cost_estimate=pl.CostEstimate(flops=0, bytes_accessed=60_000_000, transcendentals=0),
        name="bias_words",
    )(rel, x, y, table)


def lane_halves(rows):
    lane = lax.broadcasted_iota(jnp.int32, (rows, 128), 1)
    return lane < 64, lane >= 64


def attend_kernel(unit_ref, q_ref, k_ref, v_ref, w_ref, col_ref, row_ref, p_ref, o_ref, mask_ref):
    @pl.when(pl.program_id(0) == 0)
    def _():
        mask_ref[...] = jnp.where(col_ref[...] == row_ref[...], 0.0, NEG)

    unit = unit_ref[0]
    rows = q_ref.shape[0]
    halves = lane_halves(rows)
    q, k, v = q_ref[...], k_ref[...], v_ref[...]
    none = jnp.zeros_like(q)
    words = w_ref[0][:, :rows]
    mask = mask_ref[...]
    mixed = jnp.zeros((rows, 128), F32)
    for h in range(2):
        scores = dot_nt(jnp.where(halves[h], q, none), k)
        word = (words & 0xFFFF) if h == 0 else lax.shift_right_logical(words, 16)
        scores = scores + word.astype(F32) * unit + mask
        expo = jnp.exp(scores - jnp.max(scores, -1, keepdims=True))
        probs = (expo * (1.0 / jnp.sum(expo, -1, keepdims=True))).astype(BF16)
        p_ref[h] = probs
        mixed = mixed + dot_nn(probs, jnp.where(halves[h], v, none))
    o_ref[...] = mixed.astype(BF16)


def attend(unit, qkv, words, segments):
    pairs = words.shape[0]
    rows = qkv.shape[0]
    col = [pl.BlockSpec((rows, 128), lambda p, n=n: (0, n * pairs + p)) for n in range(3)]
    flops = pairs * 4 * 2 * rows * rows * 128
    return pl.pallas_call(
        attend_kernel,
        grid=(pairs,),
        in_specs=[
            pl.BlockSpec(memory_space=pltpu.SMEM),
            col[0],
            col[1],
            col[2],
            pl.BlockSpec((1,) + words.shape[1:], lambda p: (p, 0, 0)),
            pl.BlockSpec((rows, 1), lambda p: (0, 0)),
            pl.BlockSpec((1, rows), lambda p: (0, 0)),
        ],
        out_specs=[
            pl.BlockSpec((2, rows, rows), lambda p: (p, 0, 0)),
            pl.BlockSpec((rows, 128), lambda p: (0, p)),
        ],
        out_shape=[
            jax.ShapeDtypeStruct((2 * pairs, rows, rows), BF16),
            jax.ShapeDtypeStruct((rows, pairs * 128), BF16),
        ],
        scratch_shapes=[pltpu.VMEM((rows, rows), F32)],
        compiler_params=pltpu.CompilerParams(vmem_limit_bytes=50 * MIB),
        cost_estimate=pl.CostEstimate(flops=flops, bytes_accessed=40_000_000, transcendentals=0),
        name="attend",
    )(unit, qkv, qkv, qkv, words, segments[:, None], segments[None, :])


def attend_back_kernel(q_ref, k_ref, v_ref, g_ref, p_ref, ds_ref, dq_ref, dk_ref, dv_ref):
    rows = q_ref.shape[0]
    halves = lane_halves(rows)
    q, k, v, g = q_ref[...], k_ref[...], v_ref[...], g_ref[...]
    none = jnp.zeros_like(q)
    blank = jnp.zeros((rows, ds_ref.shape[2] - rows), BF16)
    dq = jnp.zeros((rows, 128), F32)
    dk, dv = dq, dq
    for h in range(2):
        low = p_ref[h]
        probs = low.astype(F32)
        weighted = probs * dot_nt(g, jnp.where(halves[h], v, none))
        ds = (weighted - probs * jnp.sum(weighted, -1, keepdims=True)).astype(BF16)
        ds_ref[h] = jnp.concatenate([ds, blank], 1)
        dq = dq + dot_nn(ds, jnp.where(halves[h], k, none))
        dv = dv + dot_tn(low, jnp.where(halves[h], g, none))
        dk = dk + dot_tn(ds, jnp.where(halves[h], q, none))
    dq_ref[...] = (dq * 0.125).astype(BF16)
    dk_ref[...] = dk.astype(BF16)
    dv_ref[...] = dv.astype(BF16)


def attend_back(qkv, grad, probs):
    pairs = probs.shape[0] // 2
    rows = qkv.shape[0]
    col = [pl.BlockSpec((rows, 128), lambda p, n=n: (0, n * pairs + p)) for n in range(3)]
    big = pl.BlockSpec((2, rows, rows), lambda p: (p, 0, 0))
    lanes = pl.cdiv(rows, 128) * 128
    out = jax.ShapeDtypeStruct(grad.shape, BF16)
    flops = pairs * 2 * 4 * 2 * rows * rows * 128
    return pl.pallas_call(
        attend_back_kernel,
        grid=(pairs,),
        in_specs=[col[0], col[1], col[2], col[0], big],
        out_specs=[pl.BlockSpec((2, rows, lanes), lambda p: (p, 0, 0)), col[0], col[0], col[0]],
        out_shape=[jax.ShapeDtypeStruct((2 * pairs, rows, lanes), BF16), out, out, out],
        compiler_params=pltpu.CompilerParams(vmem_limit_bytes=50 * MIB),
        cost_estimate=pl.CostEstimate(flops=flops, bytes_accessed=40_000_000, transcendentals=0),
        name="attend_back",
    )(qkv, qkv, qkv, grad, probs)


def table_kernel(length, step, levels, rel_ref, x_ref, y_ref, ds_ref, out_ref, rows_ref):
    place = pl.program_id(0)

    @pl.when(place == 0)
    def _():
        out_ref[...] = jnp.zeros_like(out_ref)
        rows_ref[...] = jnp.zeros_like(rows_ref)

    heads = ds_ref.shape[0]
    width = rel_ref.shape[2]
    level = [
        lax.broadcasted_iota(jnp.int32, (16, width), 0).astype(F32).astype(BF16) + BF16(16 * t)
        for t in range(max(levels) // 16)
    ]
    one = jnp.ones((16, width), BF16)
    none = jnp.zeros((16, width), BF16)

    def one_hot(ids, count):
        wide = jnp.broadcast_to(ids.astype(F32), (16, width)).astype(BF16)
        return [jnp.where(wide == level[t], one, none) for t in range(count // 16)]

    def body(r, _):
        for h in range(heads):
            values = ds_ref[h, pl.ds(pl.multiple_of(r * 16, 16), 16), :].astype(F32)
            for c in range(width // 128):
                rows_ref[c, pl.ds(h, 16, stride=16), :] = values[:, 128 * c : 128 * c + 128]
        total = out_ref[...]
        for n in range(16):
            grads = jnp.concatenate(
                [rows_ref[c, 16 * n : 16 * n + 16, :].astype(BF16) for c in range(width // 128)], 1
            )
            row = pl.ds(r * 16 + n, 1)
            hot = jnp.concatenate(
                one_hot(rel_ref[0, row, :], levels[0])
                + one_hot(x_ref[0, row, :], levels[1])
                + one_hot(y_ref[0, row, :], levels[2]),
                0,
            )
            total = total + dot_nt(hot, grads)
        out_ref[...] = total
        return 0

    left = length - place * step
    lax.fori_loop(0, jnp.minimum(step // 16, (left + 15) // 16), body, 0)


def table_sums(rel, x, y, ds, levels):
    step = 64
    length = rel.shape[1]
    heads, rows, lanes = ds.shape
    ids = pl.BlockSpec((1, step, lanes), lambda i: (0, i, 0))
    return pl.pallas_call(
        functools.partial(table_kernel, length, step, levels),
        grid=(rows // step,),
        in_specs=[ids, ids, ids, pl.BlockSpec((heads, step, lanes), lambda i: (0, i, 0))],
        out_specs=pl.BlockSpec((sum(levels), 16), lambda i: (0, 0)),
        out_shape=jax.ShapeDtypeStruct((sum(levels), 16), F32),
        scratch_shapes=[pltpu.VMEM((lanes // 128, 256, 128), F32)],
        compiler_params=pltpu.CompilerParams(vmem_limit_bytes=40 * MIB),
        cost_estimate=pl.CostEstimate(flops=0, bytes_accessed=120_000_000, transcendentals=0),
        name="table_sums",
    )(rel, x, y, ds)


def norm_stats(values):
    center = values - jnp.mean(values, -1, keepdims=True)
    scale = lax.rsqrt(jnp.mean(center * center, -1, keepdims=True) + EPS)
    return center * scale, scale


def norm_back(grad, normed, scale, gain):
    scaled = grad * gain
    return scale * (
        scaled
        - jnp.mean(scaled, -1, keepdims=True)
        - normed * jnp.mean(scaled * normed, -1, keepdims=True)
    )


def packed_tables(tables):
    top = functools.reduce(jnp.maximum, [jnp.max(jnp.abs(t)) for t in tables])
    top = jnp.maximum(top, 1e-30)
    words = []
    for table in tables:
        level = jnp.round((table / top + 1.0) * (0.5 * LEVELS)).astype(jnp.int32)
        level = level.reshape(table.shape[0], -1, 2)
        words.append((level[:, :, 0] + level[:, :, 1] * 65536).T)
    rel, x, y = words
    pairs = rel.shape[0]
    both = jnp.concatenate([x, y], 1)
    rel = jnp.pad(rel, ((0, 8 - pairs), (0, 128 - rel.shape[1])))
    return jnp.concatenate([jnp.pad(both, ((0, 8 - pairs), (0, 0))), rel]), (
        top * (2.0 / LEVELS)
    ).reshape(1)


def on_device(
    text_hidden,
    visual_maps,
    patch_order,
    segment_ids,
    rel_bucket,
    x_bucket,
    y_bucket,
    bn_scale,
    bn_shift,
    vis_proj,
    w_query,
    w_key,
    w_value,
    w_output,
    rel_table,
    x_table,
    y_table,
    first_gain,
    first_bias,
    w_inner,
    b_inner,
    w_outer,
    b_outer,
    second_gain,
    second_bias,
    cotangent,
):
    heads = rel_table.shape[1]
    pairs = heads // 2
    visual_len = patch_order.shape[1]
    length = segment_ids.shape[1]
    text_len = length - visual_len
    width = w_query.shape[1]
    dp, ffn = lax.axis_size("dp"), lax.axis_size("ffn")
    place, here = lax.axis_index("dp"), lax.axis_index("ffn")
    devices = dp * ffn
    rows = pl.cdiv(length, 64) * 64
    count = visual_maps.shape[0] * devices
    levels = (rel_table.shape[0], x_table.shape[0], y_table.shape[0])

    late = [w_inner.reshape(-1, width), w_outer.T.reshape(-1, width), w_output]
    late_rows = late[0].shape[0]
    late = jnp.concatenate(late, 0)
    late = lax.all_gather(late, ALL, axis=0).reshape((dp, ffn) + late.shape)

    shards = [w_query, w_key, w_value, vis_proj]
    near = gather_ffn(jnp.concatenate(shards, 0))
    begin = 0
    stacked = []
    layout = []
    for shard in shards:
        size = shard.shape[0]
        stacked.append(near[:, begin : begin + size].reshape(ffn * size, width))
        layout.append((begin * ffn, ffn * size))
        begin += size
    near = jnp.concatenate(stacked, 0)
    quads = gather_quads(near)
    parts, places = [], []
    for k, block in enumerate(quads):
        if isinstance(block, tuple):
            mine = jnp.concatenate(block, 0)
            other = jnp.concatenate([send_dp(piece, 1) for piece in block], 0)
        else:
            mine, other = block, send_dp(block, 1)
        parts += [mine, other]
        places += [place ^ (2 * k), place ^ (2 * k) ^ 1]
    query_full, key_full, value_full, proj_full = place_blocks(
        parts, jnp.stack(places).astype(jnp.int32), layout
    )

    table_words, unit = packed_tables((rel_table, x_table, y_table))
    words = bias_words(rel_bucket, x_bucket, y_bucket, table_words, rows, pairs)

    visual = visual_maps.astype(F32)
    local_mean = jnp.mean(visual, 0)
    local_spread = jnp.sum((visual - local_mean) ** 2, 0)
    average, spread = moments_all(local_mean, local_spread, visual_maps.shape[0])
    inv_std = lax.rsqrt(spread + EPS)
    normalized = (visual - average) * inv_std
    bn_rows = (normalized * bn_scale + bn_shift).astype(BF16)
    tokens = dot_nn(bn_rows, proj_full)
    picker = (patch_order[0][:, None] == jnp.arange(visual_len, dtype=jnp.int32)[None, :]).astype(
        F32
    )
    tokens = jnp.dot(picker, tokens, precision=lax.Precision.HIGHEST)
    hidden = pad_rows(jnp.concatenate([text_hidden.astype(F32), tokens], 0), rows)
    lowered = hidden.astype(BF16)
    qkv_full = jnp.concatenate([query_full, key_full, value_full], 1)
    qkv = dot_nn(lowered, qkv_full)
    qkv = jnp.concatenate([qkv[:, :width] * 0.125, qkv[:, width:]], 1).astype(BF16)

    segments = jnp.pad(segment_ids[0], (0, rows - length), constant_values=-1)
    probs, mixed = attend(unit, qkv, words, segments)

    inner_rows = w_inner.shape[0]
    columns = w_inner.shape[1]
    output_full = late[:, :, 2 * late_rows :].reshape(width, width)
    inner_w, outer_w = [
        late[:, :, n * late_rows : (n + 1) * late_rows]
        .reshape(dp, ffn, inner_rows, columns)
        .transpose(1, 0, 2, 3)
        .reshape(ffn, width, columns)
        for n in range(2)
    ]
    attended = dot_nn(mixed, output_full)
    first_n, first_r = norm_stats(hidden + attended)
    first = first_n * first_gain + first_bias
    first_low = first.astype(BF16)

    outer = first + b_outer
    acts, slopes = [], []
    for f in range(ffn):
        inner = dot_nn(first_low, inner_w[f]) + b_inner[f * columns : (f + 1) * columns]
        act, pull = jax.vjp(functools.partial(jax.nn.gelu, approximate=True), inner)
        acts.append(act.astype(BF16))
        slopes.append(pull(jnp.ones_like(inner))[0].astype(BF16))
        outer = outer + dot_nt(acts[f], outer_w[f])
    second_n, second_r = norm_stats(outer)
    output = (second_n * second_gain + second_bias).astype(BF16)[:length]
    ct = pad_rows(cotangent.astype(F32), rows)
    grad_second = norm_back(ct, second_n, second_r, second_gain)
    grad_gain_two = jnp.sum(ct * second_n, 0)
    grad_bias_two = jnp.sum(ct, 0)
    grad_outer_bias = jnp.sum(grad_second, 0)
    grad_low = grad_second.astype(BF16)
    grad_first = grad_second
    ffn_grads, inner_sums = [], []
    for f in range(ffn):
        grad_inner = dot_nn(grad_low, outer_w[f]) * slopes[f].astype(F32)
        inner_sums.append(jnp.sum(grad_inner, 0))
        grad_inner = grad_inner.astype(BF16)
        grad_first = grad_first + dot_nt(grad_inner, inner_w[f])
        grad_inner_w = dot_tn(first_low, grad_inner).astype(BF16)
        grad_outer_w = dot_tn(grad_low, acts[f]).astype(BF16)
        ffn_grads.append(
            jnp.concatenate(
                [
                    grad_inner_w.reshape(dp, inner_rows, columns),
                    grad_outer_w.reshape(dp, inner_rows, columns),
                ],
                1,
            )
        )
    ffn_shard = scatter_all(jnp.stack(ffn_grads, 1))

    grad_attn = norm_back(grad_first, first_n, first_r, first_gain)
    grad_gain_one = jnp.sum(grad_first * first_n, 0)
    grad_bias_one = jnp.sum(grad_first, 0)
    grad_attn_low = grad_attn.astype(BF16)
    grad_output_w = dot_tn(mixed, grad_attn_low).astype(BF16)
    grad_mixed = dot_nt(grad_attn_low, output_full).astype(BF16)
    early = [grad_gain_one, grad_bias_one, grad_outer_bias, grad_gain_two, grad_bias_two]
    early = sum_all(jnp.concatenate(early + inner_sums).reshape(-1, 128)).reshape(-1)

    ds, grad_q, grad_k, grad_v = attend_back(qkv, grad_mixed, probs)
    grad_hidden = (
        grad_attn
        + dot_nt(grad_q, query_full)
        + dot_nt(grad_k, key_full)
        + dot_nt(grad_v, value_full)
    )
    text_grad = grad_hidden[:text_len]
    grad_tokens = lax.dot_general(
        picker,
        grad_hidden[text_len:length],
        (((0,), (0,)), ((), ())),
        precision=lax.Precision.HIGHEST,
        preferred_element_type=F32,
    ).astype(BF16)
    grad_proj = dot_tn(bn_rows, grad_tokens).astype(BF16)
    grad_bn = dot_nt(grad_tokens, proj_full)
    bn_sums = jnp.stack([jnp.sum(grad_bn, 0), jnp.sum(grad_bn * normalized, 0)])
    bn_sums = sum_all(bn_sums)
    partials = [grad_output_w] + [dot_tn(lowered, g).astype(BF16) for g in (grad_q, grad_k, grad_v)]
    partials = [grad_proj] + partials
    shard_rows = [p.shape[0] // devices for p in partials]
    tail = scatter_all(
        jnp.concatenate([p.reshape(dp, ffn, -1, width) for p in partials], 2)
    )
    begins = [sum(shard_rows[:n]) for n in range(len(shard_rows))]
    shards = [tail[b : b + n] for b, n in zip(begins, shard_rows)]

    sums = sum_all(table_sums(rel_bucket, x_bucket, y_bucket, ds, levels))[:, :heads]
    shift_grad, scale_grad = bn_sums[0], bn_sums[1]
    visual_grad = (
        bn_scale * inv_std * (grad_bn - shift_grad / count - normalized * scale_grad / count)
    )
    return (
        output,
        text_grad,
        visual_grad,
        scale_grad,
        shift_grad,
        shards[0],
        shards[2],
        shards[3],
        shards[4],
        shards[1],
        sums[: levels[0]],
        sums[levels[0] : levels[0] + levels[1]],
        sums[levels[0] + levels[1] :],
        early[:width],
        early[width : 2 * width],
        ffn_shard[:inner_rows],
        early[5 * width :],
        ffn_shard[inner_rows:].T,
        early[2 * width : 3 * width],
        early[3 * width : 4 * width],
        early[4 * width : 5 * width],
    )


def solution(mesh):
    rows = P(ALL, None)
    cube = P(ALL, None, None)
    return jax.shard_map(
        on_device,
        mesh=mesh,
        in_specs=(rows,) * 4
        + (cube,) * 3
        + (P(),) * 2
        + (rows,) * 5
        + (P(),) * 5
        + (P("dp", "ffn"), P(), P("ffn", "dp"))
        + (P(),) * 3
        + (rows,),
        out_specs=(rows,) * 3
        + (P(),) * 2
        + (rows,) * 5
        + (P(),) * 5
        + (P("dp", "ffn"), P(), P("ffn", "dp"))
        + (P(),) * 3,
        check_vma=False,
    )
```

```python
import functools

import jax
import jax.numpy as jnp
from jax import lax
from jax.experimental import pallas as pl
from jax.experimental.pallas import tpu as pltpu
from jax.sharding import PartitionSpec as P

EPS = 1e-05
NEG = -1e30
F32 = jnp.float32
BF16 = jnp.bfloat16
ALL = ("dp", "ffn")
LEVELS = 21845.0
MIB = 2**20


def dot_nn(a, b):
    return lax.dot_general(a, b, (((1,), (0,)), ((), ())), preferred_element_type=F32)


def dot_nt(a, b):
    return lax.dot_general(a, b, (((1,), (1,)), ((), ())), preferred_element_type=F32)


def dot_tn(a, b):
    return lax.dot_general(a, b, (((0,), (0,)), ((), ())), preferred_element_type=F32)


def pad_rows(values, rows):
    return jnp.pad(values, ((0, rows - values.shape[0]), (0, 0)))


def send_dp(values, bits):
    size = lax.axis_size("dp")
    return lax.ppermute(values, "dp", [(i, i ^ bits) for i in range(size)])


def send_ffn(values, shift):
    size = lax.axis_size("ffn")
    return lax.ppermute(values, "ffn", [(i, (i + shift) % size) for i in range(size)])


def swap_ffn(values, bits):
    size = lax.axis_size("ffn")
    return lax.ppermute(values, "ffn", [(i, i ^ bits) for i in range(size)])


def exchanges():
    steps = []
    bit = 1
    while bit < lax.axis_size("ffn"):
        steps.append(functools.partial(swap_ffn, bits=bit))
        bit *= 2
    bit = 1
    while bit < lax.axis_size("dp"):
        steps.append(functools.partial(send_dp, bits=bit))
        bit *= 2
    return steps


class Sum:
    def __init__(self, values):
        self.values = values
        self.steps = exchanges()

    def step(self):
        if self.steps:
            self.values = self.values + self.steps.pop(0)(self.values)

    def finish(self):
        while self.steps:
            self.step()
        return self.values


class Gather:
    def __init__(self, own, rows):
        self.own = own
        self.rows = rows

    def along_ffn(self):
        size = lax.axis_size("ffn")
        self.far = [self.own] + [send_ffn(self.own, k) for k in range(1, size)]

    def order(self):
        size = lax.axis_size("ffn")
        here = lax.axis_index("ffn")
        if all(rows % 8 == 0 for rows in self.rows):
            self.block = order_blocks(here, self.far, self.rows)
            return
        pieces = []
        for slot in range(size):
            value = self.far[0]
            for k in range(1, size):
                value = jnp.where((here - k + size) % size == slot, self.far[k], value)
            pieces.append(value)
        begin, ordered = 0, []
        for rows in self.rows:
            ordered += [value[begin : begin + rows] for value in pieces]
            begin += rows
        self.block = jnp.concatenate(ordered, 0)

    def near(self, cut):
        quads = lax.axis_size("dp") // 2
        self.cut = cut
        if quads == 4:
            self.mine = [self.block, send_dp(self.block, 2), send_dp(self.block, 4)]
        else:
            self.mine = [self.block] + [send_dp(self.block, 2 * k) for k in range(1, quads)]

    def diagonal(self):
        self.others = [send_dp(block, 1) for block in self.mine]
        if lax.axis_size("dp") == 8:
            low = send_dp(self.mine[1][: self.cut], 4)
            high = send_dp(self.mine[2][self.cut :], 2)
            self.mine.append((low, high))

    def across(self):
        if lax.axis_size("dp") == 8:
            self.others.append(tuple(send_dp(piece, 1) for piece in self.mine[3]))

    def state(self):
        return {k: v for k, v in vars(self).items() if k in ("own", "far", "block", "mine", "others")}

    def hold(self, state):
        vars(self).update(state)

    def parts(self):
        found = []
        for k, (mine, other) in enumerate(zip(self.mine, self.others)):
            for bits, block in ((2 * k, mine), (2 * k + 1, other)):
                if isinstance(block, tuple):
                    found += [(block[0], bits, 0), (block[1], bits, self.cut)]
                else:
                    found.append((block, bits, 0))
        return found


def epoch(*values):
    return lax.optimization_barrier(values)


def pick(values, index, axis):
    return lax.dynamic_index_in_dim(values, index, axis, keepdims=False)


def plus(a, b):
    return (a.astype(F32) + b.astype(F32)).astype(BF16)


class Scatter:
    def __init__(self, mine, away, far):
        self.value = mine
        self.away = away
        self.far = far

    def core(self):
        self.got = send_dp(self.away, 1)

    def near(self):
        mine, got = self.value, self.got
        if mine.shape[0] == 4:
            half = mine.shape[1] // 2
            self.low = send_dp(plus(mine[3, :half], got[3, :half]), 4)
            self.high = send_dp(plus(mine[3, half:], got[3, half:]), 2)

    def quads(self):
        mine, got = self.value, self.got
        half = mine.shape[1] // 2
        total = mine[0].astype(F32) + got[0].astype(F32)
        for k in range(1, mine.shape[0]):
            block = mine[k].astype(F32) + got[k].astype(F32)
            if mine.shape[0] == 4 and k == 1:
                block = jnp.concatenate([block[:half] + self.low.astype(F32), block[half:]], 0)
            if mine.shape[0] == 4 and k == 2:
                block = jnp.concatenate([block[:half], block[half:] + self.high.astype(F32)], 0)
            if mine.shape[0] == 4 and k == 3:
                continue
            total = total + send_dp(block.astype(BF16), 2 * k).astype(F32)
        self.value = total.astype(BF16)

    def held(self):
        return {k: v for k, v in vars(self).items() if k != "far"}

    def hold(self, state):
        vars(self).update(state)

    def along_ffn(self):
        size = lax.axis_size("ffn")
        here = lax.axis_index("ffn")
        self.pieces = [self.far(self.value, here)]
        for k in range(1, size):
            self.pieces.append(send_ffn(self.far(self.value, (here + k) % size), k))

    def total(self):
        return sum(piece.astype(F32) for piece in self.pieces)


LIMIT = 56 * MIB


def whole(shape):
    return pl.BlockSpec(shape, lambda *_: (0,) * len(shape))


def cost(flops, nbytes):
    return pl.CostEstimate(flops=flops, bytes_accessed=nbytes, transcendentals=0)


def pack_kernel(q_ref, k_ref, v_ref, p_ref, visual_ref, out_ref):
    row = 0
    for ref in (q_ref, k_ref, v_ref, p_ref):
        out_ref[row : row + ref.shape[0], :] = ref[...]
        row += ref.shape[0]
    width = out_ref.shape[1]
    count = visual_ref.shape[0]
    visual = visual_ref[...].astype(F32)
    mean = jnp.sum(visual, 0, keepdims=True) * (1.0 / count)
    gap = visual - mean
    spread = jnp.sum(gap * gap, 0, keepdims=True)
    channels = visual_ref.shape[1]
    chunks = pl.cdiv(channels, width)
    blank = jnp.zeros((1, chunks * width - channels), F32)
    pieces = []
    for values, times in ((mean, 3), (spread, 2)):
        if chunks * width > channels:
            values = jnp.concatenate([values, blank], 1)
        for _ in range(times):
            piece = values.astype(BF16).astype(F32)
            values = values - piece
            pieces += [piece[:, n * width : (n + 1) * width] for n in range(chunks)]
    pieces += [jnp.zeros((1, width), F32)] * (out_ref.shape[0] - row - len(pieces))
    out_ref[row:, :] = jnp.concatenate(pieces, 0).astype(BF16)


def pack_first(w_query, w_key, w_value, vis_proj, visual):
    width = w_query.shape[1]
    moments = pl.cdiv(5 * pl.cdiv(visual.shape[1], width), 16) * 16
    rows = [w.shape[0] for w in (w_query, w_key, w_value, vis_proj)] + [moments]
    own = pl.pallas_call(
        pack_kernel,
        out_shape=jax.ShapeDtypeStruct((sum(rows), width), BF16),
        name="pack_first",
    )(w_query, w_key, w_value, vis_proj, visual)
    return own, rows


def order_kernel(rows, here_ref, *refs):
    parts, out_ref = refs[:-1], refs[-1]
    size = len(parts)
    here = here_ref[0]
    for index in range(size):

        @pl.when(here == index)
        def _(index=index):
            begin = 0
            for count in rows:
                for k in range(size):
                    row = begin * size + (index - k) % size * count
                    out_ref[row : row + count, :] = parts[k][begin : begin + count, :]
                begin += count


def order_blocks(here, parts, rows):
    width = parts[0].shape[1]
    return pl.pallas_call(
        functools.partial(order_kernel, rows),
        in_specs=[pl.BlockSpec(memory_space=pltpu.SMEM)]
        + [pl.BlockSpec(memory_space=pltpu.VMEM)] * len(parts),
        out_specs=pl.BlockSpec(memory_space=pltpu.VMEM),
        out_shape=jax.ShapeDtypeStruct((len(parts) * sum(rows), width), BF16),
        name="order_blocks",
    )(here.reshape(1).astype(jnp.int32), *parts)


def place_entries(parts, layout):
    entries = []
    for n, (block, _, first) in enumerate(parts):
        for begin, rows, out, base, lane in layout:
            if first <= begin and begin + rows <= first + block.shape[0]:
                entries.append((n, begin - first, rows, out, base, lane))
    return entries


def place_index(parts):
    place = lax.axis_index("dp")
    return jnp.stack([place ^ bits for _, bits, _ in parts]).astype(jnp.int32)


def part_copies(entries, place_ref, parts, outs, sems):
    copies = []
    for n, (part, begin, rows, out, base, lane) in enumerate(entries):
        target = pl.multiple_of(base + place_ref[part] * rows, 16)
        width = parts[part].shape[1]
        copies.append(
            pltpu.make_async_copy(
                parts[part].at[pl.ds(begin, rows), :],
                outs[out].at[pl.ds(target, rows), pl.ds(lane, width)],
                sems.at[n],
            )
        )
    return copies


def picked(order_col, size):
    lane = lax.broadcasted_iota(jnp.int32, (size, size), 1)
    return (order_col == lane).astype(F32)


def exact(a, b, dims):
    return lax.dot_general(
        a, b, (dims, ((), ())), precision=lax.Precision.HIGHEST, preferred_element_type=F32
    )


def first_kernel(entries, count, devices, place_ref, *refs):
    parts, refs = refs[:count], refs[count:]
    text_ref, visual_ref, order_ref, lines_ref = refs[:4]
    qkv_w_ref, proj_ref, hidden_ref, low_ref, qkv_ref, bn_ref, stats_ref = refs[4:11]
    moments_ref, sems = refs[11:]
    outs = (qkv_w_ref, proj_ref, moments_ref)
    copies = part_copies(entries, place_ref, parts, outs, sems)
    for copy in copies:
        copy.start()
    copies = [(entry[3], copy) for entry, copy in zip(entries, copies)]
    text_len, width = text_ref.shape
    visual_len, channels = visual_ref.shape
    hidden_ref[:text_len, :] = text_ref[...].astype(F32)
    low_ref[:text_len, :] = text_ref[...]
    for out, copy in copies:
        if out == 2:
            copy.wait()
    chunks = pl.cdiv(channels, width)
    moments = moments_ref[...].astype(F32).reshape(devices, -1, width)
    means = sum(moments[:, n * chunks : (n + 1) * chunks] for n in range(3))
    spreads = sum(moments[:, n * chunks : (n + 1) * chunks] for n in range(3, 5))
    average = jnp.sum(means, 0) * (1.0 / devices)
    gap = means - average[None]
    rows = visual_len * devices
    spread = (jnp.sum(spreads, 0) + visual_len * jnp.sum(gap * gap, 0)) * (1.0 / rows)
    inverse = lax.rsqrt(spread + EPS)

    def flat(values):
        pieces = [values[n : n + 1, :] for n in range(chunks)]
        return jnp.concatenate(pieces, 1)[:, :channels]

    average, inverse = flat(average), flat(inverse)
    stats_ref[0:1, :] = average
    stats_ref[1:2, :] = inverse
    normed = (visual_ref[...].astype(F32) - average) * inverse
    bn_rows = (normed * lines_ref[0:1, :] + lines_ref[1:2, :]).astype(BF16)
    bn_ref[...] = bn_rows
    for out, copy in copies:
        if out == 1:
            copy.wait()
    tokens = dot_nn(bn_rows, proj_ref[...])
    tokens = exact(picked(order_ref[...], visual_len), tokens, ((1,), (0,)))
    blank = jnp.zeros((hidden_ref.shape[0] - text_len - visual_len, width), F32)
    tokens = jnp.concatenate([tokens, blank], 0)
    hidden_ref[text_len:, :] = tokens
    low_ref[text_len:, :] = tokens.astype(BF16)
    for out, copy in copies:
        if out == 0:
            copy.wait()
    low = low_ref[...]
    for n in range(3):
        lanes = slice(n * width, (n + 1) * width)
        values = dot_nn(low, qkv_w_ref[:, lanes])
        qkv_ref[:, lanes] = (values * 0.125 if n == 0 else values).astype(BF16)


def first_rows(parts, layout, text, visual, order, lines, rows, proj_rows, moment_rows):
    devices = lax.axis_size("dp") * lax.axis_size("ffn")
    width = text.shape[1]
    channels = visual.shape[1]
    entries = place_entries(parts, layout)
    vmem = pl.BlockSpec(memory_space=pltpu.VMEM)
    shapes = [
        ((width, 3 * width), BF16),
        ((proj_rows, width), BF16),
        ((rows, width), F32),
        ((rows, width), BF16),
        ((rows, 3 * width), BF16),
        ((visual.shape[0], channels), BF16),
        ((2, channels), F32),
    ]
    return pl.pallas_call(
        functools.partial(first_kernel, entries, len(parts), devices),
        in_specs=[pl.BlockSpec(memory_space=pltpu.SMEM)]
        + [pl.BlockSpec(memory_space=pl.ANY)] * len(parts)
        + [vmem] * 4,
        out_specs=[vmem] * len(shapes),
        out_shape=[jax.ShapeDtypeStruct(*shape) for shape in shapes],
        scratch_shapes=[
            pltpu.VMEM((moment_rows * devices, width), BF16),
            pltpu.SemaphoreType.DMA((len(entries),)),
        ],
        compiler_params=pltpu.CompilerParams(vmem_limit_bytes=LIMIT),
        cost_estimate=cost(0, 25_000_000),
        name="first_rows",
    )(
        place_index(parts),
        *[block for block, _, _ in parts],
        text,
        visual,
        order,
        lines,
    )


def store_blocks(mine_ref, away_ref, core, quad, store):
    quads = mine_ref.shape[0]
    for bit in range(2):

        @pl.when(core == bit)
        def _(bit=bit):
            for dp in range(2 * quads):
                ref = mine_ref if dp % 2 == bit else away_ref
                store(ref, (dp // 2) ^ quad, dp)


def place_pair():
    place = lax.axis_index("dp")
    return jnp.stack([place % 2, place // 2]).astype(jnp.int32)


def feed_kernel(entries, count, length, ffn, place_ref, core_ref, *refs):
    parts, refs = refs[:count], refs[count:]
    mixed_ref, hidden_ref, lines_ref, inner_b_ref, ct_ref = refs[:5]
    normed_ref, scale_ref, output_ref, total_ref, sums_ref, inner_sums_ref = refs[5:11]
    out_w_ref, mine_ref, away_ref = refs[11:14]
    outer_w_ref, inner_w_ref, act_ref, slope_ref, first_ref, low_ref = refs[14:20]
    first_turned, low_turned, sems = refs[20:]
    step = pl.program_id(0)
    width = hidden_ref.shape[1]
    outs = (out_w_ref, outer_w_ref, inner_w_ref)
    gain1, bias1, outer_b, gain2, bias2 = [lines_ref[n : n + 1, :] for n in range(5)]

    @pl.when(step == 0)
    def _():
        for copy in part_copies(entries, place_ref, parts, outs, sems):
            copy.start()

    for index in range(ffn):

        @pl.when(step == index)
        def _(index=index):
            copies = part_copies(entries, place_ref, parts, outs, sems)
            for (_, _, _, out, base, _), copy in zip(entries, copies):
                if (out == 0 and index == 0) or (out > 0 and base == index * width):
                    copy.wait()

    @pl.when(step == 0)
    def _():
        attended = dot_nn(mixed_ref[...], out_w_ref[...])
        normed, scale = norm_stats(hidden_ref[...] + attended)
        first = normed * gain1 + bias1
        normed_ref[...] = normed
        scale_ref[...] = scale
        low = first.astype(BF16)
        first_ref[...] = low
        total_ref[...] = first + outer_b
        first_turned[...] = low.T

    @pl.when(step < ffn)
    def _():
        rows = pl.ds(pl.multiple_of(step * width, width), width)
        inner = dot_nn(first_ref[...], inner_w_ref[rows, :]) + inner_b_ref[step]
        root = 0.7978845608028654
        square = inner * inner
        curve = jnp.tanh(root * (inner + 0.044715 * inner * square))
        half = 0.5 + 0.5 * curve
        act = (inner * half).astype(BF16)
        act_ref[step] = act
        slope = half + 0.5 * inner * (1.0 - curve * curve) * (root + (3 * 0.044715 * root) * square)
        slope_ref[step] = slope.astype(BF16)
        total_ref[...] += dot_nt(act, outer_w_ref[rows, :])

    @pl.when(step == ffn - 1)
    def _():
        normed, scale = norm_stats(total_ref[...])
        output_ref[...] = (normed * gain2 + bias2).astype(BF16)
        row = lax.broadcasted_iota(jnp.int32, (normed.shape[0], 1), 0)
        ct = jnp.where(row < length, ct_ref[...].astype(F32), 0.0)
        grad = norm_back(ct, normed, scale, gain2)
        total_ref[...] = grad
        low = grad.astype(BF16)
        low_ref[...] = low
        low_turned[...] = low.T
        sums_ref[0:1, :] = jnp.sum(ct * normed, 0, keepdims=True)
        sums_ref[1:2, :] = jnp.sum(ct, 0, keepdims=True)
        sums_ref[2:3, :] = jnp.sum(grad, 0, keepdims=True)

    @pl.when(step >= ffn)
    def _():
        f = step - ffn
        rows = pl.ds(pl.multiple_of(f * width, width), width)
        grad = dot_nn(low_ref[...], outer_w_ref[rows, :]) * slope_ref[f].astype(F32)
        inner_sums_ref[0] = jnp.sum(grad, 0, keepdims=True)
        grad = grad.astype(BF16)
        total_ref[...] += dot_nt(grad, inner_w_ref[rows, :])
        inner = dot_nn(first_turned[...], grad).astype(BF16)
        outer = dot_nn(low_turned[...], act_ref[f]).astype(BF16)
        size = mine_ref.shape[3]

        def store(ref, slot, dp):
            ref[slot, 0, 0] = inner[dp * size : (dp + 1) * size]
            ref[slot, 1, 0] = outer[dp * size : (dp + 1) * size]

        store_blocks(mine_ref, away_ref, core_ref[0], core_ref[1], store)


def feed_forward(feeds, mixed, hidden, lines, inner_b, ct, inner_rows):
    parts, entries = [], []
    for some, layout in feeds:
        for part, *entry in place_entries(some, layout):
            entries.append((part + len(parts), *entry))
        parts += some
    rows, width = hidden.shape
    ffn, _, columns = inner_b.shape
    quads = lax.axis_size("dp") // 2
    square = whole((rows, width))
    back = lambda i: jnp.maximum(i - ffn, 0)
    block = pl.BlockSpec((quads, 2, 1, inner_rows, columns), lambda i: (0, 0, back(i), 0, 0))
    blocks = jax.ShapeDtypeStruct((quads, 2, ffn, inner_rows, columns), BF16)
    smem = pl.BlockSpec(memory_space=pltpu.SMEM)
    shapes = [
        ((rows, width), F32),
        ((rows, 1), F32),
        (ct.shape, BF16),
        ((rows, width), F32),
        ((3, width), F32),
        ((ffn, 1, columns), F32),
        ((width, width), BF16),
    ]
    return pl.pallas_call(
        functools.partial(feed_kernel, entries, len(parts), ct.shape[0], ffn),
        grid=(2 * ffn,),
        in_specs=[smem, smem]
        + [pl.BlockSpec(memory_space=pl.ANY)] * len(parts)
        + [square, square, whole(lines.shape), whole(inner_b.shape), square],
        out_specs=[square, whole((rows, 1)), square, square, whole((3, width))]
        + [pl.BlockSpec((1, 1, columns), lambda i: (back(i), 0, 0)), whole((width, width))]
        + [block, block],
        out_shape=[jax.ShapeDtypeStruct(*shape) for shape in shapes] + [blocks, blocks],
        scratch_shapes=[
            pltpu.VMEM((ffn * width, columns), BF16),
            pltpu.VMEM((ffn * width, columns), BF16),
            pltpu.VMEM((ffn, rows, columns), BF16),
            pltpu.VMEM((ffn, rows, columns), BF16),
            pltpu.VMEM((rows, width), BF16),
            pltpu.VMEM((rows, width), BF16),
            pltpu.VMEM((width, rows), BF16),
            pltpu.VMEM((width, rows), BF16),
            pltpu.SemaphoreType.DMA((len(entries),)),
        ],
        compiler_params=pltpu.CompilerParams(vmem_limit_bytes=LIMIT),
        cost_estimate=cost(0, 100_000_000),
        name="feed_forward",
    )(
        place_index(parts),
        place_pair(),
        *[part for part, _, _ in parts],
        mixed,
        hidden,
        lines,
        inner_b,
        ct,
    )


def norm_kernel(
    grad_ref, normed_ref, scale_ref, lines_ref, w_ref, out_ref, low_ref, mix_ref, sums_ref
):
    grad, normed = grad_ref[...], normed_ref[...]
    attn = norm_back(grad, normed, scale_ref[...], lines_ref[0:1, :])
    out_ref[...] = attn
    low = attn.astype(BF16)
    low_ref[...] = low
    mix_ref[...] = dot_nt(low, w_ref[...]).astype(BF16)
    sums_ref[0:1, :] = jnp.sum(grad * normed, 0, keepdims=True)
    sums_ref[1:2, :] = jnp.sum(grad, 0, keepdims=True)


def norm_rows(grad, normed, scale, lines, out_w):
    rows, width = grad.shape
    low = jax.ShapeDtypeStruct((rows, width), BF16)
    return pl.pallas_call(
        norm_kernel,
        out_shape=[
            jax.ShapeDtypeStruct((rows, width), F32),
            low,
            low,
            jax.ShapeDtypeStruct((2, width), F32),
        ],
        compiler_params=pltpu.CompilerParams(vmem_limit_bytes=LIMIT),
        cost_estimate=cost(0, 12_000_000),
        name="norm_rows",
    )(grad, normed, scale, lines, out_w)


def tail_kernel(shard, vis_shard, ffn, text_len, place_ref, *refs):
    dq, dk, dv = refs[0:2], refs[2:4], refs[4:6]
    qkv_w_ref, attn_ref, attn_low_ref, mixed_ref, low_ref, order_ref, bn_ref = refs[6:13]
    tokens_ref, mine_ref, away_ref = refs[13:]
    visual_len = bn_ref.shape[0]
    width = attn_low_ref.shape[1]
    grads = [jnp.concatenate([low[...], high[...]], 1) for low, high in (dq, dk, dv)]
    tokens = attn_ref[text_len:, :]
    for n in range(3):
        lanes = slice(n * width, (n + 1) * width)
        tokens = tokens + dot_nt(grads[n][text_len:], qkv_w_ref[:, lanes])
    picker = picked(order_ref[...], visual_len)
    tokens = exact(picker, tokens[:visual_len], ((0,), (0,))).astype(BF16)
    tokens_ref[...] = tokens
    core, quad = place_ref[0], place_ref[1]

    def spread(values, begin, rows):
        def store(ref, slot, dp):
            for f in range(ffn):
                row = (dp * ffn + f) * rows
                ref[slot, f, begin : begin + rows, :] = values[row : row + rows].astype(BF16)

        store_blocks(mine_ref, away_ref, core, quad, store)

    turned = low_ref[...].T
    for n in range(3):
        spread(dot_nn(turned, grads[n]), n * shard, shard)
    spread(dot_nn(mixed_ref[...].T, attn_low_ref[...]), 3 * shard, shard)
    spread(dot_tn(bn_ref[...], tokens), 4 * shard, vis_shard)


def tail_rows(back, qkv_w, attn, attn_low, mixed, low, order, bn_rows, text_len, shard):
    dp, ffn = lax.axis_size("dp"), lax.axis_size("ffn")
    width = attn.shape[1]
    visual_len, channels = bn_rows.shape
    vis_shard = channels // (dp * ffn)
    blocks = jax.ShapeDtypeStruct((dp // 2, ffn, 4 * shard + vis_shard, width), BF16)
    vmem = pl.BlockSpec(memory_space=pltpu.VMEM)
    grads = [g for pair in back for g in pair]
    others = [qkv_w, attn, attn_low, mixed, low, order, bn_rows]
    return pl.pallas_call(
        functools.partial(tail_kernel, shard, vis_shard, ffn, text_len),
        in_specs=[pl.BlockSpec(memory_space=pltpu.SMEM)] + [vmem] * (len(grads) + len(others)),
        out_specs=[vmem] * 3,
        out_shape=[jax.ShapeDtypeStruct((visual_len, width), BF16), blocks, blocks],
        compiler_params=pltpu.CompilerParams(vmem_limit_bytes=LIMIT),
        cost_estimate=cost(0, 40_000_000),
        name="tail_rows",
    )(place_pair(), *grads, *others)


def text_kernel(*refs):
    dq, dk, dv = refs[0:2], refs[2:4], refs[4:6]
    qkv_w_ref, attn_ref, tokens_ref, visual_ref, stats_ref, proj_ref = refs[6:12]
    text_ref, grad_bn_ref, sums_ref = refs[12:]
    text_len, width = text_ref.shape
    total = attn_ref[:text_len, :]
    for n, (low, high) in enumerate((dq, dk, dv)):
        grads = jnp.concatenate([low[:text_len, :], high[:text_len, :]], 1)
        total = total + dot_nt(grads, qkv_w_ref[:, n * width : (n + 1) * width])
    text_ref[...] = total
    grad_bn = dot_nt(tokens_ref[...], proj_ref[...])
    grad_bn_ref[...] = grad_bn
    normed = (visual_ref[...].astype(F32) - stats_ref[0:1, :]) * stats_ref[1:2, :]
    sums_ref[0:1, :] = jnp.sum(grad_bn, 0, keepdims=True)
    sums_ref[1:2, :] = jnp.sum(grad_bn * normed, 0, keepdims=True)


def text_rows(back, qkv_w, attn, tokens, visual, stats, proj, text_len):
    return pl.pallas_call(
        text_kernel,
        out_shape=[
            jax.ShapeDtypeStruct((text_len, attn.shape[1]), F32),
            jax.ShapeDtypeStruct(visual.shape, F32),
            jax.ShapeDtypeStruct((2, visual.shape[1]), F32),
        ],
        compiler_params=pltpu.CompilerParams(vmem_limit_bytes=LIMIT),
        cost_estimate=cost(0, 25_000_000),
        name="text_rows",
    )(*[g for pair in back for g in pair], qkv_w, attn, tokens, visual, stats, proj)


def bias_kernel(rows_step, rel_ref, x_ref, y_ref, tab_ref, out_ref, unit_ref, level_ref):
    pairs = out_ref.shape[0]
    table = tab_ref[...]
    top = jnp.max(jnp.max(jnp.abs(table), 1, keepdims=True), 0, keepdims=True)
    top = jnp.maximum(top, 1e-30)
    unit_ref[...] = top * (2.0 / LEVELS)
    level = jnp.floor((table / top + 1.0) * (0.5 * LEVELS) + 0.5).astype(jnp.int32)
    level_ref[0] = level[:, :128]
    level_ref[1] = level[:, 128:]
    words = []
    for n in range(2):
        low = level_ref[n, pl.ds(0, pairs, stride=2), :]
        high = level_ref[n, pl.ds(1, pairs, stride=2), :]
        words.append(low + high * 65536)
    both = [jnp.broadcast_to(words[0][p : p + 1, :], (8, 128)) for p in range(pairs)]
    rel = [jnp.broadcast_to(words[1][p : p + 1, :], (8, 128)) for p in range(pairs)]

    def look(table, index):
        return jnp.take_along_axis(table, index, axis=1, mode="promise_in_bounds")

    for c in range(out_ref.shape[2] // 128):
        for r in range(rows_step // 8):
            rows, cols = pl.ds(r * 8, 8), pl.ds(c * 128, 128)
            rel_id = rel_ref[0, rows, cols] & 31
            x_id = x_ref[0, rows, cols] & 63
            y_id = (y_ref[0, rows, cols] & 63) + 64
            for p in range(pairs):
                out_ref[p, rows, cols] = (
                    look(rel[p], rel_id) + look(both[p], x_id) + look(both[p], y_id)
                )


def bias_words(rel, x, y, table, first, steps):
    step = 64
    rows = steps * step
    pairs = table.shape[0] // 2
    lanes = pl.cdiv(rel.shape[2], 128) * 128
    ids = pl.BlockSpec((1, step, lanes), lambda i: (0, i + first, 0))
    return pl.pallas_call(
        functools.partial(bias_kernel, step),
        grid=(steps,),
        in_specs=[ids, ids, ids, whole(table.shape)],
        out_specs=[pl.BlockSpec((pairs, step, lanes), lambda i: (0, i, 0)), whole((1, 1))],
        out_shape=[
            jax.ShapeDtypeStruct((pairs, rows, lanes), jnp.int32),
            jax.ShapeDtypeStruct((1, 1), F32),
        ],
        scratch_shapes=[pltpu.VMEM((2, table.shape[0], 128), jnp.int32)],
        compiler_params=pltpu.CompilerParams(vmem_limit_bytes=LIMIT),
        cost_estimate=cost(0, 6_000_000 * steps),
        name="bias_words",
    )(rel, x, y, table)


def lane_halves(rows):
    lane = lax.broadcasted_iota(jnp.int32, (rows, 128), 1)
    return lane < 64, lane >= 64


def attend_kernel(unit_ref, q_ref, k_ref, v_ref, col_ref, row_ref, *refs):
    word_refs, (p_ref, o_ref, mask_ref) = refs[:-3], refs[-3:]

    @pl.when(pl.program_id(0) == 0)
    def _():
        mask_ref[...] = jnp.where(col_ref[...] == row_ref[...], 0.0, NEG)

    unit = unit_ref[...]
    rows = q_ref.shape[0]
    halves = lane_halves(rows)
    q, k, v = q_ref[...], k_ref[...], v_ref[...]
    none = jnp.zeros_like(q)
    words = jnp.concatenate([ref[0][:, :rows] for ref in word_refs], 0)
    mask = mask_ref[...]
    mixed = jnp.zeros((rows, 128), F32)
    for h in range(2):
        scores = dot_nt(jnp.where(halves[h], q, none), k)
        word = (words & 0xFFFF) if h == 0 else lax.shift_right_logical(words, 16)
        scores = scores + word.astype(F32) * unit + mask
        expo = jnp.exp(scores - jnp.max(scores, -1, keepdims=True))
        probs = (expo * (1.0 / jnp.sum(expo, -1, keepdims=True))).astype(BF16)
        p_ref[h] = probs
        mixed = mixed + dot_nn(probs, jnp.where(halves[h], v, none))
    o_ref[...] = mixed.astype(BF16)


def attend(unit, qkv, words, segments):
    pairs = words[0].shape[0]
    rows = qkv.shape[0]
    col = [pl.BlockSpec((rows, 128), lambda p, n=n: (0, n * pairs + p)) for n in range(3)]
    flops = pairs * 4 * 2 * rows * rows * 128
    return pl.pallas_call(
        attend_kernel,
        grid=(pairs,),
        in_specs=[
            whole((1, 1)),
            col[0],
            col[1],
            col[2],
            whole((rows, 1)),
            whole((1, rows)),
        ]
        + [pl.BlockSpec((1,) + w.shape[1:], lambda p: (p, 0, 0)) for w in words],
        out_specs=[
            pl.BlockSpec((2, rows, rows), lambda p: (p, 0, 0)),
            pl.BlockSpec((rows, 128), lambda p: (0, p)),
        ],
        out_shape=[
            jax.ShapeDtypeStruct((2 * pairs, rows, rows), BF16),
            jax.ShapeDtypeStruct((rows, pairs * 128), BF16),
        ],
        scratch_shapes=[pltpu.VMEM((rows, rows), F32)],
        compiler_params=pltpu.CompilerParams(vmem_limit_bytes=LIMIT),
        cost_estimate=cost(flops, 40_000_000),
        name="attend",
    )(unit, qkv, qkv, qkv, *segments, *words)


def attend_back_kernel(q_ref, k_ref, v_ref, g_ref, p_ref, ds_ref, dq_ref, dk_ref, dv_ref):
    rows = q_ref.shape[0]
    halves = lane_halves(rows)
    q, k, v, g = q_ref[...], k_ref[...], v_ref[...], g_ref[...]
    none = jnp.zeros_like(q)
    blank = jnp.zeros((rows, ds_ref.shape[2] - rows), BF16)
    dq = jnp.zeros((rows, 128), F32)
    dk, dv = dq, dq
    for h in range(2):
        low = p_ref[h]
        probs = low.astype(F32)
        weighted = probs * dot_nt(g, jnp.where(halves[h], v, none))
        ds = (weighted - probs * jnp.sum(weighted, -1, keepdims=True)).astype(BF16)
        ds_ref[h] = jnp.concatenate([ds, blank], 1)
        dq = dq + dot_nn(ds, jnp.where(halves[h], k, none))
        dv = dv + dot_tn(low, jnp.where(halves[h], g, none))
        dk = dk + dot_tn(ds, jnp.where(halves[h], q, none))
    dq_ref[...] = (dq * 0.125).astype(BF16)
    dk_ref[...] = dk.astype(BF16)
    dv_ref[...] = dv.astype(BF16)


def attend_back(qkv, grad, probs, first, pairs):
    every = probs.shape[0] // 2
    rows = qkv.shape[0]
    col = [pl.BlockSpec((rows, 128), lambda p, n=n: (0, n * every + p + first)) for n in range(3)]
    new = pl.BlockSpec((rows, 128), lambda p: (0, p))
    big = pl.BlockSpec((2, rows, rows), lambda p: (p + first, 0, 0))
    lanes = pl.cdiv(rows, 128) * 128
    out = jax.ShapeDtypeStruct((rows, pairs * 128), BF16)
    flops = pairs * 2 * 4 * 2 * rows * rows * 128
    return pl.pallas_call(
        attend_back_kernel,
        grid=(pairs,),
        in_specs=[col[0], col[1], col[2], col[0], big],
        out_specs=[pl.BlockSpec((2, rows, lanes), lambda p: (p, 0, 0)), new, new, new],
        out_shape=[jax.ShapeDtypeStruct((2 * pairs, rows, lanes), BF16), out, out, out],
        compiler_params=pltpu.CompilerParams(vmem_limit_bytes=LIMIT),
        cost_estimate=cost(flops, 8_000_000 * pairs),
        name="attend_back",
    )(qkv, qkv, qkv, grad, probs)


def table_kernel(first, levels, block_ref, count_ref, rel_ref, x_ref, y_ref, *refs):
    ds_refs, out_ref, rows_ref = refs[:-2], refs[-2], refs[-1]
    place = pl.program_id(0)
    step = rel_ref.shape[1]
    every = rel_ref.shape[2] // 128

    @pl.when(place == 0)
    def _():
        out_ref[...] = jnp.zeros_like(out_ref)
        rows_ref[...] = jnp.zeros_like(rows_ref)

    heads = [(ref, n) for ref in ds_refs for n in range(ref.shape[0])]

    def group(r, start, blocks):
        width = blocks * 128
        level = lax.broadcasted_iota(jnp.int32, (16, width), 0).astype(F32).astype(BF16)
        one = jnp.ones((16, width), BF16)
        none = jnp.zeros((16, width), BF16)

        def one_hot(ids, count):
            wide = jnp.broadcast_to(ids, (16, width)).astype(BF16)
            return [jnp.where(wide == level + BF16(16 * t), one, none) for t in range(count // 16)]

        rows = pl.ds(pl.multiple_of(r * 16, 16), 16)
        lanes = pl.ds(pl.multiple_of(start * 128, 128), width)
        for h, (ref, n) in enumerate(heads):
            values = ref[n, rows, lanes].astype(F32)
            for c in range(blocks):
                rows_ref[c, pl.ds(h, 16, stride=16), :] = values[:, 128 * c : 128 * c + 128]
        total = out_ref[...]
        ids = [ref[0, rows, lanes].astype(F32) for ref in (x_ref, y_ref, rel_ref)]
        counts = (levels[1], levels[2], levels[0])
        for n in range(16):
            grads = jnp.concatenate(
                [rows_ref[c, 16 * n : 16 * n + 16, :].astype(BF16) for c in range(blocks)], 1
            )
            hot = [one_hot(i[n : n + 1], count) for i, count in zip(ids, counts)]
            hot = jnp.concatenate(hot[0] + hot[1] + hot[2], 0)
            total = total + dot_nt(hot, grads)
        out_ref[...] = total

    def body(r, _):
        index = (place + first) * (step // 16) + r
        start, count = block_ref[index], count_ref[index]
        for blocks in range(1, every + 1):

            @pl.when(count == blocks)
            def _(blocks=blocks):
                group(r, start, blocks)

        return 0

    lax.fori_loop(0, step // 16, body, 0)


def table_sums(ranges, rel, x, y, ds, levels, first, steps):
    step = 64
    lanes = ds[0].shape[2]
    ids = pl.BlockSpec((1, step, lanes), lambda i, *_: (0, i + first, 0))
    return pl.pallas_call(
        functools.partial(table_kernel, first, levels),
        grid_spec=pltpu.PrefetchScalarGridSpec(
            num_scalar_prefetch=2,
            grid=(steps,),
            in_specs=[ids, ids, ids]
            + [pl.BlockSpec((d.shape[0], step, lanes), lambda i, *_: (0, i + first, 0)) for d in ds],
            out_specs=whole((sum(levels), 16)),
            scratch_shapes=[pltpu.VMEM((lanes // 128, 256, 128), F32)],
        ),
        out_shape=jax.ShapeDtypeStruct((sum(levels), 16), F32),
        compiler_params=pltpu.CompilerParams(vmem_limit_bytes=LIMIT),
        cost_estimate=cost(0, 8_000_000 * steps),
        name="table_sums",
    )(*ranges, rel, x, y, *ds)


def document_blocks(segments, rows):
    length = segments.shape[0]
    first = segments[0:rows:16]
    last = segments[jnp.minimum(jnp.arange(15, rows, 16), length - 1)]
    begin = jnp.sum(segments[None, :] < first[:, None], 1, dtype=jnp.int32)
    end = jnp.sum(segments[None, :] <= last[:, None], 1, dtype=jnp.int32)
    return begin // 128, (end + 127) // 128 - begin // 128


def norm_stats(values):
    center = values - jnp.mean(values, -1, keepdims=True)
    scale = lax.rsqrt(jnp.mean(center * center, -1, keepdims=True) + EPS)
    return center * scale, scale


def norm_back(grad, normed, scale, gain):
    scaled = grad * gain
    return scale * (
        scaled
        - jnp.mean(scaled, -1, keepdims=True)
        - normed * jnp.mean(scaled * normed, -1, keepdims=True)
    )


def on_device(
    text_hidden,
    visual_maps,
    patch_order,
    segment_ids,
    rel_bucket,
    x_bucket,
    y_bucket,
    bn_scale,
    bn_shift,
    vis_proj,
    w_query,
    w_key,
    w_value,
    w_output,
    rel_table,
    x_table,
    y_table,
    first_gain,
    first_bias,
    w_inner,
    b_inner,
    w_outer,
    b_outer,
    second_gain,
    second_bias,
    cotangent,
):
    heads = rel_table.shape[1]
    pairs = heads // 2
    visual_len = patch_order.shape[1]
    length = segment_ids.shape[1]
    text_len = length - visual_len
    width = w_query.shape[1]
    dp, ffn = lax.axis_size("dp"), lax.axis_size("ffn")
    place, here = lax.axis_index("dp"), lax.axis_index("ffn")
    devices = dp * ffn
    rows = pl.cdiv(length, 64) * 64
    count = visual_maps.shape[0] * devices
    levels = (rel_table.shape[0], x_table.shape[0], y_table.shape[0])

    inner_rows, columns = w_inner.shape
    outer_shard = w_outer.T
    steps = rows // 64

    first_set = Gather(*pack_first(w_query, w_key, w_value, vis_proj, visual_maps))
    plain = columns == width
    wide_shards = jnp.concatenate([outer_shard, w_inner], 0)
    if plain:
        late_set = Gather(
            jnp.concatenate([w_output, wide_shards], 0), [w_output.shape[0], inner_rows, inner_rows]
        )
    else:
        late_set = Gather(w_output, [w_output.shape[0]])
        wide_set = Gather(wide_shards, [inner_rows, inner_rows])

    first_set.along_ffn()
    tables = jnp.concatenate([x_table, y_table, rel_table], 0).T
    tables = jnp.pad(tables, ((0, 0), (0, 256 - tables.shape[1])))
    cuts = [0, steps * 4 // 9, steps * 7 // 9, steps]
    words = [None] * 3
    words[0], unit = bias_words(rel_bucket, x_bucket, y_bucket, tables, 0, cuts[1])
    ranges = document_blocks(segment_ids[0], rows)
    lines = jnp.stack([first_gain, first_bias, b_outer, second_gain, second_bias])
    inner_b = b_inner.reshape(ffn, 1, columns)
    segments = jnp.pad(segment_ids[0], (0, rows - length), constant_values=-1)
    segments = (segments[:, None], segments[None, :])
    bn_lines = jnp.stack([bn_scale, bn_shift])
    state, late, words[0], tables, ranges, lines, inner_b, segments, bn_lines = epoch(
        first_set.state(),
        late_set.state(),
        words[0],
        tables,
        ranges,
        lines,
        inner_b,
        segments,
        bn_lines,
    )
    first_set.hold(state)
    late_set.hold(late)

    first_set.order()
    first_set.near(3 * w_query.shape[0] * ffn)
    late_set.along_ffn()
    words[1], _ = bias_words(rel_bucket, x_bucket, y_bucket, tables, cuts[1], cuts[2] - cuts[1])
    state, late, words[1], tables = epoch(first_set.state(), late_set.state(), words[1], tables)
    first_set.hold(state)
    late_set.hold(late)

    first_set.diagonal()
    words[2], _ = bias_words(rel_bucket, x_bucket, y_bucket, tables, cuts[2], cuts[3] - cuts[2])
    late_set.order()
    state, late, words[2] = epoch(first_set.state(), late_set.state(), words[2])
    first_set.hold(state)
    late_set.hold(late)

    late_rows = w_output.shape[0] * ffn
    first_set.across()
    late_set.near(late_rows + ffn * inner_rows if plain else 0)
    layout, row = [], 0
    for n, size in enumerate(first_set.rows):
        layout.append((row, size * ffn, max(n - 2, 0), 0, n * width if n < 3 else 0))
        row += size * ffn
    order_col = patch_order.reshape(visual_len, 1)
    qkv_full, proj_full, hidden, lowered, qkv, bn_rows, bn_stats = first_rows(
        first_set.parts(),
        layout,
        text_hidden,
        visual_maps,
        order_col,
        bn_lines,
        rows,
        vis_proj.shape[0] * devices,
        first_set.rows[-1],
    )
    qkv, state = epoch(qkv, late_set.state())
    late_set.hold(state)

    late_set.diagonal()
    probs, mixed = attend(unit, qkv, words, segments)
    probs, mixed, state = epoch(probs, mixed, late_set.state())
    late_set.hold(state)
    late_set.across()
    layout = [(0, late_rows, 0, 0, 0)]
    shift = late_rows
    parts = late_set.parts()
    if not plain:
        parts = [(block, bits, 0) for block, bits, _ in parts]
        wide_set.along_ffn()
        wide_set.order()
        wide_set.near(0)
        wide_set.diagonal()
        wide_set.across()
        shift = 0
    wide_layout = [
        (shift + (n * ffn + f) * inner_rows, inner_rows, 1 + n, f * width, 0)
        for n in range(2)
        for f in range(ffn)
    ]
    feeds = [(parts, layout + wide_layout if plain else layout)]
    if not plain:
        feeds.append((wide_set.parts(), wide_layout))
    (
        first_n,
        first_r,
        output,
        grad_first,
        sums_two,
        inner_sums,
        output_full,
        mine,
        away,
    ) = feed_forward(feeds, mixed, hidden, lines, inner_b, cotangent, inner_rows)

    wide = Scatter(mine, away, lambda value, index: pick(value, index, 1))
    wide.core()
    grad_attn, attn_low, grad_mixed, sums_one = norm_rows(grad_first, first_n, first_r, lines, output_full)
    state, grad_mixed = epoch(wide.held(), grad_mixed)
    wide.hold(state)

    wide.near()
    half = pairs // 2
    back_low = attend_back(qkv, grad_mixed, probs, 0, half)
    state, back_low, qkv = epoch(wide.held(), back_low, qkv)
    wide.hold(state)

    wide.quads()
    back_high = attend_back(qkv, grad_mixed, probs, half, pairs - half)
    back = list(zip(back_low[1:], back_high[1:]))
    tokens_grad, mine, away = tail_rows(
        back,
        qkv_full,
        grad_attn,
        attn_low,
        mixed,
        lowered,
        order_col,
        bn_rows,
        text_len,
        w_query.shape[0],
    )
    ds = (back_low[0], back_high[0])
    wide.value, mine, away, ds, tokens_grad = epoch(wide.value, mine, away, ds, tokens_grad)

    wide.along_ffn()
    tail = Scatter(mine, away, lambda value, index: pick(value, index, 0))
    tail.core()
    text_grad, grad_bn, bn_sums = text_rows(
        back, qkv_full, grad_attn, tokens_grad, visual_maps, bn_stats, proj_full, text_len
    )
    state, bn_sums, ds = epoch(tail.held(), bn_sums, ds)
    tail.hold(state)

    tail.near()
    begin = (steps + 1) // 2
    low_sums = table_sums(ranges, rel_bucket, x_bucket, y_bucket, ds, levels, 0, begin)
    state, low_sums, ds, wide.pieces = epoch(tail.held(), low_sums, ds, wide.pieces)
    tail.hold(state)
    wide_sum = wide.total()
    tail.quads()
    sums = table_sums(ranges, rel_bucket, x_bucket, y_bucket, ds, levels, begin, steps - begin)
    sums = sums + low_sums
    parts = [bn_sums, sums_one, sums_two, inner_sums, sums]
    total = Sum(jnp.concatenate([part.reshape(-1) for part in parts]).reshape(-1, 128))
    for _ in range(ffn.bit_length() - 1):
        total.step()
    tail.value, total.values = epoch(tail.value, total.values)

    tail.along_ffn()
    tail_sum = tail.total()
    early = total.finish().reshape(-1)
    channels = visual_maps.shape[1]
    shift_grad, scale_grad = early[:channels], early[channels : 2 * channels]
    early = early[2 * channels :]
    sums = early[early.shape[0] - sums.size :].reshape(sums.shape)[:, :heads]
    normalized = (visual_maps.astype(F32) - bn_stats[0]) * bn_stats[1]
    visual_grad = (
        bn_scale * bn_stats[1] * (grad_bn - shift_grad / count - normalized * scale_grad / count)
    )
    shards, row = [], 0
    for size in [w_query.shape[0]] * 4 + [vis_proj.shape[0]]:
        shards.append(tail_sum[row : row + size])
        row += size
    return (
        output,
        text_grad,
        visual_grad,
        scale_grad,
        shift_grad,
        shards[4],
        shards[0],
        shards[1],
        shards[2],
        shards[3],
        sums[levels[1] + levels[2] :],
        sums[: levels[1]],
        sums[levels[1] : levels[1] + levels[2]],
        early[:width],
        early[width : 2 * width],
        wide_sum[0],
        early[5 * width : 5 * width + b_inner.shape[0]],
        wide_sum[1].T,
        early[4 * width : 5 * width],
        early[2 * width : 3 * width],
        early[3 * width : 4 * width],
    )


def solution(mesh):
    rows = P(ALL, None)
    cube = P(ALL, None, None)
    return jax.shard_map(
        on_device,
        mesh=mesh,
        in_specs=(rows,) * 4
        + (cube,) * 3
        + (P(),) * 2
        + (rows,) * 5
        + (P(),) * 5
        + (P("dp", "ffn"), P(), P("ffn", "dp"))
        + (P(),) * 3
        + (rows,),
        out_specs=(rows,) * 3
        + (P(),) * 2
        + (rows,) * 5
        + (P(),) * 5
        + (P("dp", "ffn"), P(), P("ffn", "dp"))
        + (P(),) * 3,
        check_vma=False,
    )
```

```python
import functools

import jax
import jax.numpy as jnp
from jax import lax
from jax.experimental import pallas as pl
from jax.experimental.pallas import tpu as pltpu
from jax.sharding import PartitionSpec as P

EPS = 1e-05
NEG = -1e30
F32 = jnp.float32
BF16 = jnp.bfloat16
ALL = ("dp", "ffn")
LEVELS = 21845.0
MIB = 2**20


def dot_nn(a, b):
    return lax.dot_general(a, b, (((1,), (0,)), ((), ())), preferred_element_type=F32)


def dot_nt(a, b):
    return lax.dot_general(a, b, (((1,), (1,)), ((), ())), preferred_element_type=F32)


def dot_tn(a, b):
    return lax.dot_general(a, b, (((0,), (0,)), ((), ())), preferred_element_type=F32)


def pad_rows(values, rows):
    return jnp.pad(values, ((0, rows - values.shape[0]), (0, 0)))


def send_dp(values, bits):
    size = lax.axis_size("dp")
    return lax.ppermute(values, "dp", [(i, i ^ bits) for i in range(size)])


def send_ffn(values, shift):
    size = lax.axis_size("ffn")
    return lax.ppermute(values, "ffn", [(i, (i + shift) % size) for i in range(size)])


def swap_ffn(values, bits):
    size = lax.axis_size("ffn")
    return lax.ppermute(values, "ffn", [(i, i ^ bits) for i in range(size)])


def exchanges():
    steps = []
    for axis, send in (("dp", send_dp), ("ffn", swap_ffn)):
        bit = 1
        while bit < lax.axis_size(axis):
            steps.append(functools.partial(send, bits=bit))
            bit *= 2
    return steps


class Sum:
    def __init__(self, values):
        self.values = values
        self.steps = exchanges()

    def step(self):
        if self.steps:
            self.values = self.values + self.steps.pop(0)(self.values)

    def finish(self):
        while self.steps:
            self.step()
        return self.values


class Gather:
    def __init__(self, own, rows):
        self.own = own
        self.rows = rows

    def along_ffn(self, begin=1, end=None):
        size = lax.axis_size("ffn")
        self.far = self.far[:begin] if begin > 1 else [self.own]
        self.far += [send_ffn(self.own, k) for k in range(begin, end or size)]

    def order(self):
        size = lax.axis_size("ffn")
        here = lax.axis_index("ffn")
        if all(rows % 8 == 0 for rows in self.rows):
            self.block = order_blocks(here, self.far, self.rows)
            return
        pieces = []
        for slot in range(size):
            value = self.far[0]
            for k in range(1, size):
                value = jnp.where((here - k + size) % size == slot, self.far[k], value)
            pieces.append(value)
        begin, ordered = 0, []
        for rows in self.rows:
            ordered += [value[begin : begin + rows] for value in pieces]
            begin += rows
        self.block = jnp.concatenate(ordered, 0)

    def near(self, cut):
        quads = lax.axis_size("dp") // 2
        self.cut = cut
        self.others = [send_dp(self.block, 1)]
        if quads == 4:
            self.mine = [self.block, send_dp(self.block, 2), send_dp(self.block, 4)]
        else:
            self.mine = [self.block] + [send_dp(self.block, 2 * k) for k in range(1, quads)]

    def diagonal(self):
        self.others += [send_dp(block, 1) for block in self.mine[1:]]
        if lax.axis_size("dp") == 8:
            low = send_dp(self.mine[1][: self.cut], 4)
            high = send_dp(self.mine[2][self.cut :], 2)
            self.mine.append((low, high))

    def across(self):
        if lax.axis_size("dp") == 8:
            self.others.append(tuple(send_dp(piece, 1) for piece in self.mine[3]))

    def state(self):
        return {k: v for k, v in vars(self).items() if k in ("own", "far", "block", "mine", "others")}

    def hold(self, state):
        vars(self).update(state)

    def parts(self):
        found = []
        for k, (mine, other) in enumerate(zip(self.mine, self.others)):
            for bits, block in ((2 * k, mine), (2 * k + 1, other)):
                if isinstance(block, tuple):
                    found += [(block[0], bits, 0), (block[1], bits, self.cut)]
                else:
                    found.append((block, bits, 0))
        return found


def epoch(*values):
    return lax.optimization_barrier(values)


def pick(values, index, axis):
    return lax.dynamic_index_in_dim(values, index, axis, keepdims=False)


def plus(a, b):
    return (a.astype(F32) + b.astype(F32)).astype(BF16)


class Scatter:
    def __init__(self, mine, away, far):
        self.value = mine
        self.away = away
        self.far = far

    def core(self):
        self.got = send_dp(self.away, 1)

    def near(self):
        mine, got = self.value, self.got
        if mine.shape[0] == 4:
            half = mine.shape[1] // 2
            self.low = send_dp(plus(mine[3, :half], got[3, :half]), 4)
            self.high = send_dp(plus(mine[3, half:], got[3, half:]), 2)

    def prepare(self):
        mine, got = self.value, self.got
        half = mine.shape[1] // 2
        self.blocks = []
        for k in range(1, mine.shape[0]):
            block = mine[k].astype(F32) + got[k].astype(F32)
            if mine.shape[0] == 4 and k == 1:
                block = jnp.concatenate([block[:half] + self.low.astype(F32), block[half:]], 0)
            if mine.shape[0] == 4 and k == 2:
                block = jnp.concatenate([block[:half], block[half:] + self.high.astype(F32)], 0)
            if mine.shape[0] == 4 and k == 3:
                continue
            self.blocks.append(block.astype(BF16))

    def quads(self):
        self.blocks = [send_dp(block, 2 * k) for k, block in enumerate(self.blocks, 1)]

    def join(self):
        own = self.value[0].astype(F32) + self.got[0].astype(F32)
        self.value = (own + sum(block.astype(F32) for block in self.blocks)).astype(BF16)

    def held(self):
        return {k: v for k, v in vars(self).items() if k != "far"}

    def hold(self, state):
        vars(self).update(state)

    def along_ffn(self, begin=1, end=None):
        size = lax.axis_size("ffn")
        here = lax.axis_index("ffn")
        self.pieces = self.pieces[:begin] if begin > 1 else [self.far(self.value, here)]
        for k in range(begin, end or size):
            self.pieces.append(send_ffn(self.far(self.value, (here + k) % size), k))

    def total(self):
        return sum(piece.astype(F32) for piece in self.pieces)


LIMIT = 56 * MIB


def whole(shape):
    return pl.BlockSpec(shape, lambda *_: (0,) * len(shape))


def cost(flops, nbytes):
    return pl.CostEstimate(flops=flops // 1000, bytes_accessed=nbytes // 1000, transcendentals=0)


def pack_kernel(q_ref, k_ref, v_ref, p_ref, visual_ref, out_ref):
    row = 0
    for ref in (q_ref, k_ref, v_ref, p_ref):
        out_ref[row : row + ref.shape[0], :] = ref[...]
        row += ref.shape[0]
    width = out_ref.shape[1]
    count = visual_ref.shape[0]
    visual = visual_ref[...].astype(F32)
    mean = jnp.sum(visual, 0, keepdims=True) * (1.0 / count)
    gap = visual - mean
    spread = jnp.sum(gap * gap, 0, keepdims=True)
    channels = visual_ref.shape[1]
    chunks = pl.cdiv(channels, width)
    blank = jnp.zeros((1, chunks * width - channels), F32)
    pieces = []
    for values, times in ((mean, 3), (spread, 2)):
        if chunks * width > channels:
            values = jnp.concatenate([values, blank], 1)
        for _ in range(times):
            piece = values.astype(BF16).astype(F32)
            values = values - piece
            pieces += [piece[:, n * width : (n + 1) * width] for n in range(chunks)]
    pieces += [jnp.zeros((1, width), F32)] * (out_ref.shape[0] - row - len(pieces))
    out_ref[row:, :] = jnp.concatenate(pieces, 0).astype(BF16)


def pack_first(w_query, w_key, w_value, vis_proj, visual):
    width = w_query.shape[1]
    moments = pl.cdiv(5 * pl.cdiv(visual.shape[1], width), 16) * 16
    rows = [w.shape[0] for w in (w_query, w_key, w_value, vis_proj)] + [moments]
    own = pl.pallas_call(
        pack_kernel,
        out_shape=jax.ShapeDtypeStruct((sum(rows), width), BF16),
        name="pack_first",
    )(w_query, w_key, w_value, vis_proj, visual)
    return own, rows


def order_kernel(rows, here_ref, *refs):
    parts, out_ref = refs[:-1], refs[-1]
    size = len(parts)
    here = here_ref[0]
    for index in range(size):

        @pl.when(here == index)
        def _(index=index):
            begin = 0
            for count in rows:
                for k in range(size):
                    row = begin * size + (index - k) % size * count
                    out_ref[row : row + count, :] = parts[k][begin : begin + count, :]
                begin += count


def order_blocks(here, parts, rows):
    width = parts[0].shape[1]
    return pl.pallas_call(
        functools.partial(order_kernel, rows),
        in_specs=[pl.BlockSpec(memory_space=pltpu.SMEM)]
        + [pl.BlockSpec(memory_space=pltpu.VMEM)] * len(parts),
        out_specs=pl.BlockSpec(memory_space=pltpu.VMEM),
        out_shape=jax.ShapeDtypeStruct((len(parts) * sum(rows), width), BF16),
        name="order_blocks",
    )(here.reshape(1).astype(jnp.int32), *parts)


def place_entries(parts, layout):
    entries = []
    for n, (block, _, first) in enumerate(parts):
        for begin, rows, out, base, lane in layout:
            if first <= begin and begin + rows <= first + block.shape[0]:
                entries.append((n, begin - first, rows, out, base, lane))
    return entries


def place_index(parts):
    place = lax.axis_index("dp")
    return jnp.stack([place ^ bits for _, bits, _ in parts]).astype(jnp.int32)


def part_copies(entries, place_ref, parts, outs, sems):
    copies = []
    for n, (part, begin, rows, out, base, lane) in enumerate(entries):
        target = pl.multiple_of(base + place_ref[part] * rows, 16)
        width = parts[part].shape[1]
        copies.append(
            pltpu.make_async_copy(
                parts[part].at[pl.ds(begin, rows), :],
                outs[out].at[pl.ds(target, rows), pl.ds(lane, width)],
                sems.at[n],
            )
        )
    return copies


def picked(order_col, size):
    lane = lax.broadcasted_iota(jnp.int32, (size, size), 1)
    return (order_col == lane).astype(F32)


def exact(a, b, dims):
    return lax.dot_general(
        a, b, (dims, ((), ())), precision=lax.Precision.HIGHEST, preferred_element_type=F32
    )


def first_kernel(entries, count, devices, place_ref, *refs):
    parts, refs = refs[:count], refs[count:]
    text_ref, visual_ref, order_ref, lines_ref = refs[:4]
    qkv_w_ref, proj_ref, hidden_ref, low_ref, qkv_ref, bn_ref, stats_ref = refs[4:11]
    moments_ref, sems = refs[11:]
    outs = (qkv_w_ref, proj_ref, moments_ref)
    copies = part_copies(entries, place_ref, parts, outs, sems)
    for copy in copies:
        copy.start()
    copies = [(entry[3], copy) for entry, copy in zip(entries, copies)]
    text_len, width = text_ref.shape
    visual_len, channels = visual_ref.shape
    hidden_ref[:text_len, :] = text_ref[...].astype(F32)
    low_ref[:text_len, :] = text_ref[...]
    for out, copy in copies:
        if out == 2:
            copy.wait()
    chunks = pl.cdiv(channels, width)
    moments = moments_ref[...].astype(F32).reshape(devices, -1, width)
    means = sum(moments[:, n * chunks : (n + 1) * chunks] for n in range(3))
    spreads = sum(moments[:, n * chunks : (n + 1) * chunks] for n in range(3, 5))
    average = jnp.sum(means, 0) * (1.0 / devices)
    gap = means - average[None]
    rows = visual_len * devices
    spread = (jnp.sum(spreads, 0) + visual_len * jnp.sum(gap * gap, 0)) * (1.0 / rows)
    inverse = lax.rsqrt(spread + EPS)

    def flat(values):
        pieces = [values[n : n + 1, :] for n in range(chunks)]
        return jnp.concatenate(pieces, 1)[:, :channels]

    average, inverse = flat(average), flat(inverse)
    stats_ref[0:1, :] = average
    stats_ref[1:2, :] = inverse
    normed = (visual_ref[...].astype(F32) - average) * inverse
    bn_rows = (normed * lines_ref[0:1, :] + lines_ref[1:2, :]).astype(BF16)
    bn_ref[...] = bn_rows
    for out, copy in copies:
        if out == 1:
            copy.wait()
    tokens = dot_nn(bn_rows, proj_ref[...])
    tokens = exact(picked(order_ref[...], visual_len), tokens, ((1,), (0,)))
    blank = jnp.zeros((hidden_ref.shape[0] - text_len - visual_len, width), F32)
    tokens = jnp.concatenate([tokens, blank], 0)
    hidden_ref[text_len:, :] = tokens
    low_ref[text_len:, :] = tokens.astype(BF16)
    for out, copy in copies:
        if out == 0:
            copy.wait()
    low = low_ref[...]
    for n in range(3):
        lanes = slice(n * width, (n + 1) * width)
        values = dot_nn(low, qkv_w_ref[:, lanes])
        qkv_ref[:, lanes] = (values * 0.125 if n == 0 else values).astype(BF16)


def first_rows(parts, layout, text, visual, order, lines, rows, proj_rows, moment_rows):
    devices = lax.axis_size("dp") * lax.axis_size("ffn")
    width = text.shape[1]
    channels = visual.shape[1]
    entries = place_entries(parts, layout)
    vmem = pl.BlockSpec(memory_space=pltpu.VMEM)
    shapes = [
        ((width, 3 * width), BF16),
        ((proj_rows, width), BF16),
        ((rows, width), F32),
        ((rows, width), BF16),
        ((rows, 3 * width), BF16),
        ((visual.shape[0], channels), BF16),
        ((2, channels), F32),
    ]
    return pl.pallas_call(
        functools.partial(first_kernel, entries, len(parts), devices),
        in_specs=[pl.BlockSpec(memory_space=pltpu.SMEM)]
        + [pl.BlockSpec(memory_space=pl.ANY)] * len(parts)
        + [vmem] * 4,
        out_specs=[vmem] * len(shapes),
        out_shape=[jax.ShapeDtypeStruct(*shape) for shape in shapes],
        scratch_shapes=[
            pltpu.VMEM((moment_rows * devices, width), BF16),
            pltpu.SemaphoreType.DMA((len(entries),)),
        ],
        compiler_params=pltpu.CompilerParams(vmem_limit_bytes=LIMIT),
        cost_estimate=cost(0, 25_000_000),
        name="first_rows",
    )(
        place_index(parts),
        *[block for block, _, _ in parts],
        text,
        visual,
        order,
        lines,
    )


def store_blocks(mine_ref, away_ref, core, quad, store):
    quads = mine_ref.shape[0]
    for bit in range(2):

        @pl.when(core == bit)
        def _(bit=bit):
            for dp in range(2 * quads):
                ref = mine_ref if dp % 2 == bit else away_ref
                store(ref, (dp // 2) ^ quad, dp)


def place_pair():
    place = lax.axis_index("dp")
    return jnp.stack([place % 2, place // 2]).astype(jnp.int32)


def feed_kernel(entries, count, length, ffn, place_ref, core_ref, *refs):
    parts, refs = refs[:count], refs[count:]
    mixed_ref, hidden_ref, lines_ref, inner_b_ref, ct_ref = refs[:5]
    normed_ref, scale_ref, output_ref, total_ref, sums_ref, inner_sums_ref = refs[5:11]
    out_w_ref, mine_ref, away_ref = refs[11:14]
    outer_w_ref, inner_w_ref, act_ref, slope_ref, first_ref, low_ref = refs[14:20]
    first_turned, low_turned, sems = refs[20:]
    step = pl.program_id(0)
    width = hidden_ref.shape[1]
    outs = (out_w_ref, outer_w_ref, inner_w_ref)
    gain1, bias1, outer_b, gain2, bias2 = [lines_ref[n : n + 1, :] for n in range(5)]

    @pl.when(step == 0)
    def _():
        for copy in part_copies(entries, place_ref, parts, outs, sems):
            copy.start()

    for index in range(ffn):

        @pl.when(step == index)
        def _(index=index):
            copies = part_copies(entries, place_ref, parts, outs, sems)
            for (_, _, _, out, base, _), copy in zip(entries, copies):
                if (out == 0 and index == 0) or (out > 0 and base == index * width):
                    copy.wait()

    @pl.when(step == 0)
    def _():
        attended = dot_nn(mixed_ref[...], out_w_ref[...])
        normed, scale = norm_stats(hidden_ref[...] + attended)
        first = normed * gain1 + bias1
        normed_ref[...] = normed
        scale_ref[...] = scale
        low = first.astype(BF16)
        first_ref[...] = low
        total_ref[...] = first + outer_b
        first_turned[...] = low.T

    @pl.when(step < ffn)
    def _():
        rows = pl.ds(pl.multiple_of(step * width, width), width)
        inner = dot_nn(first_ref[...], inner_w_ref[rows, :]) + inner_b_ref[step]
        root = 0.7978845608028654
        square = inner * inner
        half = 0.5 + 0.5 * jnp.tanh(inner * (root + (0.044715 * root) * square))
        act = inner * half
        slope = half + act * (1.0 - half) * (2 * root + (6 * 0.044715 * root) * square)
        slope_ref[step] = slope.astype(BF16)
        act = act.astype(BF16)
        act_ref[step] = act
        total_ref[...] += dot_nt(act, outer_w_ref[rows, :])

    @pl.when(step == ffn - 1)
    def _():
        normed, scale = norm_stats(total_ref[...])
        output_ref[...] = (normed * gain2 + bias2).astype(BF16)
        row = lax.broadcasted_iota(jnp.int32, (normed.shape[0], 1), 0)
        ct = jnp.where(row < length, ct_ref[...].astype(F32), 0.0)
        grad = norm_back(ct, normed, scale, gain2)
        total_ref[...] = grad
        low = grad.astype(BF16)
        low_ref[...] = low
        low_turned[...] = low.T
        sums_ref[0:1, :] = jnp.sum(ct * normed, 0, keepdims=True)
        sums_ref[1:2, :] = jnp.sum(ct, 0, keepdims=True)
        sums_ref[2:3, :] = jnp.sum(grad, 0, keepdims=True)

    @pl.when(step >= ffn)
    def _():
        f = step - ffn
        rows = pl.ds(pl.multiple_of(f * width, width), width)
        grad = dot_nn(low_ref[...], outer_w_ref[rows, :]) * slope_ref[f].astype(F32)
        inner_sums_ref[0] = jnp.sum(grad, 0, keepdims=True)
        grad = grad.astype(BF16)
        total_ref[...] += dot_nt(grad, inner_w_ref[rows, :])
        inner = dot_nn(first_turned[...], grad).astype(BF16)
        outer = dot_nn(low_turned[...], act_ref[f]).astype(BF16)
        size = mine_ref.shape[3]

        def store(ref, slot, dp):
            ref[slot, 0, 0] = inner[dp * size : (dp + 1) * size]
            ref[slot, 1, 0] = outer[dp * size : (dp + 1) * size]

        store_blocks(mine_ref, away_ref, core_ref[0], core_ref[1], store)


def feed_forward(feeds, mixed, hidden, lines, inner_b, ct, inner_rows):
    parts, entries = [], []
    for some, layout in feeds:
        for part, *entry in place_entries(some, layout):
            entries.append((part + len(parts), *entry))
        parts += some
    entries.sort(key=lambda entry: (entry[3] > 0, entry[4], -entry[3]))
    rows, width = hidden.shape
    ffn, _, columns = inner_b.shape
    quads = lax.axis_size("dp") // 2
    square = whole((rows, width))
    back = lambda i: jnp.maximum(i - ffn, 0)
    block = pl.BlockSpec((quads, 2, 1, inner_rows, columns), lambda i: (0, 0, back(i), 0, 0))
    blocks = jax.ShapeDtypeStruct((quads, 2, ffn, inner_rows, columns), BF16)
    smem = pl.BlockSpec(memory_space=pltpu.SMEM)
    shapes = [
        ((rows, width), F32),
        ((rows, 1), F32),
        (ct.shape, BF16),
        ((rows, width), F32),
        ((3, width), F32),
        ((ffn, 1, columns), F32),
        ((width, width), BF16),
    ]
    return pl.pallas_call(
        functools.partial(feed_kernel, entries, len(parts), ct.shape[0], ffn),
        grid=(2 * ffn,),
        in_specs=[smem, smem]
        + [pl.BlockSpec(memory_space=pl.ANY)] * len(parts)
        + [square, square, whole(lines.shape), whole(inner_b.shape), square],
        out_specs=[square, whole((rows, 1)), square, square, whole((3, width))]
        + [pl.BlockSpec((1, 1, columns), lambda i: (back(i), 0, 0)), whole((width, width))]
        + [block, block],
        out_shape=[jax.ShapeDtypeStruct(*shape) for shape in shapes] + [blocks, blocks],
        scratch_shapes=[
            pltpu.VMEM((ffn * width, columns), BF16),
            pltpu.VMEM((ffn * width, columns), BF16),
            pltpu.VMEM((ffn, rows, columns), BF16),
            pltpu.VMEM((ffn, rows, columns), BF16),
            pltpu.VMEM((rows, width), BF16),
            pltpu.VMEM((rows, width), BF16),
            pltpu.VMEM((width, rows), BF16),
            pltpu.VMEM((width, rows), BF16),
            pltpu.SemaphoreType.DMA((len(entries),)),
        ],
        compiler_params=pltpu.CompilerParams(vmem_limit_bytes=LIMIT),
        cost_estimate=cost(0, 100_000_000),
        name="feed_forward",
    )(
        place_index(parts),
        place_pair(),
        *[part for part, _, _ in parts],
        mixed,
        hidden,
        lines,
        inner_b,
        ct,
    )


def norm_kernel(
    grad_ref, normed_ref, scale_ref, lines_ref, w_ref, out_ref, low_ref, mix_ref, sums_ref
):
    grad, normed = grad_ref[...], normed_ref[...]
    attn = norm_back(grad, normed, scale_ref[...], lines_ref[0:1, :])
    out_ref[...] = attn
    low = attn.astype(BF16)
    low_ref[...] = low
    mix_ref[...] = dot_nt(low, w_ref[...]).astype(BF16)
    sums_ref[0:1, :] = jnp.sum(grad * normed, 0, keepdims=True)
    sums_ref[1:2, :] = jnp.sum(grad, 0, keepdims=True)


def norm_rows(grad, normed, scale, lines, out_w):
    rows, width = grad.shape
    low = jax.ShapeDtypeStruct((rows, width), BF16)
    return pl.pallas_call(
        norm_kernel,
        out_shape=[
            jax.ShapeDtypeStruct((rows, width), F32),
            low,
            low,
            jax.ShapeDtypeStruct((2, width), F32),
        ],
        compiler_params=pltpu.CompilerParams(vmem_limit_bytes=LIMIT),
        cost_estimate=cost(0, 12_000_000),
        name="norm_rows",
    )(grad, normed, scale, lines, out_w)


def tail_kernel(text_len, place_ref, *refs):
    inputs, (order_ref, attn_ref, tokens_ref), refs = refs[:11], refs[11:14], refs[14:]
    outputs, buffers = refs[:2], refs[2:13]
    mine, away, in_sems, out_sems = refs[13:]
    low_ref, mixed_ref, attn_low_ref, qkv_w_ref, bn_ref = buffers[6:]
    names = (6, 0, 1, 2, 3, 4, 5, 7, 8, 9, 10)
    copies = {n: pltpu.make_async_copy(inputs[n], buffers[n], in_sems.at[n]) for n in names}
    for n in names:
        copies[n].start()
    visual_len = bn_ref.shape[0]
    width = attn_low_ref.shape[1]
    core, quad = place_ref[0], place_ref[1]
    sent = []

    def spread(values, begin, n):
        values = values.astype(BF16)
        rows = values.shape[0] // (2 * mine.shape[0])

        def store(ref, slot, dp):
            ref[slot, begin : begin + rows, :] = values[dp * rows : (dp + 1) * rows]

        store_blocks(mine, away, core, quad, store)
        part = pl.ds(begin, rows)
        for k, ref in enumerate((mine, away)):
            copy = pltpu.make_async_copy(
                ref.at[:, part, :], outputs[k].at[:, part, :], out_sems.at[n, k]
            )
            copy.start()
            sent.append(copy)
        return begin + rows

    copies[6].wait()
    turned = low_ref[...].T
    begin = 0
    grads = []
    for n in range(3):
        copies[2 * n].wait()
        copies[2 * n + 1].wait()
        grads.append(jnp.concatenate([buffers[2 * n][...], buffers[2 * n + 1][...]], 1))
        begin = spread(dot_nn(turned, grads[n]), begin, n)
    copies[7].wait()
    copies[8].wait()
    begin = spread(dot_nn(mixed_ref[...].T, attn_low_ref[...]), begin, 3)
    copies[9].wait()
    tokens = attn_ref[...]
    for n in range(3):
        lanes = slice(n * width, (n + 1) * width)
        tokens = tokens + dot_nt(grads[n][text_len:], qkv_w_ref[:, lanes])
    picker = picked(order_ref[...], visual_len)
    tokens = exact(picker, tokens[:visual_len], ((0,), (0,))).astype(BF16)
    tokens_ref[...] = tokens
    copies[10].wait()
    spread(dot_tn(bn_ref[...], tokens), begin, 4)
    for copy in sent:
        copy.wait()


def tail_rows(back, qkv_w, attn, attn_low, mixed, low, order, bn_rows, text_len):
    dp, ffn = lax.axis_size("dp"), lax.axis_size("ffn")
    rows, width = attn.shape
    visual_len, channels = bn_rows.shape
    size = 4 * (width // dp) + channels // dp
    vmem = pl.BlockSpec(memory_space=pltpu.VMEM)
    anywhere = pl.BlockSpec(memory_space=pl.ANY)
    inputs = [g for pair in back for g in pair] + [low, mixed, attn_low, qkv_w, bn_rows]
    rest = rows - text_len
    tail = pl.BlockSpec((rest, width), lambda *_: (text_len // rest, 0))
    blocks = jax.ShapeDtypeStruct((dp // 2, size, width), BF16)
    return pl.pallas_call(
        functools.partial(tail_kernel, text_len),
        grid=(1,),
        in_specs=[pl.BlockSpec(memory_space=pltpu.SMEM)]
        + [anywhere] * len(inputs)
        + [whole(order.shape), tail],
        out_specs=[whole((visual_len, width))] + [anywhere] * 2,
        out_shape=[jax.ShapeDtypeStruct((visual_len, width), BF16), blocks, blocks],
        scratch_shapes=[pltpu.VMEM(x.shape, BF16) for x in inputs]
        + [
            pltpu.VMEM(blocks.shape, BF16),
            pltpu.VMEM(blocks.shape, BF16),
            pltpu.SemaphoreType.DMA((len(inputs),)),
            pltpu.SemaphoreType.DMA((5, 2)),
        ],
        compiler_params=pltpu.CompilerParams(vmem_limit_bytes=LIMIT),
        cost_estimate=cost(0, 40_000_000),
        name="tail_rows",
    )(place_pair(), *inputs, order, attn)


def batch_kernel(tokens_ref, visual_ref, stats_ref, proj_ref, grad_bn_ref, sums_ref):
    grad_bn = dot_nt(tokens_ref[...], proj_ref[...])
    grad_bn_ref[...] = grad_bn
    normed = (visual_ref[...].astype(F32) - stats_ref[0:1, :]) * stats_ref[1:2, :]
    sums_ref[0:1, :] = jnp.sum(grad_bn, 0, keepdims=True)
    sums_ref[1:2, :] = jnp.sum(grad_bn * normed, 0, keepdims=True)


def batch_rows(tokens, visual, stats, proj):
    return pl.pallas_call(
        batch_kernel,
        out_shape=[
            jax.ShapeDtypeStruct(visual.shape, F32),
            jax.ShapeDtypeStruct((2, visual.shape[1]), F32),
        ],
        compiler_params=pltpu.CompilerParams(vmem_limit_bytes=LIMIT),
        cost_estimate=cost(0, 6_000_000),
        name="batch_rows",
    )(tokens, visual, stats, proj)


def text_kernel(*refs):
    dq, dk, dv = refs[0:2], refs[2:4], refs[4:6]
    qkv_w_ref, attn_ref, text_ref = refs[6:]
    width = text_ref.shape[1]
    total = attn_ref[...]
    for n, (low, high) in enumerate((dq, dk, dv)):
        grads = jnp.concatenate([low[...], high[...]], 1)
        total = total + dot_nt(grads, qkv_w_ref[:, n * width : (n + 1) * width])
    text_ref[...] = total


def text_rows(back, qkv_w, attn, text_len):
    width = attn.shape[1]
    step = text_len // 2
    grads = [g for pair in back for g in pair]
    return pl.pallas_call(
        text_kernel,
        grid=(2,),
        in_specs=[pl.BlockSpec((step, g.shape[1]), lambda i: (i, 0)) for g in grads]
        + [whole(qkv_w.shape), pl.BlockSpec((step, width), lambda i: (i, 0))],
        out_specs=pl.BlockSpec((step, width), lambda i: (i, 0)),
        out_shape=jax.ShapeDtypeStruct((text_len, width), F32),
        compiler_params=pltpu.CompilerParams(vmem_limit_bytes=LIMIT),
        cost_estimate=cost(0, 25_000_000),
        name="text_rows",
    )(*grads, qkv_w, attn)


def lane_rows(values, width):
    lanes = values.shape[1]
    pieces = pl.cdiv(lanes, width)
    if pieces * width > lanes:
        values = jnp.concatenate([values, jnp.zeros((1, pieces * width - lanes), F32)], 1)
    return [values[:, n * width : (n + 1) * width] for n in range(pieces)]


def sums_kernel(bn_ref, one_ref, two_ref, inner_ref, *refs):
    out_ref = refs[-1]
    width = out_ref.shape[1]
    rows = []
    for n in range(bn_ref.shape[0]):
        rows += lane_rows(bn_ref[n : n + 1, :], width)
    for ref in (one_ref, two_ref):
        rows += [ref[n : n + 1, :] for n in range(ref.shape[0])]
    inner = [inner_ref[n] for n in range(inner_ref.shape[0])]
    rows += lane_rows(jnp.concatenate(inner, 1), width)
    tables = sum(ref[...] for ref in refs[:-1]).T
    blank = jnp.zeros((tables.shape[0], 256 - tables.shape[1]), F32)
    tables = jnp.concatenate([tables, blank], 1)
    group = width // 256
    for n in range(0, 12, group):
        rows.append(jnp.concatenate([tables[h : h + 1] for h in range(n, n + group)], 1))
    rows += [jnp.zeros((1, width), F32)] * (out_ref.shape[0] - len(rows))
    out_ref[...] = jnp.concatenate(rows, 0)


def pack_sums(bn_sums, one, two, inner, tables):
    width = one.shape[1]
    rows = 2 * pl.cdiv(bn_sums.shape[1], width) + 5 + inner.size // width + 12 * 256 // width
    return pl.pallas_call(
        sums_kernel,
        out_shape=jax.ShapeDtypeStruct((pl.cdiv(rows, 8) * 8, width), F32),
        cost_estimate=cost(0, 1_000_000),
        name="pack_sums",
    )(bn_sums, one, two, inner, *tables)


def finish_kernel(levels, count, *refs):
    left_ref, right_ref, grad_bn_ref, visual_ref, stats_ref, lines_ref = refs[:6]
    shift_ref, scale_ref, grad_ref, inner_ref = refs[6:10]
    vectors, tables = refs[10:15], refs[15:]
    total = left_ref[...] + right_ref[...]
    width = total.shape[1]
    channels = grad_bn_ref.shape[1]
    row = 0

    def take(lanes):
        nonlocal row
        pieces = pl.cdiv(lanes, width)
        row += pieces
        return jnp.concatenate([total[n : n + 1] for n in range(row - pieces, row)], 1)[:, :lanes]

    shift, scale = take(channels), take(channels)
    shift_ref[...] = shift.reshape(channels)
    scale_ref[...] = scale.reshape(channels)
    for ref in vectors:
        ref[...] = take(width).reshape(width)
    inner_ref[...] = take(inner_ref.shape[0]).reshape(inner_ref.shape[0])
    inverse = stats_ref[1:2, :]
    normed = (visual_ref[...].astype(F32) - stats_ref[0:1, :]) * inverse
    grad = grad_bn_ref[...] - shift * (1.0 / count) - normed * (scale * (1.0 / count))
    grad_ref[...] = lines_ref[0:1, :] * inverse * grad
    group = width // 256
    heads = []
    for n in range(12):
        lane = n % group * 256
        heads.append(total[row + n // group : row + n // group + 1, lane : lane + 256])
    heads = jnp.concatenate(heads, 0)
    begin = 0
    for ref, size in zip(tables, levels):
        ref[...] = heads[:, begin : begin + size]
        begin += size


def finish(left, right, grad_bn, visual, stats, lines, inner, levels, count):
    width = left.shape[1]
    channels = visual.shape[1]
    line = lambda n: jax.ShapeDtypeStruct((n,), F32)
    return pl.pallas_call(
        functools.partial(finish_kernel, levels, count),
        out_shape=[line(channels), line(channels), jax.ShapeDtypeStruct(visual.shape, F32)]
        + [line(inner)]
        + [line(width)] * 5
        + [jax.ShapeDtypeStruct((12, n), F32) for n in levels],
        cost_estimate=cost(0, 3_000_000),
        name="finish",
    )(left, right, grad_bn, visual, stats, lines)


def bias_kernel(rows_step, rel_ref, x_ref, y_ref, tab_ref, out_ref, unit_ref, level_ref):
    pairs = out_ref.shape[0]
    table = tab_ref[...]
    top = jnp.max(jnp.max(jnp.abs(table), 1, keepdims=True), 0, keepdims=True)
    top = jnp.maximum(top, 1e-30)
    unit_ref[...] = top * (2.0 / LEVELS)
    level = jnp.floor((table / top + 1.0) * (0.5 * LEVELS) + 0.5).astype(jnp.int32)
    level_ref[0] = level[:, :128]
    level_ref[1] = level[:, 128:]
    words = []
    for n in range(2):
        low = level_ref[n, pl.ds(0, pairs, stride=2), :]
        high = level_ref[n, pl.ds(1, pairs, stride=2), :]
        words.append(low + high * 65536)
    both = [jnp.broadcast_to(words[0][p : p + 1, :], (8, 128)) for p in range(pairs)]
    rel = [jnp.broadcast_to(words[1][p : p + 1, :], (8, 128)) for p in range(pairs)]

    def look(table, index):
        return jnp.take_along_axis(table, index, axis=1, mode="promise_in_bounds")

    for c in range(out_ref.shape[2] // 128):
        for r in range(rows_step // 8):
            rows, cols = pl.ds(r * 8, 8), pl.ds(c * 128, 128)
            rel_id = rel_ref[0, rows, cols] & 31
            x_id = x_ref[0, rows, cols] & 63
            y_id = (y_ref[0, rows, cols] & 63) + 64
            for p in range(pairs):
                out_ref[p, rows, cols] = (
                    look(rel[p], rel_id) + look(both[p], x_id) + look(both[p], y_id)
                )


def bias_words(rel, x, y, table, first, steps):
    step = 64
    rows = steps * step
    pairs = table.shape[0] // 2
    lanes = pl.cdiv(rel.shape[2], 128) * 128
    ids = pl.BlockSpec((1, step, lanes), lambda i: (0, i + first, 0))
    return pl.pallas_call(
        functools.partial(bias_kernel, step),
        grid=(steps,),
        in_specs=[ids, ids, ids, whole(table.shape)],
        out_specs=[pl.BlockSpec((pairs, step, lanes), lambda i: (0, i, 0)), whole((1, 1))],
        out_shape=[
            jax.ShapeDtypeStruct((pairs, rows, lanes), jnp.int32),
            jax.ShapeDtypeStruct((1, 1), F32),
        ],
        scratch_shapes=[pltpu.VMEM((2, table.shape[0], 128), jnp.int32)],
        compiler_params=pltpu.CompilerParams(vmem_limit_bytes=LIMIT),
        cost_estimate=cost(0, 6_000_000 * steps),
        name="bias_words",
    )(rel, x, y, table)


def lane_halves(rows):
    lane = lax.broadcasted_iota(jnp.int32, (rows, 128), 1)
    return lane < 64, lane >= 64


def attend_kernel(unit_ref, q_ref, k_ref, v_ref, col_ref, row_ref, *refs):
    word_refs, (p_ref, o_ref, mask_ref) = refs[:-3], refs[-3:]

    @pl.when(pl.program_id(0) == 0)
    def _():
        mask_ref[...] = jnp.where(col_ref[...] == row_ref[...], 0.0, NEG)

    unit = unit_ref[...]
    rows = q_ref.shape[0]
    halves = lane_halves(rows)
    q, k, v = q_ref[...], k_ref[...], v_ref[...]
    none = jnp.zeros_like(q)
    words = jnp.concatenate([ref[0][:, :rows] for ref in word_refs], 0)
    mask = mask_ref[...]
    mixed = jnp.zeros((rows, 128), F32)
    for h in range(2):
        scores = dot_nt(jnp.where(halves[h], q, none), k)
        word = (words & 0xFFFF) if h == 0 else lax.shift_right_logical(words, 16)
        scores = scores + word.astype(F32) * unit + mask
        expo = jnp.exp(scores - jnp.max(scores, -1, keepdims=True))
        probs = (expo * (1.0 / jnp.sum(expo, -1, keepdims=True))).astype(BF16)
        p_ref[h] = probs
        mixed = mixed + dot_nn(probs, jnp.where(halves[h], v, none))
    o_ref[...] = mixed.astype(BF16)


def attend(unit, qkv, words, segments):
    pairs = words[0].shape[0]
    rows = qkv.shape[0]
    col = [pl.BlockSpec((rows, 128), lambda p, n=n: (0, n * pairs + p)) for n in range(3)]
    flops = pairs * 4 * 2 * rows * rows * 128
    return pl.pallas_call(
        attend_kernel,
        grid=(pairs,),
        in_specs=[
            whole((1, 1)),
            col[0],
            col[1],
            col[2],
            whole((rows, 1)),
            whole((1, rows)),
        ]
        + [pl.BlockSpec((1,) + w.shape[1:], lambda p: (p, 0, 0)) for w in words],
        out_specs=[
            pl.BlockSpec((2, rows, rows), lambda p: (p, 0, 0)),
            pl.BlockSpec((rows, 128), lambda p: (0, p)),
        ],
        out_shape=[
            jax.ShapeDtypeStruct((2 * pairs, rows, rows), BF16),
            jax.ShapeDtypeStruct((rows, pairs * 128), BF16),
        ],
        scratch_shapes=[pltpu.VMEM((rows, rows), F32)],
        compiler_params=pltpu.CompilerParams(vmem_limit_bytes=LIMIT),
        cost_estimate=cost(flops, 40_000_000),
        name="attend",
    )(unit, qkv, qkv, qkv, *segments, *words)


def attend_back_kernel(q_ref, k_ref, v_ref, g_ref, p_ref, ds_ref, dq_ref, dk_ref, dv_ref):
    rows = q_ref.shape[0]
    halves = lane_halves(rows)
    q, k, v, g = q_ref[...], k_ref[...], v_ref[...], g_ref[...]
    none = jnp.zeros_like(q)
    blank = jnp.zeros((rows, ds_ref.shape[2] - rows), BF16)
    dq = jnp.zeros((rows, 128), F32)
    dk, dv = dq, dq
    for h in range(2):
        low = p_ref[h]
        probs = low.astype(F32)
        weighted = probs * dot_nt(g, jnp.where(halves[h], v, none))
        ds = (weighted - probs * jnp.sum(weighted, -1, keepdims=True)).astype(BF16)
        ds_ref[h] = jnp.concatenate([ds, blank], 1)
        dq = dq + dot_nn(ds, jnp.where(halves[h], k, none))
        dv = dv + dot_tn(low, jnp.where(halves[h], g, none))
        dk = dk + dot_tn(ds, jnp.where(halves[h], q, none))
    dq_ref[...] = (dq * 0.125).astype(BF16)
    dk_ref[...] = dk.astype(BF16)
    dv_ref[...] = dv.astype(BF16)


def attend_back(qkv, grad, probs, first, pairs):
    every = probs.shape[0] // 2
    rows = qkv.shape[0]
    col = [pl.BlockSpec((rows, 128), lambda p, n=n: (0, n * every + p + first)) for n in range(3)]
    new = pl.BlockSpec((rows, 128), lambda p: (0, p))
    big = pl.BlockSpec((2, rows, rows), lambda p: (p + first, 0, 0))
    lanes = pl.cdiv(rows, 128) * 128
    out = jax.ShapeDtypeStruct((rows, pairs * 128), BF16)
    flops = pairs * 2 * 4 * 2 * rows * rows * 128
    return pl.pallas_call(
        attend_back_kernel,
        grid=(pairs,),
        in_specs=[col[0], col[1], col[2], col[0], big],
        out_specs=[pl.BlockSpec((2, rows, lanes), lambda p: (p, 0, 0)), new, new, new],
        out_shape=[jax.ShapeDtypeStruct((2 * pairs, rows, lanes), BF16), out, out, out],
        compiler_params=pltpu.CompilerParams(vmem_limit_bytes=LIMIT),
        cost_estimate=cost(flops, 8_000_000 * pairs),
        name="attend_back",
    )(qkv, qkv, qkv, grad, probs)


def table_kernel(first, levels, block_ref, count_ref, rel_ref, x_ref, y_ref, *refs):
    ds_refs, out_ref, rows_ref = refs[:-2], refs[-2], refs[-1]
    place = pl.program_id(0)
    step = rel_ref.shape[1]
    every = rel_ref.shape[2] // 128

    @pl.when(place == 0)
    def _():
        out_ref[...] = jnp.zeros_like(out_ref)
        rows_ref[...] = jnp.zeros_like(rows_ref)

    heads = [(ref, n) for ref in ds_refs for n in range(ref.shape[0])]

    def group(r, start, blocks):
        width = blocks * 128
        level = lax.broadcasted_iota(jnp.int32, (16, width), 0).astype(F32).astype(BF16)
        one = jnp.ones((16, width), BF16)
        none = jnp.zeros((16, width), BF16)

        def one_hot(ids, count):
            wide = jnp.broadcast_to(ids, (16, width)).astype(BF16)
            return [jnp.where(wide == level + BF16(16 * t), one, none) for t in range(count // 16)]

        rows = pl.ds(pl.multiple_of(r * 16, 16), 16)
        lanes = pl.ds(pl.multiple_of(start * 128, 128), width)
        for h, (ref, n) in enumerate(heads):
            values = ref[n, rows, lanes].astype(F32)
            for c in range(blocks):
                rows_ref[c, pl.ds(h, 16, stride=16), :] = values[:, 128 * c : 128 * c + 128]
        total = out_ref[...]
        ids = [ref[0, rows, lanes].astype(F32) for ref in (x_ref, y_ref, rel_ref)]
        counts = (levels[1], levels[2], levels[0])
        for n in range(16):
            grads = jnp.concatenate(
                [rows_ref[c, 16 * n : 16 * n + 16, :].astype(BF16) for c in range(blocks)], 1
            )
            hot = [one_hot(i[n : n + 1], count) for i, count in zip(ids, counts)]
            hot = jnp.concatenate(hot[0] + hot[1] + hot[2], 0)
            total = total + dot_nt(hot, grads)
        out_ref[...] = total

    def body(r, _):
        index = (place + first) * (step // 16) + r
        start, count = block_ref[index], count_ref[index]
        for blocks in range(1, every + 1):

            @pl.when(count == blocks)
            def _(blocks=blocks):
                group(r, start, blocks)

        return 0

    lax.fori_loop(0, step // 16, body, 0)


def table_sums(ranges, rel, x, y, ds, levels, first, steps):
    step = 64
    lanes = ds[0].shape[2]
    ids = pl.BlockSpec((1, step, lanes), lambda i, *_: (0, i + first, 0))
    return pl.pallas_call(
        functools.partial(table_kernel, first, levels),
        grid_spec=pltpu.PrefetchScalarGridSpec(
            num_scalar_prefetch=2,
            grid=(steps,),
            in_specs=[ids, ids, ids]
            + [pl.BlockSpec((d.shape[0], step, lanes), lambda i, *_: (0, i + first, 0)) for d in ds],
            out_specs=whole((sum(levels), 16)),
            scratch_shapes=[pltpu.VMEM((lanes // 128, 256, 128), F32)],
        ),
        out_shape=jax.ShapeDtypeStruct((sum(levels), 16), F32),
        compiler_params=pltpu.CompilerParams(vmem_limit_bytes=LIMIT),
        cost_estimate=cost(0, 8_000_000 * steps),
        name="table_sums",
    )(*ranges, rel, x, y, *ds)


def document_blocks(segments, rows):
    length = segments.shape[0]
    first = segments[0:rows:16]
    last = segments[jnp.minimum(jnp.arange(15, rows, 16), length - 1)]
    begin = jnp.sum(segments[None, :] < first[:, None], 1, dtype=jnp.int32)
    end = jnp.sum(segments[None, :] <= last[:, None], 1, dtype=jnp.int32)
    return begin // 128, (end + 127) // 128 - begin // 128


def norm_stats(values):
    center = values - jnp.mean(values, -1, keepdims=True)
    scale = lax.rsqrt(jnp.mean(center * center, -1, keepdims=True) + EPS)
    return center * scale, scale


def norm_back(grad, normed, scale, gain):
    scaled = grad * gain
    return scale * (
        scaled
        - jnp.mean(scaled, -1, keepdims=True)
        - normed * jnp.mean(scaled * normed, -1, keepdims=True)
    )


def on_device(
    text_hidden,
    visual_maps,
    patch_order,
    segment_ids,
    rel_bucket,
    x_bucket,
    y_bucket,
    bn_scale,
    bn_shift,
    vis_proj,
    w_query,
    w_key,
    w_value,
    w_output,
    rel_table,
    x_table,
    y_table,
    first_gain,
    first_bias,
    w_inner,
    b_inner,
    w_outer,
    b_outer,
    second_gain,
    second_bias,
    cotangent,
):
    heads = rel_table.shape[1]
    pairs = heads // 2
    visual_len = patch_order.shape[1]
    length = segment_ids.shape[1]
    text_len = length - visual_len
    width = w_query.shape[1]
    dp, ffn = lax.axis_size("dp"), lax.axis_size("ffn")
    place, here = lax.axis_index("dp"), lax.axis_index("ffn")
    devices = dp * ffn
    rows = pl.cdiv(length, 64) * 64
    count = visual_maps.shape[0] * devices
    levels = (rel_table.shape[0], x_table.shape[0], y_table.shape[0])

    inner_rows, columns = w_inner.shape
    outer_shard = w_outer.T
    steps = rows // 64

    first_set = Gather(*pack_first(w_query, w_key, w_value, vis_proj, visual_maps))
    plain = columns == width
    wide_shards = jnp.concatenate([outer_shard, w_inner], 0)
    if plain:
        late_set = Gather(
            jnp.concatenate([w_output, wide_shards], 0), [w_output.shape[0], inner_rows, inner_rows]
        )
    else:
        late_set = Gather(w_output, [w_output.shape[0]])
        wide_set = Gather(wide_shards, [inner_rows, inner_rows])

    first_set.along_ffn()
    tables = jnp.concatenate([x_table, y_table, rel_table], 0).T
    tables = jnp.pad(tables, ((0, 0), (0, 256 - tables.shape[1])))
    cuts = [0, steps * 2 // 9, steps * 6 // 9, steps]
    words = [None] * 3
    words[0], unit = bias_words(rel_bucket, x_bucket, y_bucket, tables, 0, cuts[1])
    ranges = document_blocks(segment_ids[0], rows)
    lines = jnp.stack([first_gain, first_bias, b_outer, second_gain, second_bias])
    inner_b = b_inner.reshape(ffn, 1, columns)
    segments = jnp.pad(segment_ids[0], (0, rows - length), constant_values=-1)
    segments = (segments[:, None], segments[None, :])
    bn_lines = jnp.stack([bn_scale, bn_shift])
    state, late, words[0], tables, ranges, lines, inner_b, segments, bn_lines = epoch(
        first_set.state(),
        late_set.state(),
        words[0],
        tables,
        ranges,
        lines,
        inner_b,
        segments,
        bn_lines,
    )
    first_set.hold(state)
    late_set.hold(late)

    first_set.order()
    first_set.near(3 * w_query.shape[0] * ffn)
    late_set.along_ffn(1, ffn - 1)
    words[1], _ = bias_words(rel_bucket, x_bucket, y_bucket, tables, cuts[1], cuts[2] - cuts[1])
    state, late, words[1], tables = epoch(first_set.state(), late_set.state(), words[1], tables)
    first_set.hold(state)
    late_set.hold(late)

    first_set.diagonal()
    late_set.along_ffn(ffn - 1)
    state, late, tables = epoch(first_set.state(), late_set.state(), tables)
    first_set.hold(state)
    late_set.hold(late)

    late_set.order()
    first_set.across()
    state, late = epoch(first_set.state(), late_set.state())
    first_set.hold(state)
    late_set.hold(late)

    late_rows = w_output.shape[0] * ffn
    late_set.near(late_rows + ffn * inner_rows if plain else 0)
    layout, row = [], 0
    for n, size in enumerate(first_set.rows):
        layout.append((row, size * ffn, max(n - 2, 0), 0, n * width if n < 3 else 0))
        row += size * ffn
    order_col = patch_order.reshape(visual_len, 1)
    qkv_full, proj_full, hidden, lowered, qkv, bn_rows, bn_stats = first_rows(
        first_set.parts(),
        layout,
        text_hidden,
        visual_maps,
        order_col,
        bn_lines,
        rows,
        vis_proj.shape[0] * devices,
        first_set.rows[-1],
    )
    qkv, tables = epoch(qkv, tables)
    words[2], _ = bias_words(rel_bucket, x_bucket, y_bucket, tables, cuts[2], cuts[3] - cuts[2])
    qkv, state, words[2] = epoch(qkv, late_set.state(), words[2])
    late_set.hold(state)

    late_set.diagonal()
    probs, mixed = attend(unit, qkv, words, segments)
    probs, mixed, state = epoch(probs, mixed, late_set.state())
    late_set.hold(state)
    late_set.across()
    layout = [(0, late_rows, 0, 0, 0)]
    shift = late_rows
    parts = late_set.parts()
    if not plain:
        parts = [(block, bits, 0) for block, bits, _ in parts]
        wide_set.along_ffn()
        wide_set.order()
        wide_set.near(0)
        wide_set.diagonal()
        wide_set.across()
        shift = 0
    wide_layout = [
        (shift + (n * ffn + f) * inner_rows, inner_rows, 1 + n, f * width, 0)
        for n in range(2)
        for f in range(ffn)
    ]
    feeds = [(parts, layout + wide_layout if plain else layout)]
    if not plain:
        feeds.append((wide_set.parts(), wide_layout))
    (
        first_n,
        first_r,
        output,
        grad_first,
        sums_two,
        inner_sums,
        output_full,
        mine,
        away,
    ) = feed_forward(feeds, mixed, hidden, lines, inner_b, cotangent, inner_rows)

    wide = Scatter(mine, away, lambda value, index: pick(value, index, 1))
    wide.core()
    grad_attn, attn_low, grad_mixed, sums_one = norm_rows(grad_first, first_n, first_r, lines, output_full)
    state, grad_mixed = epoch(wide.held(), grad_mixed)
    wide.hold(state)

    wide.near()
    half = pairs - pairs // 3
    back_low = attend_back(qkv, grad_mixed, probs, 0, half)
    state, back_low, qkv = epoch(wide.held(), back_low, qkv)
    wide.hold(state)
    wide.prepare()
    wide.blocks, qkv = epoch(wide.blocks, qkv)

    wide.quads()
    back_high = attend_back(qkv, grad_mixed, probs, half, pairs - half)
    back = list(zip(back_low[1:], back_high[1:]))
    tokens_grad, mine, away = tail_rows(
        back, qkv_full, grad_attn, attn_low, mixed, lowered, order_col, bn_rows, text_len
    )
    ds = (back_low[0], back_high[0])
    wide.blocks, mine, away, ds, tokens_grad = epoch(wide.blocks, mine, away, ds, tokens_grad)

    def tail_far(value, index):
        size = 4 * (width // dp)
        square = pick(value[:size].reshape(4, ffn, -1, width), index, 1)
        return jnp.concatenate(
            [square.reshape(-1, width), pick(value[size:].reshape(ffn, -1, width), index, 0)], 0
        )

    cuts = [0, steps * 2 // 9, steps * 5 // 9, steps]
    sums = []

    def tables(ds):
        n = len(sums)
        return sums + [
            table_sums(
                ranges, rel_bucket, x_bucket, y_bucket, ds, levels, cuts[n], cuts[n + 1] - cuts[n]
            )
        ]

    tail = Scatter(mine, away, tail_far)
    tail.core()
    wide.join()
    wide.along_ffn(1, 2)
    grad_bn, bn_sums = batch_rows(tokens_grad, visual_maps, bn_stats, proj_full)
    sums = tables(ds)
    state, bn_sums, ds, sums, wide.pieces = epoch(tail.held(), bn_sums, ds, sums, wide.pieces)
    tail.hold(state)

    tail.near()
    if ffn > 2:
        wide.along_ffn(2, 3)
    sums = tables(ds)
    state, ds, sums, wide.pieces = epoch(tail.held(), ds, sums, wide.pieces)
    tail.hold(state)
    tail.prepare()
    tail.blocks, ds = epoch(tail.blocks, ds)

    tail.quads()
    if ffn > 3:
        wide.along_ffn(3)
    sums = tables(ds)
    tail.blocks, sums, back, wide.pieces = epoch(tail.blocks, sums, back, wide.pieces)

    tail.join()
    tail.along_ffn()
    total = Sum(pack_sums(bn_sums, sums_one, sums_two, inner_sums, sums))
    while len(total.steps) > ffn.bit_length() - 1:
        total.step()
    text_grad = text_rows(back, qkv_full, grad_attn, text_len)
    wide_sum = wide.total()
    tail.pieces, total.values = epoch(tail.pieces, total.values)
    tail_sum = tail.total()
    while len(total.steps) > 1:
        total.step()
    other = total.steps[0](total.values)
    (
        shift_grad,
        scale_grad,
        visual_grad,
        inner_grad,
        gain_one,
        bias_one,
        gain_two,
        bias_two,
        outer_grad,
        x_grad,
        y_grad,
        rel_grad,
    ) = finish(
        total.values,
        other,
        grad_bn,
        visual_maps,
        bn_stats,
        bn_lines,
        b_inner.shape[0],
        (levels[1], levels[2], levels[0]),
        count,
    )
    shards, row = [], 0
    for size in [w_query.shape[0]] * 4 + [vis_proj.shape[0]]:
        shards.append(tail_sum[row : row + size])
        row += size
    return (
        output,
        text_grad,
        visual_grad,
        scale_grad.reshape(-1),
        shift_grad.reshape(-1),
        shards[4],
        shards[0],
        shards[1],
        shards[2],
        shards[3],
        rel_grad.T,
        x_grad.T,
        y_grad.T,
        gain_one.reshape(-1),
        bias_one.reshape(-1),
        wide_sum[0],
        inner_grad.reshape(-1),
        wide_sum[1].T,
        outer_grad.reshape(-1),
        gain_two.reshape(-1),
        bias_two.reshape(-1),
    )


def solution(mesh):
    rows = P(ALL, None)
    cube = P(ALL, None, None)
    return jax.shard_map(
        on_device,
        mesh=mesh,
        in_specs=(rows,) * 4
        + (cube,) * 3
        + (P(),) * 2
        + (rows,) * 5
        + (P(),) * 5
        + (P("dp", "ffn"), P(), P("ffn", "dp"))
        + (P(),) * 3
        + (rows,),
        out_specs=(rows,) * 3
        + (P(),) * 2
        + (rows,) * 5
        + (P(),) * 5
        + (P("dp", "ffn"), P(), P("ffn", "dp"))
        + (P(),) * 3,
        check_vma=False,
    )
```

```python
import functools

import jax
import jax.numpy as jnp
from jax import lax
from jax.experimental import pallas as pl
from jax.experimental.pallas import tpu as pltpu
from jax.sharding import PartitionSpec as P

EPS = 1e-05
NEG = -1e30
F32 = jnp.float32
BF16 = jnp.bfloat16
ALL = ("dp", "ffn")
LEVELS = 21845.0
MIB = 2**20


def dot_nn(a, b):
    return lax.dot_general(a, b, (((1,), (0,)), ((), ())), preferred_element_type=F32)


def dot_nt(a, b):
    return lax.dot_general(a, b, (((1,), (1,)), ((), ())), preferred_element_type=F32)


def dot_tn(a, b):
    return lax.dot_general(a, b, (((0,), (0,)), ((), ())), preferred_element_type=F32)


def pad_rows(values, rows):
    return jnp.pad(values, ((0, rows - values.shape[0]), (0, 0)))


def send_dp(values, bits):
    size = lax.axis_size("dp")
    return lax.ppermute(values, "dp", [(i, i ^ bits) for i in range(size)])


def send_ffn(values, shift):
    size = lax.axis_size("ffn")
    return lax.ppermute(values, "ffn", [(i, (i + shift) % size) for i in range(size)])


def swap_ffn(values, bits):
    size = lax.axis_size("ffn")
    return lax.ppermute(values, "ffn", [(i, i ^ bits) for i in range(size)])


def exchanges():
    steps = []
    for axis, send in (("ffn", swap_ffn), ("dp", send_dp)):
        bit = 1
        while bit < lax.axis_size(axis):
            steps.append(functools.partial(send, bits=bit))
            bit *= 2
    return steps


class Sum:
    def __init__(self, values):
        self.values = values
        self.steps = exchanges()

    def step(self):
        if self.steps:
            self.values = self.values + self.steps.pop(0)(self.values)

    def finish(self):
        while self.steps:
            self.step()
        return self.values


class Gather:
    def __init__(self, own, rows):
        self.own = own
        self.rows = rows

    def along_ffn(self, begin=1, end=None):
        size = lax.axis_size("ffn")
        self.far = self.far[:begin] if begin > 1 else [self.own]
        self.far += [send_ffn(self.own, k) for k in range(begin, end or size)]

    def order(self):
        size = lax.axis_size("ffn")
        here = lax.axis_index("ffn")
        if all(rows % 8 == 0 for rows in self.rows):
            self.block = order_blocks(here, self.far, self.rows)
            return
        pieces = []
        for slot in range(size):
            value = self.far[0]
            for k in range(1, size):
                value = jnp.where((here - k + size) % size == slot, self.far[k], value)
            pieces.append(value)
        begin, ordered = 0, []
        for rows in self.rows:
            ordered += [value[begin : begin + rows] for value in pieces]
            begin += rows
        self.block = jnp.concatenate(ordered, 0)

    def near(self, cut):
        quads = lax.axis_size("dp") // 2
        self.cut = cut
        self.others = [send_dp(self.block, 1)]
        if quads == 4:
            self.mine = [self.block, send_dp(self.block, 2), send_dp(self.block, 4)]
        else:
            self.mine = [self.block] + [send_dp(self.block, 2 * k) for k in range(1, quads)]

    def diagonal(self):
        self.others += [send_dp(block, 1) for block in self.mine[1:]]
        if lax.axis_size("dp") == 8:
            low = send_dp(self.mine[1][: self.cut], 4)
            high = send_dp(self.mine[2][self.cut :], 2)
            self.mine.append((low, high))

    def across(self):
        if lax.axis_size("dp") == 8:
            self.others.append(tuple(send_dp(piece, 1) for piece in self.mine[3]))

    def state(self):
        return {k: v for k, v in vars(self).items() if k in ("own", "far", "block", "mine", "others")}

    def hold(self, state):
        vars(self).update(state)

    def parts(self):
        found = []
        for k, (mine, other) in enumerate(zip(self.mine, self.others)):
            for bits, block in ((2 * k, mine), (2 * k + 1, other)):
                if isinstance(block, tuple):
                    found += [(block[0], bits, 0), (block[1], bits, self.cut)]
                else:
                    found.append((block, bits, 0))
        return found


def epoch(*values):
    return lax.optimization_barrier(values)


def pick(values, index, axis):
    return lax.dynamic_index_in_dim(values, index, axis, keepdims=False)


def plus(a, b):
    return (a.astype(F32) + b.astype(F32)).astype(BF16)


class Scatter:
    def __init__(self, mine, away, far):
        self.value = mine
        self.away = away
        self.far = far

    def core(self):
        self.got = send_dp(self.away, 1)

    def near(self):
        mine, got = self.value, self.got
        if mine.shape[0] == 4:
            half = mine.shape[1] // 2
            self.low = send_dp(plus(mine[3, :half], got[3, :half]), 4)
            self.high = send_dp(plus(mine[3, half:], got[3, half:]), 2)

    def prepare(self):
        mine, got = self.value, self.got
        half = mine.shape[1] // 2
        self.blocks = []
        for k in range(1, mine.shape[0]):
            block = mine[k].astype(F32) + got[k].astype(F32)
            if mine.shape[0] == 4 and k == 1:
                block = jnp.concatenate([block[:half] + self.low.astype(F32), block[half:]], 0)
            if mine.shape[0] == 4 and k == 2:
                block = jnp.concatenate([block[:half], block[half:] + self.high.astype(F32)], 0)
            if mine.shape[0] == 4 and k == 3:
                continue
            self.blocks.append(block.astype(BF16))

    def quads(self):
        self.blocks = [send_dp(block, 2 * k) for k, block in enumerate(self.blocks, 1)]

    def join(self):
        own = self.value[0].astype(F32) + self.got[0].astype(F32)
        self.value = (own + sum(block.astype(F32) for block in self.blocks)).astype(BF16)

    def held(self):
        return {k: v for k, v in vars(self).items() if k != "far"}

    def hold(self, state):
        vars(self).update(state)

    def along_ffn(self, begin=1, end=None):
        size = lax.axis_size("ffn")
        here = lax.axis_index("ffn")
        self.pieces = self.pieces[:begin] if begin > 1 else [self.far(self.value, here)]
        for k in range(begin, end or size):
            self.pieces.append(send_ffn(self.far(self.value, (here + k) % size), k))

    def total(self):
        return sum(piece.astype(F32) for piece in self.pieces)


LIMIT = 56 * MIB


def whole(shape):
    return pl.BlockSpec(shape, lambda *_: (0,) * len(shape))


def cost(flops, nbytes):
    return pl.CostEstimate(flops=flops // 1000, bytes_accessed=nbytes // 1000, transcendentals=0)


def pack_kernel(q_ref, k_ref, v_ref, p_ref, visual_ref, out_ref):
    row = 0
    for ref in (q_ref, k_ref, v_ref, p_ref):
        out_ref[row : row + ref.shape[0], :] = ref[...]
        row += ref.shape[0]
    width = out_ref.shape[1]
    count = visual_ref.shape[0]
    visual = visual_ref[...].astype(F32)
    mean = jnp.sum(visual, 0, keepdims=True) * (1.0 / count)
    gap = visual - mean
    spread = jnp.sum(gap * gap, 0, keepdims=True)
    channels = visual_ref.shape[1]
    chunks = pl.cdiv(channels, width)
    blank = jnp.zeros((1, chunks * width - channels), F32)
    pieces = []
    for values, times in ((mean, 3), (spread, 2)):
        if chunks * width > channels:
            values = jnp.concatenate([values, blank], 1)
        for _ in range(times):
            piece = values.astype(BF16).astype(F32)
            values = values - piece
            pieces += [piece[:, n * width : (n + 1) * width] for n in range(chunks)]
    pieces += [jnp.zeros((1, width), F32)] * (out_ref.shape[0] - row - len(pieces))
    out_ref[row:, :] = jnp.concatenate(pieces, 0).astype(BF16)


def pack_first(w_query, w_key, w_value, vis_proj, visual):
    width = w_query.shape[1]
    moments = pl.cdiv(5 * pl.cdiv(visual.shape[1], width), 16) * 16
    rows = [w.shape[0] for w in (w_query, w_key, w_value, vis_proj)] + [moments]
    own = pl.pallas_call(
        pack_kernel,
        out_shape=jax.ShapeDtypeStruct((sum(rows), width), BF16),
        name="pack_first",
    )(w_query, w_key, w_value, vis_proj, visual)
    return own, rows


def order_kernel(rows, here_ref, *refs):
    parts, out_ref = refs[:-1], refs[-1]
    size = len(parts)
    here = here_ref[0]
    for index in range(size):

        @pl.when(here == index)
        def _(index=index):
            begin = 0
            for count in rows:
                for k in range(size):
                    row = begin * size + (index - k) % size * count
                    out_ref[row : row + count, :] = parts[k][begin : begin + count, :]
                begin += count


def order_blocks(here, parts, rows):
    width = parts[0].shape[1]
    return pl.pallas_call(
        functools.partial(order_kernel, rows),
        in_specs=[pl.BlockSpec(memory_space=pltpu.SMEM)]
        + [pl.BlockSpec(memory_space=pltpu.VMEM)] * len(parts),
        out_specs=pl.BlockSpec(memory_space=pltpu.VMEM),
        out_shape=jax.ShapeDtypeStruct((len(parts) * sum(rows), width), BF16),
        compiler_params=pltpu.CompilerParams(vmem_limit_bytes=LIMIT),
        name="order_blocks",
    )(here.reshape(1).astype(jnp.int32), *parts)


def place_entries(parts, layout):
    entries = []
    for n, (block, _, first) in enumerate(parts):
        for begin, rows, out, base, lane in layout:
            if first <= begin and begin + rows <= first + block.shape[0]:
                entries.append((n, begin - first, rows, out, base, lane))
    return entries


def place_index(parts):
    place = lax.axis_index("dp")
    return jnp.stack([place ^ bits for _, bits, _ in parts]).astype(jnp.int32)


def part_copies(entries, place_ref, parts, outs, sems):
    copies = []
    for n, (part, begin, rows, out, base, lane) in enumerate(entries):
        target = pl.multiple_of(base + place_ref[part] * rows, 16)
        width = parts[part].shape[1]
        copies.append(
            pltpu.make_async_copy(
                parts[part].at[pl.ds(begin, rows), :],
                outs[out].at[pl.ds(target, rows), pl.ds(lane, width)],
                sems.at[n],
            )
        )
    return copies


def picked(order_col, size):
    lane = lax.broadcasted_iota(jnp.int32, (size, size), 1)
    return (order_col == lane).astype(F32)


def exact(a, b, dims):
    return lax.dot_general(
        a, b, (dims, ((), ())), precision=lax.Precision.HIGHEST, preferred_element_type=F32
    )


def first_kernel(entries, count, devices, place_ref, *refs):
    parts, refs = refs[:count], refs[count:]
    text_ref, visual_ref, order_ref, lines_ref = refs[:4]
    qkv_w_ref, proj_ref, hidden_ref, low_ref, qkv_ref, bn_ref, stats_ref = refs[4:11]
    moments_ref, sems = refs[11:]
    outs = (qkv_w_ref, proj_ref, moments_ref)
    copies = part_copies(entries, place_ref, parts, outs, sems)
    for copy in copies:
        copy.start()
    copies = [(entry[3], copy) for entry, copy in zip(entries, copies)]
    text_len, width = text_ref.shape
    visual_len, channels = visual_ref.shape
    hidden_ref[:text_len, :] = text_ref[...].astype(F32)
    low_ref[:text_len, :] = text_ref[...]
    for out, copy in copies:
        if out == 2:
            copy.wait()
    chunks = pl.cdiv(channels, width)
    moments = moments_ref[...].astype(F32).reshape(devices, -1, width)
    means = sum(moments[:, n * chunks : (n + 1) * chunks] for n in range(3))
    spreads = sum(moments[:, n * chunks : (n + 1) * chunks] for n in range(3, 5))
    average = jnp.sum(means, 0) * (1.0 / devices)
    gap = means - average[None]
    rows = visual_len * devices
    spread = (jnp.sum(spreads, 0) + visual_len * jnp.sum(gap * gap, 0)) * (1.0 / rows)
    inverse = lax.rsqrt(spread + EPS)

    def flat(values):
        pieces = [values[n : n + 1, :] for n in range(chunks)]
        return jnp.concatenate(pieces, 1)[:, :channels]

    average, inverse = flat(average), flat(inverse)
    stats_ref[0:1, :] = average
    stats_ref[1:2, :] = inverse
    normed = (visual_ref[...].astype(F32) - average) * inverse
    bn_rows = (normed * lines_ref[0:1, :] + lines_ref[1:2, :]).astype(BF16)
    bn_ref[...] = bn_rows
    for out, copy in copies:
        if out == 1:
            copy.wait()
    tokens = dot_nn(bn_rows, proj_ref[...])
    tokens = exact(picked(order_ref[...], visual_len), tokens, ((1,), (0,)))
    blank = jnp.zeros((hidden_ref.shape[0] - text_len - visual_len, width), F32)
    tokens = jnp.concatenate([tokens, blank], 0)
    hidden_ref[text_len:, :] = tokens
    low_ref[text_len:, :] = tokens.astype(BF16)
    for out, copy in copies:
        if out == 0:
            copy.wait()
    low = low_ref[...]
    for n in range(3):
        lanes = slice(n * width, (n + 1) * width)
        values = dot_nn(low, qkv_w_ref[:, lanes])
        qkv_ref[:, lanes] = (values * 0.125 if n == 0 else values).astype(BF16)


def first_rows(parts, layout, text, visual, order, lines, rows, proj_rows, moment_rows):
    devices = lax.axis_size("dp") * lax.axis_size("ffn")
    width = text.shape[1]
    channels = visual.shape[1]
    entries = place_entries(parts, layout)
    vmem = pl.BlockSpec(memory_space=pltpu.VMEM)
    shapes = [
        ((width, 3 * width), BF16),
        ((proj_rows, width), BF16),
        ((rows, width), F32),
        ((rows, width), BF16),
        ((rows, 3 * width), BF16),
        ((visual.shape[0], channels), BF16),
        ((2, channels), F32),
    ]
    return pl.pallas_call(
        functools.partial(first_kernel, entries, len(parts), devices),
        in_specs=[pl.BlockSpec(memory_space=pltpu.SMEM)]
        + [pl.BlockSpec(memory_space=pl.ANY)] * len(parts)
        + [vmem] * 4,
        out_specs=[vmem] * len(shapes),
        out_shape=[jax.ShapeDtypeStruct(*shape) for shape in shapes],
        scratch_shapes=[
            pltpu.VMEM((moment_rows * devices, width), BF16),
            pltpu.SemaphoreType.DMA((len(entries),)),
        ],
        compiler_params=pltpu.CompilerParams(vmem_limit_bytes=LIMIT),
        cost_estimate=cost(0, 25_000_000),
        name="first_rows",
    )(
        place_index(parts),
        *[block for block, _, _ in parts],
        text,
        visual,
        order,
        lines,
    )


def store_blocks(mine_ref, away_ref, core, quad, store):
    quads = mine_ref.shape[0]
    for bit in range(2):

        @pl.when(core == bit)
        def _(bit=bit):
            for dp in range(2 * quads):
                ref = mine_ref if dp % 2 == bit else away_ref
                store(ref, (dp // 2) ^ quad, dp)


def place_pair():
    place = lax.axis_index("dp")
    return jnp.stack([place % 2, place // 2]).astype(jnp.int32)


def feed_kernel(entries, count, length, ffn, place_ref, core_ref, *refs):
    parts, refs = refs[:count], refs[count:]
    inputs, (lines_ref, inner_b_ref), refs = refs[:3], refs[3:5], refs[5:]
    results, (scale_ref, total_ref, sums_ref, inner_sums_ref), refs = refs[:3], refs[3:7], refs[7:]
    mine_ref, away_ref = refs[:2]
    outer_w_ref, inner_w_ref, act_ref, slope_ref, first_ref, low_ref = refs[2:8]
    first_turned, low_turned = refs[8:10]
    mixed_ref, hidden_ref, ct_ref, normed_ref, out_w_ref, output_ref = refs[10:16]
    sems, in_sems, out_sems = refs[16:]
    step = pl.program_id(0)
    width = hidden_ref.shape[1]
    outs = (out_w_ref, outer_w_ref, inner_w_ref)
    fetch = [
        pltpu.make_async_copy(source, target, in_sems.at[n])
        for n, (source, target) in enumerate(zip(inputs, (mixed_ref, hidden_ref, ct_ref)))
    ]
    leave = [
        pltpu.make_async_copy(source, target, out_sems.at[n])
        for n, (source, target) in enumerate(zip((normed_ref, out_w_ref, output_ref), results))
    ]
    gain1, bias1, outer_b, gain2, bias2 = [lines_ref[n : n + 1, :] for n in range(5)]

    @pl.when(step == 0)
    def _():
        copies = part_copies(entries, place_ref, parts, outs, sems)
        square = [copy for entry, copy in zip(entries, copies) if entry[3] == 0]
        now = [copy for entry, copy in zip(entries, copies) if entry[3] > 0 and entry[4] == 0]
        later = [copy for entry, copy in zip(entries, copies) if entry[3] > 0 and entry[4] > 0]
        for copy in [fetch[0]] + square + [fetch[1]] + now:
            copy.start()
        for copy in [fetch[0]] + square:
            copy.wait()
        for copy in later + [fetch[2], leave[1]]:
            copy.start()
        attended = dot_nn(mixed_ref[...], out_w_ref[...])
        fetch[1].wait()
        normed, scale = norm_stats(hidden_ref[...] + attended)
        first = normed * gain1 + bias1
        normed_ref[...] = normed
        scale_ref[...] = scale
        low = first.astype(BF16)
        first_ref[...] = low
        total_ref[...] = first + outer_b
        first_turned[...] = low.T
        leave[0].start()

    for index in range(ffn):

        @pl.when(step == index)
        def _(index=index):
            copies = part_copies(entries, place_ref, parts, outs, sems)
            for entry, copy in zip(entries, copies):
                if entry[3] > 0 and entry[4] == index * width:
                    copy.wait()

    @pl.when(step < ffn)
    def _():
        rows = pl.ds(pl.multiple_of(step * width, width), width)
        inner = dot_nn(first_ref[...], inner_w_ref[rows, :]) + inner_b_ref[step]
        root = 0.7978845608028654
        square = inner * inner
        half = 0.5 + 0.5 * jnp.tanh(inner * (root + (0.044715 * root) * square))
        act = inner * half
        slope = half + act * (1.0 - half) * (2 * root + (6 * 0.044715 * root) * square)
        slope_ref[step] = slope.astype(BF16)
        act = act.astype(BF16)
        act_ref[step] = act
        total_ref[...] += dot_nt(act, outer_w_ref[rows, :])

    @pl.when(step == ffn - 1)
    def _():
        fetch[2].wait()
        normed, scale = norm_stats(total_ref[...])
        output_ref[...] = (normed * gain2 + bias2).astype(BF16)[:length]
        leave[2].start()
        row = lax.broadcasted_iota(jnp.int32, (normed.shape[0], 1), 0)
        blank = jnp.zeros((normed.shape[0] - length, width), BF16)
        ct = jnp.concatenate([ct_ref[...], blank], 0).astype(F32)
        grad = norm_back(ct, normed, scale, gain2)
        total_ref[...] = grad
        low = grad.astype(BF16)
        low_ref[...] = low
        low_turned[...] = low.T
        sums_ref[0:1, :] = jnp.sum(ct * normed, 0, keepdims=True)
        sums_ref[1:2, :] = jnp.sum(ct, 0, keepdims=True)
        sums_ref[2:3, :] = jnp.sum(grad, 0, keepdims=True)

    @pl.when(step >= ffn)
    def _():
        f = step - ffn
        rows = pl.ds(pl.multiple_of(f * width, width), width)
        grad = dot_nn(low_ref[...], outer_w_ref[rows, :]) * slope_ref[f].astype(F32)
        inner_sums_ref[0] = jnp.sum(grad, 0, keepdims=True)
        grad = grad.astype(BF16)
        total_ref[...] += dot_nt(grad, inner_w_ref[rows, :])
        inner = dot_nn(first_turned[...], grad).astype(BF16)
        outer = dot_nn(low_turned[...], act_ref[f]).astype(BF16)
        size = mine_ref.shape[3]

        def store(ref, slot, dp):
            ref[slot, 0, 0] = inner[dp * size : (dp + 1) * size]
            ref[slot, 1, 0] = outer[dp * size : (dp + 1) * size]

        store_blocks(mine_ref, away_ref, core_ref[0], core_ref[1], store)

    @pl.when(step == 2 * ffn - 1)
    def _():
        for copy in leave:
            copy.wait()


def feed_forward(feeds, mixed, hidden, lines, inner_b, ct, inner_rows):
    parts, entries = [], []
    for some, layout in feeds:
        for part, *entry in place_entries(some, layout):
            entries.append((part + len(parts), *entry))
        parts += some
    entries.sort(key=lambda entry: (entry[3] > 0, entry[4], -entry[3]))
    rows, width = hidden.shape
    ffn, _, columns = inner_b.shape
    quads = lax.axis_size("dp") // 2
    square = whole((rows, width))
    back = lambda i: jnp.maximum(i - ffn, 0)
    block = pl.BlockSpec((quads, 2, 1, inner_rows, columns), lambda i: (0, 0, back(i), 0, 0))
    blocks = jax.ShapeDtypeStruct((quads, 2, ffn, inner_rows, columns), BF16)
    smem = pl.BlockSpec(memory_space=pltpu.SMEM)
    shapes = [
        ((rows, width), F32),
        ((width, width), BF16),
        (ct.shape, BF16),
        ((rows, 1), F32),
        ((rows, width), F32),
        ((3, width), F32),
        ((ffn, 1, columns), F32),
    ]
    anywhere = pl.BlockSpec(memory_space=pl.ANY)
    return pl.pallas_call(
        functools.partial(feed_kernel, entries, len(parts), ct.shape[0], ffn),
        grid=(2 * ffn,),
        in_specs=[smem, smem]
        + [anywhere] * (len(parts) + 3)
        + [whole(lines.shape), whole(inner_b.shape)],
        out_specs=[anywhere] * 3
        + [whole((rows, 1)), square, whole((3, width))]
        + [pl.BlockSpec((1, 1, columns), lambda i: (back(i), 0, 0)), block, block],
        out_shape=[jax.ShapeDtypeStruct(*shape) for shape in shapes] + [blocks, blocks],
        scratch_shapes=[
            pltpu.VMEM((ffn * width, columns), BF16),
            pltpu.VMEM((ffn * width, columns), BF16),
            pltpu.VMEM((ffn, rows, columns), BF16),
            pltpu.VMEM((ffn, rows, columns), BF16),
            pltpu.VMEM((rows, width), BF16),
            pltpu.VMEM((rows, width), BF16),
            pltpu.VMEM((width, rows), BF16),
            pltpu.VMEM((width, rows), BF16),
            pltpu.VMEM((rows, width), BF16),
            pltpu.VMEM((rows, width), F32),
            pltpu.VMEM(ct.shape, BF16),
            pltpu.VMEM((rows, width), F32),
            pltpu.VMEM((width, width), BF16),
            pltpu.VMEM(ct.shape, BF16),
            pltpu.SemaphoreType.DMA((len(entries),)),
            pltpu.SemaphoreType.DMA((3,)),
            pltpu.SemaphoreType.DMA((3,)),
        ],
        compiler_params=pltpu.CompilerParams(vmem_limit_bytes=LIMIT),
        cost_estimate=cost(0, 100_000_000),
        name="feed_forward",
    )(
        place_index(parts),
        place_pair(),
        *[part for part, _, _ in parts],
        mixed,
        hidden,
        ct,
        lines,
        inner_b,
    )


def norm_kernel(
    grad_ref, normed_ref, scale_ref, lines_ref, w_ref, out_ref, low_ref, mix_ref, sums_ref
):
    grad, normed = grad_ref[...], normed_ref[...]
    attn = norm_back(grad, normed, scale_ref[...], lines_ref[0:1, :])
    out_ref[...] = attn
    low = attn.astype(BF16)
    low_ref[...] = low
    mix_ref[...] = dot_nt(low, w_ref[...]).astype(BF16)
    sums_ref[0:1, :] = jnp.sum(grad * normed, 0, keepdims=True)
    sums_ref[1:2, :] = jnp.sum(grad, 0, keepdims=True)


def norm_rows(grad, normed, scale, lines, out_w):
    rows, width = grad.shape
    low = jax.ShapeDtypeStruct((rows, width), BF16)
    return pl.pallas_call(
        norm_kernel,
        out_shape=[
            jax.ShapeDtypeStruct((rows, width), F32),
            low,
            low,
            jax.ShapeDtypeStruct((2, width), F32),
        ],
        compiler_params=pltpu.CompilerParams(vmem_limit_bytes=LIMIT),
        cost_estimate=cost(0, 12_000_000),
        name="norm_rows",
    )(grad, normed, scale, lines, out_w)


def tail_kernel(text_len, place_ref, *refs):
    inputs, (order_ref, attn_ref, tokens_ref), refs = refs[:11], refs[11:14], refs[14:]
    outputs, buffers = refs[:2], refs[2:13]
    mine, away, in_sems, out_sems = refs[13:]
    low_ref, mixed_ref, attn_low_ref, qkv_w_ref, bn_ref = buffers[6:]
    names = (6, 0, 1, 2, 3, 4, 5, 7, 8, 9, 10)
    copies = {n: pltpu.make_async_copy(inputs[n], buffers[n], in_sems.at[n]) for n in names}
    for n in names:
        copies[n].start()
    visual_len = bn_ref.shape[0]
    width = attn_low_ref.shape[1]
    core, quad = place_ref[0], place_ref[1]
    sent = []

    def spread(values, begin, n):
        values = values.astype(BF16)
        rows = values.shape[0] // (2 * mine.shape[0])

        def store(ref, slot, dp):
            ref[slot, begin : begin + rows, :] = values[dp * rows : (dp + 1) * rows]

        store_blocks(mine, away, core, quad, store)
        part = pl.ds(begin, rows)
        for k, ref in enumerate((mine, away)):
            copy = pltpu.make_async_copy(
                ref.at[:, part, :], outputs[k].at[:, part, :], out_sems.at[n, k]
            )
            copy.start()
            sent.append(copy)
        return begin + rows

    copies[6].wait()
    turned = low_ref[...].T
    begin = 0
    grads = []
    for n in range(3):
        copies[2 * n].wait()
        copies[2 * n + 1].wait()
        grads.append(jnp.concatenate([buffers[2 * n][...], buffers[2 * n + 1][...]], 1))
        begin = spread(dot_nn(turned, grads[n]), begin, n)
    copies[7].wait()
    copies[8].wait()
    begin = spread(dot_nn(mixed_ref[...].T, attn_low_ref[...]), begin, 3)
    copies[9].wait()
    tokens = attn_ref[...]
    for n in range(3):
        lanes = slice(n * width, (n + 1) * width)
        tokens = tokens + dot_nt(grads[n][text_len:], qkv_w_ref[:, lanes])
    picker = picked(order_ref[...], visual_len)
    tokens = exact(picker, tokens[:visual_len], ((0,), (0,))).astype(BF16)
    tokens_ref[...] = tokens
    copies[10].wait()
    spread(dot_tn(bn_ref[...], tokens), begin, 4)
    for copy in sent:
        copy.wait()


def tail_rows(back, qkv_w, attn, attn_low, mixed, low, order, bn_rows, text_len):
    dp, ffn = lax.axis_size("dp"), lax.axis_size("ffn")
    rows, width = attn.shape
    visual_len, channels = bn_rows.shape
    size = 4 * (width // dp) + channels // dp
    vmem = pl.BlockSpec(memory_space=pltpu.VMEM)
    anywhere = pl.BlockSpec(memory_space=pl.ANY)
    inputs = [g for pair in back for g in pair] + [low, mixed, attn_low, qkv_w, bn_rows]
    rest = rows - text_len
    tail = pl.BlockSpec((rest, width), lambda *_: (text_len // rest, 0))
    blocks = jax.ShapeDtypeStruct((dp // 2, size, width), BF16)
    return pl.pallas_call(
        functools.partial(tail_kernel, text_len),
        grid=(1,),
        in_specs=[pl.BlockSpec(memory_space=pltpu.SMEM)]
        + [anywhere] * len(inputs)
        + [whole(order.shape), tail],
        out_specs=[whole((visual_len, width))] + [anywhere] * 2,
        out_shape=[jax.ShapeDtypeStruct((visual_len, width), BF16), blocks, blocks],
        scratch_shapes=[pltpu.VMEM(x.shape, BF16) for x in inputs]
        + [
            pltpu.VMEM(blocks.shape, BF16),
            pltpu.VMEM(blocks.shape, BF16),
            pltpu.SemaphoreType.DMA((len(inputs),)),
            pltpu.SemaphoreType.DMA((5, 2)),
        ],
        compiler_params=pltpu.CompilerParams(vmem_limit_bytes=LIMIT),
        cost_estimate=cost(0, 40_000_000),
        name="tail_rows",
    )(place_pair(), *inputs, order, attn)


def batch_kernel(tokens_ref, visual_ref, stats_ref, proj_ref, grad_bn_ref, sums_ref):
    grad_bn = dot_nt(tokens_ref[...], proj_ref[...])
    grad_bn_ref[...] = grad_bn
    normed = (visual_ref[...].astype(F32) - stats_ref[0:1, :]) * stats_ref[1:2, :]
    sums_ref[0:1, :] = jnp.sum(grad_bn, 0, keepdims=True)
    sums_ref[1:2, :] = jnp.sum(grad_bn * normed, 0, keepdims=True)


def batch_rows(tokens, visual, stats, proj):
    return pl.pallas_call(
        batch_kernel,
        out_shape=[
            jax.ShapeDtypeStruct(visual.shape, F32),
            jax.ShapeDtypeStruct((2, visual.shape[1]), F32),
        ],
        compiler_params=pltpu.CompilerParams(vmem_limit_bytes=LIMIT),
        cost_estimate=cost(0, 6_000_000),
        name="batch_rows",
    )(tokens, visual, stats, proj)


def text_kernel(*refs):
    dq, dk, dv = refs[0:2], refs[2:4], refs[4:6]
    qkv_w_ref, attn_ref, text_ref = refs[6:]
    width = text_ref.shape[1]
    total = attn_ref[...]
    for n, (low, high) in enumerate((dq, dk, dv)):
        grads = jnp.concatenate([low[...], high[...]], 1)
        total = total + dot_nt(grads, qkv_w_ref[:, n * width : (n + 1) * width])
    text_ref[...] = total


def text_rows(back, qkv_w, attn, text_len):
    width = attn.shape[1]
    step = text_len // 2
    grads = [g for pair in back for g in pair]
    return pl.pallas_call(
        text_kernel,
        grid=(2,),
        in_specs=[pl.BlockSpec((step, g.shape[1]), lambda i: (i, 0)) for g in grads]
        + [whole(qkv_w.shape), pl.BlockSpec((step, width), lambda i: (i, 0))],
        out_specs=pl.BlockSpec((step, width), lambda i: (i, 0)),
        out_shape=jax.ShapeDtypeStruct((text_len, width), F32),
        compiler_params=pltpu.CompilerParams(vmem_limit_bytes=LIMIT),
        cost_estimate=cost(0, 25_000_000),
        name="text_rows",
    )(*grads, qkv_w, attn)


def lane_rows(values, width):
    lanes = values.shape[1]
    pieces = pl.cdiv(lanes, width)
    if pieces * width > lanes:
        values = jnp.concatenate([values, jnp.zeros((1, pieces * width - lanes), F32)], 1)
    return [values[:, n * width : (n + 1) * width] for n in range(pieces)]


def sums_kernel(half_levels, bn_ref, one_ref, two_ref, inner_ref, *refs):
    out_ref = refs[-1]
    width = out_ref.shape[1]
    rows = []
    for n in range(bn_ref.shape[0]):
        rows += lane_rows(bn_ref[n : n + 1, :], width)
    for ref in (one_ref, two_ref):
        rows += [ref[n : n + 1, :] for n in range(ref.shape[0])]
    inner = [inner_ref[n] for n in range(inner_ref.shape[0])]
    rows += lane_rows(jnp.concatenate(inner, 1), width)
    halves = sum(ref[...] for ref in refs[:-1])
    tables, lane = [], 0
    for n, size in enumerate(half_levels):
        for row in (32 * n, 32 * n + 16):
            tables.append(halves[row : row + 16, lane : lane + size])
        lane += size
    tables = jnp.concatenate(tables, 1)
    blank = jnp.zeros((tables.shape[0], 256 - tables.shape[1]), F32)
    tables = jnp.concatenate([tables, blank], 1)
    group = width // 256
    for n in range(0, 12, group):
        rows.append(jnp.concatenate([tables[h : h + 1] for h in range(n, n + group)], 1))
    rows += [jnp.zeros((1, width), F32)] * (out_ref.shape[0] - len(rows))
    out_ref[...] = jnp.concatenate(rows, 0)


def pack_sums(bn_sums, one, two, inner, tables, half_levels):
    width = one.shape[1]
    rows = 2 * pl.cdiv(bn_sums.shape[1], width) + 5 + inner.size // width + 12 * 256 // width
    return pl.pallas_call(
        functools.partial(sums_kernel, half_levels),
        out_shape=jax.ShapeDtypeStruct((pl.cdiv(rows, 8) * 8, width), F32),
        cost_estimate=cost(0, 1_000_000),
        name="pack_sums",
    )(bn_sums, one, two, inner, *tables)


def finish_kernel(levels, count, *refs):
    left_ref, right_ref, grad_bn_ref, visual_ref, stats_ref, lines_ref = refs[:6]
    shift_ref, scale_ref, grad_ref, inner_ref = refs[6:10]
    vectors, tables = refs[10:15], refs[15:]
    total = left_ref[...] + right_ref[...]
    width = total.shape[1]
    channels = grad_bn_ref.shape[1]
    row = 0

    def take(lanes):
        nonlocal row
        pieces = pl.cdiv(lanes, width)
        row += pieces
        return jnp.concatenate([total[n : n + 1] for n in range(row - pieces, row)], 1)[:, :lanes]

    shift, scale = take(channels), take(channels)
    shift_ref[...] = shift.reshape(channels)
    scale_ref[...] = scale.reshape(channels)
    for ref in vectors:
        ref[...] = take(width).reshape(width)
    inner_ref[...] = take(inner_ref.shape[0]).reshape(inner_ref.shape[0])
    inverse = stats_ref[1:2, :]
    normed = (visual_ref[...].astype(F32) - stats_ref[0:1, :]) * inverse
    grad = grad_bn_ref[...] - shift * (1.0 / count) - normed * (scale * (1.0 / count))
    grad_ref[...] = lines_ref[0:1, :] * inverse * grad
    group = width // 256
    heads = []
    for n in range(12):
        lane = n % group * 256
        heads.append(total[row + n // group : row + n // group + 1, lane : lane + 256])
    heads = jnp.concatenate(heads, 0)
    begin = 0
    for ref, size in zip(tables, levels):
        ref[...] = heads[:, begin : begin + size]
        begin += size


def finish(left, right, grad_bn, visual, stats, lines, inner, levels, count):
    width = left.shape[1]
    channels = visual.shape[1]
    line = lambda n: jax.ShapeDtypeStruct((n,), F32)
    return pl.pallas_call(
        functools.partial(finish_kernel, levels, count),
        out_shape=[line(channels), line(channels), jax.ShapeDtypeStruct(visual.shape, F32)]
        + [line(inner)]
        + [line(width)] * 5
        + [jax.ShapeDtypeStruct((12, n), F32) for n in levels],
        cost_estimate=cost(0, 3_000_000),
        name="finish",
    )(left, right, grad_bn, visual, stats, lines)


def bias_kernel(rows_step, rel_ref, x_ref, y_ref, tab_ref, out_ref, unit_ref, level_ref):
    pairs = out_ref.shape[0]
    table = tab_ref[...]
    top = jnp.max(jnp.max(jnp.abs(table), 1, keepdims=True), 0, keepdims=True)
    top = jnp.maximum(top, 1e-30)
    unit_ref[...] = top * (2.0 / LEVELS)
    level = jnp.floor((table / top + 1.0) * (0.5 * LEVELS) + 0.5).astype(jnp.int32)
    level_ref[0] = level[:, :128]
    level_ref[1] = level[:, 128:]
    words = []
    for n in range(2):
        low = level_ref[n, pl.ds(0, pairs, stride=2), :]
        high = level_ref[n, pl.ds(1, pairs, stride=2), :]
        words.append(low + high * 65536)
    both = [jnp.broadcast_to(words[0][p : p + 1, :], (8, 128)) for p in range(pairs)]
    rel = [jnp.broadcast_to(words[1][p : p + 1, :], (8, 128)) for p in range(pairs)]

    def look(table, index):
        return jnp.take_along_axis(table, index, axis=1, mode="promise_in_bounds")

    for c in range(out_ref.shape[2] // 128):
        for r in range(rows_step // 8):
            rows, cols = pl.ds(r * 8, 8), pl.ds(c * 128, 128)
            rel_id = rel_ref[0, rows, cols] & 31
            x_id = x_ref[0, rows, cols] & 63
            y_id = (y_ref[0, rows, cols] & 63) + 64
            for p in range(pairs):
                out_ref[p, rows, cols] = (
                    look(rel[p], rel_id) + look(both[p], x_id) + look(both[p], y_id)
                )


def bias_words(rel, x, y, table, first, steps):
    step = 64
    rows = steps * step
    pairs = table.shape[0] // 2
    lanes = pl.cdiv(rel.shape[2], 128) * 128
    ids = pl.BlockSpec((1, step, lanes), lambda i: (0, i + first, 0))
    return pl.pallas_call(
        functools.partial(bias_kernel, step),
        grid=(steps,),
        in_specs=[ids, ids, ids, whole(table.shape)],
        out_specs=[pl.BlockSpec((pairs, step, lanes), lambda i: (0, i, 0)), whole((1, 1))],
        out_shape=[
            jax.ShapeDtypeStruct((pairs, rows, lanes), jnp.int32),
            jax.ShapeDtypeStruct((1, 1), F32),
        ],
        scratch_shapes=[pltpu.VMEM((2, table.shape[0], 128), jnp.int32)],
        compiler_params=pltpu.CompilerParams(vmem_limit_bytes=LIMIT),
        cost_estimate=cost(0, 6_000_000 * steps),
        name="bias_words",
    )(rel, x, y, table)


def lane_halves(rows):
    lane = lax.broadcasted_iota(jnp.int32, (rows, 128), 1)
    return lane < 64, lane >= 64


def attend_kernel(unit_ref, q_ref, k_ref, v_ref, col_ref, row_ref, *refs):
    word_refs, (p_ref, o_ref, mask_ref) = refs[:-3], refs[-3:]

    @pl.when(pl.program_id(0) == 0)
    def _():
        mask_ref[...] = jnp.where(col_ref[...] == row_ref[...], 0.0, NEG)

    unit = unit_ref[...]
    rows = q_ref.shape[0]
    halves = lane_halves(rows)
    q, k, v = q_ref[...], k_ref[...], v_ref[...]
    none = jnp.zeros_like(q)
    words = jnp.concatenate([ref[0][:, :rows] for ref in word_refs], 0)
    mask = mask_ref[...]
    mixed = jnp.zeros((rows, 128), F32)
    for h in range(2):
        scores = dot_nt(jnp.where(halves[h], q, none), k)
        word = (words & 0xFFFF) if h == 0 else lax.shift_right_logical(words, 16)
        scores = scores + word.astype(F32) * unit + mask
        expo = jnp.exp(scores - jnp.max(scores, -1, keepdims=True))
        probs = (expo * (1.0 / jnp.sum(expo, -1, keepdims=True))).astype(BF16)
        p_ref[h] = probs
        mixed = mixed + dot_nn(probs, jnp.where(halves[h], v, none))
    o_ref[...] = mixed.astype(BF16)


def attend(unit, qkv, words, segments):
    pairs = words[0].shape[0]
    rows = qkv.shape[0]
    col = [pl.BlockSpec((rows, 128), lambda p, n=n: (0, n * pairs + p)) for n in range(3)]
    flops = pairs * 4 * 2 * rows * rows * 128
    return pl.pallas_call(
        attend_kernel,
        grid=(pairs,),
        in_specs=[
            whole((1, 1)),
            col[0],
            col[1],
            col[2],
            whole((rows, 1)),
            whole((1, rows)),
        ]
        + [pl.BlockSpec((1,) + w.shape[1:], lambda p: (p, 0, 0)) for w in words],
        out_specs=[
            pl.BlockSpec((2, rows, rows), lambda p: (p, 0, 0)),
            pl.BlockSpec((rows, 128), lambda p: (0, p)),
        ],
        out_shape=[
            jax.ShapeDtypeStruct((2 * pairs, rows, rows), BF16),
            jax.ShapeDtypeStruct((rows, pairs * 128), BF16),
        ],
        scratch_shapes=[pltpu.VMEM((rows, rows), F32)],
        compiler_params=pltpu.CompilerParams(vmem_limit_bytes=LIMIT),
        cost_estimate=cost(flops, 40_000_000),
        name="attend",
    )(unit, qkv, qkv, qkv, *segments, *words)


def attend_back_kernel(q_ref, k_ref, v_ref, g_ref, p_ref, ds_ref, dq_ref, dk_ref, dv_ref):
    rows = q_ref.shape[0]
    halves = lane_halves(rows)
    q, k, v, g = q_ref[...], k_ref[...], v_ref[...], g_ref[...]
    none = jnp.zeros_like(q)
    blank = jnp.zeros((rows, ds_ref.shape[2] - rows), BF16)
    dq = jnp.zeros((rows, 128), F32)
    dk, dv = dq, dq
    for h in range(2):
        low = p_ref[h]
        probs = low.astype(F32)
        weighted = probs * dot_nt(g, jnp.where(halves[h], v, none))
        ds = (weighted - probs * jnp.sum(weighted, -1, keepdims=True)).astype(BF16)
        ds_ref[h] = jnp.concatenate([ds, blank], 1)
        dq = dq + dot_nn(ds, jnp.where(halves[h], k, none))
        dv = dv + dot_tn(low, jnp.where(halves[h], g, none))
        dk = dk + dot_tn(ds, jnp.where(halves[h], q, none))
    dq_ref[...] = (dq * 0.125).astype(BF16)
    dk_ref[...] = dk.astype(BF16)
    dv_ref[...] = dv.astype(BF16)


def attend_back(qkv, grad, probs, first, pairs):
    every = probs.shape[0] // 2
    rows = qkv.shape[0]
    col = [pl.BlockSpec((rows, 128), lambda p, n=n: (0, n * every + p + first)) for n in range(3)]
    new = pl.BlockSpec((rows, 128), lambda p: (0, p))
    big = pl.BlockSpec((2, rows, rows), lambda p: (p + first, 0, 0))
    lanes = pl.cdiv(rows, 128) * 128
    out = jax.ShapeDtypeStruct((rows, pairs * 128), BF16)
    flops = pairs * 2 * 4 * 2 * rows * rows * 128
    return pl.pallas_call(
        attend_back_kernel,
        grid=(pairs,),
        in_specs=[col[0], col[1], col[2], col[0], big],
        out_specs=[pl.BlockSpec((2, rows, lanes), lambda p: (p, 0, 0)), new, new, new],
        out_shape=[jax.ShapeDtypeStruct((2 * pairs, rows, lanes), BF16), out, out, out],
        compiler_params=pltpu.CompilerParams(vmem_limit_bytes=LIMIT),
        cost_estimate=cost(flops, 8_000_000 * pairs),
        name="attend_back",
    )(qkv, qkv, qkv, grad, probs)


def table_kernel(first, levels, block_ref, count_ref, rel_ref, x_ref, y_ref, *refs):
    ds_refs, out_ref, rows_ref = refs[:-2], refs[-2], refs[-1]
    place = pl.program_id(0)
    step = rel_ref.shape[1]
    every = rel_ref.shape[2] // 128

    @pl.when(place == 0)
    def _():
        out_ref[...] = jnp.zeros_like(out_ref)
        rows_ref[...] = jnp.zeros_like(rows_ref)

    heads = [(ref, n) for ref in ds_refs for n in range(ref.shape[0])]

    def group(r, start, blocks):
        width = blocks * 128
        level = lax.broadcasted_iota(jnp.int32, (16, width), 0).astype(F32).astype(BF16)
        one = jnp.ones((16, width), BF16)
        none = jnp.zeros((16, width), BF16)

        def one_hot(ids, count):
            wide = jnp.broadcast_to(ids, (16, width)).astype(BF16)
            return [jnp.where(wide == level + BF16(16 * t), one, none) for t in range(count // 16)]

        def halves(values, top):
            chosen = jnp.broadcast_to(top, (16, width)).astype(BF16) == one
            return [jnp.where(chosen, none, values), jnp.where(chosen, values, none)]

        rows = pl.ds(pl.multiple_of(r * 16, 16), 16)
        lanes = pl.ds(pl.multiple_of(start * 128, 128), width)
        for h, (ref, n) in enumerate(heads):
            values = ref[n, rows, lanes].astype(F32)
            for c in range(blocks):
                rows_ref[c, pl.ds(h, 16, stride=16), :] = values[:, 128 * c : 128 * c + 128]
        total = out_ref[...]
        ids = [ref[0, rows, lanes].astype(F32) for ref in (x_ref, y_ref, rel_ref)]
        counts = (levels[1] // 2, levels[2] // 2, levels[0] // 2)
        tops = [(i >= count).astype(F32) for i, count in zip(ids, counts)]
        rest = [i - top * count for i, top, count in zip(ids, tops, counts)]
        for n in range(16):
            grads = jnp.concatenate(
                [rows_ref[c, 16 * n : 16 * n + 16, :].astype(BF16) for c in range(blocks)], 1
            )
            hot, split = [], []
            for top, low, count in zip(tops, rest, counts):
                hot += one_hot(low[n : n + 1], count)
                split += halves(grads, top[n : n + 1])
            total = total + dot_nt(jnp.concatenate(split, 0), jnp.concatenate(hot, 0))
        out_ref[...] = total

    def body(r, _):
        index = (place + first) * (step // 16) + r
        start, count = block_ref[index], count_ref[index]
        for blocks in range(1, every + 1):

            @pl.when(count == blocks)
            def _(blocks=blocks):
                group(r, start, blocks)

        return 0

    lax.fori_loop(0, step // 16, body, 0)


def table_sums(ranges, rel, x, y, ds, levels, first, steps):
    step = 64
    lanes = ds[0].shape[2]
    ids = pl.BlockSpec((1, step, lanes), lambda i, *_: (0, i + first, 0))
    return pl.pallas_call(
        functools.partial(table_kernel, first, levels),
        grid_spec=pltpu.PrefetchScalarGridSpec(
            num_scalar_prefetch=2,
            grid=(steps,),
            in_specs=[ids, ids, ids]
            + [pl.BlockSpec((d.shape[0], step, lanes), lambda i, *_: (0, i + first, 0)) for d in ds],
            out_specs=whole((96, sum(levels) // 2)),
            scratch_shapes=[pltpu.VMEM((lanes // 128, 256, 128), F32)],
        ),
        out_shape=jax.ShapeDtypeStruct((96, sum(levels) // 2), F32),
        compiler_params=pltpu.CompilerParams(vmem_limit_bytes=LIMIT),
        cost_estimate=cost(0, 8_000_000 * steps),
        name="table_sums",
    )(*ranges, rel, x, y, *ds)


def document_blocks(segments, rows):
    length = segments.shape[0]
    first = segments[0:rows:16]
    last = segments[jnp.minimum(jnp.arange(15, rows, 16), length - 1)]
    begin = jnp.sum(segments[None, :] < first[:, None], 1, dtype=jnp.int32)
    end = jnp.sum(segments[None, :] <= last[:, None], 1, dtype=jnp.int32)
    return begin // 128, (end + 127) // 128 - begin // 128


def norm_stats(values):
    center = values - jnp.mean(values, -1, keepdims=True)
    scale = lax.rsqrt(jnp.mean(center * center, -1, keepdims=True) + EPS)
    return center * scale, scale


def norm_back(grad, normed, scale, gain):
    scaled = grad * gain
    return scale * (
        scaled
        - jnp.mean(scaled, -1, keepdims=True)
        - normed * jnp.mean(scaled * normed, -1, keepdims=True)
    )


def on_device(
    text_hidden,
    visual_maps,
    patch_order,
    segment_ids,
    rel_bucket,
    x_bucket,
    y_bucket,
    bn_scale,
    bn_shift,
    vis_proj,
    w_query,
    w_key,
    w_value,
    w_output,
    rel_table,
    x_table,
    y_table,
    first_gain,
    first_bias,
    w_inner,
    b_inner,
    w_outer,
    b_outer,
    second_gain,
    second_bias,
    cotangent,
):
    heads = rel_table.shape[1]
    pairs = heads // 2
    visual_len = patch_order.shape[1]
    length = segment_ids.shape[1]
    text_len = length - visual_len
    width = w_query.shape[1]
    dp, ffn = lax.axis_size("dp"), lax.axis_size("ffn")
    place, here = lax.axis_index("dp"), lax.axis_index("ffn")
    devices = dp * ffn
    rows = pl.cdiv(length, 64) * 64
    count = visual_maps.shape[0] * devices
    levels = (rel_table.shape[0], x_table.shape[0], y_table.shape[0])

    inner_rows, columns = w_inner.shape
    outer_shard = w_outer.T
    steps = rows // 64

    first_set = Gather(*pack_first(w_query, w_key, w_value, vis_proj, visual_maps))
    plain = columns == width
    wide_shards = jnp.concatenate([outer_shard, w_inner], 0)
    if plain:
        late_set = Gather(
            jnp.concatenate([w_output, wide_shards], 0), [w_output.shape[0], inner_rows, inner_rows]
        )
    else:
        late_set = Gather(w_output, [w_output.shape[0]])
        wide_set = Gather(wide_shards, [inner_rows, inner_rows])

    first_set.along_ffn()
    tables = jnp.concatenate([x_table, y_table, rel_table], 0).T
    tables = jnp.pad(tables, ((0, 0), (0, 256 - tables.shape[1])))
    cuts = [0, steps * 2 // 9, steps * 6 // 9, steps]
    words = [None] * 3
    words[0], unit = bias_words(rel_bucket, x_bucket, y_bucket, tables, 0, cuts[1])
    ranges = document_blocks(segment_ids[0], rows)
    lines = jnp.stack([first_gain, first_bias, b_outer, second_gain, second_bias])
    inner_b = b_inner.reshape(ffn, 1, columns)
    segments = jnp.pad(segment_ids[0], (0, rows - length), constant_values=-1)
    segments = (segments[:, None], segments[None, :])
    bn_lines = jnp.stack([bn_scale, bn_shift])
    state, late, words[0], tables, ranges, lines, inner_b, segments, bn_lines = epoch(
        first_set.state(),
        late_set.state(),
        words[0],
        tables,
        ranges,
        lines,
        inner_b,
        segments,
        bn_lines,
    )
    first_set.hold(state)
    late_set.hold(late)

    first_set.order()
    first_set.near(3 * w_query.shape[0] * ffn)
    late_set.along_ffn(1, ffn - 1)
    words[1], _ = bias_words(rel_bucket, x_bucket, y_bucket, tables, cuts[1], cuts[2] - cuts[1])
    state, late, words[1], tables = epoch(first_set.state(), late_set.state(), words[1], tables)
    first_set.hold(state)
    late_set.hold(late)

    first_set.diagonal()
    late_set.along_ffn(ffn - 1)
    state, late, tables = epoch(first_set.state(), late_set.state(), tables)
    first_set.hold(state)
    late_set.hold(late)

    late_set.order()
    first_set.across()
    state, late = epoch(first_set.state(), late_set.state())
    first_set.hold(state)
    late_set.hold(late)

    late_rows = w_output.shape[0] * ffn
    late_set.near(late_rows + ffn * inner_rows if plain else 0)
    layout, row = [], 0
    for n, size in enumerate(first_set.rows):
        layout.append((row, size * ffn, max(n - 2, 0), 0, n * width if n < 3 else 0))
        row += size * ffn
    order_col = patch_order.reshape(visual_len, 1)
    qkv_full, proj_full, hidden, lowered, qkv, bn_rows, bn_stats = first_rows(
        first_set.parts(),
        layout,
        text_hidden,
        visual_maps,
        order_col,
        bn_lines,
        rows,
        vis_proj.shape[0] * devices,
        first_set.rows[-1],
    )
    qkv, tables = epoch(qkv, tables)
    words[2], _ = bias_words(rel_bucket, x_bucket, y_bucket, tables, cuts[2], cuts[3] - cuts[2])
    qkv, state, words[2] = epoch(qkv, late_set.state(), words[2])
    late_set.hold(state)

    late_set.diagonal()
    probs, mixed = attend(unit, qkv, words, segments)
    probs, mixed, state = epoch(probs, mixed, late_set.state())
    late_set.hold(state)
    late_set.across()
    layout = [(0, late_rows, 0, 0, 0)]
    shift = late_rows
    parts = late_set.parts()
    if not plain:
        parts = [(block, bits, 0) for block, bits, _ in parts]
        wide_set.along_ffn()
        wide_set.order()
        wide_set.near(0)
        wide_set.diagonal()
        wide_set.across()
        shift = 0
    wide_layout = [
        (shift + (n * ffn + f) * inner_rows, inner_rows, 1 + n, f * width, 0)
        for n in range(2)
        for f in range(ffn)
    ]
    feeds = [(parts, layout + wide_layout if plain else layout)]
    if not plain:
        feeds.append((wide_set.parts(), wide_layout))
    (
        first_n,
        output_full,
        output,
        first_r,
        grad_first,
        sums_two,
        inner_sums,
        mine,
        away,
    ) = feed_forward(feeds, mixed, hidden, lines, inner_b, cotangent, inner_rows)

    wide = Scatter(mine, away, lambda value, index: pick(value, index, 1))
    wide.core()
    grad_attn, attn_low, grad_mixed, sums_one = norm_rows(grad_first, first_n, first_r, lines, output_full)
    state, grad_mixed = epoch(wide.held(), grad_mixed)
    wide.hold(state)

    wide.near()
    half = pairs // 2
    back_low = attend_back(qkv, grad_mixed, probs, 0, half)
    state, back_low, qkv = epoch(wide.held(), back_low, qkv)
    wide.hold(state)
    wide.prepare()
    wide.blocks, qkv = epoch(wide.blocks, qkv)

    wide.quads()
    back_high = attend_back(qkv, grad_mixed, probs, half, pairs - half)
    back = list(zip(back_low[1:], back_high[1:]))
    tokens_grad, mine, away = tail_rows(
        back, qkv_full, grad_attn, attn_low, mixed, lowered, order_col, bn_rows, text_len
    )
    ds = (back_low[0], back_high[0])
    wide.blocks, mine, away, ds, tokens_grad = epoch(wide.blocks, mine, away, ds, tokens_grad)

    def tail_far(value, index):
        size = 4 * (width // dp)
        square = pick(value[:size].reshape(4, ffn, -1, width), index, 1)
        return jnp.concatenate(
            [square.reshape(-1, width), pick(value[size:].reshape(ffn, -1, width), index, 0)], 0
        )

    cuts = [0, steps // 3, steps]
    sums = []

    def tables(ds):
        n = len(sums)
        return sums + [
            table_sums(
                ranges, rel_bucket, x_bucket, y_bucket, ds, levels, cuts[n], cuts[n + 1] - cuts[n]
            )
        ]

    tail = Scatter(mine, away, tail_far)
    tail.core()
    wide.join()
    wide.along_ffn(1, 2)
    grad_bn, bn_sums = batch_rows(tokens_grad, visual_maps, bn_stats, proj_full)
    state, bn_sums, ds, wide.pieces = epoch(tail.held(), bn_sums, ds, wide.pieces)
    tail.hold(state)

    tail.near()
    if ffn > 2:
        wide.along_ffn(2, 3)
    sums = tables(ds)
    state, ds, sums, wide.pieces = epoch(tail.held(), ds, sums, wide.pieces)
    tail.hold(state)
    tail.prepare()
    tail.blocks, ds = epoch(tail.blocks, ds)

    tail.quads()
    if ffn > 3:
        wide.along_ffn(3)
    sums = tables(ds)
    tail.blocks, sums, back, wide.pieces = epoch(tail.blocks, sums, back, wide.pieces)

    tail.join()
    tail.along_ffn(1, 2)
    total = Sum(
        pack_sums(
            bn_sums,
            sums_one,
            sums_two,
            inner_sums,
            sums,
            (levels[1] // 2, levels[2] // 2, levels[0] // 2),
        )
    )
    for _ in range(ffn.bit_length() - 1):
        total.step()
    wide_sum = wide.total()
    state, total.values, back = epoch(tail.held(), total.values, back)
    tail.hold(state)
    if ffn > 2:
        tail.along_ffn(2)
    while len(total.steps) > 1:
        total.step()
    text_grad = text_rows(back, qkv_full, grad_attn, text_len)
    tail_sum = tail.total()
    other = total.steps[0](total.values)
    (
        shift_grad,
        scale_grad,
        visual_grad,
        inner_grad,
        gain_one,
        bias_one,
        gain_two,
        bias_two,
        outer_grad,
        x_grad,
        y_grad,
        rel_grad,
    ) = finish(
        total.values,
        other,
        grad_bn,
        visual_maps,
        bn_stats,
        bn_lines,
        b_inner.shape[0],
        (levels[1], levels[2], levels[0]),
        count,
    )
    shards, row = [], 0
    for size in [w_query.shape[0]] * 4 + [vis_proj.shape[0]]:
        shards.append(tail_sum[row : row + size])
        row += size
    return (
        output,
        text_grad,
        visual_grad,
        scale_grad.reshape(-1),
        shift_grad.reshape(-1),
        shards[4],
        shards[0],
        shards[1],
        shards[2],
        shards[3],
        rel_grad.T,
        x_grad.T,
        y_grad.T,
        gain_one.reshape(-1),
        bias_one.reshape(-1),
        wide_sum[0],
        inner_grad.reshape(-1),
        wide_sum[1].T,
        outer_grad.reshape(-1),
        gain_two.reshape(-1),
        bias_two.reshape(-1),
    )


def solution(mesh):
    rows = P(ALL, None)
    cube = P(ALL, None, None)
    return jax.shard_map(
        on_device,
        mesh=mesh,
        in_specs=(rows,) * 4
        + (cube,) * 3
        + (P(),) * 2
        + (rows,) * 5
        + (P(),) * 5
        + (P("dp", "ffn"), P(), P("ffn", "dp"))
        + (P(),) * 3
        + (rows,),
        out_specs=(rows,) * 3
        + (P(),) * 2
        + (rows,) * 5
        + (P(),) * 5
        + (P("dp", "ffn"), P(), P("ffn", "dp"))
        + (P(),) * 3,
        check_vma=False,
    )
```

```python
import functools

import jax
import jax.numpy as jnp
from jax import lax
from jax.experimental import pallas as pl
from jax.experimental.pallas import tpu as pltpu
from jax.sharding import PartitionSpec as P

EPS = 1e-05
NEG = -1e30
F32 = jnp.float32
BF16 = jnp.bfloat16
ALL = ("dp", "ffn")
LEVELS = 21845.0
MIB = 2**20


def dot_nn(a, b):
    return lax.dot_general(a, b, (((1,), (0,)), ((), ())), preferred_element_type=F32)


def dot_nt(a, b):
    return lax.dot_general(a, b, (((1,), (1,)), ((), ())), preferred_element_type=F32)


def dot_tn(a, b):
    return lax.dot_general(a, b, (((0,), (0,)), ((), ())), preferred_element_type=F32)


def pad_rows(values, rows):
    return jnp.pad(values, ((0, rows - values.shape[0]), (0, 0)))


def send_dp(values, bits):
    size = lax.axis_size("dp")
    return lax.ppermute(values, "dp", [(i, i ^ bits) for i in range(size)])


def send_ffn(values, shift):
    size = lax.axis_size("ffn")
    return lax.ppermute(values, "ffn", [(i, (i + shift) % size) for i in range(size)])


def swap_ffn(values, bits):
    size = lax.axis_size("ffn")
    return lax.ppermute(values, "ffn", [(i, i ^ bits) for i in range(size)])


def exchanges():
    steps = []
    for axis, send in (("ffn", swap_ffn), ("dp", send_dp)):
        bit = 1
        while bit < lax.axis_size(axis):
            steps.append(functools.partial(send, bits=bit))
            bit *= 2
    return steps


class Sum:
    def __init__(self, values):
        self.values = values
        self.steps = exchanges()

    def step(self):
        if self.steps:
            self.values = self.values + self.steps.pop(0)(self.values)

    def finish(self):
        while self.steps:
            self.step()
        return self.values


class Gather:
    def __init__(self, own, rows, rest=0):
        self.own = own
        self.rows = rows
        self.rest = rest

    def along_ffn(self, begin=1, end=None):
        size = lax.axis_size("ffn")
        self.far = self.far[:begin] if begin > 1 else [self.own]
        self.far += [send_ffn(self.own, k) for k in range(begin, end or size)]

    def order(self):
        size = lax.axis_size("ffn")
        here = lax.axis_index("ffn")
        if all(rows % 8 == 0 for rows in self.rows):
            self.block = order_blocks(here, self.far, self.rows, self.rest)
            return
        pieces = []
        for slot in range(size):
            value = self.far[0]
            for k in range(1, size):
                value = jnp.where((here - k + size) % size == slot, self.far[k], value)
            pieces.append(value)
        begin, ordered = 0, []
        for rows in self.rows:
            ordered += [value[begin : begin + rows] for value in pieces]
            begin += rows
        self.block = jnp.concatenate(ordered, 0)

    def near(self, cut):
        quads = lax.axis_size("dp") // 2
        self.cut = cut
        self.others = [send_dp(self.block, 1)]
        if quads == 4:
            self.mine = [self.block, send_dp(self.block, 2), send_dp(self.block, 4)]
        else:
            self.mine = [self.block] + [send_dp(self.block, 2 * k) for k in range(1, quads)]

    def diagonal(self):
        self.others += [send_dp(block, 1) for block in self.mine[1:]]
        if lax.axis_size("dp") == 8:
            low = send_dp(self.mine[1][: self.cut], 4)
            high = send_dp(self.mine[2][self.cut :], 2)
            self.mine.append((low, high))

    def across(self):
        if lax.axis_size("dp") == 8:
            self.others.append(tuple(send_dp(piece, 1) for piece in self.mine[3]))

    def state(self):
        return {k: v for k, v in vars(self).items() if k in ("own", "far", "block", "mine", "others")}

    def hold(self, state):
        vars(self).update(state)

    def parts(self):
        found = []
        for k, (mine, other) in enumerate(zip(self.mine, self.others)):
            for bits, block in ((2 * k, mine), (2 * k + 1, other)):
                if isinstance(block, tuple):
                    found += [(block[0], bits, 0), (block[1], bits, self.cut)]
                else:
                    found.append((block, bits, 0))
        return found


def epoch(*values):
    return lax.optimization_barrier(values)


def pick(values, index, axis):
    return lax.dynamic_index_in_dim(values, index, axis, keepdims=False)


def plus(a, b):
    return (a.astype(F32) + b.astype(F32)).astype(BF16)


class Scatter:
    def __init__(self, mine, away, far):
        self.value = mine
        self.away = away
        self.far = far

    def ahead(self, last):
        if self.away.shape[0] == 4:
            self.first = send_dp(last, 1)

    def core(self):
        self.got = send_dp(self.away, 1)

    def near(self):
        if self.away.shape[0] == 4:
            mine, got = self.value[3], self.first
            half = mine.shape[0] // 2
            self.low = send_dp(plus(mine[:half], got[:half]), 4)
            self.high = send_dp(plus(mine[half:], got[half:]), 2)

    def prepare(self):
        mine, got = self.value, self.got
        half = mine.shape[1] // 2
        self.blocks = []
        for k in range(1, mine.shape[0]):
            block = mine[k].astype(F32) + got[k].astype(F32)
            if mine.shape[0] == 4 and k == 1:
                block = jnp.concatenate([block[:half] + self.low.astype(F32), block[half:]], 0)
            if mine.shape[0] == 4 and k == 2:
                block = jnp.concatenate([block[:half], block[half:] + self.high.astype(F32)], 0)
            if mine.shape[0] == 4 and k == 3:
                continue
            self.blocks.append(block.astype(BF16))

    def quads(self):
        self.blocks = [send_dp(block, 2 * k) for k, block in enumerate(self.blocks, 1)]

    def join(self):
        own = self.value[0].astype(F32) + self.got[0].astype(F32)
        self.value = (own + sum(block.astype(F32) for block in self.blocks)).astype(BF16)

    def held(self):
        return {k: v for k, v in vars(self).items() if k != "far"}

    def hold(self, state):
        vars(self).update(state)

    def along_ffn(self, shifts):
        size = lax.axis_size("ffn")
        here = lax.axis_index("ffn")
        if not hasattr(self, "pieces"):
            self.pieces = [self.far(self.value, here)]
        for k in shifts:
            self.pieces.append(send_ffn(self.far(self.value, (here + k) % size), k))

    def total(self):
        return sum(piece.astype(F32) for piece in self.pieces)


LIMIT = 56 * MIB


def whole(shape):
    return pl.BlockSpec(shape, lambda *_: (0,) * len(shape))


def cost(flops, nbytes):
    return pl.CostEstimate(flops=flops // 1000, bytes_accessed=nbytes // 1000, transcendentals=0)


def pack_kernel(q_ref, k_ref, v_ref, p_ref, visual_ref, out_ref):
    row = 0
    for ref in (q_ref, k_ref, v_ref, p_ref):
        out_ref[row : row + ref.shape[0], :] = ref[...]
        row += ref.shape[0]
    width = out_ref.shape[1]
    count = visual_ref.shape[0]
    visual = visual_ref[...].astype(F32)
    mean = jnp.sum(visual, 0, keepdims=True) * (1.0 / count)
    gap = visual - mean
    spread = jnp.sum(gap * gap, 0, keepdims=True)
    channels = visual_ref.shape[1]
    chunks = pl.cdiv(channels, width)
    blank = jnp.zeros((1, chunks * width - channels), F32)
    pieces = []
    for values, times in ((mean, 3), (spread, 2)):
        if chunks * width > channels:
            values = jnp.concatenate([values, blank], 1)
        for _ in range(times):
            piece = values.astype(BF16).astype(F32)
            values = values - piece
            pieces += [piece[:, n * width : (n + 1) * width] for n in range(chunks)]
    pieces += [jnp.zeros((1, width), F32)] * (out_ref.shape[0] - row - len(pieces))
    out_ref[row:, :] = jnp.concatenate(pieces, 0).astype(BF16)


def pack_first(w_query, w_key, w_value, vis_proj, visual):
    width = w_query.shape[1]
    moments = pl.cdiv(5 * pl.cdiv(visual.shape[1], width), 16) * 16
    rows = [w.shape[0] for w in (w_query, w_key, w_value, vis_proj)] + [moments]
    own = pl.pallas_call(
        pack_kernel,
        out_shape=jax.ShapeDtypeStruct((sum(rows), width), BF16),
        name="pack_first",
    )(w_query, w_key, w_value, vis_proj, visual)
    return own, rows


def order_kernel(rows, rest, here_ref, *refs):
    parts, out_ref = refs[:-1], refs[-1]
    size = len(parts)
    here = here_ref[0]
    for index in range(size):

        @pl.when(here == index)
        def _(index=index):
            begin = 0
            for count in rows:
                for k in range(size):
                    row = begin * size + (index - k) % size * count
                    out_ref[row : row + count, :] = parts[k][begin : begin + count, :]
                begin += count

    begin = sum(rows)
    for k in range(1, size if rest else 1):
        row = begin * size + (k - 1) * rest
        out_ref[row : row + rest, :] = parts[k][begin:, :]


def order_blocks(here, parts, rows, rest):
    width = parts[0].shape[1]
    count = len(parts)
    return pl.pallas_call(
        functools.partial(order_kernel, rows, rest),
        in_specs=[pl.BlockSpec(memory_space=pltpu.SMEM)]
        + [pl.BlockSpec(memory_space=pltpu.VMEM)] * len(parts),
        out_specs=pl.BlockSpec(memory_space=pltpu.VMEM),
        out_shape=jax.ShapeDtypeStruct((count * sum(rows) + (count - 1) * rest, width), BF16),
        compiler_params=pltpu.CompilerParams(vmem_limit_bytes=LIMIT),
        name="order_blocks",
    )(here.reshape(1).astype(jnp.int32), *parts)


def place_entries(parts, layout):
    entries = []
    for n, (block, _, first) in enumerate(parts):
        for begin, rows, out, base, lane in layout:
            if first <= begin and begin + rows <= first + block.shape[0]:
                entries.append((n, begin - first, rows, out, base, lane))
    return entries


def place_bits(parts):
    return [bits for _, bits, _ in parts]


def part_copies(entries, bits, place, parts, outs, sems):
    copies = []
    for n, (part, begin, rows, out, base, lane) in enumerate(entries):
        target = pl.multiple_of(base + (place ^ bits[part]) * rows, 16)
        width = parts[part].shape[1]
        copies.append(
            pltpu.make_async_copy(
                parts[part].at[pl.ds(begin, rows), :],
                outs[out].at[pl.ds(target, rows), pl.ds(lane, width)],
                sems.at[n],
            )
        )
    return copies


def picked(order, size):
    row = lax.broadcasted_iota(jnp.int32, (size, size), 0)
    return (order == row).astype(F32)


def exact(a, b, dims):
    return lax.dot_general(
        a, b, (dims, ((), ())), precision=lax.Precision.HIGHEST, preferred_element_type=F32
    )


def first_kernel(entries, bits, devices, place_ref, *refs):
    parts, refs = refs[: len(bits)], refs[len(bits) :]
    text_ref, visual_ref, order_ref, lines_ref = refs[:4]
    qkv_w_ref, proj_ref, hidden_ref, turned_ref, qkv_ref, bn_ref, stats_ref = refs[4:11]
    moments_ref, low_ref, sems = refs[11:]
    outs = (qkv_w_ref, proj_ref, moments_ref)
    copies = part_copies(entries, bits, place_ref[0], parts, outs, sems)
    for copy in copies:
        copy.start()
    copies = [(entry[3], copy) for entry, copy in zip(entries, copies)]
    text_len, width = text_ref.shape
    visual_len, channels = visual_ref.shape
    hidden_ref[:text_len, :] = text_ref[...].astype(F32)
    low_ref[:text_len, :] = text_ref[...]
    for out, copy in copies:
        if out == 2:
            copy.wait()
    chunks = pl.cdiv(channels, width)
    moments = moments_ref[...].astype(F32).reshape(devices, -1, width)
    means = sum(moments[:, n * chunks : (n + 1) * chunks] for n in range(3))
    spreads = sum(moments[:, n * chunks : (n + 1) * chunks] for n in range(3, 5))
    average = jnp.sum(means, 0) * (1.0 / devices)
    gap = means - average[None]
    rows = visual_len * devices
    spread = (jnp.sum(spreads, 0) + visual_len * jnp.sum(gap * gap, 0)) * (1.0 / rows)
    inverse = lax.rsqrt(spread + EPS)

    def flat(values):
        pieces = [values[n : n + 1, :] for n in range(chunks)]
        return jnp.concatenate(pieces, 1)[:, :channels]

    average, inverse = flat(average), flat(inverse)
    stats_ref[0:1, :] = average
    stats_ref[1:2, :] = inverse
    normed = (visual_ref[...].astype(F32) - average) * inverse
    bn_rows = (normed * lines_ref[0:1, :] + lines_ref[1:2, :]).astype(BF16)
    bn_ref[...] = bn_rows
    for out, copy in copies:
        if out == 1:
            copy.wait()
    tokens = dot_nn(bn_rows, proj_ref[...])
    tokens = exact(picked(order_ref[...], visual_len), tokens, ((0,), (0,)))
    blank = jnp.zeros((hidden_ref.shape[0] - text_len - visual_len, width), F32)
    tokens = jnp.concatenate([tokens, blank], 0)
    hidden_ref[text_len:, :] = tokens
    low_ref[text_len:, :] = tokens.astype(BF16)
    for out, copy in copies:
        if out == 0:
            copy.wait()
    low = low_ref[...]
    turned_ref[...] = low.T
    for n in range(3):
        lanes = slice(n * width, (n + 1) * width)
        values = dot_nn(low, qkv_w_ref[:, lanes])
        qkv_ref[:, lanes] = (values * 0.125 if n == 0 else values).astype(BF16)


def first_rows(place, parts, layout, text, visual, order, lines, rows, proj_rows, moment_rows):
    devices = lax.axis_size("dp") * lax.axis_size("ffn")
    width = text.shape[1]
    channels = visual.shape[1]
    entries = place_entries(parts, layout)
    vmem = pl.BlockSpec(memory_space=pltpu.VMEM)
    shapes = [
        ((width, 3 * width), BF16),
        ((proj_rows, width), BF16),
        ((rows, width), F32),
        ((width, rows), BF16),
        ((rows, 3 * width), BF16),
        ((visual.shape[0], channels), BF16),
        ((2, channels), F32),
    ]
    return pl.pallas_call(
        functools.partial(first_kernel, entries, place_bits(parts), devices),
        in_specs=[pl.BlockSpec(memory_space=pltpu.SMEM)]
        + [pl.BlockSpec(memory_space=pl.ANY)] * len(parts)
        + [vmem] * 4,
        out_specs=[vmem] * len(shapes),
        out_shape=[jax.ShapeDtypeStruct(*shape) for shape in shapes],
        scratch_shapes=[
            pltpu.VMEM((moment_rows * devices, width), BF16),
            pltpu.VMEM((rows, width), BF16),
            pltpu.SemaphoreType.DMA((len(entries),)),
        ],
        compiler_params=pltpu.CompilerParams(vmem_limit_bytes=LIMIT),
        cost_estimate=cost(0, 25_000_000),
        name="first_rows",
    )(
        place,
        *[block for block, _, _ in parts],
        text,
        visual,
        order,
        lines,
    )


def store_blocks(mine_ref, away_ref, place, store):
    quads = mine_ref.shape[0]
    core, quad = place % 2, place // 2
    for bit in range(2):

        @pl.when(core == bit)
        def _(bit=bit):
            for dp in range(2 * quads):
                ref = mine_ref if dp % 2 == bit else away_ref
                store(ref, (dp // 2) ^ quad, dp)


def feed_kernel(entries, bits, length, ffn, place_ref, *refs):
    parts, refs = refs[: len(bits)], refs[len(bits) :]
    inputs, (lines_ref, inner_b_ref), refs = refs[:3], refs[3:5], refs[5:]
    results, (scale_ref, total_ref, sums_ref, inner_sums_ref), refs = refs[:3], refs[3:7], refs[7:]
    mine_ref, away_ref, last_ref = refs[:3]
    outer_w_ref, inner_w_ref, act_ref, slope_ref, first_ref, low_ref = refs[3:9]
    first_turned, low_turned = refs[9:11]
    mixed_ref, hidden_ref, ct_ref, normed_ref, out_w_ref, output_ref = refs[11:17]
    sems, in_sems, out_sems = refs[17:]
    step = pl.program_id(0)
    width = hidden_ref.shape[1]
    outs = (out_w_ref, outer_w_ref, inner_w_ref)
    fetch = [
        pltpu.make_async_copy(source, target, in_sems.at[n])
        for n, (source, target) in enumerate(zip(inputs, (mixed_ref, hidden_ref, ct_ref)))
    ]
    leave = [
        pltpu.make_async_copy(source, target, out_sems.at[n])
        for n, (source, target) in enumerate(zip((normed_ref, out_w_ref, output_ref), results))
    ]
    gain1, bias1, outer_b, gain2, bias2 = [lines_ref[n : n + 1, :] for n in range(5)]

    @pl.when(step == 0)
    def _():
        copies = part_copies(entries, bits, place_ref[0], parts, outs, sems)
        square = [copy for entry, copy in zip(entries, copies) if entry[3] == 0]
        now = [copy for entry, copy in zip(entries, copies) if entry[3] > 0 and entry[4] == 0]
        later = [copy for entry, copy in zip(entries, copies) if entry[3] > 0 and entry[4] > 0]
        for copy in [fetch[0]] + square + [fetch[1]] + now:
            copy.start()
        for copy in [fetch[0]] + square:
            copy.wait()
        for copy in later + [fetch[2], leave[1]]:
            copy.start()
        attended = dot_nn(mixed_ref[...], out_w_ref[...])
        fetch[1].wait()
        normed, scale = norm_stats(hidden_ref[...] + attended)
        first = normed * gain1 + bias1
        normed_ref[...] = normed
        scale_ref[...] = scale
        low = first.astype(BF16)
        first_ref[...] = low
        total_ref[...] = first + outer_b
        first_turned[...] = low.T
        leave[0].start()

    for index in range(ffn):

        @pl.when(step == index)
        def _(index=index):
            copies = part_copies(entries, bits, place_ref[0], parts, outs, sems)
            for entry, copy in zip(entries, copies):
                if entry[3] > 0 and entry[4] == index * width:
                    copy.wait()

    @pl.when(step < ffn)
    def _():
        rows = pl.ds(pl.multiple_of(step * width, width), width)
        inner = dot_nn(first_ref[...], inner_w_ref[rows, :]) + inner_b_ref[place_ref[1 + step]]
        root = 0.7978845608028654
        square = inner * inner
        half = 0.5 + 0.5 * jnp.tanh(inner * (root + (0.044715 * root) * square))
        act = inner * half
        slope = half + act * (1.0 - half) * (2 * root + (6 * 0.044715 * root) * square)
        slope_ref[step] = slope.astype(BF16)
        act = act.astype(BF16)
        act_ref[step] = act
        total_ref[...] += dot_nt(act, outer_w_ref[rows, :])

    @pl.when(step == ffn - 1)
    def _():
        fetch[2].wait()
        normed, scale = norm_stats(total_ref[...])
        output_ref[...] = (normed * gain2 + bias2).astype(BF16)[:length]
        leave[2].start()
        row = lax.broadcasted_iota(jnp.int32, (normed.shape[0], 1), 0)
        blank = jnp.zeros((normed.shape[0] - length, width), BF16)
        ct = jnp.concatenate([ct_ref[...], blank], 0).astype(F32)
        grad = norm_back(ct, normed, scale, gain2)
        total_ref[...] = grad
        low = grad.astype(BF16)
        low_ref[...] = low
        low_turned[...] = low.T
        sums_ref[0:1, :] = jnp.sum(ct * normed, 0, keepdims=True)
        sums_ref[1:2, :] = jnp.sum(ct, 0, keepdims=True)
        sums_ref[2:3, :] = jnp.sum(grad, 0, keepdims=True)

    @pl.when(step >= ffn)
    def _():
        f = step - ffn
        rows = pl.ds(pl.multiple_of(f * width, width), width)
        grad = dot_nn(low_ref[...], outer_w_ref[rows, :]) * slope_ref[f].astype(F32)
        inner_sums_ref[place_ref[1 + f]] = jnp.sum(grad, 0, keepdims=True)
        grad = grad.astype(BF16)
        total_ref[...] += dot_nt(grad, inner_w_ref[rows, :])
        inner = dot_nn(first_turned[...], grad).astype(BF16)
        outer = dot_nn(low_turned[...], act_ref[f]).astype(BF16)
        size = mine_ref.shape[3]

        def store(ref, slot, dp):
            ref[slot, 0, 0] = inner[dp * size : (dp + 1) * size]
            ref[slot, 1, 0] = outer[dp * size : (dp + 1) * size]
            if ref is away_ref:

                @pl.when(slot == away_ref.shape[0] - 1)
                def _():
                    last_ref[0, 0] = inner[dp * size : (dp + 1) * size]
                    last_ref[1, 0] = outer[dp * size : (dp + 1) * size]

        store_blocks(mine_ref, away_ref, place_ref[0], store)

    @pl.when(step == 2 * ffn - 1)
    def _():
        for copy in leave:
            copy.wait()


def feed_forward(place, feeds, mixed, hidden, lines, inner_b, ct, inner_rows):
    parts, entries = [], []
    for some, layout in feeds:
        for part, *entry in place_entries(some, layout):
            entries.append((part + len(parts), *entry))
        parts += some
    entries.sort(key=lambda entry: (entry[3] > 0, entry[4], -entry[3]))
    rows, width = hidden.shape
    ffn, _, columns = inner_b.shape
    quads = lax.axis_size("dp") // 2
    square = whole((rows, width))
    back = lambda i: jnp.maximum(i - ffn, 0)
    block = pl.BlockSpec((quads, 2, 1, inner_rows, columns), lambda i: (0, 0, back(i), 0, 0))
    blocks = jax.ShapeDtypeStruct((quads, 2, ffn, inner_rows, columns), BF16)
    last = pl.BlockSpec((2, 1, inner_rows, columns), lambda i: (0, back(i), 0, 0))
    smem = pl.BlockSpec(memory_space=pltpu.SMEM)
    shapes = [
        ((rows, width), F32),
        ((width, width), BF16),
        (ct.shape, BF16),
        ((rows, 1), F32),
        ((rows, width), F32),
        ((3, width), F32),
        ((ffn, 1, columns), F32),
    ]
    anywhere = pl.BlockSpec(memory_space=pl.ANY)
    return pl.pallas_call(
        functools.partial(feed_kernel, entries, place_bits(parts), ct.shape[0], ffn),
        grid=(2 * ffn,),
        in_specs=[smem]
        + [anywhere] * (len(parts) + 3)
        + [whole(lines.shape), whole(inner_b.shape)],
        out_specs=[anywhere] * 3
        + [whole((rows, 1)), square, whole((3, width))]
        + [whole((ffn, 1, columns)), block, block, last],
        out_shape=[jax.ShapeDtypeStruct(*shape) for shape in shapes]
        + [blocks, blocks, jax.ShapeDtypeStruct((2, ffn, inner_rows, columns), BF16)],
        scratch_shapes=[
            pltpu.VMEM((ffn * width, columns), BF16),
            pltpu.VMEM((ffn * width, columns), BF16),
            pltpu.VMEM((ffn, rows, columns), BF16),
            pltpu.VMEM((ffn, rows, columns), BF16),
            pltpu.VMEM((rows, width), BF16),
            pltpu.VMEM((rows, width), BF16),
            pltpu.VMEM((width, rows), BF16),
            pltpu.VMEM((width, rows), BF16),
            pltpu.VMEM((rows, width), BF16),
            pltpu.VMEM((rows, width), F32),
            pltpu.VMEM(ct.shape, BF16),
            pltpu.VMEM((rows, width), F32),
            pltpu.VMEM((width, width), BF16),
            pltpu.VMEM(ct.shape, BF16),
            pltpu.SemaphoreType.DMA((len(entries),)),
            pltpu.SemaphoreType.DMA((3,)),
            pltpu.SemaphoreType.DMA((3,)),
        ],
        compiler_params=pltpu.CompilerParams(vmem_limit_bytes=LIMIT),
        cost_estimate=cost(0, 100_000_000),
        name="feed_forward",
    )(
        place,
        *[part for part, _, _ in parts],
        mixed,
        hidden,
        ct,
        lines,
        inner_b,
    )


def norm_kernel(
    grad_ref, normed_ref, scale_ref, lines_ref, w_ref, out_ref, low_ref, mix_ref, sums_ref
):
    grad, normed = grad_ref[...], normed_ref[...]
    attn = norm_back(grad, normed, scale_ref[...], lines_ref[0:1, :])
    out_ref[...] = attn
    low = attn.astype(BF16)
    low_ref[...] = low
    mix_ref[...] = dot_nt(low, w_ref[...]).astype(BF16)
    sums_ref[0:1, :] = jnp.sum(grad * normed, 0, keepdims=True)
    sums_ref[1:2, :] = jnp.sum(grad, 0, keepdims=True)


def norm_rows(grad, normed, scale, lines, out_w):
    rows, width = grad.shape
    low = jax.ShapeDtypeStruct((rows, width), BF16)
    return pl.pallas_call(
        norm_kernel,
        out_shape=[
            jax.ShapeDtypeStruct((rows, width), F32),
            low,
            low,
            jax.ShapeDtypeStruct((2, width), F32),
        ],
        compiler_params=pltpu.CompilerParams(vmem_limit_bytes=LIMIT),
        cost_estimate=cost(0, 12_000_000),
        name="norm_rows",
    )(grad, normed, scale, lines, out_w)


def tail_kernel(text_len, place_ref, *refs):
    inputs, (order_ref, attn_ref, tokens_ref), refs = refs[:11], refs[11:14], refs[14:]
    outputs, buffers = refs[:3], refs[3:14]
    mine, away, in_sems, out_sems = refs[14:]
    low_ref, mixed_ref, attn_low_ref, qkv_w_ref, bn_ref = buffers[6:]
    names = (6, 0, 1, 2, 3, 4, 5, 7, 8, 9, 10)
    copies = {n: pltpu.make_async_copy(inputs[n], buffers[n], in_sems.at[n]) for n in names}
    for n in names:
        copies[n].start()
    visual_len = bn_ref.shape[0]
    width = attn_low_ref.shape[1]
    sent = []

    def spread(values, begin, n):
        values = values.astype(BF16)
        rows = values.shape[0] // (2 * mine.shape[0])

        def store(ref, slot, dp):
            ref[slot, begin : begin + rows, :] = values[dp * rows : (dp + 1) * rows]

        store_blocks(mine, away, place_ref[0], store)
        part = pl.ds(begin, rows)
        for k, ref in enumerate((mine, away)):
            copy = pltpu.make_async_copy(
                ref.at[:, part, :], outputs[k].at[:, part, :], out_sems.at[n, k]
            )
            copy.start()
            sent.append(copy)
        copy = pltpu.make_async_copy(
            away.at[away.shape[0] - 1, part, :], outputs[2].at[part, :], out_sems.at[n, 2]
        )
        copy.start()
        sent.append(copy)
        return begin + rows

    copies[6].wait()
    turned = low_ref[...]
    begin = 0
    grads = []
    for n in range(3):
        copies[2 * n].wait()
        copies[2 * n + 1].wait()
        grads.append(jnp.concatenate([buffers[2 * n][...], buffers[2 * n + 1][...]], 1))
        begin = spread(dot_nn(turned, grads[n]), begin, n)
    copies[7].wait()
    copies[8].wait()
    begin = spread(dot_nn(mixed_ref[...].T, attn_low_ref[...]), begin, 3)
    copies[9].wait()
    tokens = attn_ref[...]
    for n in range(3):
        lanes = slice(n * width, (n + 1) * width)
        tokens = tokens + dot_nt(grads[n][text_len:], qkv_w_ref[:, lanes])
    picker = picked(order_ref[...], visual_len)
    tokens = exact(picker, tokens[:visual_len], ((1,), (0,))).astype(BF16)
    tokens_ref[...] = tokens
    copies[10].wait()
    spread(dot_tn(bn_ref[...], tokens), begin, 4)
    for copy in sent:
        copy.wait()


def tail_rows(place, back, qkv_w, attn, attn_low, mixed, low, order, bn_rows, text_len):
    dp, ffn = lax.axis_size("dp"), lax.axis_size("ffn")
    rows, width = attn.shape
    visual_len, channels = bn_rows.shape
    size = 4 * (width // dp) + channels // dp
    vmem = pl.BlockSpec(memory_space=pltpu.VMEM)
    anywhere = pl.BlockSpec(memory_space=pl.ANY)
    inputs = [g for pair in back for g in pair] + [low, mixed, attn_low, qkv_w, bn_rows]
    rest = rows - text_len
    tail = pl.BlockSpec((rest, width), lambda *_: (text_len // rest, 0))
    blocks = jax.ShapeDtypeStruct((dp // 2, size, width), BF16)
    return pl.pallas_call(
        functools.partial(tail_kernel, text_len),
        grid=(1,),
        in_specs=[pl.BlockSpec(memory_space=pltpu.SMEM)]
        + [anywhere] * len(inputs)
        + [whole(order.shape), tail],
        out_specs=[whole((visual_len, width))] + [anywhere] * 3,
        out_shape=[jax.ShapeDtypeStruct((visual_len, width), BF16), blocks, blocks]
        + [jax.ShapeDtypeStruct((size, width), BF16)],
        scratch_shapes=[pltpu.VMEM(x.shape, BF16) for x in inputs]
        + [
            pltpu.VMEM(blocks.shape, BF16),
            pltpu.VMEM(blocks.shape, BF16),
            pltpu.SemaphoreType.DMA((len(inputs),)),
            pltpu.SemaphoreType.DMA((5, 3)),
        ],
        compiler_params=pltpu.CompilerParams(vmem_limit_bytes=LIMIT),
        cost_estimate=cost(0, 40_000_000),
        name="tail_rows",
    )(place, *inputs, order, attn)


def batch_kernel(tokens_ref, visual_ref, stats_ref, proj_ref, grad_bn_ref, sums_ref):
    grad_bn = dot_nt(proj_ref[...], tokens_ref[...]).T
    grad_bn_ref[...] = grad_bn
    normed = (visual_ref[...].astype(F32) - stats_ref[0:1, :]) * stats_ref[1:2, :]
    sums_ref[0:1, :] = jnp.sum(grad_bn, 0, keepdims=True)
    sums_ref[1:2, :] = jnp.sum(grad_bn * normed, 0, keepdims=True)


def batch_rows(tokens, visual, stats, proj):
    return pl.pallas_call(
        batch_kernel,
        out_shape=[
            jax.ShapeDtypeStruct(visual.shape, F32),
            jax.ShapeDtypeStruct((2, visual.shape[1]), F32),
        ],
        compiler_params=pltpu.CompilerParams(vmem_limit_bytes=LIMIT),
        cost_estimate=cost(0, 6_000_000),
        name="batch_rows",
    )(tokens, visual, stats, proj)


def text_kernel(*refs):
    dq, dk, dv = refs[0:2], refs[2:4], refs[4:6]
    qkv_w_ref, attn_ref, text_ref = refs[6:]
    width = text_ref.shape[1]
    total = attn_ref[...]
    for n, (low, high) in enumerate((dq, dk, dv)):
        grads = jnp.concatenate([low[...], high[...]], 1)
        total = total + dot_nt(grads, qkv_w_ref[:, n * width : (n + 1) * width])
    text_ref[...] = total


def text_rows(back, qkv_w, attn, text_len):
    width = attn.shape[1]
    step = text_len // 2
    grads = [g for pair in back for g in pair]
    return pl.pallas_call(
        text_kernel,
        grid=(2,),
        in_specs=[pl.BlockSpec((step, g.shape[1]), lambda i: (i, 0)) for g in grads]
        + [whole(qkv_w.shape), pl.BlockSpec((step, width), lambda i: (i, 0))],
        out_specs=pl.BlockSpec((step, width), lambda i: (i, 0)),
        out_shape=jax.ShapeDtypeStruct((text_len, width), F32),
        compiler_params=pltpu.CompilerParams(vmem_limit_bytes=LIMIT),
        cost_estimate=cost(0, 25_000_000),
        name="text_rows",
    )(*grads, qkv_w, attn)


def lane_rows(values, width):
    lanes = values.shape[1]
    pieces = pl.cdiv(lanes, width)
    if pieces * width > lanes:
        values = jnp.concatenate([values, jnp.zeros((1, pieces * width - lanes), F32)], 1)
    return [values[:, n * width : (n + 1) * width] for n in range(pieces)]


def sums_kernel(half_levels, bn_ref, one_ref, two_ref, inner_ref, *refs):
    out_ref = refs[-1]
    width = out_ref.shape[1]
    rows = []
    for n in range(bn_ref.shape[0]):
        rows += lane_rows(bn_ref[n : n + 1, :], width)
    for ref in (one_ref, two_ref):
        rows += [ref[n : n + 1, :] for n in range(ref.shape[0])]
    inner = [inner_ref[n] for n in range(inner_ref.shape[0])]
    rows += lane_rows(jnp.concatenate(inner, 1), width)
    halves = sum(ref[...] for ref in refs[:-1])
    tables, lane = [], 0
    for n, size in enumerate(half_levels):
        for row in (32 * n, 32 * n + 16):
            tables.append(halves[row : row + 16, lane : lane + size])
        lane += size
    tables = jnp.concatenate(tables, 1)
    blank = jnp.zeros((tables.shape[0], 256 - tables.shape[1]), F32)
    tables = jnp.concatenate([tables, blank], 1)
    group = width // 256
    for n in range(0, 12, group):
        rows.append(jnp.concatenate([tables[h : h + 1] for h in range(n, n + group)], 1))
    rows += [jnp.zeros((1, width), F32)] * (out_ref.shape[0] - len(rows))
    out_ref[...] = jnp.concatenate(rows, 0)


def pack_sums(bn_sums, one, two, inner, tables, half_levels):
    width = one.shape[1]
    rows = 2 * pl.cdiv(bn_sums.shape[1], width) + 5 + inner.size // width + 12 * 256 // width
    return pl.pallas_call(
        functools.partial(sums_kernel, half_levels),
        out_shape=jax.ShapeDtypeStruct((pl.cdiv(rows, 8) * 8, width), F32),
        cost_estimate=cost(0, 1_000_000),
        name="pack_sums",
    )(bn_sums, one, two, inner, *tables)


def finish_kernel(levels, count, *refs):
    left_ref, right_ref, grad_bn_ref, visual_ref, stats_ref, lines_ref = refs[:6]
    shift_ref, scale_ref, grad_ref, inner_ref = refs[6:10]
    vectors, tables = refs[10:15], refs[15:]
    total = left_ref[...] + right_ref[...]
    width = total.shape[1]
    channels = grad_bn_ref.shape[1]
    row = 0

    def take(lanes):
        nonlocal row
        pieces = pl.cdiv(lanes, width)
        row += pieces
        return jnp.concatenate([total[n : n + 1] for n in range(row - pieces, row)], 1)[:, :lanes]

    shift, scale = take(channels), take(channels)
    shift_ref[...] = shift.reshape(channels)
    scale_ref[...] = scale.reshape(channels)
    for ref in vectors:
        ref[...] = take(width).reshape(width)
    inner_ref[...] = take(inner_ref.shape[0]).reshape(inner_ref.shape[0])
    inverse = stats_ref[1:2, :]
    normed = (visual_ref[...].astype(F32) - stats_ref[0:1, :]) * inverse
    grad = grad_bn_ref[...] - shift * (1.0 / count) - normed * (scale * (1.0 / count))
    grad_ref[...] = lines_ref[0:1, :] * inverse * grad
    group = width // 256
    heads = []
    for n in range(12):
        lane = n % group * 256
        heads.append(total[row + n // group : row + n // group + 1, lane : lane + 256])
    heads = jnp.concatenate(heads, 0)
    begin = 0
    for ref, size in zip(tables, levels):
        ref[...] = heads[:, begin : begin + size]
        begin += size


def finish(left, right, grad_bn, visual, stats, lines, inner, levels, count):
    width = left.shape[1]
    channels = visual.shape[1]
    line = lambda n: jax.ShapeDtypeStruct((n,), F32)
    return pl.pallas_call(
        functools.partial(finish_kernel, levels, count),
        out_shape=[line(channels), line(channels), jax.ShapeDtypeStruct(visual.shape, F32)]
        + [line(inner)]
        + [line(width)] * 5
        + [jax.ShapeDtypeStruct((12, n), F32) for n in levels],
        cost_estimate=cost(0, 3_000_000),
        name="finish",
    )(left, right, grad_bn, visual, stats, lines)


def bias_kernel(rows_step, rel_ref, x_ref, y_ref, tab_ref, out_ref, unit_ref, level_ref):
    pairs = out_ref.shape[0]
    table = tab_ref[...]
    top = jnp.max(jnp.max(jnp.abs(table), 1, keepdims=True), 0, keepdims=True)
    top = jnp.maximum(top, 1e-30)
    unit_ref[...] = top * (2.0 / LEVELS)
    level = jnp.floor((table / top + 1.0) * (0.5 * LEVELS) + 0.5).astype(jnp.int32)
    level_ref[0] = level[:, :128]
    level_ref[1] = level[:, 128:]
    words = []
    for n in range(2):
        low = level_ref[n, pl.ds(0, pairs, stride=2), :]
        high = level_ref[n, pl.ds(1, pairs, stride=2), :]
        words.append(low + high * 65536)
    both = [jnp.broadcast_to(words[0][p : p + 1, :], (8, 128)) for p in range(pairs)]
    rel = [jnp.broadcast_to(words[1][p : p + 1, :], (8, 128)) for p in range(pairs)]

    def look(table, index):
        return jnp.take_along_axis(table, index, axis=1, mode="promise_in_bounds")

    for c in range(out_ref.shape[2] // 128):
        for r in range(rows_step // 8):
            rows, cols = pl.ds(r * 8, 8), pl.ds(c * 128, 128)
            rel_id = rel_ref[0, rows, cols] & 31
            x_id = x_ref[0, rows, cols] & 63
            y_id = (y_ref[0, rows, cols] & 63) + 64
            for p in range(pairs):
                out_ref[p, rows, cols] = (
                    look(rel[p], rel_id) + look(both[p], x_id) + look(both[p], y_id)
                )


def bias_words(rel, x, y, table, first, steps):
    step = 64
    rows = steps * step
    pairs = table.shape[0] // 2
    lanes = pl.cdiv(rel.shape[2], 128) * 128
    ids = pl.BlockSpec((1, step, lanes), lambda i: (0, i + first, 0))
    return pl.pallas_call(
        functools.partial(bias_kernel, step),
        grid=(steps,),
        in_specs=[ids, ids, ids, whole(table.shape)],
        out_specs=[pl.BlockSpec((pairs, step, lanes), lambda i: (0, i, 0)), whole((1, 1))],
        out_shape=[
            jax.ShapeDtypeStruct((pairs, rows, lanes), jnp.int32),
            jax.ShapeDtypeStruct((1, 1), F32),
        ],
        scratch_shapes=[pltpu.VMEM((2, table.shape[0], 128), jnp.int32)],
        compiler_params=pltpu.CompilerParams(vmem_limit_bytes=LIMIT),
        cost_estimate=cost(0, 6_000_000 * steps),
        name="bias_words",
    )(rel, x, y, table)


def lane_halves(rows):
    lane = lax.broadcasted_iota(jnp.int32, (rows, 128), 1)
    return lane < 64, lane >= 64


def attend_kernel(unit_ref, q_ref, k_ref, v_ref, row_ref, *refs):
    word_refs, (p_ref, o_ref, mask_ref) = refs[:-3], refs[-3:]

    @pl.when(pl.program_id(0) == 0)
    def _():
        row = row_ref[...].astype(F32)
        col = jnp.broadcast_to(row, (8, row.shape[1])).T[:, :1]
        mask_ref[...] = jnp.where(col == row, 0.0, NEG)

    unit = unit_ref[...]
    rows = q_ref.shape[0]
    halves = lane_halves(rows)
    q, k, v = q_ref[...], k_ref[...], v_ref[...]
    none = jnp.zeros_like(q)
    words = jnp.concatenate([ref[0][:, :rows] for ref in word_refs], 0)
    mask = mask_ref[...]
    mixed = jnp.zeros((rows, 128), F32)
    for h in range(2):
        scores = dot_nt(jnp.where(halves[h], q, none), k)
        word = (words & 0xFFFF) if h == 0 else lax.shift_right_logical(words, 16)
        scores = scores + word.astype(F32) * unit + mask
        expo = jnp.exp(scores - jnp.max(scores, -1, keepdims=True))
        probs = (expo * (1.0 / jnp.sum(expo, -1, keepdims=True))).astype(BF16)
        p_ref[h] = probs
        mixed = mixed + dot_nn(probs, jnp.where(halves[h], v, none))
    o_ref[...] = mixed.astype(BF16)


def attend(unit, qkv, words, segments):
    pairs = words[0].shape[0]
    rows = qkv.shape[0]
    col = [pl.BlockSpec((rows, 128), lambda p, n=n: (0, n * pairs + p)) for n in range(3)]
    flops = pairs * 4 * 2 * rows * rows * 128
    return pl.pallas_call(
        attend_kernel,
        grid=(pairs,),
        in_specs=[
            whole((1, 1)),
            col[0],
            col[1],
            col[2],
            whole((1, rows)),
        ]
        + [pl.BlockSpec((1,) + w.shape[1:], lambda p: (p, 0, 0)) for w in words],
        out_specs=[
            pl.BlockSpec((2, rows, rows), lambda p: (p, 0, 0)),
            pl.BlockSpec((rows, 128), lambda p: (0, p)),
        ],
        out_shape=[
            jax.ShapeDtypeStruct((2 * pairs, rows, rows), BF16),
            jax.ShapeDtypeStruct((rows, pairs * 128), BF16),
        ],
        scratch_shapes=[pltpu.VMEM((rows, rows), F32)],
        compiler_params=pltpu.CompilerParams(vmem_limit_bytes=LIMIT),
        cost_estimate=cost(flops, 40_000_000),
        name="attend",
    )(unit, qkv, qkv, qkv, segments, *words)


def attend_back_kernel(q_ref, k_ref, v_ref, g_ref, p_ref, ds_ref, dq_ref, dk_ref, dv_ref):
    rows = q_ref.shape[0]
    halves = lane_halves(rows)
    q, k, v, g = q_ref[...], k_ref[...], v_ref[...], g_ref[...]
    none = jnp.zeros_like(q)
    blank = jnp.zeros((rows, ds_ref.shape[2] - rows), BF16)
    dq = jnp.zeros((rows, 128), F32)
    dk, dv = dq, dq
    for h in range(2):
        low = p_ref[h]
        probs = low.astype(F32)
        weighted = probs * dot_nt(g, jnp.where(halves[h], v, none))
        ds = (weighted - probs * jnp.sum(weighted, -1, keepdims=True)).astype(BF16)
        ds_ref[h] = jnp.concatenate([ds, blank], 1)
        dq = dq + dot_nn(ds, jnp.where(halves[h], k, none))
        dv = dv + dot_tn(low, jnp.where(halves[h], g, none))
        dk = dk + dot_tn(ds, jnp.where(halves[h], q, none))
    dq_ref[...] = (dq * 0.125).astype(BF16)
    dk_ref[...] = dk.astype(BF16)
    dv_ref[...] = dv.astype(BF16)


def attend_back(qkv, grad, probs, first, pairs):
    every = probs.shape[0] // 2
    rows = qkv.shape[0]
    col = [pl.BlockSpec((rows, 128), lambda p, n=n: (0, n * every + p + first)) for n in range(3)]
    new = pl.BlockSpec((rows, 128), lambda p: (0, p))
    big = pl.BlockSpec((2, rows, rows), lambda p: (p + first, 0, 0))
    lanes = pl.cdiv(rows, 128) * 128
    out = jax.ShapeDtypeStruct((rows, pairs * 128), BF16)
    flops = pairs * 2 * 4 * 2 * rows * rows * 128
    return pl.pallas_call(
        attend_back_kernel,
        grid=(pairs,),
        in_specs=[col[0], col[1], col[2], col[0], big],
        out_specs=[pl.BlockSpec((2, rows, lanes), lambda p: (p, 0, 0)), new, new, new],
        out_shape=[jax.ShapeDtypeStruct((2 * pairs, rows, lanes), BF16), out, out, out],
        compiler_params=pltpu.CompilerParams(vmem_limit_bytes=LIMIT),
        cost_estimate=cost(flops, 8_000_000 * pairs),
        name="attend_back",
    )(qkv, qkv, qkv, grad, probs)


def table_kernel(first, levels, block_ref, count_ref, rel_ref, x_ref, y_ref, *refs):
    ds_refs, out_ref = refs[:-1], refs[-1]
    place = pl.program_id(0)
    step = rel_ref.shape[1]
    every = rel_ref.shape[2] // 128

    @pl.when(place == 0)
    def _():
        out_ref[...] = jnp.zeros_like(out_ref)

    heads = sum(ref.shape[0] for ref in ds_refs)

    def group(r, start, blocks):
        width = blocks * 128
        level = lax.broadcasted_iota(jnp.int32, (16, width), 0).astype(F32).astype(BF16)
        one = jnp.ones((16, width), BF16)
        none = jnp.zeros((16, width), BF16)

        def one_hot(ids, count):
            wide = jnp.broadcast_to(ids, (16, width)).astype(BF16)
            return [jnp.where(wide == level + BF16(16 * t), one, none) for t in range(count // 16)]

        def halves(values, top):
            chosen = jnp.broadcast_to(top, (16, width)).astype(BF16) == one
            return [jnp.where(chosen, none, values), jnp.where(chosen, values, none)]

        rows = pl.ds(pl.multiple_of(r * 16, 16), 16)
        lanes = pl.ds(pl.multiple_of(start * 128, 128), width)
        values = [ref[:, rows, lanes] for ref in ds_refs]
        values.append(jnp.zeros((16 - heads, 16, width), BF16))
        values = jnp.transpose(jnp.concatenate(values, 0), (1, 0, 2))
        total = out_ref[...]
        ids = [ref[0, rows, lanes].astype(F32) for ref in (x_ref, y_ref, rel_ref)]
        counts = (levels[1] // 2, levels[2] // 2, levels[0] // 2)
        tops = [(i >= count).astype(F32) for i, count in zip(ids, counts)]
        rest = [i - top * count for i, top, count in zip(ids, tops, counts)]
        for n in range(16):
            grads = values[n]
            hot, split = [], []
            for top, low, count in zip(tops, rest, counts):
                hot += one_hot(low[n : n + 1], count)
                split += halves(grads, top[n : n + 1])
            total = total + dot_nt(jnp.concatenate(split, 0), jnp.concatenate(hot, 0))
        out_ref[...] = total

    def body(r, _):
        index = (place + first) * (step // 16) + r
        start, count = block_ref[index], count_ref[index]
        for blocks in range(1, every + 1):

            @pl.when(count == blocks)
            def _(blocks=blocks):
                group(r, start, blocks)

        return 0

    lax.fori_loop(0, step // 16, body, 0)


def table_sums(ranges, rel, x, y, ds, levels, first, steps):
    step = 96
    lanes = ds[0].shape[2]
    ids = pl.BlockSpec((1, step, lanes), lambda i, *_: (0, i + first, 0))
    return pl.pallas_call(
        functools.partial(table_kernel, first, levels),
        grid_spec=pltpu.PrefetchScalarGridSpec(
            num_scalar_prefetch=2,
            grid=(steps,),
            in_specs=[ids, ids, ids]
            + [pl.BlockSpec((d.shape[0], step, lanes), lambda i, *_: (0, i + first, 0)) for d in ds],
            out_specs=whole((96, sum(levels) // 2)),
        ),
        out_shape=jax.ShapeDtypeStruct((96, sum(levels) // 2), F32),
        compiler_params=pltpu.CompilerParams(vmem_limit_bytes=LIMIT),
        cost_estimate=cost(0, 8_000_000 * steps),
        name="table_sums",
    )(*ranges, rel, x, y, *ds)


def document_blocks(segments, rows):
    length = segments.shape[0]
    first = segments[0:rows:16]
    last = segments[jnp.minimum(jnp.arange(15, rows, 16), length - 1)]
    begin = jnp.sum(segments[None, :] < first[:, None], 1, dtype=jnp.int32)
    end = jnp.sum(segments[None, :] <= last[:, None], 1, dtype=jnp.int32)
    return begin // 128, (end + 127) // 128 - begin // 128


def norm_stats(values):
    center = values - jnp.mean(values, -1, keepdims=True)
    scale = lax.rsqrt(jnp.mean(center * center, -1, keepdims=True) + EPS)
    return center * scale, scale


def norm_back(grad, normed, scale, gain):
    scaled = grad * gain
    return scale * (
        scaled
        - jnp.mean(scaled, -1, keepdims=True)
        - normed * jnp.mean(scaled * normed, -1, keepdims=True)
    )


def on_device(
    text_hidden,
    visual_maps,
    patch_order,
    segment_ids,
    rel_bucket,
    x_bucket,
    y_bucket,
    bn_scale,
    bn_shift,
    vis_proj,
    w_query,
    w_key,
    w_value,
    w_output,
    rel_table,
    x_table,
    y_table,
    first_gain,
    first_bias,
    w_inner,
    b_inner,
    w_outer,
    b_outer,
    second_gain,
    second_bias,
    cotangent,
):
    heads = rel_table.shape[1]
    pairs = heads // 2
    visual_len = patch_order.shape[1]
    length = segment_ids.shape[1]
    text_len = length - visual_len
    width = w_query.shape[1]
    dp, ffn = lax.axis_size("dp"), lax.axis_size("ffn")
    place = lax.axis_index("dp")
    devices = dp * ffn
    rows = pl.cdiv(length, 64) * 64
    count = visual_maps.shape[0] * devices
    levels = (rel_table.shape[0], x_table.shape[0], y_table.shape[0])

    inner_rows, columns = w_inner.shape
    outer_shard = w_outer.T
    steps = rows // 64

    first_set = Gather(*pack_first(w_query, w_key, w_value, vis_proj, visual_maps))
    plain = columns == width
    early = plain and dp == 8
    here = lax.axis_index("ffn")
    wide_shards = jnp.concatenate([outer_shard, w_inner], 0)
    if early:
        late_set = Gather(
            jnp.concatenate([w_output, wide_shards], 0), [w_output.shape[0]], 2 * inner_rows
        )
    elif plain:
        late_set = Gather(
            jnp.concatenate([w_output, wide_shards], 0), [w_output.shape[0], inner_rows, inner_rows]
        )
    else:
        late_set = Gather(w_output, [w_output.shape[0]])
        wide_set = Gather(wide_shards, [inner_rows, inner_rows])

    first_set.own, wide_shards = epoch(first_set.own, wide_shards)
    first_set.along_ffn()
    wides = [wide_shards]
    if early:
        wides += [send_dp(wide_shards, 2), send_dp(wide_shards, 4)]
    tables = jnp.concatenate([x_table, y_table, rel_table], 0).T
    tables = jnp.pad(tables, ((0, 0), (0, 256 - tables.shape[1])))
    cuts = [0, steps // 9, steps * 7 // 9, steps]
    words = [None] * 3
    words[0], unit = bias_words(rel_bucket, x_bucket, y_bucket, tables, 0, cuts[1])
    ranges = document_blocks(segment_ids[0], rows)
    lines = jnp.stack([first_gain, first_bias, b_outer, second_gain, second_bias])
    inner_b = b_inner.reshape(ffn, 1, columns)
    segments = jnp.pad(segment_ids, ((0, 0), (0, rows - length)), constant_values=-1)
    bn_lines = jnp.stack([bn_scale, bn_shift])
    order = [(here - k + ffn) % ffn if early else jnp.int32(k) for k in range(ffn)]
    place = jnp.stack([place] + order).astype(jnp.int32)
    state, late, place, wides, words[0], tables, ranges, lines, inner_b, segments, bn_lines = epoch(
        first_set.state(),
        late_set.state(),
        place,
        wides,
        words[0],
        tables,
        ranges,
        lines,
        inner_b,
        segments,
        bn_lines,
    )
    first_set.hold(state)
    late_set.hold(late)

    first_set.order()
    first_set.near(3 * w_query.shape[0] * ffn)
    late_set.along_ffn(1, ffn - 1)
    words[1], _ = bias_words(rel_bucket, x_bucket, y_bucket, tables, cuts[1], cuts[2] - cuts[1])
    state, late, words[1], tables = epoch(first_set.state(), late_set.state(), words[1], tables)
    first_set.hold(state)
    late_set.hold(late)

    first_set.diagonal()
    late_set.along_ffn(ffn - 1)
    state, late, tables = epoch(first_set.state(), late_set.state(), tables)
    first_set.hold(state)
    late_set.hold(late)

    late_set.order()
    first_set.across()
    state, late = epoch(first_set.state(), late_set.state())
    first_set.hold(state)
    late_set.hold(late)

    late_rows = w_output.shape[0] * ffn
    late_set.near(late_rows + (inner_rows if early else ffn * inner_rows) if plain else 0)
    if early:
        wides += [send_dp(wide, 1) for wide in wides[:2]]
    layout, row = [], 0
    for n, size in enumerate(first_set.rows):
        layout.append((row, size * ffn, max(n - 2, 0), 0, n * width if n < 3 else 0))
        row += size * ffn
    qkv_full, proj_full, hidden, lowered, qkv, bn_rows, bn_stats = first_rows(
        place,
        first_set.parts(),
        layout,
        text_hidden,
        visual_maps,
        patch_order,
        bn_lines,
        rows,
        vis_proj.shape[0] * devices,
        first_set.rows[-1],
    )
    qkv, tables = epoch(qkv, tables)
    words[2], _ = bias_words(rel_bucket, x_bucket, y_bucket, tables, cuts[2], cuts[3] - cuts[2])
    qkv, state, words[2], wides = epoch(qkv, late_set.state(), words[2], wides)
    late_set.hold(state)

    late_set.diagonal()
    if early:
        wides.append(send_dp(wides[1], 4))
    probs, mixed = attend(unit, qkv, words, segments)
    probs, mixed, state, wides = epoch(probs, mixed, late_set.state(), wides)
    late_set.hold(state)
    late_set.across()
    layout = [(0, late_rows, 0, 0, 0)]
    shift = late_rows
    parts = late_set.parts()
    if not plain:
        parts = [(block, bits, 0) for block, bits, _ in parts]
        wide_set.along_ffn()
        wide_set.order()
        wide_set.near(0)
        wide_set.diagonal()
        wide_set.across()
        shift = 0
    wide_layout = [
        (shift + (n * ffn + f) * inner_rows, inner_rows, 1 + n, f * width, 0)
        for n in range(2)
        for f in range(ffn)
    ]
    feeds = [(parts, layout + wide_layout if plain else layout)]
    if not plain:
        feeds.append((wide_set.parts(), wide_layout))
    if early:
        near_layout = [(n * inner_rows, inner_rows, 1 + n, 0, 0) for n in range(2)]
        far_layout = [
            (late_rows + (2 * k - 2 + n) * inner_rows, inner_rows, 1 + n, k * width, 0)
            for k in range(1, ffn)
            for n in range(2)
        ]
        own, from_x, from_y, other, other_x, from_xy = wides
        crossed = [send_dp(from_y, 1), send_dp(from_xy, 1)]
        blocks = [own, other, from_x, other_x, from_y, crossed[0], from_xy, crossed[1]]
        feeds = [
            (parts, layout + far_layout),
            ([(block, bits, 0) for bits, block in enumerate(blocks)], near_layout),
        ]
    (
        first_n,
        output_full,
        output,
        first_r,
        grad_first,
        sums_two,
        inner_sums,
        mine,
        away,
        last,
    ) = feed_forward(place, feeds, mixed, hidden, lines, inner_b, cotangent, inner_rows)

    def wide_far(value, index):
        return pick(value, (here - index + ffn) % ffn if early else index, 1)

    wide = Scatter(mine, away, wide_far)
    wide.ahead(last)
    state, grad_first = epoch(wide.held(), grad_first)
    wide.hold(state)
    wide.near()
    wide.core()
    grad_attn, attn_low, grad_mixed, sums_one = norm_rows(
        grad_first, first_n, first_r, lines, output_full
    )
    half = pairs // 3
    back_low = attend_back(qkv, grad_mixed, probs, 0, half)
    state, back_low, qkv = epoch(wide.held(), back_low, qkv)
    wide.hold(state)
    wide.prepare()
    wide.blocks, qkv = epoch(wide.blocks, qkv)

    wide.quads()
    back_high = attend_back(qkv, grad_mixed, probs, half, pairs - half)
    back = list(zip(back_low[1:], back_high[1:]))
    tokens_grad, mine, away, last = tail_rows(
        place, back, qkv_full, grad_attn, attn_low, mixed, lowered, patch_order, bn_rows, text_len
    )
    ds = (back_low[0], back_high[0])
    wide.blocks, mine, away, last, ds, tokens_grad = epoch(
        wide.blocks, mine, away, last, ds, tokens_grad
    )

    def tail_far(value, index):
        size = 4 * (width // dp)
        square = pick(value[:size].reshape(4, ffn, -1, width), index, 1)
        return jnp.concatenate(
            [square.reshape(-1, width), pick(value[size:].reshape(ffn, -1, width), index, 0)], 0
        )

    cuts = [0, rows // 96 // 3, rows // 96]
    sums = []

    def tables(ds):
        n = len(sums)
        return sums + [
            table_sums(
                ranges, rel_bucket, x_bucket, y_bucket, ds, levels, cuts[n], cuts[n + 1] - cuts[n]
            )
        ]

    tail = Scatter(mine, away, tail_far)
    tail.ahead(last)
    wide.join()
    state, wide.value, tokens_grad = epoch(tail.held(), wide.value, tokens_grad)
    tail.hold(state)
    tail.near()
    tail.core()
    wide.along_ffn([1])
    grad_bn, bn_sums = batch_rows(tokens_grad, visual_maps, bn_stats, proj_full)
    sums = tables(ds)
    state, bn_sums, ds, sums, wide.pieces = epoch(tail.held(), bn_sums, ds, sums, wide.pieces)
    tail.hold(state)
    tail.prepare()
    tail.blocks, ds = epoch(tail.blocks, ds)

    tail.quads()
    wide.along_ffn(range(2, ffn))
    sums = tables(ds)
    tail.blocks, sums, back, wide.pieces = epoch(tail.blocks, sums, back, wide.pieces)

    tail.join()
    tail.along_ffn([1])
    total = Sum(
        pack_sums(
            bn_sums,
            sums_one,
            sums_two,
            inner_sums,
            sums,
            (levels[1] // 2, levels[2] // 2, levels[0] // 2),
        )
    )
    for _ in range(ffn.bit_length() - 1):
        total.step()
    wide_sum = wide.total()
    state, total.values, back = epoch(tail.held(), total.values, back)
    tail.hold(state)
    tail.along_ffn(range(2, ffn))
    while len(total.steps) > 1:
        total.step()
    text_grad = text_rows(back, qkv_full, grad_attn, text_len)
    tail_sum = tail.total()
    other = total.steps[0](total.values)
    (
        shift_grad,
        scale_grad,
        visual_grad,
        inner_grad,
        gain_one,
        bias_one,
        gain_two,
        bias_two,
        outer_grad,
        x_grad,
        y_grad,
        rel_grad,
    ) = finish(
        total.values,
        other,
        grad_bn,
        visual_maps,
        bn_stats,
        bn_lines,
        b_inner.shape[0],
        (levels[1], levels[2], levels[0]),
        count,
    )
    shards, row = [], 0
    for size in [w_query.shape[0]] * 4 + [vis_proj.shape[0]]:
        shards.append(tail_sum[row : row + size])
        row += size
    return (
        output,
        text_grad,
        visual_grad,
        scale_grad.reshape(-1),
        shift_grad.reshape(-1),
        shards[4],
        shards[0],
        shards[1],
        shards[2],
        shards[3],
        rel_grad.T,
        x_grad.T,
        y_grad.T,
        gain_one.reshape(-1),
        bias_one.reshape(-1),
        wide_sum[0],
        inner_grad.reshape(-1),
        wide_sum[1].T,
        outer_grad.reshape(-1),
        gain_two.reshape(-1),
        bias_two.reshape(-1),
    )


def solution(mesh):
    rows = P(ALL, None)
    cube = P(ALL, None, None)
    return jax.shard_map(
        on_device,
        mesh=mesh,
        in_specs=(rows,) * 4
        + (cube,) * 3
        + (P(),) * 2
        + (rows,) * 5
        + (P(),) * 5
        + (P("dp", "ffn"), P(), P("ffn", "dp"))
        + (P(),) * 3
        + (rows,),
        out_specs=(rows,) * 3
        + (P(),) * 2
        + (rows,) * 5
        + (P(),) * 5
        + (P("dp", "ffn"), P(), P("ffn", "dp"))
        + (P(),) * 3,
        check_vma=False,
    )
```

```python
import functools

import jax
import jax.numpy as jnp
from jax import lax
from jax.experimental import pallas as pl
from jax.experimental.pallas import tpu as pltpu
from jax.sharding import PartitionSpec as P

EPS = 1e-05
NEG = -1e30
F32 = jnp.float32
BF16 = jnp.bfloat16
ALL = ("dp", "ffn")
LEVELS = 21845.0
MIB = 2**20


def dot_nn(a, b):
    return lax.dot_general(a, b, (((1,), (0,)), ((), ())), preferred_element_type=F32)


def dot_nt(a, b):
    return lax.dot_general(a, b, (((1,), (1,)), ((), ())), preferred_element_type=F32)


def dot_tn(a, b):
    return lax.dot_general(a, b, (((0,), (0,)), ((), ())), preferred_element_type=F32)


def pad_rows(values, rows):
    return jnp.pad(values, ((0, rows - values.shape[0]), (0, 0)))


def send_dp(values, bits):
    size = lax.axis_size("dp")
    return lax.ppermute(values, "dp", [(i, i ^ bits) for i in range(size)])


def send_ffn(values, shift):
    size = lax.axis_size("ffn")
    return lax.ppermute(values, "ffn", [(i, (i + shift) % size) for i in range(size)])


def swap_ffn(values, bits):
    size = lax.axis_size("ffn")
    return lax.ppermute(values, "ffn", [(i, i ^ bits) for i in range(size)])


def exchanges():
    steps = []
    for axis, send in (("ffn", swap_ffn), ("dp", send_dp)):
        bit = 1
        while bit < lax.axis_size(axis):
            steps.append(functools.partial(send, bits=bit))
            bit *= 2
    return steps


class Sum:
    def __init__(self, values):
        self.values = values
        self.steps = exchanges()

    def step(self):
        if self.steps:
            self.values = self.values + self.steps.pop(0)(self.values)

    def finish(self):
        while self.steps:
            self.step()
        return self.values


class Gather:
    def __init__(self, own, rows, rest=0):
        self.own = own
        self.rows = rows
        self.rest = rest

    def along_ffn(self, begin=1, end=None):
        size = lax.axis_size("ffn")
        self.far = self.far[:begin] if begin > 1 else [self.own]
        self.far += [send_ffn(self.own, k) for k in range(begin, end or size)]

    def order(self):
        size = lax.axis_size("ffn")
        here = lax.axis_index("ffn")
        if all(rows % 8 == 0 for rows in self.rows):
            self.block = order_blocks(here, self.far, self.rows, self.rest)
            return
        pieces = []
        for slot in range(size):
            value = self.far[0]
            for k in range(1, size):
                value = jnp.where((here - k + size) % size == slot, self.far[k], value)
            pieces.append(value)
        begin, ordered = 0, []
        for rows in self.rows:
            ordered += [value[begin : begin + rows] for value in pieces]
            begin += rows
        self.block = jnp.concatenate(ordered, 0)

    def near(self, cut):
        quads = lax.axis_size("dp") // 2
        self.cut = cut
        self.others = [send_dp(self.block, 1)]
        if quads == 4:
            self.mine = [self.block, send_dp(self.block, 2), send_dp(self.block, 4)]
        else:
            self.mine = [self.block] + [send_dp(self.block, 2 * k) for k in range(1, quads)]

    def diagonal(self):
        self.others += [send_dp(block, 1) for block in self.mine[1:]]
        if lax.axis_size("dp") == 8:
            low = send_dp(self.mine[1][: self.cut], 4)
            high = send_dp(self.mine[2][self.cut :], 2)
            self.mine.append((low, high))

    def across(self):
        if lax.axis_size("dp") == 8:
            self.others.append(tuple(send_dp(piece, 1) for piece in self.mine[3]))

    def state(self):
        return {k: v for k, v in vars(self).items() if k in ("own", "far", "block", "mine", "others")}

    def hold(self, state):
        vars(self).update(state)

    def parts(self):
        found = []
        for k, (mine, other) in enumerate(zip(self.mine, self.others)):
            for bits, block in ((2 * k, mine), (2 * k + 1, other)):
                if isinstance(block, tuple):
                    found += [(block[0], bits, 0), (block[1], bits, self.cut)]
                else:
                    found.append((block, bits, 0))
        return found


def epoch(*values):
    return lax.optimization_barrier(values)


def pick(values, index, axis):
    return lax.dynamic_index_in_dim(values, index, axis, keepdims=False)


def plus(a, b):
    return (a.astype(F32) + b.astype(F32)).astype(BF16)


class Scatter:
    def __init__(self, mine, away, far):
        self.value = mine
        self.away = away
        self.far = far

    def ahead(self, last):
        if self.away.shape[0] == 4:
            self.first = send_dp(last, 1)

    def core(self):
        self.got = send_dp(self.away, 1)

    def near(self):
        if self.away.shape[0] == 4:
            mine, got = self.value[3], self.first
            half = mine.shape[0] // 2
            self.low = send_dp(plus(mine[:half], got[:half]), 4)
            self.high = send_dp(plus(mine[half:], got[half:]), 2)

    def prepare(self):
        mine, got = self.value, self.got
        half = mine.shape[1] // 2
        self.blocks = []
        for k in range(1, mine.shape[0]):
            block = mine[k].astype(F32) + got[k].astype(F32)
            if mine.shape[0] == 4 and k == 1:
                block = jnp.concatenate([block[:half] + self.low.astype(F32), block[half:]], 0)
            if mine.shape[0] == 4 and k == 2:
                block = jnp.concatenate([block[:half], block[half:] + self.high.astype(F32)], 0)
            if mine.shape[0] == 4 and k == 3:
                continue
            self.blocks.append(block.astype(BF16))

    def quads(self):
        self.blocks = [send_dp(block, 2 * k) for k, block in enumerate(self.blocks, 1)]

    def join(self):
        own = self.value[0].astype(F32) + self.got[0].astype(F32)
        self.value = (own + sum(block.astype(F32) for block in self.blocks)).astype(BF16)

    def held(self):
        return {k: v for k, v in vars(self).items() if k != "far"}

    def hold(self, state):
        vars(self).update(state)

    def along_ffn(self, shifts):
        size = lax.axis_size("ffn")
        here = lax.axis_index("ffn")
        if not hasattr(self, "pieces"):
            self.pieces = [self.far(self.value, here)]
        for k in shifts:
            self.pieces.append(send_ffn(self.far(self.value, (here + k) % size), k))

    def total(self):
        return sum(piece.astype(F32) for piece in self.pieces)


LIMIT = 56 * MIB


def whole(shape):
    return pl.BlockSpec(shape, lambda *_: (0,) * len(shape))


def cost(flops, nbytes):
    return pl.CostEstimate(flops=flops // 1000, bytes_accessed=nbytes // 1000, transcendentals=0)


def pack_kernel(q_ref, k_ref, v_ref, p_ref, visual_ref, out_ref):
    row = 0
    for ref in (q_ref, k_ref, v_ref, p_ref):
        out_ref[row : row + ref.shape[0], :] = ref[...]
        row += ref.shape[0]
    width = out_ref.shape[1]
    count = visual_ref.shape[0]
    visual = visual_ref[...].astype(F32)
    mean = jnp.sum(visual, 0, keepdims=True) * (1.0 / count)
    gap = visual - mean
    spread = jnp.sum(gap * gap, 0, keepdims=True)
    channels = visual_ref.shape[1]
    chunks = pl.cdiv(channels, width)
    blank = jnp.zeros((1, chunks * width - channels), F32)
    pieces = []
    for values, times in ((mean, 3), (spread, 2)):
        if chunks * width > channels:
            values = jnp.concatenate([values, blank], 1)
        for _ in range(times):
            piece = values.astype(BF16).astype(F32)
            values = values - piece
            pieces += [piece[:, n * width : (n + 1) * width] for n in range(chunks)]
    pieces += [jnp.zeros((1, width), F32)] * (out_ref.shape[0] - row - len(pieces))
    out_ref[row:, :] = jnp.concatenate(pieces, 0).astype(BF16)


def pack_first(w_query, w_key, w_value, vis_proj, visual):
    width = w_query.shape[1]
    moments = pl.cdiv(5 * pl.cdiv(visual.shape[1], width), 16) * 16
    rows = [w.shape[0] for w in (w_query, w_key, w_value, vis_proj)] + [moments]
    own = pl.pallas_call(
        pack_kernel,
        out_shape=jax.ShapeDtypeStruct((sum(rows), width), BF16),
        name="pack_first",
    )(w_query, w_key, w_value, vis_proj, visual)
    return own, rows


def order_kernel(rows, rest, here_ref, *refs):
    parts, out_ref = refs[:-1], refs[-1]
    size = len(parts)
    here = here_ref[0]
    for index in range(size):

        @pl.when(here == index)
        def _(index=index):
            begin = 0
            for count in rows:
                for k in range(size):
                    row = begin * size + (index - k) % size * count
                    out_ref[row : row + count, :] = parts[k][begin : begin + count, :]
                begin += count

    begin = sum(rows)
    for k in range(1, size if rest else 1):
        row = begin * size + (k - 1) * rest
        out_ref[row : row + rest, :] = parts[k][begin:, :]


def order_blocks(here, parts, rows, rest):
    width = parts[0].shape[1]
    count = len(parts)
    return pl.pallas_call(
        functools.partial(order_kernel, rows, rest),
        in_specs=[pl.BlockSpec(memory_space=pltpu.SMEM)]
        + [pl.BlockSpec(memory_space=pltpu.VMEM)] * len(parts),
        out_specs=pl.BlockSpec(memory_space=pltpu.VMEM),
        out_shape=jax.ShapeDtypeStruct((count * sum(rows) + (count - 1) * rest, width), BF16),
        compiler_params=pltpu.CompilerParams(vmem_limit_bytes=LIMIT),
        name="order_blocks",
    )(here.reshape(1).astype(jnp.int32), *parts)


def place_entries(parts, layout):
    entries = []
    for n, (block, _, first) in enumerate(parts):
        for begin, rows, out, base, lane in layout:
            if first <= begin and begin + rows <= first + block.shape[0]:
                entries.append((n, begin - first, rows, out, base, lane))
    return entries


def place_bits(parts):
    return [bits for _, bits, _ in parts]


def part_copies(entries, bits, place, parts, outs, sems):
    copies = []
    for n, (part, begin, rows, out, base, lane) in enumerate(entries):
        target = pl.multiple_of(base + (place ^ bits[part]) * rows, 16)
        width = parts[part].shape[1]
        copies.append(
            pltpu.make_async_copy(
                parts[part].at[pl.ds(begin, rows), :],
                outs[out].at[pl.ds(target, rows), pl.ds(lane, width)],
                sems.at[n],
            )
        )
    return copies


def picked(order, size):
    row = lax.broadcasted_iota(jnp.int32, (size, size), 0)
    return (order == row).astype(F32)


def exact(a, b, dims):
    return lax.dot_general(
        a, b, (dims, ((), ())), precision=lax.Precision.HIGHEST, preferred_element_type=F32
    )


def first_kernel(entries, bits, devices, place_ref, *refs):
    parts, refs = refs[: len(bits)], refs[len(bits) :]
    text_ref, visual_ref, order_ref, lines_ref = refs[:4]
    qkv_w_ref, proj_ref, hidden_ref, turned_ref, qkv_ref, bn_ref, stats_ref = refs[4:11]
    moments_ref, low_ref, sems = refs[11:]
    outs = (qkv_w_ref, proj_ref, moments_ref)
    copies = part_copies(entries, bits, place_ref[0], parts, outs, sems)
    for copy in copies:
        copy.start()
    copies = [(entry[3], copy) for entry, copy in zip(entries, copies)]
    text_len, width = text_ref.shape
    visual_len, channels = visual_ref.shape
    hidden_ref[:text_len, :] = text_ref[...].astype(F32)
    low_ref[:text_len, :] = text_ref[...]
    for out, copy in copies:
        if out == 2:
            copy.wait()
    chunks = pl.cdiv(channels, width)
    moments = moments_ref[...].astype(F32).reshape(devices, -1, width)
    means = sum(moments[:, n * chunks : (n + 1) * chunks] for n in range(3))
    spreads = sum(moments[:, n * chunks : (n + 1) * chunks] for n in range(3, 5))
    average = jnp.sum(means, 0) * (1.0 / devices)
    gap = means - average[None]
    rows = visual_len * devices
    spread = (jnp.sum(spreads, 0) + visual_len * jnp.sum(gap * gap, 0)) * (1.0 / rows)
    inverse = lax.rsqrt(spread + EPS)

    def flat(values):
        pieces = [values[n : n + 1, :] for n in range(chunks)]
        return jnp.concatenate(pieces, 1)[:, :channels]

    average, inverse = flat(average), flat(inverse)
    stats_ref[0:1, :] = average
    stats_ref[1:2, :] = inverse
    normed = (visual_ref[...].astype(F32) - average) * inverse
    bn_rows = (normed * lines_ref[0:1, :] + lines_ref[1:2, :]).astype(BF16)
    bn_ref[...] = bn_rows
    for out, copy in copies:
        if out == 1:
            copy.wait()
    tokens = dot_nn(bn_rows, proj_ref[...])
    tokens = exact(picked(order_ref[...], visual_len), tokens, ((0,), (0,)))
    blank = jnp.zeros((hidden_ref.shape[0] - text_len - visual_len, width), F32)
    tokens = jnp.concatenate([tokens, blank], 0)
    hidden_ref[text_len:, :] = tokens
    low_ref[text_len:, :] = tokens.astype(BF16)
    for out, copy in copies:
        if out == 0:
            copy.wait()
    low = low_ref[...]
    turned_ref[...] = low.T
    for n in range(3):
        lanes = slice(n * width, (n + 1) * width)
        values = dot_nn(low, qkv_w_ref[:, lanes])
        qkv_ref[:, lanes] = (values * 0.125 if n == 0 else values).astype(BF16)


def first_rows(place, parts, layout, text, visual, order, lines, rows, proj_rows, moment_rows):
    devices = lax.axis_size("dp") * lax.axis_size("ffn")
    width = text.shape[1]
    channels = visual.shape[1]
    entries = place_entries(parts, layout)
    vmem = pl.BlockSpec(memory_space=pltpu.VMEM)
    shapes = [
        ((width, 3 * width), BF16),
        ((proj_rows, width), BF16),
        ((rows, width), F32),
        ((width, rows), BF16),
        ((rows, 3 * width), BF16),
        ((visual.shape[0], channels), BF16),
        ((2, channels), F32),
    ]
    return pl.pallas_call(
        functools.partial(first_kernel, entries, place_bits(parts), devices),
        in_specs=[pl.BlockSpec(memory_space=pltpu.SMEM)]
        + [pl.BlockSpec(memory_space=pl.ANY)] * len(parts)
        + [vmem] * 4,
        out_specs=[vmem] * len(shapes),
        out_shape=[jax.ShapeDtypeStruct(*shape) for shape in shapes],
        scratch_shapes=[
            pltpu.VMEM((moment_rows * devices, width), BF16),
            pltpu.VMEM((rows, width), BF16),
            pltpu.SemaphoreType.DMA((len(entries),)),
        ],
        compiler_params=pltpu.CompilerParams(vmem_limit_bytes=LIMIT),
        cost_estimate=cost(0, 25_000_000),
        name="first_rows",
    )(
        place,
        *[block for block, _, _ in parts],
        text,
        visual,
        order,
        lines,
    )


def store_blocks(mine_ref, away_ref, place, store):
    quads = mine_ref.shape[0]
    core, quad = place % 2, place // 2
    for bit in range(2):

        @pl.when(core == bit)
        def _(bit=bit):
            for dp in range(2 * quads):
                ref = mine_ref if dp % 2 == bit else away_ref
                store(ref, (dp // 2) ^ quad, dp)


def feed_kernel(entries, bits, length, ffn, place_ref, *refs):
    parts, refs = refs[: len(bits)], refs[len(bits) :]
    inputs, (lines_ref, inner_b_ref), refs = refs[:3], refs[3:5], refs[5:]
    results, (scale_ref, total_ref, sums_ref, inner_sums_ref), refs = refs[:3], refs[3:7], refs[7:]
    mine_ref, away_ref, last_ref = refs[:3]
    outer_w_ref, inner_w_ref, act_ref, slope_ref, first_ref, low_ref = refs[3:9]
    first_turned, low_turned = refs[9:11]
    mixed_ref, hidden_ref, ct_ref, normed_ref, out_w_ref, output_ref = refs[11:17]
    sems, in_sems, out_sems = refs[17:]
    step = pl.program_id(0)
    width = hidden_ref.shape[1]
    outs = (out_w_ref, outer_w_ref, inner_w_ref)
    fetch = [
        pltpu.make_async_copy(source, target, in_sems.at[n])
        for n, (source, target) in enumerate(zip(inputs, (mixed_ref, hidden_ref, ct_ref)))
    ]
    leave = [
        pltpu.make_async_copy(source, target, out_sems.at[n])
        for n, (source, target) in enumerate(zip((normed_ref, out_w_ref, output_ref), results))
    ]
    gain1, bias1, outer_b, gain2, bias2 = [lines_ref[n : n + 1, :] for n in range(5)]

    @pl.when(step == 0)
    def _():
        copies = part_copies(entries, bits, place_ref[0], parts, outs, sems)
        square = [copy for entry, copy in zip(entries, copies) if entry[3] == 0]
        now = [copy for entry, copy in zip(entries, copies) if entry[3] > 0 and entry[4] == 0]
        later = [copy for entry, copy in zip(entries, copies) if entry[3] > 0 and entry[4] > 0]
        for copy in [fetch[0]] + square + [fetch[1]] + now:
            copy.start()
        for copy in [fetch[0]] + square:
            copy.wait()
        for copy in later + [fetch[2], leave[1]]:
            copy.start()
        attended = dot_nn(mixed_ref[...], out_w_ref[...])
        fetch[1].wait()
        normed, scale = norm_stats(hidden_ref[...] + attended)
        first = normed * gain1 + bias1
        normed_ref[...] = normed
        scale_ref[...] = scale
        low = first.astype(BF16)
        first_ref[...] = low
        total_ref[...] = first + outer_b
        first_turned[...] = low.T
        leave[0].start()

    for index in range(ffn):

        @pl.when(step == index)
        def _(index=index):
            copies = part_copies(entries, bits, place_ref[0], parts, outs, sems)
            for entry, copy in zip(entries, copies):
                if entry[3] > 0 and entry[4] == index * width:
                    copy.wait()

    @pl.when(step < ffn)
    def _():
        rows = pl.ds(pl.multiple_of(step * width, width), width)
        inner = dot_nn(first_ref[...], inner_w_ref[rows, :]) + inner_b_ref[place_ref[1 + step]]
        root = 0.7978845608028654
        square = inner * inner
        half = 0.5 + 0.5 * jnp.tanh(inner * (root + (0.044715 * root) * square))
        act = inner * half
        slope = half + act * (1.0 - half) * (2 * root + (6 * 0.044715 * root) * square)
        slope_ref[step] = slope.astype(BF16)
        act = act.astype(BF16)
        act_ref[step] = act
        total_ref[...] += dot_nt(act, outer_w_ref[rows, :])

    @pl.when(step == ffn - 1)
    def _():
        fetch[2].wait()
        normed, scale = norm_stats(total_ref[...])
        output_ref[...] = (normed * gain2 + bias2).astype(BF16)[:length]
        leave[2].start()
        row = lax.broadcasted_iota(jnp.int32, (normed.shape[0], 1), 0)
        blank = jnp.zeros((normed.shape[0] - length, width), BF16)
        ct = jnp.concatenate([ct_ref[...], blank], 0).astype(F32)
        grad = norm_back(ct, normed, scale, gain2)
        total_ref[...] = grad
        low = grad.astype(BF16)
        low_ref[...] = low
        low_turned[...] = low.T
        sums_ref[0:1, :] = jnp.sum(ct * normed, 0, keepdims=True)
        sums_ref[1:2, :] = jnp.sum(ct, 0, keepdims=True)
        sums_ref[2:3, :] = jnp.sum(grad, 0, keepdims=True)

    @pl.when(step >= ffn)
    def _():
        f = step - ffn
        rows = pl.ds(pl.multiple_of(f * width, width), width)
        grad = dot_nn(low_ref[...], outer_w_ref[rows, :]) * slope_ref[f].astype(F32)
        inner_sums_ref[place_ref[1 + f]] = jnp.sum(grad, 0, keepdims=True)
        grad = grad.astype(BF16)
        total_ref[...] += dot_nt(grad, inner_w_ref[rows, :])
        inner = dot_nn(first_turned[...], grad).astype(BF16)
        outer = dot_nn(low_turned[...], act_ref[f]).astype(BF16)
        size = mine_ref.shape[3]

        def store(ref, slot, dp):
            ref[slot, 0, 0] = inner[dp * size : (dp + 1) * size]
            ref[slot, 1, 0] = outer[dp * size : (dp + 1) * size]
            if ref is away_ref:

                @pl.when(slot == away_ref.shape[0] - 1)
                def _():
                    last_ref[0, 0] = inner[dp * size : (dp + 1) * size]
                    last_ref[1, 0] = outer[dp * size : (dp + 1) * size]

        store_blocks(mine_ref, away_ref, place_ref[0], store)

    @pl.when(step == 2 * ffn - 1)
    def _():
        for copy in leave:
            copy.wait()


def feed_forward(place, feeds, mixed, hidden, lines, inner_b, ct, inner_rows):
    parts, entries = [], []
    for some, layout in feeds:
        for part, *entry in place_entries(some, layout):
            entries.append((part + len(parts), *entry))
        parts += some
    entries.sort(key=lambda entry: (entry[3] > 0, entry[4], -entry[3]))
    rows, width = hidden.shape
    ffn, _, columns = inner_b.shape
    quads = lax.axis_size("dp") // 2
    square = whole((rows, width))
    back = lambda i: jnp.maximum(i - ffn, 0)
    block = pl.BlockSpec((quads, 2, 1, inner_rows, columns), lambda i: (0, 0, back(i), 0, 0))
    blocks = jax.ShapeDtypeStruct((quads, 2, ffn, inner_rows, columns), BF16)
    last = pl.BlockSpec((2, 1, inner_rows, columns), lambda i: (0, back(i), 0, 0))
    smem = pl.BlockSpec(memory_space=pltpu.SMEM)
    shapes = [
        ((rows, width), F32),
        ((width, width), BF16),
        (ct.shape, BF16),
        ((rows, 1), F32),
        ((rows, width), F32),
        ((3, width), F32),
        ((ffn, 1, columns), F32),
    ]
    anywhere = pl.BlockSpec(memory_space=pl.ANY)
    return pl.pallas_call(
        functools.partial(feed_kernel, entries, place_bits(parts), ct.shape[0], ffn),
        grid=(2 * ffn,),
        in_specs=[smem]
        + [anywhere] * (len(parts) + 3)
        + [whole(lines.shape), whole(inner_b.shape)],
        out_specs=[anywhere] * 3
        + [whole((rows, 1)), square, whole((3, width))]
        + [whole((ffn, 1, columns)), block, block, last],
        out_shape=[jax.ShapeDtypeStruct(*shape) for shape in shapes]
        + [blocks, blocks, jax.ShapeDtypeStruct((2, ffn, inner_rows, columns), BF16)],
        scratch_shapes=[
            pltpu.VMEM((ffn * width, columns), BF16),
            pltpu.VMEM((ffn * width, columns), BF16),
            pltpu.VMEM((ffn, rows, columns), BF16),
            pltpu.VMEM((ffn, rows, columns), BF16),
            pltpu.VMEM((rows, width), BF16),
            pltpu.VMEM((rows, width), BF16),
            pltpu.VMEM((width, rows), BF16),
            pltpu.VMEM((width, rows), BF16),
            pltpu.VMEM((rows, width), BF16),
            pltpu.VMEM((rows, width), F32),
            pltpu.VMEM(ct.shape, BF16),
            pltpu.VMEM((rows, width), F32),
            pltpu.VMEM((width, width), BF16),
            pltpu.VMEM(ct.shape, BF16),
            pltpu.SemaphoreType.DMA((len(entries),)),
            pltpu.SemaphoreType.DMA((3,)),
            pltpu.SemaphoreType.DMA((3,)),
        ],
        compiler_params=pltpu.CompilerParams(vmem_limit_bytes=LIMIT),
        cost_estimate=cost(0, 100_000_000),
        name="feed_forward",
    )(
        place,
        *[part for part, _, _ in parts],
        mixed,
        hidden,
        ct,
        lines,
        inner_b,
    )


def norm_kernel(
    grad_ref, normed_ref, scale_ref, lines_ref, w_ref, out_ref, low_ref, mix_ref, sums_ref
):
    grad, normed = grad_ref[...], normed_ref[...]
    attn = norm_back(grad, normed, scale_ref[...], lines_ref[0:1, :])
    out_ref[...] = attn
    low = attn.astype(BF16)
    low_ref[...] = low
    mix_ref[...] = dot_nt(low, w_ref[...]).astype(BF16)
    sums_ref[0:1, :] = jnp.sum(grad * normed, 0, keepdims=True)
    sums_ref[1:2, :] = jnp.sum(grad, 0, keepdims=True)


def norm_rows(grad, normed, scale, lines, out_w):
    rows, width = grad.shape
    low = jax.ShapeDtypeStruct((rows, width), BF16)
    return pl.pallas_call(
        norm_kernel,
        out_shape=[
            jax.ShapeDtypeStruct((rows, width), F32),
            low,
            low,
            jax.ShapeDtypeStruct((2, width), F32),
        ],
        compiler_params=pltpu.CompilerParams(vmem_limit_bytes=LIMIT),
        cost_estimate=cost(0, 12_000_000),
        name="norm_rows",
    )(grad, normed, scale, lines, out_w)


def tail_kernel(text_len, place_ref, *refs):
    inputs, (order_ref, attn_ref, tokens_ref), refs = refs[:11], refs[11:14], refs[14:]
    outputs, buffers = refs[:3], refs[3:14]
    mine, away, in_sems, out_sems = refs[14:]
    low_ref, mixed_ref, attn_low_ref, qkv_w_ref, bn_ref = buffers[6:]
    names = (6, 0, 1, 2, 3, 4, 5, 7, 8, 9, 10)
    copies = {n: pltpu.make_async_copy(inputs[n], buffers[n], in_sems.at[n]) for n in names}
    for n in names:
        copies[n].start()
    visual_len = bn_ref.shape[0]
    width = attn_low_ref.shape[1]
    sent = []

    def spread(values, begin, n):
        values = values.astype(BF16)
        rows = values.shape[0] // (2 * mine.shape[0])

        def store(ref, slot, dp):
            ref[slot, begin : begin + rows, :] = values[dp * rows : (dp + 1) * rows]

        store_blocks(mine, away, place_ref[0], store)
        part = pl.ds(begin, rows)
        for k, ref in enumerate((mine, away)):
            copy = pltpu.make_async_copy(
                ref.at[:, part, :], outputs[k].at[:, part, :], out_sems.at[n, k]
            )
            copy.start()
            sent.append(copy)
        copy = pltpu.make_async_copy(
            away.at[away.shape[0] - 1, part, :], outputs[2].at[part, :], out_sems.at[n, 2]
        )
        copy.start()
        sent.append(copy)
        return begin + rows

    copies[6].wait()
    turned = low_ref[...]
    begin = 0
    grads = []
    for n in range(3):
        copies[2 * n].wait()
        copies[2 * n + 1].wait()
        grads.append(jnp.concatenate([buffers[2 * n][...], buffers[2 * n + 1][...]], 1))
        begin = spread(dot_nn(turned, grads[n]), begin, n)
    copies[7].wait()
    copies[8].wait()
    begin = spread(dot_nn(mixed_ref[...].T, attn_low_ref[...]), begin, 3)
    copies[9].wait()
    tokens = attn_ref[...]
    for n in range(3):
        lanes = slice(n * width, (n + 1) * width)
        tokens = tokens + dot_nt(grads[n][text_len:], qkv_w_ref[:, lanes])
    picker = picked(order_ref[...], visual_len)
    tokens = exact(picker, tokens[:visual_len], ((1,), (0,))).astype(BF16)
    tokens_ref[...] = tokens
    copies[10].wait()
    spread(dot_tn(bn_ref[...], tokens), begin, 4)
    for copy in sent:
        copy.wait()


def tail_rows(place, back, qkv_w, attn, attn_low, mixed, low, order, bn_rows, text_len):
    dp, ffn = lax.axis_size("dp"), lax.axis_size("ffn")
    rows, width = attn.shape
    visual_len, channels = bn_rows.shape
    size = 4 * (width // dp) + channels // dp
    vmem = pl.BlockSpec(memory_space=pltpu.VMEM)
    anywhere = pl.BlockSpec(memory_space=pl.ANY)
    inputs = [g for pair in back for g in pair] + [low, mixed, attn_low, qkv_w, bn_rows]
    rest = rows - text_len
    tail = pl.BlockSpec((rest, width), lambda *_: (text_len // rest, 0))
    blocks = jax.ShapeDtypeStruct((dp // 2, size, width), BF16)
    return pl.pallas_call(
        functools.partial(tail_kernel, text_len),
        grid=(1,),
        in_specs=[pl.BlockSpec(memory_space=pltpu.SMEM)]
        + [anywhere] * len(inputs)
        + [whole(order.shape), tail],
        out_specs=[whole((visual_len, width))] + [anywhere] * 3,
        out_shape=[jax.ShapeDtypeStruct((visual_len, width), BF16), blocks, blocks]
        + [jax.ShapeDtypeStruct((size, width), BF16)],
        scratch_shapes=[pltpu.VMEM(x.shape, BF16) for x in inputs]
        + [
            pltpu.VMEM(blocks.shape, BF16),
            pltpu.VMEM(blocks.shape, BF16),
            pltpu.SemaphoreType.DMA((len(inputs),)),
            pltpu.SemaphoreType.DMA((5, 3)),
        ],
        compiler_params=pltpu.CompilerParams(vmem_limit_bytes=LIMIT),
        cost_estimate=cost(0, 40_000_000),
        name="tail_rows",
    )(place, *inputs, order, attn)


def batch_kernel(tokens_ref, visual_ref, stats_ref, proj_ref, grad_bn_ref, sums_ref):
    grad_bn = dot_nt(proj_ref[...], tokens_ref[...]).T
    grad_bn_ref[...] = grad_bn
    normed = (visual_ref[...].astype(F32) - stats_ref[0:1, :]) * stats_ref[1:2, :]
    sums_ref[0:1, :] = jnp.sum(grad_bn, 0, keepdims=True)
    sums_ref[1:2, :] = jnp.sum(grad_bn * normed, 0, keepdims=True)


def batch_rows(tokens, visual, stats, proj):
    return pl.pallas_call(
        batch_kernel,
        out_shape=[
            jax.ShapeDtypeStruct(visual.shape, F32),
            jax.ShapeDtypeStruct((2, visual.shape[1]), F32),
        ],
        compiler_params=pltpu.CompilerParams(vmem_limit_bytes=LIMIT),
        cost_estimate=cost(0, 6_000_000),
        name="batch_rows",
    )(tokens, visual, stats, proj)


def text_kernel(*refs):
    dq, dk, dv = refs[0:2], refs[2:4], refs[4:6]
    qkv_w_ref, attn_ref, text_ref = refs[6:]
    width = text_ref.shape[1]
    total = attn_ref[...]
    for n, (low, high) in enumerate((dq, dk, dv)):
        grads = jnp.concatenate([low[...], high[...]], 1)
        total = total + dot_nt(grads, qkv_w_ref[:, n * width : (n + 1) * width])
    text_ref[...] = total


def text_rows(back, qkv_w, attn, text_len):
    width = attn.shape[1]
    step = text_len // 2
    grads = [g for pair in back for g in pair]
    return pl.pallas_call(
        text_kernel,
        grid=(2,),
        in_specs=[pl.BlockSpec((step, g.shape[1]), lambda i: (i, 0)) for g in grads]
        + [whole(qkv_w.shape), pl.BlockSpec((step, width), lambda i: (i, 0))],
        out_specs=pl.BlockSpec((step, width), lambda i: (i, 0)),
        out_shape=jax.ShapeDtypeStruct((text_len, width), F32),
        compiler_params=pltpu.CompilerParams(vmem_limit_bytes=LIMIT),
        cost_estimate=cost(0, 25_000_000),
        name="text_rows",
    )(*grads, qkv_w, attn)


def lane_rows(values, width):
    lanes = values.shape[1]
    pieces = pl.cdiv(lanes, width)
    if pieces * width > lanes:
        values = jnp.concatenate([values, jnp.zeros((1, pieces * width - lanes), F32)], 1)
    return [values[:, n * width : (n + 1) * width] for n in range(pieces)]


def sums_kernel(half_levels, bn_ref, one_ref, two_ref, inner_ref, *refs):
    out_ref = refs[-1]
    width = out_ref.shape[1]
    rows = []
    for n in range(bn_ref.shape[0]):
        rows += lane_rows(bn_ref[n : n + 1, :], width)
    for ref in (one_ref, two_ref):
        rows += [ref[n : n + 1, :] for n in range(ref.shape[0])]
    inner = [inner_ref[n] for n in range(inner_ref.shape[0])]
    rows += lane_rows(jnp.concatenate(inner, 1), width)
    halves = sum(ref[...] for ref in refs[:-1])
    tables, lane = [], 0
    for n, size in enumerate(half_levels):
        for row in (32 * n, 32 * n + 16):
            tables.append(halves[row : row + 16, lane : lane + size])
        lane += size
    tables = jnp.concatenate(tables, 1)
    blank = jnp.zeros((tables.shape[0], 256 - tables.shape[1]), F32)
    tables = jnp.concatenate([tables, blank], 1)
    group = width // 256
    for n in range(0, 12, group):
        rows.append(jnp.concatenate([tables[h : h + 1] for h in range(n, n + group)], 1))
    rows += [jnp.zeros((1, width), F32)] * (out_ref.shape[0] - len(rows))
    out_ref[...] = jnp.concatenate(rows, 0)


def pack_sums(bn_sums, one, two, inner, tables, half_levels):
    width = one.shape[1]
    rows = 2 * pl.cdiv(bn_sums.shape[1], width) + 5 + inner.size // width + 12 * 256 // width
    return pl.pallas_call(
        functools.partial(sums_kernel, half_levels),
        out_shape=jax.ShapeDtypeStruct((pl.cdiv(rows, 8) * 8, width), F32),
        cost_estimate=cost(0, 1_000_000),
        name="pack_sums",
    )(bn_sums, one, two, inner, *tables)


def finish_kernel(levels, count, *refs):
    left_ref, right_ref, grad_bn_ref, visual_ref, stats_ref, lines_ref = refs[:6]
    shift_ref, scale_ref, grad_ref, inner_ref = refs[6:10]
    vectors, tables = refs[10:15], refs[15:]
    total = left_ref[...] + right_ref[...]
    width = total.shape[1]
    channels = grad_bn_ref.shape[1]
    row = 0

    def take(lanes):
        nonlocal row
        pieces = pl.cdiv(lanes, width)
        row += pieces
        return jnp.concatenate([total[n : n + 1] for n in range(row - pieces, row)], 1)[:, :lanes]

    shift, scale = take(channels), take(channels)
    shift_ref[...] = shift.reshape(channels)
    scale_ref[...] = scale.reshape(channels)
    for ref in vectors:
        ref[...] = take(width).reshape(width)
    inner_ref[...] = take(inner_ref.shape[0]).reshape(inner_ref.shape[0])
    inverse = stats_ref[1:2, :]
    normed = (visual_ref[...].astype(F32) - stats_ref[0:1, :]) * inverse
    grad = grad_bn_ref[...] - shift * (1.0 / count) - normed * (scale * (1.0 / count))
    grad_ref[...] = lines_ref[0:1, :] * inverse * grad
    group = width // 256
    heads = []
    for n in range(12):
        lane = n % group * 256
        heads.append(total[row + n // group : row + n // group + 1, lane : lane + 256])
    heads = jnp.concatenate(heads, 0)
    begin = 0
    for ref, size in zip(tables, levels):
        ref[...] = heads[:, begin : begin + size]
        begin += size


def finish(left, right, grad_bn, visual, stats, lines, inner, levels, count):
    width = left.shape[1]
    channels = visual.shape[1]
    line = lambda n: jax.ShapeDtypeStruct((n,), F32)
    return pl.pallas_call(
        functools.partial(finish_kernel, levels, count),
        out_shape=[line(channels), line(channels), jax.ShapeDtypeStruct(visual.shape, F32)]
        + [line(inner)]
        + [line(width)] * 5
        + [jax.ShapeDtypeStruct((12, n), F32) for n in levels],
        cost_estimate=cost(0, 3_000_000),
        name="finish",
    )(left, right, grad_bn, visual, stats, lines)


def bias_kernel(rows_step, rel_ref, x_ref, y_ref, tab_ref, out_ref, unit_ref, level_ref):
    pairs = out_ref.shape[0]
    table = tab_ref[...]
    top = jnp.max(jnp.max(jnp.abs(table), 1, keepdims=True), 0, keepdims=True)
    top = jnp.maximum(top, 1e-30)
    unit_ref[...] = top * (2.0 / LEVELS)
    level = jnp.floor((table / top + 1.0) * (0.5 * LEVELS) + 0.5).astype(jnp.int32)
    level_ref[0] = level[:, :128]
    level_ref[1] = level[:, 128:]
    words = []
    for n in range(2):
        low = level_ref[n, pl.ds(0, pairs, stride=2), :]
        high = level_ref[n, pl.ds(1, pairs, stride=2), :]
        words.append(low + high * 65536)
    both = [jnp.broadcast_to(words[0][p : p + 1, :], (8, 128)) for p in range(pairs)]
    rel = [jnp.broadcast_to(words[1][p : p + 1, :], (8, 128)) for p in range(pairs)]

    def look(table, index):
        return jnp.take_along_axis(table, index, axis=1, mode="promise_in_bounds")

    for c in range(out_ref.shape[2] // 128):
        for r in range(rows_step // 8):
            rows, cols = pl.ds(r * 8, 8), pl.ds(c * 128, 128)
            rel_id = rel_ref[0, rows, cols] & 31
            x_id = x_ref[0, rows, cols] & 63
            y_id = (y_ref[0, rows, cols] & 63) + 64
            for p in range(pairs):
                out_ref[p, rows, cols] = (
                    look(rel[p], rel_id) + look(both[p], x_id) + look(both[p], y_id)
                )


def bias_words(rel, x, y, table, first, steps):
    step = 64
    rows = steps * step
    pairs = table.shape[0] // 2
    lanes = pl.cdiv(rel.shape[2], 128) * 128
    ids = pl.BlockSpec((1, step, lanes), lambda i: (0, i + first, 0))
    return pl.pallas_call(
        functools.partial(bias_kernel, step),
        grid=(steps,),
        in_specs=[ids, ids, ids, whole(table.shape)],
        out_specs=[pl.BlockSpec((pairs, step, lanes), lambda i: (0, i, 0)), whole((1, 1))],
        out_shape=[
            jax.ShapeDtypeStruct((pairs, rows, lanes), jnp.int32),
            jax.ShapeDtypeStruct((1, 1), F32),
        ],
        scratch_shapes=[pltpu.VMEM((2, table.shape[0], 128), jnp.int32)],
        compiler_params=pltpu.CompilerParams(vmem_limit_bytes=LIMIT),
        cost_estimate=cost(0, 6_000_000 * steps),
        name="bias_words",
    )(rel, x, y, table)


def lane_halves(rows):
    lane = lax.broadcasted_iota(jnp.int32, (rows, 128), 1)
    return lane < 64, lane >= 64


def attend_kernel(unit_ref, q_ref, k_ref, v_ref, row_ref, *refs):
    word_refs, (p_ref, o_ref, mask_ref) = refs[:-3], refs[-3:]

    @pl.when(pl.program_id(0) == 0)
    def _():
        row = row_ref[...].astype(F32)
        col = jnp.broadcast_to(row, (8, row.shape[1])).T[:, :1]
        mask_ref[...] = jnp.where(col == row, 0.0, NEG)

    unit = unit_ref[...]
    rows = q_ref.shape[0]
    halves = lane_halves(rows)
    q, k, v = q_ref[...], k_ref[...], v_ref[...]
    none = jnp.zeros_like(q)
    words = jnp.concatenate([ref[0][:, :rows] for ref in word_refs], 0)
    mask = mask_ref[...]
    mixed = jnp.zeros((rows, 128), F32)
    for h in range(2):
        scores = dot_nt(jnp.where(halves[h], q, none), k)
        word = (words & 0xFFFF) if h == 0 else lax.shift_right_logical(words, 16)
        scores = scores + word.astype(F32) * unit + mask
        expo = jnp.exp(scores - jnp.max(scores, -1, keepdims=True))
        probs = (expo * (1.0 / jnp.sum(expo, -1, keepdims=True))).astype(BF16)
        p_ref[h] = probs
        mixed = mixed + dot_nn(probs, jnp.where(halves[h], v, none))
    o_ref[...] = mixed.astype(BF16)


def attend(unit, qkv, words, segments):
    pairs = words[0].shape[0]
    rows = qkv.shape[0]
    col = [pl.BlockSpec((rows, 128), lambda p, n=n: (0, n * pairs + p)) for n in range(3)]
    flops = pairs * 4 * 2 * rows * rows * 128
    return pl.pallas_call(
        attend_kernel,
        grid=(pairs,),
        in_specs=[
            whole((1, 1)),
            col[0],
            col[1],
            col[2],
            whole((1, rows)),
        ]
        + [pl.BlockSpec((1,) + w.shape[1:], lambda p: (p, 0, 0)) for w in words],
        out_specs=[
            pl.BlockSpec((2, rows, rows), lambda p: (p, 0, 0)),
            pl.BlockSpec((rows, 128), lambda p: (0, p)),
        ],
        out_shape=[
            jax.ShapeDtypeStruct((2 * pairs, rows, rows), BF16),
            jax.ShapeDtypeStruct((rows, pairs * 128), BF16),
        ],
        scratch_shapes=[pltpu.VMEM((rows, rows), F32)],
        compiler_params=pltpu.CompilerParams(vmem_limit_bytes=LIMIT),
        cost_estimate=cost(flops, 40_000_000),
        name="attend",
    )(unit, qkv, qkv, qkv, segments, *words)


def attend_back_kernel(q_ref, k_ref, v_ref, g_ref, p_ref, ds_ref, dq_ref, dk_ref, dv_ref):
    rows = q_ref.shape[0]
    halves = lane_halves(rows)
    q, k, v, g = q_ref[...], k_ref[...], v_ref[...], g_ref[...]
    none = jnp.zeros_like(q)
    blank = jnp.zeros((rows, ds_ref.shape[2] - rows), BF16)
    dq = jnp.zeros((rows, 128), F32)
    dk, dv = dq, dq
    for h in range(2):
        low = p_ref[h]
        probs = low.astype(F32)
        weighted = probs * dot_nt(g, jnp.where(halves[h], v, none))
        ds = (weighted - probs * jnp.sum(weighted, -1, keepdims=True)).astype(BF16)
        ds_ref[h] = jnp.concatenate([ds, blank], 1)
        dq = dq + dot_nn(ds, jnp.where(halves[h], k, none))
        dv = dv + dot_tn(low, jnp.where(halves[h], g, none))
        dk = dk + dot_tn(ds, jnp.where(halves[h], q, none))
    dq_ref[...] = (dq * 0.125).astype(BF16)
    dk_ref[...] = dk.astype(BF16)
    dv_ref[...] = dv.astype(BF16)


def attend_back(qkv, grad, probs, first, pairs):
    every = probs.shape[0] // 2
    rows = qkv.shape[0]
    col = [pl.BlockSpec((rows, 128), lambda p, n=n: (0, n * every + p + first)) for n in range(3)]
    new = pl.BlockSpec((rows, 128), lambda p: (0, p))
    big = pl.BlockSpec((2, rows, rows), lambda p: (p + first, 0, 0))
    lanes = pl.cdiv(rows, 128) * 128
    out = jax.ShapeDtypeStruct((rows, pairs * 128), BF16)
    flops = pairs * 2 * 4 * 2 * rows * rows * 128
    return pl.pallas_call(
        attend_back_kernel,
        grid=(pairs,),
        in_specs=[col[0], col[1], col[2], col[0], big],
        out_specs=[pl.BlockSpec((2, rows, lanes), lambda p: (p, 0, 0)), new, new, new],
        out_shape=[jax.ShapeDtypeStruct((2 * pairs, rows, lanes), BF16), out, out, out],
        compiler_params=pltpu.CompilerParams(vmem_limit_bytes=LIMIT),
        cost_estimate=cost(flops, 8_000_000 * pairs),
        name="attend_back",
    )(qkv, qkv, qkv, grad, probs)


GROUP = 48


def table_kernel(first, levels, block_ref, count_ref, rel_ref, x_ref, y_ref, *refs):
    ds_refs, out_ref = refs[:-1], refs[-1]
    place = pl.program_id(0)
    step = rel_ref.shape[1]
    every = rel_ref.shape[2] // 128
    heads = sum(ref.shape[0] for ref in ds_refs)
    counts = (levels[1] // 2, levels[2] // 2, levels[0] // 2)

    @pl.when(place == 0)
    def _():
        out_ref[...] = jnp.zeros_like(out_ref)

    def group(r, start, blocks):
        width = blocks * 128
        level = lax.broadcasted_iota(jnp.int32, (16, width), 0).astype(F32).astype(BF16)
        one = jnp.ones((16, width), BF16)
        none = jnp.zeros((16, width), BF16)

        def one_hot(ids, count):
            wide = jnp.broadcast_to(ids, (16, width)).astype(BF16)
            return [jnp.where(wide == level + BF16(16 * t), one, none) for t in range(count // 16)]

        def halves(values, top):
            chosen = jnp.broadcast_to(top, (16, width)).astype(BF16) == one
            return [jnp.where(chosen, none, values), jnp.where(chosen, values, none)]

        rows = pl.ds(pl.multiple_of(r * GROUP, GROUP), GROUP)
        lanes = pl.ds(pl.multiple_of(start * 128, 128), width)
        values = [ref[:, rows, lanes] for ref in ds_refs]
        values.append(jnp.zeros((16 - heads, GROUP, width), BF16))
        values = jnp.transpose(jnp.concatenate(values, 0), (1, 0, 2))
        ids = [ref[0, rows, lanes].astype(F32) for ref in (x_ref, y_ref, rel_ref)]
        tops = [(i >= count).astype(F32) for i, count in zip(ids, counts)]
        rest = [i - top * count for i, top, count in zip(ids, tops, counts)]
        total = out_ref[...]
        for begin in range(0, GROUP, 2):
            lefts, rights = [], []
            for n in (begin, begin + 1):
                hot, split = [], []
                for top, low, count in zip(tops, rest, counts):
                    hot += one_hot(low[n : n + 1], count)
                    split += halves(values[n], top[n : n + 1])
                lefts.append(jnp.concatenate(split, 0))
                rights.append(jnp.concatenate(hot, 0))
            total = total + dot_nt(jnp.concatenate(lefts, 1), jnp.concatenate(rights, 1))
        out_ref[...] = total

    def body(r, _):
        index = (place + first) * (step // GROUP) + r
        count = jnp.maximum(count_ref[index], 2)
        start = jnp.minimum(block_ref[index], every - count)
        for blocks in range(2, every + 1):

            @pl.when(count == blocks)
            def _(blocks=blocks):
                group(r, start, blocks)

        return 0

    lax.fori_loop(0, step // GROUP, body, 0)


def table_sums(ranges, rel, x, y, ds, levels, first, steps):
    step = 2 * GROUP
    lanes = ds[0].shape[2]
    ids = pl.BlockSpec((1, step, lanes), lambda i, *_: (0, i + first, 0))
    return pl.pallas_call(
        functools.partial(table_kernel, first, levels),
        grid_spec=pltpu.PrefetchScalarGridSpec(
            num_scalar_prefetch=2,
            grid=(steps,),
            in_specs=[ids, ids, ids]
            + [pl.BlockSpec((d.shape[0], step, lanes), lambda i, *_: (0, i + first, 0)) for d in ds],
            out_specs=whole((96, sum(levels) // 2)),
        ),
        out_shape=jax.ShapeDtypeStruct((96, sum(levels) // 2), F32),
        compiler_params=pltpu.CompilerParams(vmem_limit_bytes=LIMIT),
        cost_estimate=cost(0, 8_000_000 * steps),
        name="table_sums",
    )(*ranges, rel, x, y, *ds)


def document_blocks(segments, rows):
    length = segments.shape[0]
    first = segments[0:rows:GROUP]
    last = segments[jnp.minimum(jnp.arange(GROUP - 1, rows, GROUP), length - 1)]
    begin = jnp.sum(segments[None, :] < first[:, None], 1, dtype=jnp.int32)
    end = jnp.sum(segments[None, :] <= last[:, None], 1, dtype=jnp.int32)
    return begin // 128, (end + 127) // 128 - begin // 128


def norm_stats(values):
    center = values - jnp.mean(values, -1, keepdims=True)
    scale = lax.rsqrt(jnp.mean(center * center, -1, keepdims=True) + EPS)
    return center * scale, scale


def norm_back(grad, normed, scale, gain):
    scaled = grad * gain
    return scale * (
        scaled
        - jnp.mean(scaled, -1, keepdims=True)
        - normed * jnp.mean(scaled * normed, -1, keepdims=True)
    )


def on_device(
    text_hidden,
    visual_maps,
    patch_order,
    segment_ids,
    rel_bucket,
    x_bucket,
    y_bucket,
    bn_scale,
    bn_shift,
    vis_proj,
    w_query,
    w_key,
    w_value,
    w_output,
    rel_table,
    x_table,
    y_table,
    first_gain,
    first_bias,
    w_inner,
    b_inner,
    w_outer,
    b_outer,
    second_gain,
    second_bias,
    cotangent,
):
    heads = rel_table.shape[1]
    pairs = heads // 2
    visual_len = patch_order.shape[1]
    length = segment_ids.shape[1]
    text_len = length - visual_len
    width = w_query.shape[1]
    dp, ffn = lax.axis_size("dp"), lax.axis_size("ffn")
    place = lax.axis_index("dp")
    devices = dp * ffn
    rows = pl.cdiv(length, 64) * 64
    count = visual_maps.shape[0] * devices
    levels = (rel_table.shape[0], x_table.shape[0], y_table.shape[0])

    inner_rows, columns = w_inner.shape
    outer_shard = w_outer.T
    steps = rows // 64

    first_set = Gather(*pack_first(w_query, w_key, w_value, vis_proj, visual_maps))
    plain = columns == width
    early = plain and dp == 8
    here = lax.axis_index("ffn")
    wide_shards = jnp.concatenate([outer_shard, w_inner], 0)
    if early:
        late_set = Gather(
            jnp.concatenate([w_output, wide_shards], 0), [w_output.shape[0]], 2 * inner_rows
        )
    elif plain:
        late_set = Gather(
            jnp.concatenate([w_output, wide_shards], 0), [w_output.shape[0], inner_rows, inner_rows]
        )
    else:
        late_set = Gather(w_output, [w_output.shape[0]])
        wide_set = Gather(wide_shards, [inner_rows, inner_rows])

    first_set.own, wide_shards = epoch(first_set.own, wide_shards)
    first_set.along_ffn()
    wides = [wide_shards]
    if early:
        wides += [send_dp(wide_shards, 2), send_dp(wide_shards, 4)]
    tables = jnp.concatenate([x_table, y_table, rel_table], 0).T
    tables = jnp.pad(tables, ((0, 0), (0, 256 - tables.shape[1])))
    cuts = [0, steps // 9, steps * 7 // 9, steps]
    words = [None] * 3
    words[0], unit = bias_words(rel_bucket, x_bucket, y_bucket, tables, 0, cuts[1])
    ranges = document_blocks(segment_ids[0], rows)
    lines = jnp.stack([first_gain, first_bias, b_outer, second_gain, second_bias])
    inner_b = b_inner.reshape(ffn, 1, columns)
    segments = jnp.pad(segment_ids, ((0, 0), (0, rows - length)), constant_values=-1)
    bn_lines = jnp.stack([bn_scale, bn_shift])
    order = [(here - k + ffn) % ffn if early else jnp.int32(k) for k in range(ffn)]
    place = jnp.stack([place] + order).astype(jnp.int32)
    state, late, place, wides, words[0], tables, ranges, lines, inner_b, segments, bn_lines = epoch(
        first_set.state(),
        late_set.state(),
        place,
        wides,
        words[0],
        tables,
        ranges,
        lines,
        inner_b,
        segments,
        bn_lines,
    )
    first_set.hold(state)
    late_set.hold(late)

    first_set.order()
    first_set.near(3 * w_query.shape[0] * ffn)
    late_set.along_ffn(1, ffn - 1)
    words[1], _ = bias_words(rel_bucket, x_bucket, y_bucket, tables, cuts[1], cuts[2] - cuts[1])
    state, late, words[1], tables = epoch(first_set.state(), late_set.state(), words[1], tables)
    first_set.hold(state)
    late_set.hold(late)

    first_set.diagonal()
    late_set.along_ffn(ffn - 1)
    state, late, tables = epoch(first_set.state(), late_set.state(), tables)
    first_set.hold(state)
    late_set.hold(late)

    late_set.order()
    first_set.across()
    state, late = epoch(first_set.state(), late_set.state())
    first_set.hold(state)
    late_set.hold(late)

    late_rows = w_output.shape[0] * ffn
    late_set.near(late_rows + (inner_rows if early else ffn * inner_rows) if plain else 0)
    if early:
        wides += [send_dp(wide, 1) for wide in wides[:2]]
    layout, row = [], 0
    for n, size in enumerate(first_set.rows):
        layout.append((row, size * ffn, max(n - 2, 0), 0, n * width if n < 3 else 0))
        row += size * ffn
    qkv_full, proj_full, hidden, lowered, qkv, bn_rows, bn_stats = first_rows(
        place,
        first_set.parts(),
        layout,
        text_hidden,
        visual_maps,
        patch_order,
        bn_lines,
        rows,
        vis_proj.shape[0] * devices,
        first_set.rows[-1],
    )
    qkv, tables = epoch(qkv, tables)
    words[2], _ = bias_words(rel_bucket, x_bucket, y_bucket, tables, cuts[2], cuts[3] - cuts[2])
    qkv, state, words[2], wides = epoch(qkv, late_set.state(), words[2], wides)
    late_set.hold(state)

    late_set.diagonal()
    if early:
        wides.append(send_dp(wides[1], 4))
    probs, mixed = attend(unit, qkv, words, segments)
    probs, mixed, state, wides = epoch(probs, mixed, late_set.state(), wides)
    late_set.hold(state)
    late_set.across()
    layout = [(0, late_rows, 0, 0, 0)]
    shift = late_rows
    parts = late_set.parts()
    if not plain:
        parts = [(block, bits, 0) for block, bits, _ in parts]
        wide_set.along_ffn()
        wide_set.order()
        wide_set.near(0)
        wide_set.diagonal()
        wide_set.across()
        shift = 0
    wide_layout = [
        (shift + (n * ffn + f) * inner_rows, inner_rows, 1 + n, f * width, 0)
        for n in range(2)
        for f in range(ffn)
    ]
    feeds = [(parts, layout + wide_layout if plain else layout)]
    if not plain:
        feeds.append((wide_set.parts(), wide_layout))
    if early:
        near_layout = [(n * inner_rows, inner_rows, 1 + n, 0, 0) for n in range(2)]
        far_layout = [
            (late_rows + (2 * k - 2 + n) * inner_rows, inner_rows, 1 + n, k * width, 0)
            for k in range(1, ffn)
            for n in range(2)
        ]
        own, from_x, from_y, other, other_x, from_xy = wides
        crossed = [send_dp(from_y, 1), send_dp(from_xy, 1)]
        blocks = [own, other, from_x, other_x, from_y, crossed[0], from_xy, crossed[1]]
        feeds = [
            (parts, layout + far_layout),
            ([(block, bits, 0) for bits, block in enumerate(blocks)], near_layout),
        ]
    (
        first_n,
        output_full,
        output,
        first_r,
        grad_first,
        sums_two,
        inner_sums,
        mine,
        away,
        last,
    ) = feed_forward(place, feeds, mixed, hidden, lines, inner_b, cotangent, inner_rows)

    def wide_far(value, index):
        return pick(value, (here - index + ffn) % ffn if early else index, 1)

    wide = Scatter(mine, away, wide_far)
    wide.ahead(last)
    state, grad_first = epoch(wide.held(), grad_first)
    wide.hold(state)
    wide.near()
    wide.core()
    grad_attn, attn_low, grad_mixed, sums_one = norm_rows(
        grad_first, first_n, first_r, lines, output_full
    )
    half = pairs // 3
    back_low = attend_back(qkv, grad_mixed, probs, 0, half)
    state, back_low, qkv = epoch(wide.held(), back_low, qkv)
    wide.hold(state)
    wide.prepare()
    wide.blocks, qkv = epoch(wide.blocks, qkv)

    wide.quads()
    back_high = attend_back(qkv, grad_mixed, probs, half, pairs - half)
    back = list(zip(back_low[1:], back_high[1:]))
    tokens_grad, mine, away, last = tail_rows(
        place, back, qkv_full, grad_attn, attn_low, mixed, lowered, patch_order, bn_rows, text_len
    )
    ds = (back_low[0], back_high[0])
    wide.blocks, mine, away, last, ds, tokens_grad = epoch(
        wide.blocks, mine, away, last, ds, tokens_grad
    )

    def tail_far(value, index):
        size = 4 * (width // dp)
        square = pick(value[:size].reshape(4, ffn, -1, width), index, 1)
        return jnp.concatenate(
            [square.reshape(-1, width), pick(value[size:].reshape(ffn, -1, width), index, 0)], 0
        )

    groups = rows // (2 * GROUP)
    cuts = [0, groups]
    sums = []

    def tables(ds):
        n = len(sums)
        return sums + [
            table_sums(
                ranges, rel_bucket, x_bucket, y_bucket, ds, levels, cuts[n], cuts[n + 1] - cuts[n]
            )
        ]

    tail = Scatter(mine, away, tail_far)
    tail.ahead(last)
    wide.join()
    state, wide.value, tokens_grad = epoch(tail.held(), wide.value, tokens_grad)
    tail.hold(state)
    tail.near()
    tail.core()
    wide.along_ffn([1])
    grad_bn, bn_sums = batch_rows(tokens_grad, visual_maps, bn_stats, proj_full)
    state, bn_sums, ds, wide.pieces = epoch(tail.held(), bn_sums, ds, wide.pieces)
    tail.hold(state)
    tail.prepare()
    tail.blocks, ds = epoch(tail.blocks, ds)

    tail.quads()
    wide.along_ffn(range(2, ffn))
    sums = tables(ds)
    tail.blocks, sums, back, wide.pieces = epoch(tail.blocks, sums, back, wide.pieces)

    tail.join()
    tail.along_ffn([1])
    total = Sum(
        pack_sums(
            bn_sums,
            sums_one,
            sums_two,
            inner_sums,
            sums,
            (levels[1] // 2, levels[2] // 2, levels[0] // 2),
        )
    )
    for _ in range(ffn.bit_length() - 1):
        total.step()
    wide_sum = wide.total()
    state, total.values, back = epoch(tail.held(), total.values, back)
    tail.hold(state)
    tail.along_ffn(range(2, ffn))
    while len(total.steps) > 1:
        total.step()
    text_grad = text_rows(back, qkv_full, grad_attn, text_len)
    tail_sum = tail.total()
    other = total.steps[0](total.values)
    (
        shift_grad,
        scale_grad,
        visual_grad,
        inner_grad,
        gain_one,
        bias_one,
        gain_two,
        bias_two,
        outer_grad,
        x_grad,
        y_grad,
        rel_grad,
    ) = finish(
        total.values,
        other,
        grad_bn,
        visual_maps,
        bn_stats,
        bn_lines,
        b_inner.shape[0],
        (levels[1], levels[2], levels[0]),
        count,
    )
    shards, row = [], 0
    for size in [w_query.shape[0]] * 4 + [vis_proj.shape[0]]:
        shards.append(tail_sum[row : row + size])
        row += size
    return (
        output,
        text_grad,
        visual_grad,
        scale_grad.reshape(-1),
        shift_grad.reshape(-1),
        shards[4],
        shards[0],
        shards[1],
        shards[2],
        shards[3],
        rel_grad.T,
        x_grad.T,
        y_grad.T,
        gain_one.reshape(-1),
        bias_one.reshape(-1),
        wide_sum[0],
        inner_grad.reshape(-1),
        wide_sum[1].T,
        outer_grad.reshape(-1),
        gain_two.reshape(-1),
        bias_two.reshape(-1),
    )


def solution(mesh):
    rows = P(ALL, None)
    cube = P(ALL, None, None)
    return jax.shard_map(
        on_device,
        mesh=mesh,
        in_specs=(rows,) * 4
        + (cube,) * 3
        + (P(),) * 2
        + (rows,) * 5
        + (P(),) * 5
        + (P("dp", "ffn"), P(), P("ffn", "dp"))
        + (P(),) * 3
        + (rows,),
        out_specs=(rows,) * 3
        + (P(),) * 2
        + (rows,) * 5
        + (P(),) * 5
        + (P("dp", "ffn"), P(), P("ffn", "dp"))
        + (P(),) * 3,
        check_vma=False,
    )
```

```python
import functools

import jax
import jax.numpy as jnp
from jax import lax
from jax.experimental import pallas as pl
from jax.experimental.pallas import tpu as pltpu
from jax.sharding import PartitionSpec as P

EPS = 1e-05
NEG = -1e30
F32 = jnp.float32
BF16 = jnp.bfloat16
ALL = ("dp", "ffn")
LEVELS = 21845.0
MIB = 2**20


def dot_nn(a, b):
    return lax.dot_general(a, b, (((1,), (0,)), ((), ())), preferred_element_type=F32)


def dot_nt(a, b):
    return lax.dot_general(a, b, (((1,), (1,)), ((), ())), preferred_element_type=F32)


def dot_tn(a, b):
    return lax.dot_general(a, b, (((0,), (0,)), ((), ())), preferred_element_type=F32)


def pad_rows(values, rows):
    return jnp.pad(values, ((0, rows - values.shape[0]), (0, 0)))


def send_dp(values, bits):
    size = lax.axis_size("dp")
    return lax.ppermute(values, "dp", [(i, i ^ bits) for i in range(size)])


def send_ffn(values, shift):
    size = lax.axis_size("ffn")
    return lax.ppermute(values, "ffn", [(i, (i + shift) % size) for i in range(size)])


def swap_ffn(values, bits):
    size = lax.axis_size("ffn")
    return lax.ppermute(values, "ffn", [(i, i ^ bits) for i in range(size)])


def exchanges():
    steps = []
    for axis, send in (("ffn", swap_ffn), ("dp", send_dp)):
        bit = 1
        while bit < lax.axis_size(axis):
            steps.append(functools.partial(send, bits=bit))
            bit *= 2
    return steps


class Sum:
    def __init__(self, values):
        self.values = values
        self.steps = exchanges()

    def step(self):
        if self.steps:
            self.values = self.values + self.steps.pop(0)(self.values)

    def finish(self):
        while self.steps:
            self.step()
        return self.values


class Gather:
    def __init__(self, own, rows, rest=0):
        self.own = own
        self.rows = rows
        self.rest = rest

    def along_ffn(self, begin=1, end=None):
        size = lax.axis_size("ffn")
        self.far = self.far[:begin] if begin > 1 else [self.own]
        self.far += [send_ffn(self.own, k) for k in range(begin, end or size)]

    def order(self):
        size = lax.axis_size("ffn")
        here = lax.axis_index("ffn")
        if all(rows % 8 == 0 for rows in self.rows):
            self.block = order_blocks(here, self.far, self.rows, self.rest)
            return
        pieces = []
        for slot in range(size):
            value = self.far[0]
            for k in range(1, size):
                value = jnp.where((here - k + size) % size == slot, self.far[k], value)
            pieces.append(value)
        begin, ordered = 0, []
        for rows in self.rows:
            ordered += [value[begin : begin + rows] for value in pieces]
            begin += rows
        self.block = jnp.concatenate(ordered, 0)

    def near(self, cut):
        quads = lax.axis_size("dp") // 2
        self.cut = cut
        self.others = [send_dp(self.block, 1)]
        if quads == 4:
            self.mine = [self.block, send_dp(self.block, 2), send_dp(self.block, 4)]
        else:
            self.mine = [self.block] + [send_dp(self.block, 2 * k) for k in range(1, quads)]

    def diagonal(self):
        self.others += [send_dp(block, 1) for block in self.mine[1:]]
        if lax.axis_size("dp") == 8:
            low = send_dp(self.mine[1][: self.cut], 4)
            high = send_dp(self.mine[2][self.cut :], 2)
            self.mine.append((low, high))

    def across(self):
        if lax.axis_size("dp") == 8:
            self.others.append(tuple(send_dp(piece, 1) for piece in self.mine[3]))

    def state(self):
        return {k: v for k, v in vars(self).items() if k in ("own", "far", "block", "mine", "others")}

    def hold(self, state):
        vars(self).update(state)

    def parts(self):
        found = []
        for k, (mine, other) in enumerate(zip(self.mine, self.others)):
            for bits, block in ((2 * k, mine), (2 * k + 1, other)):
                if isinstance(block, tuple):
                    found += [(block[0], bits, 0), (block[1], bits, self.cut)]
                else:
                    found.append((block, bits, 0))
        return found


def epoch(*values):
    return lax.optimization_barrier(values)


def pick(values, index, axis):
    return lax.dynamic_index_in_dim(values, index, axis, keepdims=False)


def plus(a, b):
    return (a.astype(F32) + b.astype(F32)).astype(BF16)


class Scatter:
    def __init__(self, mine, away, far):
        self.value = mine
        self.away = away
        self.far = far

    def ahead(self, last):
        if self.away.shape[0] == 4:
            self.first = send_dp(last, 1)

    def core(self):
        self.got = send_dp(self.away, 1)

    def near(self):
        if self.away.shape[0] == 4:
            mine, got = self.value[3], self.first
            half = mine.shape[0] // 2
            self.low = send_dp(plus(mine[:half], got[:half]), 4)
            self.high = send_dp(plus(mine[half:], got[half:]), 2)

    def prepare(self):
        mine, got = self.value, self.got
        half = mine.shape[1] // 2
        self.blocks = []
        for k in range(1, mine.shape[0]):
            block = mine[k].astype(F32) + got[k].astype(F32)
            if mine.shape[0] == 4 and k == 1:
                block = jnp.concatenate([block[:half] + self.low.astype(F32), block[half:]], 0)
            if mine.shape[0] == 4 and k == 2:
                block = jnp.concatenate([block[:half], block[half:] + self.high.astype(F32)], 0)
            if mine.shape[0] == 4 and k == 3:
                continue
            self.blocks.append(block.astype(BF16))

    def quads(self):
        self.blocks = [send_dp(block, 2 * k) for k, block in enumerate(self.blocks, 1)]

    def join(self):
        own = self.value[0].astype(F32) + self.got[0].astype(F32)
        self.value = (own + sum(block.astype(F32) for block in self.blocks)).astype(BF16)

    def held(self):
        return {k: v for k, v in vars(self).items() if k != "far"}

    def hold(self, state):
        vars(self).update(state)

    def along_ffn(self, shifts):
        size = lax.axis_size("ffn")
        here = lax.axis_index("ffn")
        if not hasattr(self, "pieces"):
            self.pieces = [self.far(self.value, here)]
        for k in shifts:
            self.pieces.append(send_ffn(self.far(self.value, (here + k) % size), k))

    def total(self):
        return sum(piece.astype(F32) for piece in self.pieces)


LIMIT = 56 * MIB


def whole(shape):
    return pl.BlockSpec(shape, lambda *_: (0,) * len(shape))


def cost(flops, nbytes):
    return pl.CostEstimate(flops=flops // 1000, bytes_accessed=nbytes // 1000, transcendentals=0)


def pack_kernel(q_ref, k_ref, v_ref, p_ref, visual_ref, out_ref):
    row = 0
    for ref in (q_ref, k_ref, v_ref, p_ref):
        out_ref[row : row + ref.shape[0], :] = ref[...]
        row += ref.shape[0]
    width = out_ref.shape[1]
    count = visual_ref.shape[0]
    visual = visual_ref[...].astype(F32)
    mean = jnp.sum(visual, 0, keepdims=True) * (1.0 / count)
    gap = visual - mean
    spread = jnp.sum(gap * gap, 0, keepdims=True)
    high = mean.astype(BF16)
    rest = (mean - high.astype(F32)).astype(BF16)
    flat = jnp.concatenate([high.astype(F32), rest.astype(F32), spread], 1)
    rows = [flat[:, n * width : (n + 1) * width] for n in range(out_ref.shape[0] - row)]
    out_ref[row:, :] = jnp.concatenate(rows, 0).astype(BF16)


def pack_first(w_query, w_key, w_value, vis_proj, visual):
    width = w_query.shape[1]
    moments = 3 * visual.shape[1] // width
    rows = [w.shape[0] for w in (w_query, w_key, w_value, vis_proj)] + [moments]
    own = pl.pallas_call(
        pack_kernel,
        out_shape=jax.ShapeDtypeStruct((sum(rows), width), BF16),
        name="pack_first",
    )(w_query, w_key, w_value, vis_proj, visual)
    return own, rows


def order_kernel(rows, rest, here_ref, *refs):
    parts, out_ref = refs[:-1], refs[-1]
    size = len(parts)
    here = here_ref[0]
    for index in range(size):

        @pl.when(here == index)
        def _(index=index):
            begin = 0
            for count in rows:
                for k in range(size):
                    row = begin * size + (index - k) % size * count
                    out_ref[row : row + count, :] = parts[k][begin : begin + count, :]
                begin += count

    begin = sum(rows)
    for k in range(1, size if rest else 1):
        row = begin * size + (k - 1) * rest
        out_ref[row : row + rest, :] = parts[k][begin:, :]


def order_blocks(here, parts, rows, rest):
    width = parts[0].shape[1]
    count = len(parts)
    return pl.pallas_call(
        functools.partial(order_kernel, rows, rest),
        in_specs=[pl.BlockSpec(memory_space=pltpu.SMEM)]
        + [pl.BlockSpec(memory_space=pltpu.VMEM)] * len(parts),
        out_specs=pl.BlockSpec(memory_space=pltpu.VMEM),
        out_shape=jax.ShapeDtypeStruct((count * sum(rows) + (count - 1) * rest, width), BF16),
        compiler_params=pltpu.CompilerParams(vmem_limit_bytes=LIMIT),
        name="order_blocks",
    )(here.reshape(1).astype(jnp.int32), *parts)


def place_entries(parts, layout):
    entries = []
    for n, (block, _, first) in enumerate(parts):
        for begin, rows, out, base, lane in layout:
            if first <= begin and begin + rows <= first + block.shape[0]:
                entries.append((n, begin - first, rows, out, base, lane))
    return entries


def place_bits(parts):
    return [bits for _, bits, _ in parts]


def part_copies(entries, bits, place, parts, outs, sems):
    copies = []
    for n, (part, begin, rows, out, base, lane) in enumerate(entries):
        target = pl.multiple_of(base + (place ^ bits[part]) * rows, 16)
        width = parts[part].shape[1]
        copies.append(
            pltpu.make_async_copy(
                parts[part].at[pl.ds(begin, rows), :],
                outs[out].at[pl.ds(target, rows), pl.ds(lane, width)],
                sems.at[n],
            )
        )
    return copies


def picked(order, size):
    row = lax.broadcasted_iota(jnp.int32, (size, size), 0)
    return (order == row).astype(F32)


def exact(a, b, dims):
    return lax.dot_general(
        a, b, (dims, ((), ())), precision=lax.Precision.HIGHEST, preferred_element_type=F32
    )


def first_kernel(entries, bits, devices, place_ref, *refs):
    parts, refs = refs[: len(bits)], refs[len(bits) :]
    text_ref, visual_ref, order_ref, lines_ref = refs[:4]
    qkv_w_ref, proj_ref, hidden_ref, turned_ref, qkv_ref, bn_ref, stats_ref = refs[4:11]
    moments_ref, low_ref, sems = refs[11:]
    outs = (qkv_w_ref, proj_ref, moments_ref)
    copies = part_copies(entries, bits, place_ref[0], parts, outs, sems)
    for copy in copies:
        copy.start()
    copies = [(entry[3], copy) for entry, copy in zip(entries, copies)]
    text_len, width = text_ref.shape
    visual_len, channels = visual_ref.shape
    hidden_ref[:text_len, :] = text_ref[...].astype(F32)
    low_ref[:text_len, :] = text_ref[...]
    for out, copy in copies:
        if out == 2:
            copy.wait()
    moments = moments_ref[...].astype(F32).reshape(devices, -1, width)
    moments = jnp.concatenate([moments[:, n] for n in range(moments.shape[1])], 1)
    means = moments[:, :channels] + moments[:, channels : 2 * channels]
    spreads = moments[:, 2 * channels :]
    average = jnp.sum(means, 0, keepdims=True) * (1.0 / devices)
    gap = means - average
    rows = visual_len * devices
    spread = jnp.sum(spreads, 0, keepdims=True) + visual_len * jnp.sum(gap * gap, 0, keepdims=True)
    inverse = lax.rsqrt(spread * (1.0 / rows) + EPS)
    stats_ref[0:1, :] = average
    stats_ref[1:2, :] = inverse
    normed = (visual_ref[...].astype(F32) - average) * inverse
    bn_rows = (normed * lines_ref[0:1, :] + lines_ref[1:2, :]).astype(BF16)
    bn_ref[...] = bn_rows
    for out, copy in copies:
        if out == 1:
            copy.wait()
    tokens = dot_nn(bn_rows, proj_ref[...])
    tokens = exact(picked(order_ref[...], visual_len), tokens, ((0,), (0,)))
    blank = jnp.zeros((hidden_ref.shape[0] - text_len - visual_len, width), F32)
    tokens = jnp.concatenate([tokens, blank], 0)
    hidden_ref[text_len:, :] = tokens
    low_ref[text_len:, :] = tokens.astype(BF16)
    for out, copy in copies:
        if out == 0:
            copy.wait()
    low = low_ref[...]
    turned_ref[...] = low.T
    for n in range(3):
        lanes = slice(n * width, (n + 1) * width)
        values = dot_nn(low, qkv_w_ref[:, lanes])
        qkv_ref[:, lanes] = (values * 0.125 if n == 0 else values).astype(BF16)


def first_rows(place, parts, layout, text, visual, order, lines, rows, proj_rows, moment_rows):
    devices = lax.axis_size("dp") * lax.axis_size("ffn")
    width = text.shape[1]
    channels = visual.shape[1]
    entries = place_entries(parts, layout)
    vmem = pl.BlockSpec(memory_space=pltpu.VMEM)
    shapes = [
        ((width, 3 * width), BF16),
        ((proj_rows, width), BF16),
        ((rows, width), F32),
        ((width, rows), BF16),
        ((rows, 3 * width), BF16),
        ((visual.shape[0], channels), BF16),
        ((2, channels), F32),
    ]
    return pl.pallas_call(
        functools.partial(first_kernel, entries, place_bits(parts), devices),
        in_specs=[pl.BlockSpec(memory_space=pltpu.SMEM)]
        + [pl.BlockSpec(memory_space=pl.ANY)] * len(parts)
        + [vmem] * 4,
        out_specs=[vmem] * len(shapes),
        out_shape=[jax.ShapeDtypeStruct(*shape) for shape in shapes],
        scratch_shapes=[
            pltpu.VMEM((moment_rows * devices, width), BF16),
            pltpu.VMEM((rows, width), BF16),
            pltpu.SemaphoreType.DMA((len(entries),)),
        ],
        compiler_params=pltpu.CompilerParams(vmem_limit_bytes=LIMIT),
        cost_estimate=cost(0, 25_000_000),
        name="first_rows",
    )(
        place,
        *[block for block, _, _ in parts],
        text,
        visual,
        order,
        lines,
    )


def store_blocks(mine_ref, away_ref, place, store):
    quads = mine_ref.shape[0]
    core, quad = place % 2, place // 2
    for bit in range(2):

        @pl.when(core == bit)
        def _(bit=bit):
            for dp in range(2 * quads):
                ref = mine_ref if dp % 2 == bit else away_ref
                store(ref, (dp // 2) ^ quad, dp)


def feed_kernel(entries, bits, length, ffn, place_ref, *refs):
    parts, refs = refs[: len(bits)], refs[len(bits) :]
    inputs, (lines_ref, inner_b_ref), refs = refs[:3], refs[3:5], refs[5:]
    results, (scale_ref, total_ref, sums_ref, inner_sums_ref), refs = refs[:3], refs[3:7], refs[7:]
    mine_ref, away_ref, last_ref = refs[:3]
    outer_w_ref, inner_w_ref, act_ref, slope_ref, first_ref, low_ref = refs[3:9]
    first_turned, low_turned = refs[9:11]
    mixed_ref, hidden_ref, ct_ref, normed_ref, out_w_ref, output_ref = refs[11:17]
    sems, in_sems, out_sems = refs[17:]
    step = pl.program_id(0)
    width = hidden_ref.shape[1]
    outs = (out_w_ref, outer_w_ref, inner_w_ref)
    fetch = [
        pltpu.make_async_copy(source, target, in_sems.at[n])
        for n, (source, target) in enumerate(zip(inputs, (mixed_ref, hidden_ref, ct_ref)))
    ]
    leave = [
        pltpu.make_async_copy(source, target, out_sems.at[n])
        for n, (source, target) in enumerate(zip((normed_ref, out_w_ref, output_ref), results))
    ]
    gain1, bias1, outer_b, gain2, bias2 = [lines_ref[n : n + 1, :] for n in range(5)]

    @pl.when(step == 0)
    def _():
        copies = part_copies(entries, bits, place_ref[0], parts, outs, sems)
        square = [copy for entry, copy in zip(entries, copies) if entry[3] == 0]
        now = [copy for entry, copy in zip(entries, copies) if entry[3] > 0 and entry[4] == 0]
        later = [copy for entry, copy in zip(entries, copies) if entry[3] > 0 and entry[4] > 0]
        for copy in [fetch[0]] + square + [fetch[1]] + now:
            copy.start()
        for copy in [fetch[0]] + square:
            copy.wait()
        for copy in later + [fetch[2], leave[1]]:
            copy.start()
        attended = dot_nn(mixed_ref[...], out_w_ref[...])
        fetch[1].wait()
        normed, scale = norm_stats(hidden_ref[...] + attended)
        first = normed * gain1 + bias1
        normed_ref[...] = normed
        scale_ref[...] = scale
        low = first.astype(BF16)
        first_ref[...] = low
        total_ref[...] = first + outer_b
        first_turned[...] = low.T
        leave[0].start()

    for index in range(ffn):

        @pl.when(step == index)
        def _(index=index):
            copies = part_copies(entries, bits, place_ref[0], parts, outs, sems)
            for entry, copy in zip(entries, copies):
                if entry[3] > 0 and entry[4] == index * width:
                    copy.wait()

    @pl.when(step < ffn)
    def _():
        rows = pl.ds(pl.multiple_of(step * width, width), width)
        inner = dot_nn(first_ref[...], inner_w_ref[rows, :]) + inner_b_ref[place_ref[1 + step]]
        root = 0.7978845608028654
        square = inner * inner
        half = 0.5 + 0.5 * jnp.tanh(inner * (root + (0.044715 * root) * square))
        act = inner * half
        slope = half + act * (1.0 - half) * (2 * root + (6 * 0.044715 * root) * square)
        slope_ref[step] = slope.astype(BF16)
        act = act.astype(BF16)
        act_ref[step] = act
        total_ref[...] += dot_nt(act, outer_w_ref[rows, :])

    @pl.when(step == ffn - 1)
    def _():
        fetch[2].wait()
        normed, scale = norm_stats(total_ref[...])
        output_ref[...] = (normed * gain2 + bias2).astype(BF16)[:length]
        leave[2].start()
        row = lax.broadcasted_iota(jnp.int32, (normed.shape[0], 1), 0)
        blank = jnp.zeros((normed.shape[0] - length, width), BF16)
        ct = jnp.concatenate([ct_ref[...], blank], 0).astype(F32)
        grad = norm_back(ct, normed, scale, gain2)
        total_ref[...] = grad
        low = grad.astype(BF16)
        low_ref[...] = low
        low_turned[...] = low.T
        sums_ref[0:1, :] = jnp.sum(ct * normed, 0, keepdims=True)
        sums_ref[1:2, :] = jnp.sum(ct, 0, keepdims=True)
        sums_ref[2:3, :] = jnp.sum(grad, 0, keepdims=True)

    @pl.when(step >= ffn)
    def _():
        f = step - ffn
        rows = pl.ds(pl.multiple_of(f * width, width), width)
        grad = dot_nn(low_ref[...], outer_w_ref[rows, :]) * slope_ref[f].astype(F32)
        inner_sums_ref[place_ref[1 + f]] = jnp.sum(grad, 0, keepdims=True)
        grad = grad.astype(BF16)
        total_ref[...] += dot_nt(grad, inner_w_ref[rows, :])
        inner = dot_nn(first_turned[...], grad).astype(BF16)
        outer = dot_nn(low_turned[...], act_ref[f]).astype(BF16)
        size = mine_ref.shape[3]

        def store(ref, slot, dp):
            ref[slot, 0, 0] = inner[dp * size : (dp + 1) * size]
            ref[slot, 1, 0] = outer[dp * size : (dp + 1) * size]
            if ref is away_ref:

                @pl.when(slot == away_ref.shape[0] - 1)
                def _():
                    last_ref[0, 0] = inner[dp * size : (dp + 1) * size]
                    last_ref[1, 0] = outer[dp * size : (dp + 1) * size]

        store_blocks(mine_ref, away_ref, place_ref[0], store)

    @pl.when(step == 2 * ffn - 1)
    def _():
        for copy in leave:
            copy.wait()


def feed_forward(place, feeds, mixed, hidden, lines, inner_b, ct, inner_rows):
    parts, entries = [], []
    for some, layout in feeds:
        for part, *entry in place_entries(some, layout):
            entries.append((part + len(parts), *entry))
        parts += some
    entries.sort(key=lambda entry: (entry[3] > 0, entry[4], -entry[3]))
    rows, width = hidden.shape
    ffn, _, columns = inner_b.shape
    quads = lax.axis_size("dp") // 2
    square = whole((rows, width))
    back = lambda i: jnp.maximum(i - ffn, 0)
    block = pl.BlockSpec((quads, 2, 1, inner_rows, columns), lambda i: (0, 0, back(i), 0, 0))
    blocks = jax.ShapeDtypeStruct((quads, 2, ffn, inner_rows, columns), BF16)
    last = pl.BlockSpec((2, 1, inner_rows, columns), lambda i: (0, back(i), 0, 0))
    smem = pl.BlockSpec(memory_space=pltpu.SMEM)
    shapes = [
        ((rows, width), F32),
        ((width, width), BF16),
        (ct.shape, BF16),
        ((rows, 1), F32),
        ((rows, width), F32),
        ((3, width), F32),
        ((ffn, 1, columns), F32),
    ]
    anywhere = pl.BlockSpec(memory_space=pl.ANY)
    return pl.pallas_call(
        functools.partial(feed_kernel, entries, place_bits(parts), ct.shape[0], ffn),
        grid=(2 * ffn,),
        in_specs=[smem]
        + [anywhere] * (len(parts) + 3)
        + [whole(lines.shape), whole(inner_b.shape)],
        out_specs=[anywhere] * 3
        + [whole((rows, 1)), square, whole((3, width))]
        + [whole((ffn, 1, columns)), block, block, last],
        out_shape=[jax.ShapeDtypeStruct(*shape) for shape in shapes]
        + [blocks, blocks, jax.ShapeDtypeStruct((2, ffn, inner_rows, columns), BF16)],
        scratch_shapes=[
            pltpu.VMEM((ffn * width, columns), BF16),
            pltpu.VMEM((ffn * width, columns), BF16),
            pltpu.VMEM((ffn, rows, columns), BF16),
            pltpu.VMEM((ffn, rows, columns), BF16),
            pltpu.VMEM((rows, width), BF16),
            pltpu.VMEM((rows, width), BF16),
            pltpu.VMEM((width, rows), BF16),
            pltpu.VMEM((width, rows), BF16),
            pltpu.VMEM((rows, width), BF16),
            pltpu.VMEM((rows, width), F32),
            pltpu.VMEM(ct.shape, BF16),
            pltpu.VMEM((rows, width), F32),
            pltpu.VMEM((width, width), BF16),
            pltpu.VMEM(ct.shape, BF16),
            pltpu.SemaphoreType.DMA((len(entries),)),
            pltpu.SemaphoreType.DMA((3,)),
            pltpu.SemaphoreType.DMA((3,)),
        ],
        compiler_params=pltpu.CompilerParams(vmem_limit_bytes=LIMIT),
        cost_estimate=cost(0, 100_000_000),
        name="feed_forward",
    )(
        place,
        *[part for part, _, _ in parts],
        mixed,
        hidden,
        ct,
        lines,
        inner_b,
    )


def norm_kernel(
    grad_ref, normed_ref, scale_ref, lines_ref, w_ref, out_ref, low_ref, mix_ref, sums_ref
):
    grad, normed = grad_ref[...], normed_ref[...]
    attn = norm_back(grad, normed, scale_ref[...], lines_ref[0:1, :])
    out_ref[...] = attn
    low = attn.astype(BF16)
    low_ref[...] = low
    mix_ref[...] = dot_nt(low, w_ref[...]).astype(BF16)
    sums_ref[0:1, :] = jnp.sum(grad * normed, 0, keepdims=True)
    sums_ref[1:2, :] = jnp.sum(grad, 0, keepdims=True)


def norm_rows(grad, normed, scale, lines, out_w):
    rows, width = grad.shape
    low = jax.ShapeDtypeStruct((rows, width), BF16)
    return pl.pallas_call(
        norm_kernel,
        out_shape=[
            jax.ShapeDtypeStruct((rows, width), F32),
            low,
            low,
            jax.ShapeDtypeStruct((2, width), F32),
        ],
        compiler_params=pltpu.CompilerParams(vmem_limit_bytes=LIMIT),
        cost_estimate=cost(0, 12_000_000),
        name="norm_rows",
    )(grad, normed, scale, lines, out_w)


def tail_kernel(text_len, place_ref, *refs):
    inputs, (order_ref, attn_ref, tokens_ref), refs = refs[:11], refs[11:14], refs[14:]
    outputs, buffers = refs[:3], refs[3:14]
    mine, away, in_sems, out_sems = refs[14:]
    low_ref, mixed_ref, attn_low_ref, qkv_w_ref, bn_ref = buffers[6:]
    names = (6, 0, 1, 2, 3, 4, 5, 7, 8, 9, 10)
    copies = {n: pltpu.make_async_copy(inputs[n], buffers[n], in_sems.at[n]) for n in names}
    for n in names:
        copies[n].start()
    visual_len = bn_ref.shape[0]
    width = attn_low_ref.shape[1]
    sent = []

    def spread(values, begin, n):
        values = values.astype(BF16)
        rows = values.shape[0] // (2 * mine.shape[0])

        def store(ref, slot, dp):
            ref[slot, begin : begin + rows, :] = values[dp * rows : (dp + 1) * rows]

        store_blocks(mine, away, place_ref[0], store)
        part = pl.ds(begin, rows)
        for k, ref in enumerate((mine, away)):
            copy = pltpu.make_async_copy(
                ref.at[:, part, :], outputs[k].at[:, part, :], out_sems.at[n, k]
            )
            copy.start()
            sent.append(copy)
        copy = pltpu.make_async_copy(
            away.at[away.shape[0] - 1, part, :], outputs[2].at[part, :], out_sems.at[n, 2]
        )
        copy.start()
        sent.append(copy)
        return begin + rows

    copies[6].wait()
    turned = low_ref[...]
    begin = 0
    grads = []
    for n in range(3):
        copies[2 * n].wait()
        copies[2 * n + 1].wait()
        grads.append(jnp.concatenate([buffers[2 * n][...], buffers[2 * n + 1][...]], 1))
        begin = spread(dot_nn(turned, grads[n]), begin, n)
    copies[7].wait()
    copies[8].wait()
    begin = spread(dot_nn(mixed_ref[...].T, attn_low_ref[...]), begin, 3)
    copies[9].wait()
    tokens = attn_ref[...]
    for n in range(3):
        lanes = slice(n * width, (n + 1) * width)
        tokens = tokens + dot_nt(grads[n][text_len:], qkv_w_ref[:, lanes])
    picker = picked(order_ref[...], visual_len)
    tokens = exact(picker, tokens[:visual_len], ((1,), (0,))).astype(BF16)
    tokens_ref[...] = tokens
    copies[10].wait()
    spread(dot_tn(bn_ref[...], tokens), begin, 4)
    for copy in sent:
        copy.wait()


def tail_rows(place, back, qkv_w, attn, attn_low, mixed, low, order, bn_rows, text_len):
    dp, ffn = lax.axis_size("dp"), lax.axis_size("ffn")
    rows, width = attn.shape
    visual_len, channels = bn_rows.shape
    size = 4 * (width // dp) + channels // dp
    vmem = pl.BlockSpec(memory_space=pltpu.VMEM)
    anywhere = pl.BlockSpec(memory_space=pl.ANY)
    inputs = [g for pair in back for g in pair] + [low, mixed, attn_low, qkv_w, bn_rows]
    rest = rows - text_len
    tail = pl.BlockSpec((rest, width), lambda *_: (text_len // rest, 0))
    blocks = jax.ShapeDtypeStruct((dp // 2, size, width), BF16)
    return pl.pallas_call(
        functools.partial(tail_kernel, text_len),
        grid=(1,),
        in_specs=[pl.BlockSpec(memory_space=pltpu.SMEM)]
        + [anywhere] * len(inputs)
        + [whole(order.shape), tail],
        out_specs=[whole((visual_len, width))] + [anywhere] * 3,
        out_shape=[jax.ShapeDtypeStruct((visual_len, width), BF16), blocks, blocks]
        + [jax.ShapeDtypeStruct((size, width), BF16)],
        scratch_shapes=[pltpu.VMEM(x.shape, BF16) for x in inputs]
        + [
            pltpu.VMEM(blocks.shape, BF16),
            pltpu.VMEM(blocks.shape, BF16),
            pltpu.SemaphoreType.DMA((len(inputs),)),
            pltpu.SemaphoreType.DMA((5, 3)),
        ],
        compiler_params=pltpu.CompilerParams(vmem_limit_bytes=LIMIT),
        cost_estimate=cost(0, 40_000_000),
        name="tail_rows",
    )(place, *inputs, order, attn)


def batch_kernel(tokens_ref, visual_ref, stats_ref, proj_ref, grad_bn_ref, sums_ref):
    grad_bn = dot_nt(proj_ref[...], tokens_ref[...]).T
    grad_bn_ref[...] = grad_bn
    normed = (visual_ref[...].astype(F32) - stats_ref[0:1, :]) * stats_ref[1:2, :]
    sums_ref[0:1, :] = jnp.sum(grad_bn, 0, keepdims=True)
    sums_ref[1:2, :] = jnp.sum(grad_bn * normed, 0, keepdims=True)


def batch_rows(tokens, visual, stats, proj):
    return pl.pallas_call(
        batch_kernel,
        out_shape=[
            jax.ShapeDtypeStruct(visual.shape, F32),
            jax.ShapeDtypeStruct((2, visual.shape[1]), F32),
        ],
        compiler_params=pltpu.CompilerParams(vmem_limit_bytes=LIMIT),
        cost_estimate=cost(0, 6_000_000),
        name="batch_rows",
    )(tokens, visual, stats, proj)


def text_kernel(*refs):
    dq, dk, dv = refs[0:2], refs[2:4], refs[4:6]
    qkv_w_ref, attn_ref, text_ref = refs[6:]
    width = text_ref.shape[1]
    total = attn_ref[...]
    for n, (low, high) in enumerate((dq, dk, dv)):
        grads = jnp.concatenate([low[...], high[...]], 1)
        total = total + dot_nt(grads, qkv_w_ref[:, n * width : (n + 1) * width])
    text_ref[...] = total


def text_rows(back, qkv_w, attn, text_len):
    width = attn.shape[1]
    step = text_len // 2
    grads = [g for pair in back for g in pair]
    return pl.pallas_call(
        text_kernel,
        grid=(2,),
        in_specs=[pl.BlockSpec((step, g.shape[1]), lambda i: (i, 0)) for g in grads]
        + [whole(qkv_w.shape), pl.BlockSpec((step, width), lambda i: (i, 0))],
        out_specs=pl.BlockSpec((step, width), lambda i: (i, 0)),
        out_shape=jax.ShapeDtypeStruct((text_len, width), F32),
        compiler_params=pltpu.CompilerParams(vmem_limit_bytes=LIMIT),
        cost_estimate=cost(0, 25_000_000),
        name="text_rows",
    )(*grads, qkv_w, attn)


def lane_rows(values, width):
    lanes = values.shape[1]
    pieces = pl.cdiv(lanes, width)
    if pieces * width > lanes:
        values = jnp.concatenate([values, jnp.zeros((1, pieces * width - lanes), F32)], 1)
    return [values[:, n * width : (n + 1) * width] for n in range(pieces)]


def sums_kernel(half_levels, bn_ref, one_ref, two_ref, inner_ref, *refs):
    out_ref = refs[-1]
    width = out_ref.shape[1]
    rows = []
    for n in range(bn_ref.shape[0]):
        rows += lane_rows(bn_ref[n : n + 1, :], width)
    for ref in (one_ref, two_ref):
        rows += [ref[n : n + 1, :] for n in range(ref.shape[0])]
    inner = [inner_ref[n] for n in range(inner_ref.shape[0])]
    rows += lane_rows(jnp.concatenate(inner, 1), width)
    halves = sum(ref[...] for ref in refs[:-1])
    tables, lane = [], 0
    for n, size in enumerate(half_levels):
        for row in (32 * n, 32 * n + 16):
            tables.append(halves[row : row + 16, lane : lane + size])
        lane += size
    tables = jnp.concatenate(tables, 1)
    blank = jnp.zeros((tables.shape[0], 256 - tables.shape[1]), F32)
    tables = jnp.concatenate([tables, blank], 1)
    group = width // 256
    for n in range(0, 12, group):
        rows.append(jnp.concatenate([tables[h : h + 1] for h in range(n, n + group)], 1))
    rows += [jnp.zeros((1, width), F32)] * (out_ref.shape[0] - len(rows))
    out_ref[...] = jnp.concatenate(rows, 0)


def pack_sums(bn_sums, one, two, inner, tables, half_levels):
    width = one.shape[1]
    rows = 2 * pl.cdiv(bn_sums.shape[1], width) + 5 + inner.size // width + 12 * 256 // width
    return pl.pallas_call(
        functools.partial(sums_kernel, half_levels),
        out_shape=jax.ShapeDtypeStruct((pl.cdiv(rows, 8) * 8, width), F32),
        cost_estimate=cost(0, 1_000_000),
        name="pack_sums",
    )(bn_sums, one, two, inner, *tables)


def finish_kernel(levels, count, *refs):
    left_ref, right_ref, grad_bn_ref, visual_ref, stats_ref, lines_ref = refs[:6]
    shift_ref, scale_ref, grad_ref, inner_ref = refs[6:10]
    vectors, tables = refs[10:15], refs[15:]
    total = left_ref[...] + right_ref[...]
    width = total.shape[1]
    channels = grad_bn_ref.shape[1]
    row = 0

    def take(lanes):
        nonlocal row
        pieces = pl.cdiv(lanes, width)
        row += pieces
        return jnp.concatenate([total[n : n + 1] for n in range(row - pieces, row)], 1)[:, :lanes]

    shift, scale = take(channels), take(channels)
    shift_ref[...] = shift.reshape(channels)
    scale_ref[...] = scale.reshape(channels)
    for ref in vectors:
        ref[...] = take(width).reshape(width)
    inner_ref[...] = take(inner_ref.shape[0]).reshape(inner_ref.shape[0])
    inverse = stats_ref[1:2, :]
    normed = (visual_ref[...].astype(F32) - stats_ref[0:1, :]) * inverse
    grad = grad_bn_ref[...] - shift * (1.0 / count) - normed * (scale * (1.0 / count))
    grad_ref[...] = lines_ref[0:1, :] * inverse * grad
    group = width // 256
    heads = []
    for n in range(12):
        lane = n % group * 256
        heads.append(total[row + n // group : row + n // group + 1, lane : lane + 256])
    heads = jnp.concatenate(heads, 0)
    begin = 0
    for ref, size in zip(tables, levels):
        ref[...] = heads[:, begin : begin + size]
        begin += size


def finish(left, right, grad_bn, visual, stats, lines, inner, levels, count):
    width = left.shape[1]
    channels = visual.shape[1]
    line = lambda n: jax.ShapeDtypeStruct((n,), F32)
    return pl.pallas_call(
        functools.partial(finish_kernel, levels, count),
        out_shape=[line(channels), line(channels), jax.ShapeDtypeStruct(visual.shape, F32)]
        + [line(inner)]
        + [line(width)] * 5
        + [jax.ShapeDtypeStruct((12, n), F32) for n in levels],
        cost_estimate=cost(0, 3_000_000),
        name="finish",
    )(left, right, grad_bn, visual, stats, lines)


def bias_kernel(rows_step, rel_ref, x_ref, y_ref, tab_ref, out_ref, unit_ref, level_ref):
    pairs = out_ref.shape[0]
    table = tab_ref[...]
    top = jnp.max(jnp.max(jnp.abs(table), 1, keepdims=True), 0, keepdims=True)
    top = jnp.maximum(top, 1e-30)
    unit_ref[...] = top * (2.0 / LEVELS)
    level = jnp.floor((table / top + 1.0) * (0.5 * LEVELS) + 0.5).astype(jnp.int32)
    level_ref[0] = level[:, :128]
    level_ref[1] = level[:, 128:]
    words = []
    for n in range(2):
        low = level_ref[n, pl.ds(0, pairs, stride=2), :]
        high = level_ref[n, pl.ds(1, pairs, stride=2), :]
        words.append(low + high * 65536)
    both = [jnp.broadcast_to(words[0][p : p + 1, :], (8, 128)) for p in range(pairs)]
    rel = [jnp.broadcast_to(words[1][p : p + 1, :], (8, 128)) for p in range(pairs)]

    def look(table, index):
        return jnp.take_along_axis(table, index, axis=1, mode="promise_in_bounds")

    for c in range(out_ref.shape[2] // 128):
        for r in range(rows_step // 8):
            rows, cols = pl.ds(r * 8, 8), pl.ds(c * 128, 128)
            rel_id = rel_ref[0, rows, cols] & 31
            x_id = x_ref[0, rows, cols] & 63
            y_id = (y_ref[0, rows, cols] & 63) + 64
            for p in range(pairs):
                out_ref[p, rows, cols] = (
                    look(rel[p], rel_id) + look(both[p], x_id) + look(both[p], y_id)
                )


def bias_words(rel, x, y, table, first, steps):
    step = 64
    rows = steps * step
    pairs = table.shape[0] // 2
    lanes = pl.cdiv(rel.shape[2], 128) * 128
    ids = pl.BlockSpec((1, step, lanes), lambda i: (0, i + first, 0))
    return pl.pallas_call(
        functools.partial(bias_kernel, step),
        grid=(steps,),
        in_specs=[ids, ids, ids, whole(table.shape)],
        out_specs=[pl.BlockSpec((pairs, step, lanes), lambda i: (0, i, 0)), whole((1, 1))],
        out_shape=[
            jax.ShapeDtypeStruct((pairs, rows, lanes), jnp.int32),
            jax.ShapeDtypeStruct((1, 1), F32),
        ],
        scratch_shapes=[pltpu.VMEM((2, table.shape[0], 128), jnp.int32)],
        compiler_params=pltpu.CompilerParams(vmem_limit_bytes=LIMIT),
        cost_estimate=cost(0, 6_000_000 * steps),
        name="bias_words",
    )(rel, x, y, table)


def lane_halves(rows):
    lane = lax.broadcasted_iota(jnp.int32, (rows, 128), 1)
    return lane < 64, lane >= 64


def attend_kernel(unit_ref, q_ref, k_ref, v_ref, row_ref, *refs):
    word_refs, (p_ref, o_ref, mask_ref) = refs[:-3], refs[-3:]

    @pl.when(pl.program_id(0) == 0)
    def _():
        row = row_ref[...].astype(F32)
        col = jnp.broadcast_to(row, (8, row.shape[1])).T[:, :1]
        mask_ref[...] = jnp.where(col == row, 0.0, NEG)

    unit = unit_ref[...]
    rows = q_ref.shape[0]
    halves = lane_halves(rows)
    q, k, v = q_ref[...], k_ref[...], v_ref[...]
    none = jnp.zeros_like(q)
    words = jnp.concatenate([ref[0][:, :rows] for ref in word_refs], 0)
    mask = mask_ref[...]
    mixed = jnp.zeros((rows, 128), F32)
    for h in range(2):
        scores = dot_nt(jnp.where(halves[h], q, none), k)
        word = (words & 0xFFFF) if h == 0 else lax.shift_right_logical(words, 16)
        scores = scores + word.astype(F32) * unit + mask
        expo = jnp.exp(scores - jnp.max(scores, -1, keepdims=True))
        probs = (expo * (1.0 / jnp.sum(expo, -1, keepdims=True))).astype(BF16)
        p_ref[h] = probs
        mixed = mixed + dot_nn(probs, jnp.where(halves[h], v, none))
    o_ref[...] = mixed.astype(BF16)


def attend(unit, qkv, words, segments):
    pairs = words[0].shape[0]
    rows = qkv.shape[0]
    col = [pl.BlockSpec((rows, 128), lambda p, n=n: (0, n * pairs + p)) for n in range(3)]
    flops = pairs * 4 * 2 * rows * rows * 128
    return pl.pallas_call(
        attend_kernel,
        grid=(pairs,),
        in_specs=[
            whole((1, 1)),
            col[0],
            col[1],
            col[2],
            whole((1, rows)),
        ]
        + [pl.BlockSpec((1,) + w.shape[1:], lambda p: (p, 0, 0)) for w in words],
        out_specs=[
            pl.BlockSpec((2, rows, rows), lambda p: (p, 0, 0)),
            pl.BlockSpec((rows, 128), lambda p: (0, p)),
        ],
        out_shape=[
            jax.ShapeDtypeStruct((2 * pairs, rows, rows), BF16),
            jax.ShapeDtypeStruct((rows, pairs * 128), BF16),
        ],
        scratch_shapes=[pltpu.VMEM((rows, rows), F32)],
        compiler_params=pltpu.CompilerParams(vmem_limit_bytes=LIMIT),
        cost_estimate=cost(flops, 40_000_000),
        name="attend",
    )(unit, qkv, qkv, qkv, segments, *words)


def attend_back_kernel(q_ref, k_ref, v_ref, g_ref, p_ref, ds_ref, dq_ref, dk_ref, dv_ref):
    rows = q_ref.shape[0]
    halves = lane_halves(rows)
    q, k, v, g = q_ref[...], k_ref[...], v_ref[...], g_ref[...]
    none = jnp.zeros_like(q)
    blank = jnp.zeros((rows, ds_ref.shape[2] - rows), BF16)
    dq = jnp.zeros((rows, 128), F32)
    dk, dv = dq, dq
    for h in range(2):
        low = p_ref[h]
        probs = low.astype(F32)
        weighted = probs * dot_nt(g, jnp.where(halves[h], v, none))
        ds = (weighted - probs * jnp.sum(weighted, -1, keepdims=True)).astype(BF16)
        ds_ref[h] = jnp.concatenate([ds, blank], 1)
        dq = dq + dot_nn(ds, jnp.where(halves[h], k, none))
        dv = dv + dot_tn(low, jnp.where(halves[h], g, none))
        dk = dk + dot_tn(ds, jnp.where(halves[h], q, none))
    dq_ref[...] = (dq * 0.125).astype(BF16)
    dk_ref[...] = dk.astype(BF16)
    dv_ref[...] = dv.astype(BF16)


def attend_back(qkv, grad, probs, first, pairs):
    every = probs.shape[0] // 2
    rows = qkv.shape[0]
    col = [pl.BlockSpec((rows, 128), lambda p, n=n: (0, n * every + p + first)) for n in range(3)]
    new = pl.BlockSpec((rows, 128), lambda p: (0, p))
    big = pl.BlockSpec((2, rows, rows), lambda p: (p + first, 0, 0))
    lanes = pl.cdiv(rows, 128) * 128
    out = jax.ShapeDtypeStruct((rows, pairs * 128), BF16)
    flops = pairs * 2 * 4 * 2 * rows * rows * 128
    return pl.pallas_call(
        attend_back_kernel,
        grid=(pairs,),
        in_specs=[col[0], col[1], col[2], col[0], big],
        out_specs=[pl.BlockSpec((2, rows, lanes), lambda p: (p, 0, 0)), new, new, new],
        out_shape=[jax.ShapeDtypeStruct((2 * pairs, rows, lanes), BF16), out, out, out],
        compiler_params=pltpu.CompilerParams(vmem_limit_bytes=LIMIT),
        cost_estimate=cost(flops, 8_000_000 * pairs),
        name="attend_back",
    )(qkv, qkv, qkv, grad, probs)


GROUP = 48


def table_kernel(first, levels, block_ref, count_ref, rel_ref, x_ref, y_ref, *refs):
    ds_refs, out_ref = refs[:-1], refs[-1]
    place = pl.program_id(0)
    step = rel_ref.shape[1]
    every = rel_ref.shape[2] // 128
    heads = sum(ref.shape[0] for ref in ds_refs)
    counts = (levels[1] // 2, levels[2] // 2, levels[0] // 2)

    @pl.when(place == 0)
    def _():
        out_ref[...] = jnp.zeros_like(out_ref)

    def group(r, start, blocks):
        width = blocks * 128
        level = lax.broadcasted_iota(jnp.int32, (16, width), 0).astype(F32).astype(BF16)
        one = jnp.ones((16, width), BF16)
        none = jnp.zeros((16, width), BF16)

        def one_hot(ids, count):
            wide = jnp.broadcast_to(ids, (16, width)).astype(BF16)
            return [jnp.where(wide == level + BF16(16 * t), one, none) for t in range(count // 16)]

        def halves(values, top):
            chosen = jnp.broadcast_to(top, (16, width)).astype(BF16) == one
            return [jnp.where(chosen, none, values), jnp.where(chosen, values, none)]

        rows = pl.ds(pl.multiple_of(r * GROUP, GROUP), GROUP)
        lanes = pl.ds(pl.multiple_of(start * 128, 128), width)
        values = [ref[:, rows, lanes] for ref in ds_refs]
        values.append(jnp.zeros((16 - heads, GROUP, width), BF16))
        values = jnp.transpose(jnp.concatenate(values, 0), (1, 0, 2))
        ids = [ref[0, rows, lanes].astype(F32) for ref in (x_ref, y_ref, rel_ref)]
        tops = [(i >= count).astype(F32) for i, count in zip(ids, counts)]
        rest = [i - top * count for i, top, count in zip(ids, tops, counts)]
        total = out_ref[...]
        for begin in range(0, GROUP, 2):
            lefts, rights = [], []
            for n in (begin, begin + 1):
                hot, split = [], []
                for top, low, count in zip(tops, rest, counts):
                    hot += one_hot(low[n : n + 1], count)
                    split += halves(values[n], top[n : n + 1])
                lefts.append(jnp.concatenate(split, 0))
                rights.append(jnp.concatenate(hot, 0))
            total = total + dot_nt(jnp.concatenate(lefts, 1), jnp.concatenate(rights, 1))
        out_ref[...] = total

    def body(r, _):
        index = (place + first) * (step // GROUP) + r
        count = jnp.maximum(count_ref[index], 2)
        start = jnp.minimum(block_ref[index], every - count)
        for blocks in range(2, every + 1):

            @pl.when(count == blocks)
            def _(blocks=blocks):
                group(r, start, blocks)

        return 0

    lax.fori_loop(0, step // GROUP, body, 0)


def table_sums(ranges, rel, x, y, ds, levels, first, steps):
    step = 2 * GROUP
    lanes = ds[0].shape[2]
    ids = pl.BlockSpec((1, step, lanes), lambda i, *_: (0, i + first, 0))
    return pl.pallas_call(
        functools.partial(table_kernel, first, levels),
        grid_spec=pltpu.PrefetchScalarGridSpec(
            num_scalar_prefetch=2,
            grid=(steps,),
            in_specs=[ids, ids, ids]
            + [pl.BlockSpec((d.shape[0], step, lanes), lambda i, *_: (0, i + first, 0)) for d in ds],
            out_specs=whole((96, sum(levels) // 2)),
        ),
        out_shape=jax.ShapeDtypeStruct((96, sum(levels) // 2), F32),
        compiler_params=pltpu.CompilerParams(vmem_limit_bytes=LIMIT),
        cost_estimate=cost(0, 8_000_000 * steps),
        name="table_sums",
    )(*ranges, rel, x, y, *ds)


def document_blocks(segments, rows):
    length = segments.shape[0]
    first = segments[0:rows:GROUP]
    last = segments[jnp.minimum(jnp.arange(GROUP - 1, rows, GROUP), length - 1)]
    begin = jnp.sum(segments[None, :] < first[:, None], 1, dtype=jnp.int32)
    end = jnp.sum(segments[None, :] <= last[:, None], 1, dtype=jnp.int32)
    return begin // 128, (end + 127) // 128 - begin // 128


def norm_stats(values):
    center = values - jnp.mean(values, -1, keepdims=True)
    scale = lax.rsqrt(jnp.mean(center * center, -1, keepdims=True) + EPS)
    return center * scale, scale


def norm_back(grad, normed, scale, gain):
    scaled = grad * gain
    return scale * (
        scaled
        - jnp.mean(scaled, -1, keepdims=True)
        - normed * jnp.mean(scaled * normed, -1, keepdims=True)
    )


def on_device(
    text_hidden,
    visual_maps,
    patch_order,
    segment_ids,
    rel_bucket,
    x_bucket,
    y_bucket,
    bn_scale,
    bn_shift,
    vis_proj,
    w_query,
    w_key,
    w_value,
    w_output,
    rel_table,
    x_table,
    y_table,
    first_gain,
    first_bias,
    w_inner,
    b_inner,
    w_outer,
    b_outer,
    second_gain,
    second_bias,
    cotangent,
):
    heads = rel_table.shape[1]
    pairs = heads // 2
    visual_len = patch_order.shape[1]
    length = segment_ids.shape[1]
    text_len = length - visual_len
    width = w_query.shape[1]
    dp, ffn = lax.axis_size("dp"), lax.axis_size("ffn")
    place = lax.axis_index("dp")
    devices = dp * ffn
    rows = pl.cdiv(length, 64) * 64
    count = visual_maps.shape[0] * devices
    levels = (rel_table.shape[0], x_table.shape[0], y_table.shape[0])

    inner_rows, columns = w_inner.shape
    outer_shard = w_outer.T
    steps = rows // 64

    first_set = Gather(*pack_first(w_query, w_key, w_value, vis_proj, visual_maps))
    plain = columns == width
    early = plain and dp == 8
    here = lax.axis_index("ffn")
    wide_shards = jnp.concatenate([outer_shard, w_inner], 0)
    if early:
        late_set = Gather(
            jnp.concatenate([w_output, wide_shards], 0), [w_output.shape[0]], 2 * inner_rows
        )
    elif plain:
        late_set = Gather(
            jnp.concatenate([w_output, wide_shards], 0), [w_output.shape[0], inner_rows, inner_rows]
        )
    else:
        late_set = Gather(w_output, [w_output.shape[0]])
        wide_set = Gather(wide_shards, [inner_rows, inner_rows])

    first_set.own, wide_shards = epoch(first_set.own, wide_shards)
    first_set.along_ffn()
    wides = [wide_shards]
    if early:
        wides += [send_dp(wide_shards, 2), send_dp(wide_shards, 4)]
    tables = jnp.concatenate([x_table, y_table, rel_table], 0).T
    tables = jnp.pad(tables, ((0, 0), (0, 256 - tables.shape[1])))
    cuts = [0, steps // 9, steps * 7 // 9, steps]
    words = [None] * 3
    words[0], unit = bias_words(rel_bucket, x_bucket, y_bucket, tables, 0, cuts[1])
    ranges = document_blocks(segment_ids[0], rows)
    lines = jnp.stack([first_gain, first_bias, b_outer, second_gain, second_bias])
    inner_b = b_inner.reshape(ffn, 1, columns)
    segments = jnp.pad(segment_ids, ((0, 0), (0, rows - length)), constant_values=-1)
    bn_lines = jnp.stack([bn_scale, bn_shift])
    order = [(here - k + ffn) % ffn if early else jnp.int32(k) for k in range(ffn)]
    place = jnp.stack([place] + order).astype(jnp.int32)
    state, late, place, wides, words[0], tables, ranges, lines, inner_b, segments, bn_lines = epoch(
        first_set.state(),
        late_set.state(),
        place,
        wides,
        words[0],
        tables,
        ranges,
        lines,
        inner_b,
        segments,
        bn_lines,
    )
    first_set.hold(state)
    late_set.hold(late)

    first_set.order()
    first_set.near(3 * w_query.shape[0] * ffn)
    late_set.along_ffn(1, ffn - 1)
    words[1], _ = bias_words(rel_bucket, x_bucket, y_bucket, tables, cuts[1], cuts[2] - cuts[1])
    state, late, words[1], tables = epoch(first_set.state(), late_set.state(), words[1], tables)
    first_set.hold(state)
    late_set.hold(late)

    first_set.diagonal()
    late_set.along_ffn(ffn - 1)
    state, late, tables = epoch(first_set.state(), late_set.state(), tables)
    first_set.hold(state)
    late_set.hold(late)

    late_set.order()
    first_set.across()
    state, late = epoch(first_set.state(), late_set.state())
    first_set.hold(state)
    late_set.hold(late)

    late_rows = w_output.shape[0] * ffn
    late_set.near(late_rows + (inner_rows if early else ffn * inner_rows) if plain else 0)
    if early:
        wides += [send_dp(wide, 1) for wide in wides[:2]]
    layout, row = [], 0
    for n, size in enumerate(first_set.rows):
        layout.append((row, size * ffn, max(n - 2, 0), 0, n * width if n < 3 else 0))
        row += size * ffn
    qkv_full, proj_full, hidden, lowered, qkv, bn_rows, bn_stats = first_rows(
        place,
        first_set.parts(),
        layout,
        text_hidden,
        visual_maps,
        patch_order,
        bn_lines,
        rows,
        vis_proj.shape[0] * devices,
        first_set.rows[-1],
    )
    qkv, tables = epoch(qkv, tables)
    words[2], _ = bias_words(rel_bucket, x_bucket, y_bucket, tables, cuts[2], cuts[3] - cuts[2])
    qkv, state, words[2], wides = epoch(qkv, late_set.state(), words[2], wides)
    late_set.hold(state)

    late_set.diagonal()
    if early:
        wides.append(send_dp(wides[1], 4))
    probs, mixed = attend(unit, qkv, words, segments)
    probs, mixed, state, wides = epoch(probs, mixed, late_set.state(), wides)
    late_set.hold(state)
    late_set.across()
    layout = [(0, late_rows, 0, 0, 0)]
    shift = late_rows
    parts = late_set.parts()
    if not plain:
        parts = [(block, bits, 0) for block, bits, _ in parts]
        wide_set.along_ffn()
        wide_set.order()
        wide_set.near(0)
        wide_set.diagonal()
        wide_set.across()
        shift = 0
    wide_layout = [
        (shift + (n * ffn + f) * inner_rows, inner_rows, 1 + n, f * width, 0)
        for n in range(2)
        for f in range(ffn)
    ]
    feeds = [(parts, layout + wide_layout if plain else layout)]
    if not plain:
        feeds.append((wide_set.parts(), wide_layout))
    if early:
        near_layout = [(n * inner_rows, inner_rows, 1 + n, 0, 0) for n in range(2)]
        far_layout = [
            (late_rows + (2 * k - 2 + n) * inner_rows, inner_rows, 1 + n, k * width, 0)
            for k in range(1, ffn)
            for n in range(2)
        ]
        own, from_x, from_y, other, other_x, from_xy = wides
        crossed = [send_dp(from_y, 1), send_dp(from_xy, 1)]
        blocks = [own, other, from_x, other_x, from_y, crossed[0], from_xy, crossed[1]]
        feeds = [
            (parts, layout + far_layout),
            ([(block, bits, 0) for bits, block in enumerate(blocks)], near_layout),
        ]
    (
        first_n,
        output_full,
        output,
        first_r,
        grad_first,
        sums_two,
        inner_sums,
        mine,
        away,
        last,
    ) = feed_forward(place, feeds, mixed, hidden, lines, inner_b, cotangent, inner_rows)

    def wide_far(value, index):
        return pick(value, (here - index + ffn) % ffn if early else index, 1)

    wide = Scatter(mine, away, wide_far)
    wide.ahead(last)
    state, grad_first = epoch(wide.held(), grad_first)
    wide.hold(state)
    wide.near()
    wide.core()
    grad_attn, attn_low, grad_mixed, sums_one = norm_rows(
        grad_first, first_n, first_r, lines, output_full
    )
    half = pairs // 3
    back_low = attend_back(qkv, grad_mixed, probs, 0, half)
    state, back_low, qkv = epoch(wide.held(), back_low, qkv)
    wide.hold(state)
    wide.prepare()
    wide.blocks, qkv = epoch(wide.blocks, qkv)

    wide.quads()
    back_high = attend_back(qkv, grad_mixed, probs, half, pairs - half)
    back = list(zip(back_low[1:], back_high[1:]))
    tokens_grad, mine, away, last = tail_rows(
        place, back, qkv_full, grad_attn, attn_low, mixed, lowered, patch_order, bn_rows, text_len
    )
    ds = (back_low[0], back_high[0])
    wide.blocks, mine, away, last, ds, tokens_grad = epoch(
        wide.blocks, mine, away, last, ds, tokens_grad
    )

    def tail_far(value, index):
        size = 4 * (width // dp)
        square = pick(value[:size].reshape(4, ffn, -1, width), index, 1)
        return jnp.concatenate(
            [square.reshape(-1, width), pick(value[size:].reshape(ffn, -1, width), index, 0)], 0
        )

    groups = rows // (2 * GROUP)
    cuts = [0, groups]
    sums = []

    def tables(ds):
        n = len(sums)
        return sums + [
            table_sums(
                ranges, rel_bucket, x_bucket, y_bucket, ds, levels, cuts[n], cuts[n + 1] - cuts[n]
            )
        ]

    tail = Scatter(mine, away, tail_far)
    tail.ahead(last)
    wide.join()
    state, wide.value, tokens_grad = epoch(tail.held(), wide.value, tokens_grad)
    tail.hold(state)
    tail.near()
    tail.core()
    wide.along_ffn([1])
    grad_bn, bn_sums = batch_rows(tokens_grad, visual_maps, bn_stats, proj_full)
    state, bn_sums, ds, wide.pieces = epoch(tail.held(), bn_sums, ds, wide.pieces)
    tail.hold(state)
    tail.prepare()
    tail.blocks, ds = epoch(tail.blocks, ds)

    tail.quads()
    wide.along_ffn(range(2, ffn))
    sums = tables(ds)
    tail.blocks, sums, back, wide.pieces = epoch(tail.blocks, sums, back, wide.pieces)

    tail.join()
    tail.along_ffn([1])
    total = Sum(
        pack_sums(
            bn_sums,
            sums_one,
            sums_two,
            inner_sums,
            sums,
            (levels[1] // 2, levels[2] // 2, levels[0] // 2),
        )
    )
    for _ in range(ffn.bit_length() - 1):
        total.step()
    wide_sum = wide.total()
    state, total.values, back = epoch(tail.held(), total.values, back)
    tail.hold(state)
    tail.along_ffn(range(2, ffn))
    while len(total.steps) > 1:
        total.step()
    text_grad = text_rows(back, qkv_full, grad_attn, text_len)
    other = total.steps[0](total.values)
    (
        shift_grad,
        scale_grad,
        visual_grad,
        inner_grad,
        gain_one,
        bias_one,
        gain_two,
        bias_two,
        outer_grad,
        x_grad,
        y_grad,
        rel_grad,
    ) = finish(
        total.values,
        other,
        grad_bn,
        visual_maps,
        bn_stats,
        bn_lines,
        b_inner.shape[0],
        (levels[1], levels[2], levels[0]),
        count,
    )
    shards, row = [], 0
    for size in [w_query.shape[0]] * 4 + [vis_proj.shape[0]]:
        shards.append(sum(piece[row : row + size].astype(F32) for piece in tail.pieces))
        row += size
    return (
        output,
        text_grad,
        visual_grad,
        scale_grad.reshape(-1),
        shift_grad.reshape(-1),
        shards[4],
        shards[0],
        shards[1],
        shards[2],
        shards[3],
        rel_grad.T,
        x_grad.T,
        y_grad.T,
        gain_one.reshape(-1),
        bias_one.reshape(-1),
        wide_sum[0],
        inner_grad.reshape(-1),
        wide_sum[1].T,
        outer_grad.reshape(-1),
        gain_two.reshape(-1),
        bias_two.reshape(-1),
    )


def solution(mesh):
    rows = P(ALL, None)
    cube = P(ALL, None, None)
    return jax.shard_map(
        on_device,
        mesh=mesh,
        in_specs=(rows,) * 4
        + (cube,) * 3
        + (P(),) * 2
        + (rows,) * 5
        + (P(),) * 5
        + (P("dp", "ffn"), P(), P("ffn", "dp"))
        + (P(),) * 3
        + (rows,),
        out_specs=(rows,) * 3
        + (P(),) * 2
        + (rows,) * 5
        + (P(),) * 5
        + (P("dp", "ffn"), P(), P("ffn", "dp"))
        + (P(),) * 3,
        check_vma=False,
    )
```

```python
import functools

import jax
import jax.numpy as jnp
from jax import lax
from jax.experimental import pallas as pl
from jax.experimental.pallas import tpu as pltpu
from jax.sharding import PartitionSpec as P

EPS = 1e-05
NEG = -1e30
F32 = jnp.float32
BF16 = jnp.bfloat16
ALL = ("dp", "ffn")
LEVELS = 21845.0
MIB = 2**20


def dot_nn(a, b):
    return lax.dot_general(a, b, (((1,), (0,)), ((), ())), preferred_element_type=F32)


def dot_nt(a, b):
    return lax.dot_general(a, b, (((1,), (1,)), ((), ())), preferred_element_type=F32)


def dot_tn(a, b):
    return lax.dot_general(a, b, (((0,), (0,)), ((), ())), preferred_element_type=F32)


def pad_rows(values, rows):
    return jnp.pad(values, ((0, rows - values.shape[0]), (0, 0)))


def send_dp(values, bits):
    size = lax.axis_size("dp")
    return lax.ppermute(values, "dp", [(i, i ^ bits) for i in range(size)])


def send_ffn(values, shift):
    size = lax.axis_size("ffn")
    return lax.ppermute(values, "ffn", [(i, (i + shift) % size) for i in range(size)])


def swap_ffn(values, bits):
    size = lax.axis_size("ffn")
    return lax.ppermute(values, "ffn", [(i, i ^ bits) for i in range(size)])


def exchanges():
    steps = []
    for axis, send in (("ffn", swap_ffn), ("dp", send_dp)):
        bit = 1
        while bit < lax.axis_size(axis):
            steps.append(functools.partial(send, bits=bit))
            bit *= 2
    return steps


class Sum:
    def __init__(self, values):
        self.values = values
        self.steps = exchanges()

    def step(self):
        if self.steps:
            self.values = self.values + self.steps.pop(0)(self.values)

    def finish(self):
        while self.steps:
            self.step()
        return self.values


class Gather:
    def __init__(self, own, rows, rest=0):
        self.own = own
        self.rows = rows
        self.rest = rest

    def along_ffn(self, begin=1, end=None):
        size = lax.axis_size("ffn")
        self.far = self.far[:begin] if begin > 1 else [self.own]
        self.far += [send_ffn(self.own, k) for k in range(begin, end or size)]

    def order(self):
        size = lax.axis_size("ffn")
        here = lax.axis_index("ffn")
        if all(rows % 8 == 0 for rows in self.rows):
            self.block = order_blocks(here, self.far, self.rows, self.rest)
            return
        pieces = []
        for slot in range(size):
            value = self.far[0]
            for k in range(1, size):
                value = jnp.where((here - k + size) % size == slot, self.far[k], value)
            pieces.append(value)
        begin, ordered = 0, []
        for rows in self.rows:
            ordered += [value[begin : begin + rows] for value in pieces]
            begin += rows
        self.block = jnp.concatenate(ordered, 0)

    def near(self, cut):
        quads = lax.axis_size("dp") // 2
        self.cut = cut
        self.others = [send_dp(self.block, 1)]
        if quads == 4:
            self.mine = [self.block, send_dp(self.block, 2), send_dp(self.block, 4)]
        else:
            self.mine = [self.block] + [send_dp(self.block, 2 * k) for k in range(1, quads)]

    def diagonal(self):
        self.others += [send_dp(block, 1) for block in self.mine[1:]]
        if lax.axis_size("dp") == 8:
            low = send_dp(self.mine[1][: self.cut], 4)
            high = send_dp(self.mine[2][self.cut :], 2)
            self.mine.append((low, high))

    def across(self):
        if lax.axis_size("dp") == 8:
            self.others.append(tuple(send_dp(piece, 1) for piece in self.mine[3]))

    def state(self):
        return {k: v for k, v in vars(self).items() if k in ("own", "far", "block", "mine", "others")}

    def hold(self, state):
        vars(self).update(state)

    def parts(self):
        found = []
        for k, (mine, other) in enumerate(zip(self.mine, self.others)):
            for bits, block in ((2 * k, mine), (2 * k + 1, other)):
                if isinstance(block, tuple):
                    found += [(block[0], bits, 0), (block[1], bits, self.cut)]
                else:
                    found.append((block, bits, 0))
        return found


def epoch(*values):
    return lax.optimization_barrier(values)


def pick(values, index, axis):
    return lax.dynamic_index_in_dim(values, index, axis, keepdims=False)


def plus(a, b):
    return (a.astype(F32) + b.astype(F32)).astype(BF16)


class Scatter:
    def __init__(self, mine, away, far):
        self.value = mine
        self.away = away
        self.far = far

    def ahead(self, last):
        if self.away.shape[0] == 4:
            self.first = send_dp(last, 1)

    def core(self):
        self.got = send_dp(self.away, 1)

    def near(self):
        if self.away.shape[0] == 4:
            mine, got = self.value[3], self.first
            half = mine.shape[0] // 2
            self.low = send_dp(plus(mine[:half], got[:half]), 4)
            self.high = send_dp(plus(mine[half:], got[half:]), 2)

    def prepare(self):
        mine, got = self.value, self.got
        half = mine.shape[1] // 2
        self.blocks = []
        for k in range(1, mine.shape[0]):
            block = mine[k].astype(F32) + got[k].astype(F32)
            if mine.shape[0] == 4 and k == 1:
                block = jnp.concatenate([block[:half] + self.low.astype(F32), block[half:]], 0)
            if mine.shape[0] == 4 and k == 2:
                block = jnp.concatenate([block[:half], block[half:] + self.high.astype(F32)], 0)
            if mine.shape[0] == 4 and k == 3:
                continue
            self.blocks.append(block.astype(BF16))

    def quads(self):
        self.blocks = [send_dp(block, 2 * k) for k, block in enumerate(self.blocks, 1)]

    def join(self):
        own = self.value[0].astype(F32) + self.got[0].astype(F32)
        self.value = (own + sum(block.astype(F32) for block in self.blocks)).astype(BF16)

    def held(self):
        return {k: v for k, v in vars(self).items() if k != "far"}

    def hold(self, state):
        vars(self).update(state)

    def along_ffn(self, shifts):
        size = lax.axis_size("ffn")
        here = lax.axis_index("ffn")
        if not hasattr(self, "pieces"):
            self.pieces = [self.far(self.value, here)]
        for k in shifts:
            self.pieces.append(send_ffn(self.far(self.value, (here + k) % size), k))

    def total(self):
        return sum(piece.astype(F32) for piece in self.pieces)


LIMIT = 56 * MIB


def whole(shape):
    return pl.BlockSpec(shape, lambda *_: (0,) * len(shape))


def cost(flops, nbytes):
    return pl.CostEstimate(flops=flops // 1000, bytes_accessed=nbytes // 1000, transcendentals=0)


def pack_kernel(q_ref, k_ref, v_ref, p_ref, visual_ref, *refs):
    out_ref = refs[-1]
    if len(refs) > 1:
        output_ref, outer_ref, inner_ref, out_ref, wide_ref, late_ref = refs
        size, first = inner_ref.shape[0], output_ref.shape[0]
        late_ref[:first, :] = output_ref[...]
        for n, value in enumerate((outer_ref[...], inner_ref[...])):
            wide_ref[n * size : (n + 1) * size, :] = value
            late_ref[first + n * size : first + (n + 1) * size, :] = value
    row = 0
    for ref in (q_ref, k_ref, v_ref, p_ref):
        out_ref[row : row + ref.shape[0], :] = ref[...]
        row += ref.shape[0]
    width = out_ref.shape[1]
    count = visual_ref.shape[0]
    visual = visual_ref[...].astype(F32)
    mean = jnp.sum(visual, 0, keepdims=True) * (1.0 / count)
    gap = visual - mean
    spread = jnp.sum(gap * gap, 0, keepdims=True)
    high = mean.astype(BF16)
    rest = (mean - high.astype(F32)).astype(BF16)
    flat = jnp.concatenate([high.astype(F32), rest.astype(F32), spread], 1)
    rows = [flat[:, n * width : (n + 1) * width] for n in range(out_ref.shape[0] - row)]
    out_ref[row:, :] = jnp.concatenate(rows, 0).astype(BF16)


def pack_first(w_query, w_key, w_value, vis_proj, visual, late=()):
    width = w_query.shape[1]
    moments = 3 * visual.shape[1] // width
    rows = [w.shape[0] for w in (w_query, w_key, w_value, vis_proj)] + [moments]
    sizes = [sum(rows)]
    if late:
        sizes += [2 * late[2].shape[0], late[0].shape[0] + 2 * late[2].shape[0]]
    packed = pl.pallas_call(
        pack_kernel,
        out_shape=[jax.ShapeDtypeStruct((size, width), BF16) for size in sizes],
        name="pack_first",
    )(w_query, w_key, w_value, vis_proj, visual, *late)
    return packed, rows


def order_kernel(rows, rest, here_ref, *refs):
    parts, out_ref = refs[:-1], refs[-1]
    size = len(parts)
    here = here_ref[0]
    for index in range(size):

        @pl.when(here == index)
        def _(index=index):
            begin = 0
            for count in rows:
                for k in range(size):
                    row = begin * size + (index - k) % size * count
                    out_ref[row : row + count, :] = parts[k][begin : begin + count, :]
                begin += count

    begin = sum(rows)
    for k in range(1, size if rest else 1):
        row = begin * size + (k - 1) * rest
        out_ref[row : row + rest, :] = parts[k][begin:, :]


def order_blocks(here, parts, rows, rest):
    width = parts[0].shape[1]
    count = len(parts)
    return pl.pallas_call(
        functools.partial(order_kernel, rows, rest),
        in_specs=[pl.BlockSpec(memory_space=pltpu.SMEM)]
        + [pl.BlockSpec(memory_space=pltpu.VMEM)] * len(parts),
        out_specs=pl.BlockSpec(memory_space=pltpu.VMEM),
        out_shape=jax.ShapeDtypeStruct((count * sum(rows) + (count - 1) * rest, width), BF16),
        compiler_params=pltpu.CompilerParams(vmem_limit_bytes=LIMIT),
        name="order_blocks",
    )(here.reshape(1).astype(jnp.int32), *parts)


def place_entries(parts, layout):
    entries = []
    for n, (block, _, first) in enumerate(parts):
        for begin, rows, out, base, lane in layout:
            if first <= begin and begin + rows <= first + block.shape[0]:
                entries.append((n, begin - first, rows, out, base, lane))
    return entries


def place_bits(parts):
    return [bits for _, bits, _ in parts]


def part_copies(entries, bits, place, parts, outs, sems):
    copies = []
    for n, (part, begin, rows, out, base, lane) in enumerate(entries):
        target = pl.multiple_of(base + (place ^ bits[part]) * rows, 16)
        width = parts[part].shape[1]
        copies.append(
            pltpu.make_async_copy(
                parts[part].at[pl.ds(begin, rows), :],
                outs[out].at[pl.ds(target, rows), pl.ds(lane, width)],
                sems.at[n],
            )
        )
    return copies


def picked(order, size):
    row = lax.broadcasted_iota(jnp.int32, (size, size), 0)
    return (order == row).astype(F32)


def exact(a, b, dims):
    return lax.dot_general(
        a, b, (dims, ((), ())), precision=lax.Precision.HIGHEST, preferred_element_type=F32
    )


def first_kernel(entries, bits, devices, place_ref, *refs):
    parts, refs = refs[: len(bits)], refs[len(bits) :]
    text_ref, visual_ref, order_ref, lines_ref = refs[:4]
    qkv_w_ref, proj_ref, hidden_ref, turned_ref, qkv_ref, bn_ref, stats_ref = refs[4:11]
    moments_ref, low_ref, sems = refs[11:]
    outs = (qkv_w_ref, proj_ref, moments_ref)
    copies = part_copies(entries, bits, place_ref[0], parts, outs, sems)
    for copy in copies:
        copy.start()
    copies = [(entry[3], copy) for entry, copy in zip(entries, copies)]
    text_len, width = text_ref.shape
    visual_len, channels = visual_ref.shape
    hidden_ref[:text_len, :] = text_ref[...].astype(F32)
    low_ref[:text_len, :] = text_ref[...]
    for out, copy in copies:
        if out == 2:
            copy.wait()
    moments = moments_ref[...].astype(F32).reshape(devices, -1, width)
    moments = jnp.concatenate([moments[:, n] for n in range(moments.shape[1])], 1)
    means = moments[:, :channels] + moments[:, channels : 2 * channels]
    spreads = moments[:, 2 * channels :]
    average = jnp.sum(means, 0, keepdims=True) * (1.0 / devices)
    gap = means - average
    rows = visual_len * devices
    spread = jnp.sum(spreads, 0, keepdims=True) + visual_len * jnp.sum(gap * gap, 0, keepdims=True)
    inverse = lax.rsqrt(spread * (1.0 / rows) + EPS)
    stats_ref[0:1, :] = average
    stats_ref[1:2, :] = inverse
    normed = (visual_ref[...].astype(F32) - average) * inverse
    bn_rows = (normed * lines_ref[0:1, :] + lines_ref[1:2, :]).astype(BF16)
    bn_ref[...] = bn_rows
    for out, copy in copies:
        if out == 1:
            copy.wait()
    tokens = dot_nn(bn_rows, proj_ref[...])
    tokens = exact(picked(order_ref[...], visual_len), tokens, ((0,), (0,)))
    blank = jnp.zeros((hidden_ref.shape[0] - text_len - visual_len, width), F32)
    tokens = jnp.concatenate([tokens, blank], 0)
    hidden_ref[text_len:, :] = tokens
    low_ref[text_len:, :] = tokens.astype(BF16)
    for out, copy in copies:
        if out == 0:
            copy.wait()
    low = low_ref[...]
    turned_ref[...] = low.T
    for n in range(3):
        lanes = slice(n * width, (n + 1) * width)
        values = dot_nn(low, qkv_w_ref[:, lanes])
        qkv_ref[:, lanes] = (values * 0.125 if n == 0 else values).astype(BF16)


def first_rows(place, parts, layout, text, visual, order, lines, rows, proj_rows, moment_rows):
    devices = lax.axis_size("dp") * lax.axis_size("ffn")
    width = text.shape[1]
    channels = visual.shape[1]
    entries = place_entries(parts, layout)
    vmem = pl.BlockSpec(memory_space=pltpu.VMEM)
    shapes = [
        ((width, 3 * width), BF16),
        ((proj_rows, width), BF16),
        ((rows, width), F32),
        ((width, rows), BF16),
        ((rows, 3 * width), BF16),
        ((visual.shape[0], channels), BF16),
        ((2, channels), F32),
    ]
    return pl.pallas_call(
        functools.partial(first_kernel, entries, place_bits(parts), devices),
        in_specs=[pl.BlockSpec(memory_space=pltpu.SMEM)]
        + [pl.BlockSpec(memory_space=pl.ANY)] * len(parts)
        + [vmem] * 4,
        out_specs=[vmem] * len(shapes),
        out_shape=[jax.ShapeDtypeStruct(*shape) for shape in shapes],
        scratch_shapes=[
            pltpu.VMEM((moment_rows * devices, width), BF16),
            pltpu.VMEM((rows, width), BF16),
            pltpu.SemaphoreType.DMA((len(entries),)),
        ],
        compiler_params=pltpu.CompilerParams(vmem_limit_bytes=LIMIT),
        cost_estimate=cost(0, 25_000_000),
        name="first_rows",
    )(
        place,
        *[block for block, _, _ in parts],
        text,
        visual,
        order,
        lines,
    )


def store_blocks(mine_ref, away_ref, place, store):
    quads = mine_ref.shape[0]
    core, quad = place % 2, place // 2
    for bit in range(2):

        @pl.when(core == bit)
        def _(bit=bit):
            for dp in range(2 * quads):
                ref = mine_ref if dp % 2 == bit else away_ref
                store(ref, (dp // 2) ^ quad, dp)


def feed_kernel(entries, bits, length, ffn, place_ref, *refs):
    parts, refs = refs[: len(bits)], refs[len(bits) :]
    inputs, (lines_ref, inner_b_ref), refs = refs[:3], refs[3:5], refs[5:]
    results, (scale_ref, total_ref, sums_ref, inner_sums_ref), refs = refs[:3], refs[3:7], refs[7:]
    mine_ref, away_ref, last_ref = refs[:3]
    outer_w_ref, inner_w_ref, act_ref, slope_ref, first_ref, low_ref = refs[3:9]
    first_turned, low_turned = refs[9:11]
    mixed_ref, hidden_ref, ct_ref, normed_ref, out_w_ref, output_ref = refs[11:17]
    sems, in_sems, out_sems = refs[17:]
    step = pl.program_id(0)
    width = hidden_ref.shape[1]
    outs = (out_w_ref, outer_w_ref, inner_w_ref)
    fetch = [
        pltpu.make_async_copy(source, target, in_sems.at[n])
        for n, (source, target) in enumerate(zip(inputs, (mixed_ref, hidden_ref, ct_ref)))
    ]
    leave = [
        pltpu.make_async_copy(source, target, out_sems.at[n])
        for n, (source, target) in enumerate(zip((normed_ref, out_w_ref, output_ref), results))
    ]
    gain1, bias1, outer_b, gain2, bias2 = [lines_ref[n : n + 1, :] for n in range(5)]

    @pl.when(step == 0)
    def _():
        copies = part_copies(entries, bits, place_ref[0], parts, outs, sems)
        square = [copy for entry, copy in zip(entries, copies) if entry[3] == 0]
        now = [copy for entry, copy in zip(entries, copies) if entry[3] > 0 and entry[4] == 0]
        later = [copy for entry, copy in zip(entries, copies) if entry[3] > 0 and entry[4] > 0]
        for copy in [fetch[0]] + square + [fetch[1]] + now:
            copy.start()
        for copy in [fetch[0]] + square:
            copy.wait()
        for copy in later + [fetch[2], leave[1]]:
            copy.start()
        attended = dot_nn(mixed_ref[...], out_w_ref[...])
        fetch[1].wait()
        normed, scale = norm_stats(hidden_ref[...] + attended)
        first = normed * gain1 + bias1
        normed_ref[...] = normed
        scale_ref[...] = scale
        low = first.astype(BF16)
        first_ref[...] = low
        total_ref[...] = first + outer_b
        first_turned[...] = low.T
        leave[0].start()

    for index in range(ffn):

        @pl.when(step == index)
        def _(index=index):
            copies = part_copies(entries, bits, place_ref[0], parts, outs, sems)
            for entry, copy in zip(entries, copies):
                if entry[3] > 0 and entry[4] == index * width:
                    copy.wait()

    @pl.when(step < ffn)
    def _():
        rows = pl.ds(pl.multiple_of(step * width, width), width)
        inner = dot_nn(first_ref[...], inner_w_ref[rows, :]) + inner_b_ref[place_ref[1 + step]]
        root = 0.7978845608028654
        square = inner * inner
        half = 0.5 + 0.5 * jnp.tanh(inner * (root + (0.044715 * root) * square))
        act = inner * half
        slope = half + act * (1.0 - half) * (2 * root + (6 * 0.044715 * root) * square)
        slope_ref[step] = slope.astype(BF16)
        act = act.astype(BF16)
        act_ref[step] = act
        total_ref[...] += dot_nt(act, outer_w_ref[rows, :])

    @pl.when(step == ffn - 1)
    def _():
        fetch[2].wait()
        normed, scale = norm_stats(total_ref[...])
        output_ref[...] = (normed * gain2 + bias2).astype(BF16)[:length]
        leave[2].start()
        row = lax.broadcasted_iota(jnp.int32, (normed.shape[0], 1), 0)
        blank = jnp.zeros((normed.shape[0] - length, width), BF16)
        ct = jnp.concatenate([ct_ref[...], blank], 0).astype(F32)
        grad = norm_back(ct, normed, scale, gain2)
        total_ref[...] = grad
        low = grad.astype(BF16)
        low_ref[...] = low
        low_turned[...] = low.T
        sums_ref[0:1, :] = jnp.sum(ct * normed, 0, keepdims=True)
        sums_ref[1:2, :] = jnp.sum(ct, 0, keepdims=True)
        sums_ref[2:3, :] = jnp.sum(grad, 0, keepdims=True)

    @pl.when(step >= ffn)
    def _():
        f = step - ffn
        rows = pl.ds(pl.multiple_of(f * width, width), width)
        grad = dot_nn(low_ref[...], outer_w_ref[rows, :]) * slope_ref[f].astype(F32)
        inner_sums_ref[place_ref[1 + f]] = jnp.sum(grad, 0, keepdims=True)
        grad = grad.astype(BF16)
        total_ref[...] += dot_nt(grad, inner_w_ref[rows, :])
        inner = dot_nn(first_turned[...], grad).astype(BF16)
        outer = dot_nn(low_turned[...], act_ref[f]).astype(BF16)
        size = mine_ref.shape[3]

        def store(ref, slot, dp):
            ref[slot, 0, 0] = inner[dp * size : (dp + 1) * size]
            ref[slot, 1, 0] = outer[dp * size : (dp + 1) * size]
            if ref is away_ref:

                @pl.when(slot == away_ref.shape[0] - 1)
                def _():
                    last_ref[0, 0] = inner[dp * size : (dp + 1) * size]
                    last_ref[1, 0] = outer[dp * size : (dp + 1) * size]

        store_blocks(mine_ref, away_ref, place_ref[0], store)

    @pl.when(step == 2 * ffn - 1)
    def _():
        for copy in leave:
            copy.wait()


def feed_forward(place, feeds, mixed, hidden, lines, inner_b, ct, inner_rows):
    parts, entries = [], []
    for some, layout in feeds:
        for part, *entry in place_entries(some, layout):
            entries.append((part + len(parts), *entry))
        parts += some
    entries.sort(key=lambda entry: (entry[3] > 0, entry[4], -entry[3]))
    rows, width = hidden.shape
    ffn, _, columns = inner_b.shape
    quads = lax.axis_size("dp") // 2
    square = whole((rows, width))
    back = lambda i: jnp.maximum(i - ffn, 0)
    block = pl.BlockSpec((quads, 2, 1, inner_rows, columns), lambda i: (0, 0, back(i), 0, 0))
    blocks = jax.ShapeDtypeStruct((quads, 2, ffn, inner_rows, columns), BF16)
    last = pl.BlockSpec((2, 1, inner_rows, columns), lambda i: (0, back(i), 0, 0))
    smem = pl.BlockSpec(memory_space=pltpu.SMEM)
    shapes = [
        ((rows, width), F32),
        ((width, width), BF16),
        (ct.shape, BF16),
        ((rows, 1), F32),
        ((rows, width), F32),
        ((3, width), F32),
        ((ffn, 1, columns), F32),
    ]
    anywhere = pl.BlockSpec(memory_space=pl.ANY)
    return pl.pallas_call(
        functools.partial(feed_kernel, entries, place_bits(parts), ct.shape[0], ffn),
        grid=(2 * ffn,),
        in_specs=[smem]
        + [anywhere] * (len(parts) + 3)
        + [whole(lines.shape), whole(inner_b.shape)],
        out_specs=[anywhere] * 3
        + [whole((rows, 1)), square, whole((3, width))]
        + [whole((ffn, 1, columns)), block, block, last],
        out_shape=[jax.ShapeDtypeStruct(*shape) for shape in shapes]
        + [blocks, blocks, jax.ShapeDtypeStruct((2, ffn, inner_rows, columns), BF16)],
        scratch_shapes=[
            pltpu.VMEM((ffn * width, columns), BF16),
            pltpu.VMEM((ffn * width, columns), BF16),
            pltpu.VMEM((ffn, rows, columns), BF16),
            pltpu.VMEM((ffn, rows, columns), BF16),
            pltpu.VMEM((rows, width), BF16),
            pltpu.VMEM((rows, width), BF16),
            pltpu.VMEM((width, rows), BF16),
            pltpu.VMEM((width, rows), BF16),
            pltpu.VMEM((rows, width), BF16),
            pltpu.VMEM((rows, width), F32),
            pltpu.VMEM(ct.shape, BF16),
            pltpu.VMEM((rows, width), F32),
            pltpu.VMEM((width, width), BF16),
            pltpu.VMEM(ct.shape, BF16),
            pltpu.SemaphoreType.DMA((len(entries),)),
            pltpu.SemaphoreType.DMA((3,)),
            pltpu.SemaphoreType.DMA((3,)),
        ],
        compiler_params=pltpu.CompilerParams(vmem_limit_bytes=LIMIT),
        cost_estimate=cost(0, 100_000_000),
        name="feed_forward",
    )(
        place,
        *[part for part, _, _ in parts],
        mixed,
        hidden,
        ct,
        lines,
        inner_b,
    )


def norm_kernel(
    grad_ref, normed_ref, scale_ref, lines_ref, w_ref, out_ref, low_ref, mix_ref, sums_ref
):
    grad, normed = grad_ref[...], normed_ref[...]
    attn = norm_back(grad, normed, scale_ref[...], lines_ref[0:1, :])
    out_ref[...] = attn
    low = attn.astype(BF16)
    low_ref[...] = low
    mix_ref[...] = dot_nt(low, w_ref[...]).astype(BF16)
    sums_ref[0:1, :] = jnp.sum(grad * normed, 0, keepdims=True)
    sums_ref[1:2, :] = jnp.sum(grad, 0, keepdims=True)


def norm_rows(grad, normed, scale, lines, out_w):
    rows, width = grad.shape
    low = jax.ShapeDtypeStruct((rows, width), BF16)
    return pl.pallas_call(
        norm_kernel,
        out_shape=[
            jax.ShapeDtypeStruct((rows, width), F32),
            low,
            low,
            jax.ShapeDtypeStruct((2, width), F32),
        ],
        compiler_params=pltpu.CompilerParams(vmem_limit_bytes=LIMIT),
        cost_estimate=cost(0, 12_000_000),
        name="norm_rows",
    )(grad, normed, scale, lines, out_w)


def tail_kernel(text_len, place_ref, *refs):
    inputs, (order_ref, attn_ref, tokens_ref), refs = refs[:11], refs[11:14], refs[14:]
    outputs, buffers = refs[:3], refs[3:14]
    mine, away, in_sems, out_sems = refs[14:]
    low_ref, mixed_ref, attn_low_ref, qkv_w_ref, bn_ref = buffers[6:]
    names = (6, 0, 1, 2, 3, 4, 5, 7, 8, 9, 10)
    copies = {n: pltpu.make_async_copy(inputs[n], buffers[n], in_sems.at[n]) for n in names}
    for n in names:
        copies[n].start()
    visual_len = bn_ref.shape[0]
    width = attn_low_ref.shape[1]
    sent = []

    def spread(values, begin, n):
        values = values.astype(BF16)
        rows = values.shape[0] // (2 * mine.shape[0])

        def store(ref, slot, dp):
            ref[slot, begin : begin + rows, :] = values[dp * rows : (dp + 1) * rows]

        store_blocks(mine, away, place_ref[0], store)
        part = pl.ds(begin, rows)
        for k, ref in enumerate((mine, away)):
            copy = pltpu.make_async_copy(
                ref.at[:, part, :], outputs[k].at[:, part, :], out_sems.at[n, k]
            )
            copy.start()
            sent.append(copy)
        copy = pltpu.make_async_copy(
            away.at[away.shape[0] - 1, part, :], outputs[2].at[part, :], out_sems.at[n, 2]
        )
        copy.start()
        sent.append(copy)
        return begin + rows

    copies[6].wait()
    turned = low_ref[...]
    begin = 0
    grads = []
    for n in range(3):
        copies[2 * n].wait()
        copies[2 * n + 1].wait()
        grads.append(jnp.concatenate([buffers[2 * n][...], buffers[2 * n + 1][...]], 1))
        begin = spread(dot_nn(turned, grads[n]), begin, n)
    copies[7].wait()
    copies[8].wait()
    begin = spread(dot_nn(mixed_ref[...].T, attn_low_ref[...]), begin, 3)
    copies[9].wait()
    tokens = attn_ref[...]
    for n in range(3):
        lanes = slice(n * width, (n + 1) * width)
        tokens = tokens + dot_nt(grads[n][text_len:], qkv_w_ref[:, lanes])
    picker = picked(order_ref[...], visual_len)
    tokens = exact(picker, tokens[:visual_len], ((1,), (0,))).astype(BF16)
    tokens_ref[...] = tokens
    copies[10].wait()
    spread(dot_tn(bn_ref[...], tokens), begin, 4)
    for copy in sent:
        copy.wait()


def tail_rows(place, back, qkv_w, attn, attn_low, mixed, low, order, bn_rows, text_len):
    dp, ffn = lax.axis_size("dp"), lax.axis_size("ffn")
    rows, width = attn.shape
    visual_len, channels = bn_rows.shape
    size = 4 * (width // dp) + channels // dp
    vmem = pl.BlockSpec(memory_space=pltpu.VMEM)
    anywhere = pl.BlockSpec(memory_space=pl.ANY)
    inputs = [g for pair in back for g in pair] + [low, mixed, attn_low, qkv_w, bn_rows]
    rest = rows - text_len
    tail = pl.BlockSpec((rest, width), lambda *_: (text_len // rest, 0))
    blocks = jax.ShapeDtypeStruct((dp // 2, size, width), BF16)
    return pl.pallas_call(
        functools.partial(tail_kernel, text_len),
        grid=(1,),
        in_specs=[pl.BlockSpec(memory_space=pltpu.SMEM)]
        + [anywhere] * len(inputs)
        + [whole(order.shape), tail],
        out_specs=[whole((visual_len, width))] + [anywhere] * 3,
        out_shape=[jax.ShapeDtypeStruct((visual_len, width), BF16), blocks, blocks]
        + [jax.ShapeDtypeStruct((size, width), BF16)],
        scratch_shapes=[pltpu.VMEM(x.shape, BF16) for x in inputs]
        + [
            pltpu.VMEM(blocks.shape, BF16),
            pltpu.VMEM(blocks.shape, BF16),
            pltpu.SemaphoreType.DMA((len(inputs),)),
            pltpu.SemaphoreType.DMA((5, 3)),
        ],
        compiler_params=pltpu.CompilerParams(vmem_limit_bytes=LIMIT),
        cost_estimate=cost(0, 40_000_000),
        name="tail_rows",
    )(place, *inputs, order, attn)


def batch_kernel(tokens_ref, visual_ref, stats_ref, proj_ref, grad_bn_ref, sums_ref):
    grad_bn = dot_nt(proj_ref[...], tokens_ref[...]).T
    grad_bn_ref[...] = grad_bn
    normed = (visual_ref[...].astype(F32) - stats_ref[0:1, :]) * stats_ref[1:2, :]
    sums_ref[0:1, :] = jnp.sum(grad_bn, 0, keepdims=True)
    sums_ref[1:2, :] = jnp.sum(grad_bn * normed, 0, keepdims=True)


def batch_rows(tokens, visual, stats, proj):
    return pl.pallas_call(
        batch_kernel,
        out_shape=[
            jax.ShapeDtypeStruct(visual.shape, F32),
            jax.ShapeDtypeStruct((2, visual.shape[1]), F32),
        ],
        compiler_params=pltpu.CompilerParams(vmem_limit_bytes=LIMIT),
        cost_estimate=cost(0, 6_000_000),
        name="batch_rows",
    )(tokens, visual, stats, proj)


def text_kernel(*refs):
    dq, dk, dv = refs[0:2], refs[2:4], refs[4:6]
    qkv_w_ref, attn_ref, text_ref = refs[6:]
    width = text_ref.shape[1]
    total = attn_ref[...]
    for n, (low, high) in enumerate((dq, dk, dv)):
        grads = jnp.concatenate([low[...], high[...]], 1)
        total = total + dot_nt(grads, qkv_w_ref[:, n * width : (n + 1) * width])
    text_ref[...] = total


def text_rows(back, qkv_w, attn, text_len):
    width = attn.shape[1]
    step = text_len // 2
    grads = [g for pair in back for g in pair]
    return pl.pallas_call(
        text_kernel,
        grid=(2,),
        in_specs=[pl.BlockSpec((step, g.shape[1]), lambda i: (i, 0)) for g in grads]
        + [whole(qkv_w.shape), pl.BlockSpec((step, width), lambda i: (i, 0))],
        out_specs=pl.BlockSpec((step, width), lambda i: (i, 0)),
        out_shape=jax.ShapeDtypeStruct((text_len, width), F32),
        compiler_params=pltpu.CompilerParams(vmem_limit_bytes=LIMIT),
        cost_estimate=cost(0, 25_000_000),
        name="text_rows",
    )(*grads, qkv_w, attn)


def lane_rows(values, width):
    lanes = values.shape[1]
    pieces = pl.cdiv(lanes, width)
    if pieces * width > lanes:
        values = jnp.concatenate([values, jnp.zeros((1, pieces * width - lanes), F32)], 1)
    return [values[:, n * width : (n + 1) * width] for n in range(pieces)]


def sums_kernel(half_levels, bn_ref, one_ref, two_ref, inner_ref, *refs):
    out_ref = refs[-1]
    width = out_ref.shape[1]
    rows = []
    for n in range(bn_ref.shape[0]):
        rows += lane_rows(bn_ref[n : n + 1, :], width)
    for ref in (one_ref, two_ref):
        rows += [ref[n : n + 1, :] for n in range(ref.shape[0])]
    inner = [inner_ref[n] for n in range(inner_ref.shape[0])]
    rows += lane_rows(jnp.concatenate(inner, 1), width)
    halves = sum(ref[...] for ref in refs[:-1])
    tables, lane = [], 0
    for n, size in enumerate(half_levels):
        for row in (32 * n, 32 * n + 16):
            tables.append(halves[row : row + 16, lane : lane + size])
        lane += size
    tables = jnp.concatenate(tables, 1)
    blank = jnp.zeros((tables.shape[0], 256 - tables.shape[1]), F32)
    tables = jnp.concatenate([tables, blank], 1)
    group = width // 256
    for n in range(0, 12, group):
        rows.append(jnp.concatenate([tables[h : h + 1] for h in range(n, n + group)], 1))
    rows += [jnp.zeros((1, width), F32)] * (out_ref.shape[0] - len(rows))
    out_ref[...] = jnp.concatenate(rows, 0)


def pack_sums(bn_sums, one, two, inner, tables, half_levels):
    width = one.shape[1]
    rows = 2 * pl.cdiv(bn_sums.shape[1], width) + 5 + inner.size // width + 12 * 256 // width
    return pl.pallas_call(
        functools.partial(sums_kernel, half_levels),
        out_shape=jax.ShapeDtypeStruct((pl.cdiv(rows, 8) * 8, width), F32),
        cost_estimate=cost(0, 1_000_000),
        name="pack_sums",
    )(bn_sums, one, two, inner, *tables)


def finish_kernel(levels, count, *refs):
    left_ref, right_ref, grad_bn_ref, visual_ref, stats_ref, lines_ref = refs[:6]
    shift_ref, scale_ref, grad_ref, inner_ref = refs[6:10]
    vectors, tables = refs[10:15], refs[15:]
    total = left_ref[...] + right_ref[...]
    width = total.shape[1]
    channels = grad_bn_ref.shape[1]
    row = 0

    def take(lanes):
        nonlocal row
        pieces = pl.cdiv(lanes, width)
        row += pieces
        return jnp.concatenate([total[n : n + 1] for n in range(row - pieces, row)], 1)[:, :lanes]

    shift, scale = take(channels), take(channels)
    shift_ref[...] = shift.reshape(channels)
    scale_ref[...] = scale.reshape(channels)
    for ref in vectors:
        ref[...] = take(width).reshape(width)
    inner_ref[...] = take(inner_ref.shape[0]).reshape(inner_ref.shape[0])
    inverse = stats_ref[1:2, :]
    normed = (visual_ref[...].astype(F32) - stats_ref[0:1, :]) * inverse
    grad = grad_bn_ref[...] - shift * (1.0 / count) - normed * (scale * (1.0 / count))
    grad_ref[...] = lines_ref[0:1, :] * inverse * grad
    group = width // 256
    heads = []
    for n in range(12):
        lane = n % group * 256
        heads.append(total[row + n // group : row + n // group + 1, lane : lane + 256])
    heads = jnp.concatenate(heads, 0)
    begin = 0
    for ref, size in zip(tables, levels):
        ref[...] = heads[:, begin : begin + size]
        begin += size


def finish(left, right, grad_bn, visual, stats, lines, inner, levels, count):
    width = left.shape[1]
    channels = visual.shape[1]
    line = lambda n: jax.ShapeDtypeStruct((n,), F32)
    return pl.pallas_call(
        functools.partial(finish_kernel, levels, count),
        out_shape=[line(channels), line(channels), jax.ShapeDtypeStruct(visual.shape, F32)]
        + [line(inner)]
        + [line(width)] * 5
        + [jax.ShapeDtypeStruct((12, n), F32) for n in levels],
        cost_estimate=cost(0, 3_000_000),
        name="finish",
    )(left, right, grad_bn, visual, stats, lines)


def bias_kernel(rows_step, rel_ref, x_ref, y_ref, tab_ref, out_ref, unit_ref, level_ref):
    pairs = out_ref.shape[0]
    table = tab_ref[...]
    top = jnp.max(jnp.max(jnp.abs(table), 1, keepdims=True), 0, keepdims=True)
    top = jnp.maximum(top, 1e-30)
    unit_ref[...] = top * (2.0 / LEVELS)
    level = jnp.floor((table / top + 1.0) * (0.5 * LEVELS) + 0.5).astype(jnp.int32)
    level_ref[0] = level[:, :128]
    level_ref[1] = level[:, 128:]
    words = []
    for n in range(2):
        low = level_ref[n, pl.ds(0, pairs, stride=2), :]
        high = level_ref[n, pl.ds(1, pairs, stride=2), :]
        words.append(low + high * 65536)
    both = [jnp.broadcast_to(words[0][p : p + 1, :], (8, 128)) for p in range(pairs)]
    rel = [jnp.broadcast_to(words[1][p : p + 1, :], (8, 128)) for p in range(pairs)]

    def look(table, index):
        return jnp.take_along_axis(table, index, axis=1, mode="promise_in_bounds")

    for c in range(out_ref.shape[2] // 128):
        for r in range(rows_step // 8):
            rows, cols = pl.ds(r * 8, 8), pl.ds(c * 128, 128)
            rel_id = rel_ref[0, rows, cols] & 31
            x_id = x_ref[0, rows, cols] & 63
            y_id = (y_ref[0, rows, cols] & 63) + 64
            for p in range(pairs):
                out_ref[p, rows, cols] = (
                    look(rel[p], rel_id) + look(both[p], x_id) + look(both[p], y_id)
                )


def bias_words(rel, x, y, table, first, steps):
    step = 64
    rows = steps * step
    pairs = table.shape[0] // 2
    lanes = pl.cdiv(rel.shape[2], 128) * 128
    ids = pl.BlockSpec((1, step, lanes), lambda i: (0, i + first, 0))
    return pl.pallas_call(
        functools.partial(bias_kernel, step),
        grid=(steps,),
        in_specs=[ids, ids, ids, whole(table.shape)],
        out_specs=[pl.BlockSpec((pairs, step, lanes), lambda i: (0, i, 0)), whole((1, 1))],
        out_shape=[
            jax.ShapeDtypeStruct((pairs, rows, lanes), jnp.int32),
            jax.ShapeDtypeStruct((1, 1), F32),
        ],
        scratch_shapes=[pltpu.VMEM((2, table.shape[0], 128), jnp.int32)],
        compiler_params=pltpu.CompilerParams(vmem_limit_bytes=LIMIT),
        cost_estimate=cost(0, 6_000_000 * steps),
        name="bias_words",
    )(rel, x, y, table)


def lane_halves(rows):
    lane = lax.broadcasted_iota(jnp.int32, (rows, 128), 1)
    return lane < 64, lane >= 64


def attend_kernel(unit_ref, q_ref, k_ref, v_ref, row_ref, *refs):
    word_refs, (p_ref, o_ref, mask_ref) = refs[:-3], refs[-3:]

    @pl.when(pl.program_id(0) == 0)
    def _():
        row = row_ref[...].astype(F32)
        col = jnp.broadcast_to(row, (8, row.shape[1])).T[:, :1]
        mask_ref[...] = jnp.where(col == row, 0.0, NEG)

    unit = unit_ref[...]
    rows = q_ref.shape[0]
    halves = lane_halves(rows)
    q, k, v = q_ref[...], k_ref[...], v_ref[...]
    none = jnp.zeros_like(q)
    words = jnp.concatenate([ref[0][:, :rows] for ref in word_refs], 0)
    mask = mask_ref[...]
    mixed = jnp.zeros((rows, 128), F32)
    for h in range(2):
        scores = dot_nt(jnp.where(halves[h], q, none), k)
        word = (words & 0xFFFF) if h == 0 else lax.shift_right_logical(words, 16)
        scores = scores + word.astype(F32) * unit + mask
        expo = jnp.exp(scores - jnp.max(scores, -1, keepdims=True))
        probs = (expo * (1.0 / jnp.sum(expo, -1, keepdims=True))).astype(BF16)
        p_ref[h] = probs
        mixed = mixed + dot_nn(probs, jnp.where(halves[h], v, none))
    o_ref[...] = mixed.astype(BF16)


def attend(unit, qkv, words, segments):
    pairs = words[0].shape[0]
    rows = qkv.shape[0]
    col = [pl.BlockSpec((rows, 128), lambda p, n=n: (0, n * pairs + p)) for n in range(3)]
    flops = pairs * 4 * 2 * rows * rows * 128
    return pl.pallas_call(
        attend_kernel,
        grid=(pairs,),
        in_specs=[
            whole((1, 1)),
            col[0],
            col[1],
            col[2],
            whole((1, rows)),
        ]
        + [pl.BlockSpec((1,) + w.shape[1:], lambda p: (p, 0, 0)) for w in words],
        out_specs=[
            pl.BlockSpec((2, rows, rows), lambda p: (p, 0, 0)),
            pl.BlockSpec((rows, 128), lambda p: (0, p)),
        ],
        out_shape=[
            jax.ShapeDtypeStruct((2 * pairs, rows, rows), BF16),
            jax.ShapeDtypeStruct((rows, pairs * 128), BF16),
        ],
        scratch_shapes=[pltpu.VMEM((rows, rows), F32)],
        compiler_params=pltpu.CompilerParams(vmem_limit_bytes=LIMIT),
        cost_estimate=cost(flops, 40_000_000),
        name="attend",
    )(unit, qkv, qkv, qkv, segments, *words)


def attend_back_kernel(q_ref, k_ref, v_ref, g_ref, p_ref, ds_ref, dq_ref, dk_ref, dv_ref):
    rows = q_ref.shape[0]
    halves = lane_halves(rows)
    q, k, v, g = q_ref[...], k_ref[...], v_ref[...], g_ref[...]
    none = jnp.zeros_like(q)
    blank = jnp.zeros((rows, ds_ref.shape[2] - rows), BF16)
    dq = jnp.zeros((rows, 128), F32)
    dk, dv = dq, dq
    for h in range(2):
        low = p_ref[h]
        probs = low.astype(F32)
        weighted = probs * dot_nt(g, jnp.where(halves[h], v, none))
        ds = (weighted - probs * jnp.sum(weighted, -1, keepdims=True)).astype(BF16)
        ds_ref[h] = jnp.concatenate([ds, blank], 1)
        dq = dq + dot_nn(ds, jnp.where(halves[h], k, none))
        dv = dv + dot_tn(low, jnp.where(halves[h], g, none))
        dk = dk + dot_tn(ds, jnp.where(halves[h], q, none))
    dq_ref[...] = (dq * 0.125).astype(BF16)
    dk_ref[...] = dk.astype(BF16)
    dv_ref[...] = dv.astype(BF16)


def attend_back(qkv, grad, probs, first, pairs):
    every = probs.shape[0] // 2
    rows = qkv.shape[0]
    col = [pl.BlockSpec((rows, 128), lambda p, n=n: (0, n * every + p + first)) for n in range(3)]
    new = pl.BlockSpec((rows, 128), lambda p: (0, p))
    big = pl.BlockSpec((2, rows, rows), lambda p: (p + first, 0, 0))
    lanes = pl.cdiv(rows, 128) * 128
    out = jax.ShapeDtypeStruct((rows, pairs * 128), BF16)
    flops = pairs * 2 * 4 * 2 * rows * rows * 128
    return pl.pallas_call(
        attend_back_kernel,
        grid=(pairs,),
        in_specs=[col[0], col[1], col[2], col[0], big],
        out_specs=[pl.BlockSpec((2, rows, lanes), lambda p: (p, 0, 0)), new, new, new],
        out_shape=[jax.ShapeDtypeStruct((2 * pairs, rows, lanes), BF16), out, out, out],
        compiler_params=pltpu.CompilerParams(vmem_limit_bytes=LIMIT),
        cost_estimate=cost(flops, 8_000_000 * pairs),
        name="attend_back",
    )(qkv, qkv, qkv, grad, probs)


GROUP = 48


def table_kernel(first, levels, block_ref, count_ref, rel_ref, x_ref, y_ref, *refs):
    ds_refs, out_ref = refs[:-1], refs[-1]
    place = pl.program_id(0)
    step = rel_ref.shape[1]
    every = rel_ref.shape[2] // 128
    heads = sum(ref.shape[0] for ref in ds_refs)
    counts = (levels[1] // 2, levels[2] // 2, levels[0] // 2)

    @pl.when(place == 0)
    def _():
        out_ref[...] = jnp.zeros_like(out_ref)

    def group(r, start, blocks):
        width = blocks * 128
        level = lax.broadcasted_iota(jnp.int32, (16, width), 0).astype(F32).astype(BF16)
        one = jnp.ones((16, width), BF16)
        none = jnp.zeros((16, width), BF16)

        def one_hot(ids, count):
            wide = jnp.broadcast_to(ids, (16, width)).astype(BF16)
            return [jnp.where(wide == level + BF16(16 * t), one, none) for t in range(count // 16)]

        def halves(values, top):
            chosen = jnp.broadcast_to(top, (16, width)).astype(BF16) == one
            return [jnp.where(chosen, none, values), jnp.where(chosen, values, none)]

        rows = pl.ds(pl.multiple_of(r * GROUP, GROUP), GROUP)
        lanes = pl.ds(pl.multiple_of(start * 128, 128), width)
        values = [ref[:, rows, lanes] for ref in ds_refs]
        values.append(jnp.zeros((16 - heads, GROUP, width), BF16))
        values = jnp.transpose(jnp.concatenate(values, 0), (1, 0, 2))
        ids = [ref[0, rows, lanes].astype(F32) for ref in (x_ref, y_ref, rel_ref)]
        tops = [(i >= count).astype(F32) for i, count in zip(ids, counts)]
        rest = [i - top * count for i, top, count in zip(ids, tops, counts)]
        total = out_ref[...]
        for begin in range(0, GROUP, 2):
            lefts, rights = [], []
            for n in (begin, begin + 1):
                hot, split = [], []
                for top, low, count in zip(tops, rest, counts):
                    hot += one_hot(low[n : n + 1], count)
                    split += halves(values[n], top[n : n + 1])
                lefts.append(jnp.concatenate(split, 0))
                rights.append(jnp.concatenate(hot, 0))
            total = total + dot_nt(jnp.concatenate(lefts, 1), jnp.concatenate(rights, 1))
        out_ref[...] = total

    def body(r, _):
        index = (place + first) * (step // GROUP) + r
        count = jnp.maximum(count_ref[index], 2)
        start = jnp.minimum(block_ref[index], every - count)
        for blocks in range(2, every + 1):

            @pl.when(count == blocks)
            def _(blocks=blocks):
                group(r, start, blocks)

        return 0

    lax.fori_loop(0, step // GROUP, body, 0)


def table_sums(ranges, rel, x, y, ds, levels, first, steps):
    step = 2 * GROUP
    lanes = ds[0].shape[2]
    ids = pl.BlockSpec((1, step, lanes), lambda i, *_: (0, i + first, 0))
    return pl.pallas_call(
        functools.partial(table_kernel, first, levels),
        grid_spec=pltpu.PrefetchScalarGridSpec(
            num_scalar_prefetch=2,
            grid=(steps,),
            in_specs=[ids, ids, ids]
            + [pl.BlockSpec((d.shape[0], step, lanes), lambda i, *_: (0, i + first, 0)) for d in ds],
            out_specs=whole((96, sum(levels) // 2)),
        ),
        out_shape=jax.ShapeDtypeStruct((96, sum(levels) // 2), F32),
        compiler_params=pltpu.CompilerParams(vmem_limit_bytes=LIMIT),
        cost_estimate=cost(0, 8_000_000 * steps),
        name="table_sums",
    )(*ranges, rel, x, y, *ds)


def document_blocks(segments, rows):
    length = segments.shape[0]
    first = segments[0:rows:GROUP]
    last = segments[jnp.minimum(jnp.arange(GROUP - 1, rows, GROUP), length - 1)]
    begin = jnp.sum(segments[None, :] < first[:, None], 1, dtype=jnp.int32)
    end = jnp.sum(segments[None, :] <= last[:, None], 1, dtype=jnp.int32)
    return begin // 128, (end + 127) // 128 - begin // 128


def norm_stats(values):
    center = values - jnp.mean(values, -1, keepdims=True)
    scale = lax.rsqrt(jnp.mean(center * center, -1, keepdims=True) + EPS)
    return center * scale, scale


def norm_back(grad, normed, scale, gain):
    scaled = grad * gain
    return scale * (
        scaled
        - jnp.mean(scaled, -1, keepdims=True)
        - normed * jnp.mean(scaled * normed, -1, keepdims=True)
    )


def on_device(
    text_hidden,
    visual_maps,
    patch_order,
    segment_ids,
    rel_bucket,
    x_bucket,
    y_bucket,
    bn_scale,
    bn_shift,
    vis_proj,
    w_query,
    w_key,
    w_value,
    w_output,
    rel_table,
    x_table,
    y_table,
    first_gain,
    first_bias,
    w_inner,
    b_inner,
    w_outer,
    b_outer,
    second_gain,
    second_bias,
    cotangent,
):
    heads = rel_table.shape[1]
    pairs = heads // 2
    visual_len = patch_order.shape[1]
    length = segment_ids.shape[1]
    text_len = length - visual_len
    width = w_query.shape[1]
    dp, ffn = lax.axis_size("dp"), lax.axis_size("ffn")
    place = lax.axis_index("dp")
    devices = dp * ffn
    rows = pl.cdiv(length, 64) * 64
    count = visual_maps.shape[0] * devices
    levels = (rel_table.shape[0], x_table.shape[0], y_table.shape[0])

    inner_rows, columns = w_inner.shape
    outer_shard = w_outer.T
    steps = rows // 64

    plain = columns == width
    early = plain and dp == 8
    here = lax.axis_index("ffn")
    packed, sizes = pack_first(
        w_query,
        w_key,
        w_value,
        vis_proj,
        visual_maps,
        (w_output, outer_shard, w_inner) if early else (),
    )
    first_set = Gather(packed[0], sizes)
    wide_shards = packed[1] if early else jnp.concatenate([outer_shard, w_inner], 0)
    if early:
        late_set = Gather(packed[2], [w_output.shape[0]], 2 * inner_rows)
    elif plain:
        late_set = Gather(
            jnp.concatenate([w_output, wide_shards], 0), [w_output.shape[0], inner_rows, inner_rows]
        )
    else:
        late_set = Gather(w_output, [w_output.shape[0]])
        wide_set = Gather(wide_shards, [inner_rows, inner_rows])

    first_set.own, wide_shards = epoch(first_set.own, wide_shards)
    first_set.along_ffn()
    wides = [wide_shards]
    if early:
        wides += [send_dp(wide_shards, 2), send_dp(wide_shards, 4)]
    tables = jnp.concatenate([x_table, y_table, rel_table], 0).T
    tables = jnp.pad(tables, ((0, 0), (0, 256 - tables.shape[1])))
    cut = steps * 7 // 9
    words = [None] * 2
    ranges = document_blocks(segment_ids[0], rows)
    lines = jnp.stack([first_gain, first_bias, b_outer, second_gain, second_bias])
    inner_b = b_inner.reshape(ffn, 1, columns)
    segments = jnp.pad(segment_ids, ((0, 0), (0, rows - length)), constant_values=-1)
    bn_lines = jnp.stack([bn_scale, bn_shift])
    order = [(here - k + ffn) % ffn if early else jnp.int32(k) for k in range(ffn)]
    place = jnp.stack([place] + order).astype(jnp.int32)
    state, late, place, wides, tables, ranges, lines, inner_b, segments, bn_lines = epoch(
        first_set.state(),
        late_set.state(),
        place,
        wides,
        tables,
        ranges,
        lines,
        inner_b,
        segments,
        bn_lines,
    )
    first_set.hold(state)
    late_set.hold(late)

    first_set.order()
    first_set.near(3 * w_query.shape[0] * ffn)
    late_set.along_ffn(1, ffn - 1)
    words[0], unit = bias_words(rel_bucket, x_bucket, y_bucket, tables, 0, cut)
    state, late, words[0], tables = epoch(first_set.state(), late_set.state(), words[0], tables)
    first_set.hold(state)
    late_set.hold(late)

    first_set.diagonal()
    late_set.along_ffn(ffn - 1)
    state, late, tables = epoch(first_set.state(), late_set.state(), tables)
    first_set.hold(state)
    late_set.hold(late)

    late_set.order()
    first_set.across()
    state, late = epoch(first_set.state(), late_set.state())
    first_set.hold(state)
    late_set.hold(late)

    late_rows = w_output.shape[0] * ffn
    late_set.near(late_rows + (inner_rows if early else ffn * inner_rows) if plain else 0)
    if early:
        wides += [send_dp(wide, 1) for wide in wides[:2]]
    layout, row = [], 0
    for n, size in enumerate(first_set.rows):
        layout.append((row, size * ffn, max(n - 2, 0), 0, n * width if n < 3 else 0))
        row += size * ffn
    qkv_full, proj_full, hidden, lowered, qkv, bn_rows, bn_stats = first_rows(
        place,
        first_set.parts(),
        layout,
        text_hidden,
        visual_maps,
        patch_order,
        bn_lines,
        rows,
        vis_proj.shape[0] * devices,
        first_set.rows[-1],
    )
    qkv, tables = epoch(qkv, tables)
    words[1], _ = bias_words(rel_bucket, x_bucket, y_bucket, tables, cut, steps - cut)
    qkv, state, words[1], wides = epoch(qkv, late_set.state(), words[1], wides)
    late_set.hold(state)

    late_set.diagonal()
    if early:
        wides.append(send_dp(wides[1], 4))
    probs, mixed = attend(unit, qkv, words, segments)
    probs, mixed, state, wides = epoch(probs, mixed, late_set.state(), wides)
    late_set.hold(state)
    late_set.across()
    layout = [(0, late_rows, 0, 0, 0)]
    shift = late_rows
    parts = late_set.parts()
    if not plain:
        parts = [(block, bits, 0) for block, bits, _ in parts]
        wide_set.along_ffn()
        wide_set.order()
        wide_set.near(0)
        wide_set.diagonal()
        wide_set.across()
        shift = 0
    wide_layout = [
        (shift + (n * ffn + f) * inner_rows, inner_rows, 1 + n, f * width, 0)
        for n in range(2)
        for f in range(ffn)
    ]
    feeds = [(parts, layout + wide_layout if plain else layout)]
    if not plain:
        feeds.append((wide_set.parts(), wide_layout))
    if early:
        near_layout = [(n * inner_rows, inner_rows, 1 + n, 0, 0) for n in range(2)]
        far_layout = [
            (late_rows + (2 * k - 2 + n) * inner_rows, inner_rows, 1 + n, k * width, 0)
            for k in range(1, ffn)
            for n in range(2)
        ]
        own, from_x, from_y, other, other_x, from_xy = wides
        crossed = [send_dp(from_y, 1), send_dp(from_xy, 1)]
        blocks = [own, other, from_x, other_x, from_y, crossed[0], from_xy, crossed[1]]
        feeds = [
            (parts, layout + far_layout),
            ([(block, bits, 0) for bits, block in enumerate(blocks)], near_layout),
        ]
    (
        first_n,
        output_full,
        output,
        first_r,
        grad_first,
        sums_two,
        inner_sums,
        mine,
        away,
        last,
    ) = feed_forward(place, feeds, mixed, hidden, lines, inner_b, cotangent, inner_rows)

    def wide_far(value, index):
        return pick(value, (here - index + ffn) % ffn if early else index, 1)

    wide = Scatter(mine, away, wide_far)
    wide.ahead(last)
    state, grad_first = epoch(wide.held(), grad_first)
    wide.hold(state)
    wide.near()
    wide.core()
    grad_attn, attn_low, grad_mixed, sums_one = norm_rows(
        grad_first, first_n, first_r, lines, output_full
    )
    half = pairs // 3
    back_low = attend_back(qkv, grad_mixed, probs, 0, half)
    state, back_low, qkv = epoch(wide.held(), back_low, qkv)
    wide.hold(state)
    wide.prepare()
    wide.blocks, qkv = epoch(wide.blocks, qkv)

    wide.quads()
    back_high = attend_back(qkv, grad_mixed, probs, half, pairs - half)
    back = list(zip(back_low[1:], back_high[1:]))
    tokens_grad, mine, away, last = tail_rows(
        place, back, qkv_full, grad_attn, attn_low, mixed, lowered, patch_order, bn_rows, text_len
    )
    ds = (back_low[0], back_high[0])
    wide.blocks, mine, away, last, ds, tokens_grad = epoch(
        wide.blocks, mine, away, last, ds, tokens_grad
    )

    def tail_far(value, index):
        size = 4 * (width // dp)
        square = pick(value[:size].reshape(4, ffn, -1, width), index, 1)
        return jnp.concatenate(
            [square.reshape(-1, width), pick(value[size:].reshape(ffn, -1, width), index, 0)], 0
        )

    groups = rows // (2 * GROUP)
    cuts = [0, groups]
    sums = []

    def tables(ds):
        n = len(sums)
        return sums + [
            table_sums(
                ranges, rel_bucket, x_bucket, y_bucket, ds, levels, cuts[n], cuts[n + 1] - cuts[n]
            )
        ]

    tail = Scatter(mine, away, tail_far)
    tail.ahead(last)
    wide.join()
    state, wide.value, tokens_grad = epoch(tail.held(), wide.value, tokens_grad)
    tail.hold(state)
    tail.near()
    tail.core()
    wide.along_ffn([1])
    grad_bn, bn_sums = batch_rows(tokens_grad, visual_maps, bn_stats, proj_full)
    state, bn_sums, ds, wide.pieces = epoch(tail.held(), bn_sums, ds, wide.pieces)
    tail.hold(state)
    tail.prepare()
    tail.blocks, ds = epoch(tail.blocks, ds)

    tail.quads()
    wide.along_ffn(range(2, ffn))
    sums = tables(ds)
    tail.blocks, sums, back, wide.pieces = epoch(tail.blocks, sums, back, wide.pieces)

    tail.join()
    tail.along_ffn([1])
    total = Sum(
        pack_sums(
            bn_sums,
            sums_one,
            sums_two,
            inner_sums,
            sums,
            (levels[1] // 2, levels[2] // 2, levels[0] // 2),
        )
    )
    for _ in range(ffn.bit_length() - 1):
        total.step()
    wide_sum = wide.total()
    state, total.values, back = epoch(tail.held(), total.values, back)
    tail.hold(state)
    tail.along_ffn(range(2, ffn))
    while len(total.steps) > 1:
        total.step()
    text_grad = text_rows(back, qkv_full, grad_attn, text_len)
    other = total.steps[0](total.values)
    (
        shift_grad,
        scale_grad,
        visual_grad,
        inner_grad,
        gain_one,
        bias_one,
        gain_two,
        bias_two,
        outer_grad,
        x_grad,
        y_grad,
        rel_grad,
    ) = finish(
        total.values,
        other,
        grad_bn,
        visual_maps,
        bn_stats,
        bn_lines,
        b_inner.shape[0],
        (levels[1], levels[2], levels[0]),
        count,
    )
    shards, row = [], 0
    for size in [w_query.shape[0]] * 4 + [vis_proj.shape[0]]:
        shards.append(sum(piece[row : row + size].astype(F32) for piece in tail.pieces))
        row += size
    return (
        output,
        text_grad,
        visual_grad,
        scale_grad.reshape(-1),
        shift_grad.reshape(-1),
        shards[4],
        shards[0],
        shards[1],
        shards[2],
        shards[3],
        rel_grad.T,
        x_grad.T,
        y_grad.T,
        gain_one.reshape(-1),
        bias_one.reshape(-1),
        wide_sum[0],
        inner_grad.reshape(-1),
        wide_sum[1].T,
        outer_grad.reshape(-1),
        gain_two.reshape(-1),
        bias_two.reshape(-1),
    )


def solution(mesh):
    rows = P(ALL, None)
    cube = P(ALL, None, None)
    return jax.shard_map(
        on_device,
        mesh=mesh,
        in_specs=(rows,) * 4
        + (cube,) * 3
        + (P(),) * 2
        + (rows,) * 5
        + (P(),) * 5
        + (P("dp", "ffn"), P(), P("ffn", "dp"))
        + (P(),) * 3
        + (rows,),
        out_specs=(rows,) * 3
        + (P(),) * 2
        + (rows,) * 5
        + (P(),) * 5
        + (P("dp", "ffn"), P(), P("ffn", "dp"))
        + (P(),) * 3,
        check_vma=False,
    )
```
